32 devices in a mesh: dp: 8 (over y, x, core), mp: 4 (over z).
Axes of the slice: x: 2, y: 2, z: 4, core: 2. Of those that a mesh axis runs over, the one named last changes fastest.
Arguments:
- slot_owner: int32 [512, 2, 32, 1], P('dp'), may hold values from 0 to 7; in each aligned block of 4096 rows (0 to 4095, 4096 to 8191, ..., all dimensions but the last counted through in order) at most 1024 rows name the same one
- slot_row: int32 [512, 2, 32], P('dp'), may hold values from 0 to 4095
- slot_count: int32 [512, 2], P('dp'), may hold values from 1 to 32
- item_qid: int32 [512], replicated, may hold values from 0 to 4095
- positive: int32 [512], P('dp'), may hold values from 0 to 511, each once
- log_prior: float32 [4096], replicated, may hold values from -12 to -6
- embedding: float32 [32768, 128], P('dp'), may hold values from -6 to 6
- embedding_mom: float32 [32768, 128], P('dp'), may hold values from -1.1444092e-05 to 1.1444092e-05
- embedding_avg: float32 [32768, 128], P('dp'), may hold values from -6 to 6
- w_in: float32 [2, 128, 256], replicated, may hold values from -0.5 to 0.5
- w_in_mom: float32 [2, 128, 256], replicated, may hold values from -3.8146973e-05 to 3.8146973e-05
- w_in_avg: float32 [2, 128, 256], replicated, may hold values from -0.5 to 0.5
- norm_gain: float32 [2, 256], replicated, may hold values from 0.5 to 1.5
- norm_gain_mom: float32 [2, 256], replicated, may hold values from -0.00012207031 to 0.00012207031
- norm_gain_avg: float32 [2, 256], replicated, may hold values from 0.5 to 1.5
- w_qkv: float32 [2, 256, 3, 512], P(None, None, None, 'mp'), may hold values from -0.375 to 0.375
- w_qkv_mom: float32 [2, 256, 3, 512], P(None, None, None, 'mp'), may hold values from -3.8146973e-05 to 3.8146973e-05
- w_qkv_avg: float32 [2, 256, 3, 512], P(None, None, None, 'mp'), may hold values from -0.375 to 0.375
- w_out: float32 [2, 512, 256], P(None, 'mp'), may hold values from -0.5 to 0.5
- w_out_mom: float32 [2, 512, 256], P(None, 'mp'), may hold values from -3.8146973e-05 to 3.8146973e-05
- w_out_avg: float32 [2, 512, 256], P(None, 'mp'), may hold values from -0.5 to 0.5
- w_one: float32 [2, 256, 1024], P(None, None, 'mp'), may hold values from -0.375 to 0.375
- w_one_mom: float32 [2, 256, 1024], P(None, None, 'mp'), may hold values from -3.8146973e-05 to 3.8146973e-05
- w_one_avg: float32 [2, 256, 1024], P(None, None, 'mp'), may hold values from -0.375 to 0.375
- w_two: float32 [2, 1024, 512], P(None, 'mp'), may hold values from -0.1875 to 0.1875
- w_two_mom: float32 [2, 1024, 512], P(None, 'mp'), may hold values from -3.8146973e-05 to 3.8146973e-05
- w_two_avg: float32 [2, 1024, 512], P(None, 'mp'), may hold values from -0.1875 to 0.1875
- w_three: float32 [2, 512, 256], replicated, may hold values from -0.25 to 0.25
- w_three_mom: float32 [2, 512, 256], replicated, may hold values from -3.8146973e-05 to 3.8146973e-05
- w_three_avg: float32 [2, 512, 256], replicated, may hold values from -0.25 to 0.25
Outputs:
- loss_sum: float32 [], replicated
- clip_norm: float32 [], replicated
- new_embedding: float32 [32768, 128], P('dp')
- new_embedding_mom: float32 [32768, 128], P('dp')
- new_embedding_avg: float32 [32768, 128], P('dp')
- new_w_in: float32 [2, 128, 256], replicated
- new_w_in_mom: float32 [2, 128, 256], replicated
- new_w_in_avg: float32 [2, 128, 256], replicated
- new_norm_gain: float32 [2, 256], replicated
- new_norm_gain_mom: float32 [2, 256], replicated
- new_norm_gain_avg: float32 [2, 256], replicated
- new_w_qkv: float32 [2, 256, 3, 512], P(None, None, None, 'mp')
- new_w_qkv_mom: float32 [2, 256, 3, 512], P(None, None, None, 'mp')
- new_w_qkv_avg: float32 [2, 256, 3, 512], P(None, None, None, 'mp')
- new_w_out: float32 [2, 512, 256], P(None, 'mp')
- new_w_out_mom: float32 [2, 512, 256], P(None, 'mp')
- new_w_out_avg: float32 [2, 512, 256], P(None, 'mp')
- new_w_one: float32 [2, 256, 1024], P(None, None, 'mp')
- new_w_one_mom: float32 [2, 256, 1024], P(None, None, 'mp')
- new_w_one_avg: float32 [2, 256, 1024], P(None, None, 'mp')
- new_w_two: float32 [2, 1024, 512], P(None, 'mp')
- new_w_two_mom: float32 [2, 1024, 512], P(None, 'mp')
- new_w_two_avg: float32 [2, 1024, 512], P(None, 'mp')
- new_w_three: float32 [2, 512, 256], replicated
- new_w_three_mom: float32 [2, 512, 256], replicated
- new_w_three_avg: float32 [2, 512, 256], replicated
The draws below stay inside these ranges and needn't reach their ends.
Inputs may be any that keep to these rules, and one draw needn't show every extreme that they name: `slot_owner`: in the rows of one index of dp (4096 slots) no owner is named more than 1024 times, a bound that some block reaches. `positive`: each pair index appears once.
All inputs are finite; a program needn't handle non-finite values.
Results may differ from the reference program's by a relative error of at most 0.028.
Values may be sent and summed in bfloat16 or wider, within the bound.
A program may use at most 128 MiB of HBM per device.

```python
import math
import jax
import jax.numpy as jnp
import numpy as np
from jax import lax

E = 128
W = 256
H = 8
DH = 64
F1 = 1024
F2 = 512
S = 32
LOGQ_N = 4096
ROWS_DEV = 4096
PAIRS = 512
ROWS = 32768
REQ = 4096
CAP = 1024
N_DP = 8


def set_ends(values, stream_key, low, high):
    shape = values.shape
    index_at = [jax.random.randint(jax.random.fold_in(stream_key, axis), (), 0, shape[axis]) for axis in range(len(shape))]
    values = values.at[tuple(index_at)].set(low)
    longest = shape.index(max(shape))
    index_at[longest] = (index_at[longest] + 1) % shape[longest]
    return values.at[tuple(index_at)].set(high)


def level_of(key, dims, split, least, high):
    def one(dim, parts):
        heights = jax.random.uniform(jax.random.fold_in(jax.random.fold_in(key, 6), dim), (parts,), jnp.float32, least / len(split), high / len(split))
        return jnp.repeat(jnp.exp(heights), dims[dim] // parts).reshape((-1,) + (1,) * (len(dims) - dim - 1))

    level = one(*split[0])
    for cut in split[1:]:
        level = level * one(*cut)
    return level


def rank_table(amount, lean):
    loads = [(1 << 20) // math.isqrt(grade ** lean) + 1 for grade in range(1, amount + 1)]
    spread = 1 + sum(loads) // (1 << 30)
    return np.cumsum(np.array([max(1, weight // spread) for weight in loads]))


def ranked_ids(rng, shape, count, lean):
    grid = rank_table(count, lean)
    pick = jax.random.randint(jax.random.fold_in(rng, 1), shape, 0, int(grid[count - 1]))
    grade = jnp.searchsorted(jnp.asarray(grid, jnp.int32), pick, side="right")
    return jax.random.permutation(jax.random.fold_in(rng, 2), count)[grade].astype(jnp.int32)


def assign_block(key, own, number, rows, number_of, top, limit, lean):
    sequence = jax.random.permutation(key, number_of)
    packed, usual = portions_of(number_of, rows * top, limit, lean, True), portions_of(number_of, rows * top, limit, lean, False)
    places = jnp.arange(number_of)

    def named(tallies, turn):
        used = int((tallies > 0).sum())
        fixed = max(1, used // 4)
        shifted = fixed + (places - fixed + turn * (used - fixed)) % max(1, number_of - fixed)
        return jnp.zeros((number_of,), jnp.int32).at[sequence[jnp.where(places < fixed, places, shifted)]].set(jnp.asarray(tallies, jnp.int32))

    tallies = jnp.where(number % 4 == 0, named(packed, number // 4), named(usual, number - number // 4 - 1))
    mixed = jax.random.permutation(jax.random.fold_in(own, 3), number_of)
    giver, receiver = mixed[0:number_of // 2 * 2:2], mixed[1:number_of // 2 * 2:2]
    slack = jnp.minimum(tallies[giver] - 1, limit - tallies[receiver]) // 2
    slack = jnp.where((giver == sequence[0]) | (receiver == sequence[0]) | (tallies[receiver] == 0), 0, jnp.maximum(slack, 0))
    shifted = jax.random.randint(jax.random.fold_in(own, 4), (number_of // 2,), 0, 1 << 20) % (slack + 1)
    tallies = tallies.at[giver].add(-shifted).at[receiver].add(shifted)
    items = jnp.searchsorted(jnp.cumsum(tallies), jnp.arange(rows * top), side="right").astype(jnp.int32)
    grid = items.reshape(top, rows).T
    grid = grid[jax.random.permutation(jax.random.fold_in(own, 1), rows)]
    turn = jax.random.randint(jax.random.fold_in(own, 2), (rows, 1), 0, top)
    return jnp.take_along_axis(grid, (jnp.arange(top)[None, :] + turn) % top, axis=1)


def portions_of(count, total, bound, lean, full):
    loads = [(1 << 20) // math.isqrt(rank ** lean) + 1 for rank in range(1, count + 1)]
    largest = bound if full else min(bound, max(-(-total // count), total * loads[0] // sum(loads)))
    least = 1 if total - largest >= count - 1 else 0
    given, rest = [largest] + [least] * (count - 1), total - largest - least * (count - 1)
    while rest > 0:
        free = [i for i in range(1, count) if given[i] < largest] or [i for i in range(1, count) if given[i] < bound]
        whole, left = sum([loads[i] for i in free]), rest
        for i in free:
            extra = min(bound - given[i], max(1, left * loads[i] // whole), rest)
            given[i] = given[i] + extra
            rest = rest - extra
    return np.array(given)


def normal_values(own_key, shape, width, most, split=(), held_as=jnp.bfloat16):
    drawn = width * jax.random.normal(own_key, shape, jnp.float32)
    if split:
        drawn = drawn * level_of(own_key, shape, split, -0.22, 0.18)
    return jnp.clip(drawn, -most, most).astype(held_as)


def setup_inputs(seed: int = 0) -> dict:
    key_list = jax.random.split(jax.random.key(seed), 31)
    slot_owner_keys = jax.random.split(jax.random.fold_in(key_list[0], 1), PAIRS * 2 * S // REQ)
    slot_owner_turns = jax.random.permutation(jax.random.fold_in(key_list[0], 3), PAIRS * 2 * S // REQ)
    slot_owner = jax.vmap(lambda own, number: assign_block(jax.random.fold_in(key_list[0], 2), own, number, REQ, N_DP, 1, CAP, 2))(slot_owner_keys, slot_owner_turns).reshape((PAIRS, 2, S, 1))
    slot_row = set_ends(ranked_ids(key_list[1], (PAIRS, 2, S), ROWS_DEV, 2), jax.random.fold_in(key_list[1], 3), 0, ROWS_DEV - 1).astype(jnp.int32)
    slot_count = set_ends(jax.random.randint(key_list[2], (PAIRS, 2), 1, S + 1), jax.random.fold_in(key_list[2], 1), 1, S).astype(jnp.int32)
    item_qid = set_ends(ranked_ids(key_list[3], (PAIRS,), LOGQ_N, 2), jax.random.fold_in(key_list[3], 3), 0, LOGQ_N - 1).astype(jnp.int32)
    positive = jax.random.permutation(key_list[4], PAIRS).astype(jnp.int32)
    log_prior = jnp.clip(jax.random.uniform(key_list[5], (LOGQ_N,), jnp.float32, -12.0, -6.0), -12.0, -6.0)
    embedding = normal_values(key_list[6], (ROWS, E), 1.0, 6.0, ((0, 8),), jnp.float32)
    embedding_mom = normal_values(key_list[7], (ROWS, E), 0.000002, 1.1444091796875e-05, ((0, 8),), jnp.float32)
    embedding_avg = normal_values(key_list[8], (ROWS, E), 1.0, 6.0, ((0, 8),), jnp.float32)
    w_in = normal_values(key_list[9], (2, E, W), E ** -0.5, 0.5, (), jnp.float32)
    w_in_mom = normal_values(key_list[10], (2, E, W), 0.000006, 3.814697265625e-05, (), jnp.float32)
    w_in_avg = normal_values(key_list[11], (2, E, W), E ** -0.5, 0.5, (), jnp.float32)
    norm_gain = jnp.clip(1.0 + 0.1 * jax.random.normal(key_list[12], (2, W), jnp.float32), 0.5, 1.5)
    norm_gain_mom = normal_values(key_list[13], (2, W), 0.00002, 0.00012207031, (), jnp.float32)
    norm_gain_avg = jnp.clip(1.0 + 0.1 * jax.random.normal(key_list[14], (2, W), jnp.float32), 0.5, 1.5)
    w_qkv = normal_values(key_list[15], (2, W, 3, H * DH), W ** -0.5, 0.375, ((3, 4),), jnp.float32)
    w_qkv_mom = normal_values(key_list[16], (2, W, 3, H * DH), 0.000006, 3.814697265625e-05, ((3, 4),), jnp.float32)
    w_qkv_avg = normal_values(key_list[17], (2, W, 3, H * DH), W ** -0.5, 0.375, ((3, 4),), jnp.float32)
    w_out = normal_values(key_list[18], (2, H * DH, W), (H * DH // 4) ** -0.5, 0.5, ((1, 4),), jnp.float32)
    w_out_mom = normal_values(key_list[19], (2, H * DH, W), 0.000006, 3.814697265625e-05, ((1, 4),), jnp.float32)
    w_out_avg = normal_values(key_list[20], (2, H * DH, W), (H * DH // 4) ** -0.5, 0.5, ((1, 4),), jnp.float32)
    w_one = normal_values(key_list[21], (2, W, F1), W ** -0.5, 0.375, ((2, 4),), jnp.float32)
    w_one_mom = normal_values(key_list[22], (2, W, F1), 0.000006, 3.814697265625e-05, ((2, 4),), jnp.float32)
    w_one_avg = normal_values(key_list[23], (2, W, F1), W ** -0.5, 0.375, ((2, 4),), jnp.float32)
    w_two = normal_values(key_list[24], (2, F1, F2), F1 ** -0.5, 0.1875, ((1, 4),), jnp.float32)
    w_two_mom = normal_values(key_list[25], (2, F1, F2), 0.000006, 3.814697265625e-05, ((1, 4),), jnp.float32)
    w_two_avg = normal_values(key_list[26], (2, F1, F2), F1 ** -0.5, 0.1875, ((1, 4),), jnp.float32)
    w_three = normal_values(key_list[27], (2, F2, W), F2 ** -0.5, 0.25, (), jnp.float32)
    w_three_mom = normal_values(key_list[28], (2, F2, W), 0.000006, 3.814697265625e-05, (), jnp.float32)
    w_three_avg = normal_values(key_list[29], (2, F2, W), F2 ** -0.5, 0.25, (), jnp.float32)
    return dict(slot_owner=slot_owner, slot_row=slot_row, slot_count=slot_count, item_qid=item_qid, positive=positive, log_prior=log_prior, embedding=embedding, embedding_mom=embedding_mom, embedding_avg=embedding_avg, w_in=w_in, w_in_mom=w_in_mom, w_in_avg=w_in_avg, norm_gain=norm_gain, norm_gain_mom=norm_gain_mom, norm_gain_avg=norm_gain_avg, w_qkv=w_qkv, w_qkv_mom=w_qkv_mom, w_qkv_avg=w_qkv_avg, w_out=w_out, w_out_mom=w_out_mom, w_out_avg=w_out_avg, w_one=w_one, w_one_mom=w_one_mom, w_one_avg=w_one_avg, w_two=w_two, w_two_mom=w_two_mom, w_two_avg=w_two_avg, w_three=w_three, w_three_mom=w_three_mom, w_three_avg=w_three_avg)


EPS = 1e-06
INV_TEMP = 20.0
CLIP_NORM = 0.1
ROW_RATE = 150000.0
GAIN_RATE = 8000.0
MATRIX_RATE = 600.0
MOMENTUM = 0.9
AVERAGE_DECAY = 0.6
HIGHEST = lax.Precision.HIGHEST

@jax.custom_vjp
def low(v):
    return lax.optimization_barrier(v.astype(jnp.bfloat16)).astype(jnp.float32)

@jax.custom_vjp
def low_back(v):
    return v

def low_keep(v):
    return (low(v), None)

def low_pass(kept, grad):
    return (grad,)

def back_keep(v):
    return (v, None)

def back_low(kept, grad):
    return (low(grad),)
low.defvjp(low_keep, low_pass)
low_back.defvjp(back_keep, back_low)

def rounded(value):
    return low(low_back(value))

def contract(spec, left, right):
    return jnp.einsum(spec, left, right, precision=HIGHEST)

def rms_norm(hidden, gains):
    return hidden * lax.rsqrt(lax.optimization_barrier(jnp.mean(hidden * hidden, -1, keepdims=True)) + EPS) * gains[None, :, None, :]

def unit_length(vector):
    return vector * lax.rsqrt(lax.optimization_barrier(jnp.sum(vector * vector, -1, keepdims=True)) + EPS)

def forward(params, slot_owner, slot_row, slot_count, item_qid, positive, log_prior):
    embedding, w_in, norm_gain, w_qkv, w_out, w_one, w_two, w_three = params
    pair_count, towers, slots = slot_row.shape
    row_ids = (slot_owner[..., 0] * ROWS_DEV + slot_row).astype(jnp.int32)
    embedded = low(embedding[row_ids])
    live_mask = (jnp.arange(slots)[None, None, :] < slot_count[:, :, None]).astype(jnp.float32)
    live_count = slot_count.astype(jnp.float32)
    hidden = low_back(contract('ptse,ted->ptsd', embedded, low(w_in)))
    normed = rounded(rms_norm(hidden, norm_gain))
    qkv = rounded(contract('ptsd,tdcf->ptscf', normed, low(w_qkv)))
    heads_all = qkv.reshape(pair_count, towers, slots, 3, H, DH)
    scores = contract('ptshd,ptrhd->pthsr', heads_all[:, :, :, 0], heads_all[:, :, :, 1]) * 0.125
    scores = low_back(jnp.where(live_mask[:, :, None, None, :] > 0, scores, -1000000000.0))
    attention = rounded(jax.nn.softmax(scores, -1))
    mixture = rounded(contract('pthsr,ptrhd->ptshd', attention, heads_all[:, :, :, 2]).reshape(pair_count, towers, slots, H * DH))
    branch = low_back(contract('ptsf,tfd->ptsd', mixture, low(w_out)))
    summed = hidden + branch
    pooled = rounded(lax.optimization_barrier(jnp.sum(summed * live_mask[..., None], 2)) / live_count[..., None])
    first_pre = low_back(contract('ptd,tdf->ptf', pooled, low(w_one)))
    act_one = rounded(jax.nn.gelu(first_pre))
    second_pre = low_back(contract('ptf,tfg->ptg', act_one, low(w_two)))
    act_two = rounded(jax.nn.gelu(second_pre))
    third_pre = low_back(contract('ptg,tgd->ptd', act_two, low(w_three)))
    vectors = rounded(unit_length(third_pre))
    prior = log_prior[item_qid]
    logits = low_back(INV_TEMP * jnp.dot(vectors[:, 0], vectors[:, 1].T, precision=HIGHEST) - prior[None, :])
    peak = lax.optimization_barrier(jnp.max(logits, 1, keepdims=True))
    log_total = peak[:, 0] + jnp.log(lax.optimization_barrier(jnp.sum(jnp.exp(logits - peak), 1)))
    picked = jnp.take_along_axis(logits, positive[:, None], 1)[:, 0]
    total = jnp.sum(log_total - picked)
    return (total / pair_count, total)

def update(weight, grad, moment, average, factor, rate):
    clipped = grad * factor
    moment_new = MOMENTUM * moment + clipped
    weight_new = weight - rate * (clipped + MOMENTUM * moment_new)
    average_new = AVERAGE_DECAY * average + (1.0 - AVERAGE_DECAY) * weight_new
    return [weight_new, moment_new, average_new]

def reference(slot_owner, slot_row, slot_count, item_qid, positive, log_prior, embedding, embedding_mom, embedding_avg, w_in, w_in_mom, w_in_avg, norm_gain, norm_gain_mom, norm_gain_avg, w_qkv, w_qkv_mom, w_qkv_avg, w_out, w_out_mom, w_out_avg, w_one, w_one_mom, w_one_avg, w_two, w_two_mom, w_two_avg, w_three, w_three_mom, w_three_avg):
    params = (embedding, w_in, norm_gain, w_qkv, w_out, w_one, w_two, w_three)
    states = ((embedding_mom, embedding_avg), (w_in_mom, w_in_avg), (norm_gain_mom, norm_gain_avg), (w_qkv_mom, w_qkv_avg), (w_out_mom, w_out_avg), (w_one_mom, w_one_avg), (w_two_mom, w_two_avg), (w_three_mom, w_three_avg))
    rates = (ROW_RATE, MATRIX_RATE, GAIN_RATE, MATRIX_RATE, MATRIX_RATE, MATRIX_RATE, MATRIX_RATE, MATRIX_RATE)

    def loss_of(*weights):
        return forward(weights, slot_owner, slot_row, slot_count, item_qid, positive, log_prior)
    mean_loss, pull, total = jax.vjp(loss_of, *params, has_aux=True)
    grads = pull(jnp.ones((), mean_loss.dtype))
    norm = jnp.sqrt(sum((jnp.sum(grad * grad) for grad in grads)))
    factor = jnp.minimum(1.0, CLIP_NORM / norm)
    done = []
    for weight, grad, pair_state, rate in zip(params, grads, states, rates):
        done.extend(update(weight, grad, pair_state[0], pair_state[1], factor, rate))
    return (total, norm, done[0], done[1], done[2], done[3], done[4], done[5], done[6], done[7], done[8], done[9], done[10], done[11], done[12], done[13], done[14], done[15], done[16], done[17], done[18], done[19], done[20], done[21], done[22], done[23])
```

```python
import functools

import jax
import jax.numpy as jnp
from jax import lax
from jax.experimental import pallas as pl
from jax.experimental.pallas import tpu as pltpu
from jax.sharding import PartitionSpec as P

DH = 64
EPS = 1e-06
INV_TEMP = 20.0
CLIP_NORM = 0.1
ROW_RATE = 150000.0
GAIN_RATE = 8000.0
MATRIX_RATE = 600.0
MOMENTUM = 0.9
AVERAGE_DECAY = 0.6

MESH = pl.DeviceIdType.MESH
LANES = 128
F32 = jnp.float32
BF16 = jnp.bfloat16
I32 = jnp.int32
VMEM = pl.BlockSpec(memory_space=pltpu.VMEM)
SMEM = pl.BlockSpec(memory_space=pltpu.SMEM)
DMA = pltpu.SemaphoreType.DMA


def nn(a, b):
    return lax.dot_general(a, b, (((1,), (0,)), ((), ())), preferred_element_type=F32)


def nt(a, b):
    return lax.dot_general(a, b, (((1,), (1,)), ((), ())), preferred_element_type=F32)


def tn(a, b):
    return lax.dot_general(a, b, (((0,), (0,)), ((), ())), preferred_element_type=F32)


def iota(shape, dim):
    return lax.broadcasted_iota(I32, shape, dim)


def split(value):
    high = value.astype(BF16)
    return high, (value - high.astype(F32)).astype(BF16)


def shape(dims, dtype):
    return jax.ShapeDtypeStruct(tuple(dims), dtype)


def params(limit, **more):
    return pltpu.CompilerParams(vmem_limit_bytes=limit << 20, **more)


def lists_of(owner, row, owners, capacity):
    chunks = owner.shape[0]
    width = owners * capacity
    his = width // LANES
    sub = iota((owners, LANES), 0)
    hot = [(owner[c : c + 1, :] == sub).astype(BF16) for c in range(chunks)]
    hots = jnp.concatenate([h.astype(F32) for h in hot], 0).astype(BF16)
    before = (iota((LANES, LANES), 0) < iota((LANES, LANES), 1)).astype(BF16)
    earlier = nn(hots, before)
    totals = nn(hots, jnp.ones((LANES, LANES), BF16))
    base = (sub * capacity).astype(F32)
    places = []
    for c in range(chunks):
        cut = slice(c * owners, (c + 1) * owners)
        at = hots[cut].astype(F32) * (earlier[cut] + base)
        here = jnp.sum(at, 0, keepdims=True).astype(I32)
        places.append(jnp.where(owner[c : c + 1, :] < owners, here, width))
        base = base + totals[cut]
    acc = jnp.zeros((his, 4 * LANES), F32)
    for c in range(chunks):
        place = places[c]
        value = row[c : c + 1, :]
        token = iota((1, LANES), 1) + c * LANES
        left = (lax.shift_right_logical(place, 7) == iota((his, LANES), 0)).astype(BF16)
        low = (place & 127) == iota((LANES, LANES), 0)
        parts = [lax.shift_right_logical(value, 6), value & 63, lax.shift_right_logical(token, 6), token & 63]
        right = jnp.concatenate([jnp.where(low, part.astype(F32), 0.0) for part in parts], 0)
        acc = acc + nt(left, right.astype(BF16))
    cuts = [acc[:, k * LANES : (k + 1) * LANES].astype(I32) for k in range(4)]
    return places, cuts[0] * 64 + cuts[1], cuts[2] * 64 + cuts[3]


def prep_kernel(owners, capacity, owner, row, own_owner, own_row, lists, inverse, own_place):
    per = capacity // LANES
    _, rows, tokens = lists_of(owner[...], row[...] + 1, owners, capacity)
    places, own_rows, _ = lists_of(own_owner[...], own_row[...], owners, capacity)
    rows = rows - 1
    inverse[...] = tokens
    for d in range(owners):
        lists[d, 0:per, :] = rows[d * per : (d + 1) * per, :]
        lists[d, per : 2 * per, :] = own_rows[d * per : (d + 1) * per, :]
    for c, place in enumerate(places):
        own_place[c : c + 1, :] = jnp.where(place < owners * capacity, place, 0)


def enter(plane, line):
    me, part = lax.axis_index("dp"), lax.axis_index("mp")
    barrier = pltpu.get_barrier_semaphore()
    for k in range(1, plane):
        pl.semaphore_signal(barrier, inc=1, device_id=(lax.rem(me + k, plane), part), device_id_type=MESH)
    for k in range(1, line):
        pl.semaphore_signal(barrier, inc=1, device_id=(me, lax.rem(part + k, line)), device_id_type=MESH)
    pl.semaphore_wait(barrier, max(plane - 1, 0) + max(line - 1, 0))
    return me, part


def send(source, target, out_sem, in_sem, device):
    copy = pltpu.make_async_remote_copy(
        src_ref=source, dst_ref=target, send_sem=out_sem, recv_sem=in_sem, device_id=device, device_id_type=MESH
    )
    copy.start()
    return copy


def asks_kernel(plane, lists, extra, got_lists, got_extra, out_sems, in_sems, own_sems):
    me, part = enter(plane, 0)
    copies = []
    for k in range(1, plane):
        peer = lax.rem(me + k, plane)
        copies.append(send(lists.at[peer], got_lists.at[me], out_sems.at[0, k], in_sems.at[0, k], (peer, part)))
        copies.append(send(extra, got_extra.at[me], out_sems.at[1, k], in_sems.at[1, k], (peer, part)))
    mine = [
        pltpu.make_async_copy(lists.at[me], got_lists.at[me], own_sems.at[0]),
        pltpu.make_async_copy(extra, got_extra.at[me], own_sems.at[1]),
    ]
    for copy in mine:
        copy.start()
    for copy in mine + copies:
        copy.wait()


def gather_rows(capacity, ids, table, target):
    def body(i, carry):
        at = pl.multiple_of(i * 16, 16)
        rows = [table[pl.ds(ids(at + u), 1), :] for u in range(16)]
        target[pl.ds(at, 16), :] = jnp.concatenate(rows, 0).astype(BF16)
        return carry

    lax.fori_loop(0, capacity // 16, body, 0)


def fetch_kernel(plane, capacity, ids, place, table, out, sent, got, wide, out_sems, in_sems):
    me, part = enter(plane, 0)
    copies = []
    for k in range(1, plane):
        peer = lax.rem(me + k, plane)
        gather_rows(capacity, lambda j, peer=peer: ids[peer, j], table, sent.at[peer])
        copies.append(send(sent.at[peer], got.at[me], out_sems.at[k], in_sems.at[k], (peer, part)))
    gather_rows(capacity, lambda j: ids[me, j], table, sent.at[me])
    wide[pl.ds(pl.multiple_of(me * capacity, capacity), capacity), :] = sent[me].astype(F32)
    for k in range(1, plane):
        peer = lax.rem(me - k + plane, plane)
        copies[k - 1].wait_recv()
        wide[pl.ds(pl.multiple_of(peer * capacity, capacity), capacity), :] = got[peer].astype(F32)
    gather_rows(out.shape[0], lambda j: place[j], wide, out)
    for copy in copies:
        copy.wait_send()


def slots_kernel(line, mine, out, out_sems, in_sems, own_sem):
    me, part = enter(0, line)
    copies = []
    for k in range(1, line):
        peer = lax.rem(part + k, line)
        copies.append(send(mine, out.at[part], out_sems.at[k], in_sems.at[k], (me, peer)))
    own = pltpu.make_async_copy(mine, out.at[part], own_sem)
    own.start()
    own.wait()
    for copy in copies:
        copy.wait()


def return_kernel(plane, capacity, tokens, rows, out, wide, sent, out_sems, in_sems, own_sem):
    me, part = enter(plane, 0)
    wide[...] = rows[...].astype(F32)
    copies = []
    for k in range(1, plane):
        peer = lax.rem(me + k, plane)
        gather_rows(capacity, lambda j, peer=peer: tokens[peer, j], wide, sent.at[peer])
        copies.append(send(sent.at[peer], out.at[me], out_sems.at[k], in_sems.at[k], (peer, part)))
    gather_rows(capacity, lambda j: tokens[me, j], wide, sent.at[me])
    own = pltpu.make_async_copy(sent.at[me], out.at[me], own_sem)
    own.start()
    own.wait()
    for copy in copies:
        copy.wait()


def scatter_kernel(capacity, ids, counts, rows, out, square, wide):
    out[...] = jnp.zeros_like(out)
    for d in range(rows.shape[0]):
        wide[...] = rows[d].astype(F32)
        count = counts[d]

        def one(j):
            at = ids[d, j]
            out[pl.ds(at, 1), :] = out[pl.ds(at, 1), :] + wide[pl.ds(j, 1), :]

        def body(i, carry):
            for u in range(8):
                one(i * 8 + u)
            return carry

        def rest(j, carry):
            one(j)
            return carry

        full = lax.shift_right_logical(count, 3)
        lax.fori_loop(0, full, body, 0)
        lax.fori_loop(full * 8, count, rest, 0)

    def add(i, total):
        block = out[pl.ds(pl.multiple_of(i * 64, 64), 64), :]
        block = block * block
        for r in range(8):
            total = total + block[r * 8 : (r + 1) * 8, :]
        return total

    square[...] = lax.fori_loop(0, out.shape[0] // 64, add, jnp.zeros((8, LANES), F32))


def norm_kernel(plane, line, table_sq, dense_sq, got_table, got_dense, out_sems, in_sems, own_sems):
    me, part = enter(plane, line)
    copies = []
    for k in range(1, plane):
        peer = lax.rem(me + k, plane)
        copies.append(send(table_sq, got_table.at[me], out_sems.at[0, k], in_sems.at[0, k], (peer, part)))
    for k in range(1, line):
        peer = lax.rem(part + k, line)
        copies.append(send(dense_sq, got_dense.at[part], out_sems.at[1, k], in_sems.at[1, k], (me, peer)))
    mine = [
        pltpu.make_async_copy(table_sq, got_table.at[me], own_sems.at[0]),
        pltpu.make_async_copy(dense_sq, got_dense.at[part], own_sems.at[1]),
    ]
    for copy in mine:
        copy.start()
    for copy in mine + copies:
        copy.wait()


def chain(index, values):
    out = jnp.full(index.shape, values[0], values[0].dtype)
    for k in range(1, len(values)):
        out = jnp.where(index >= k, values[k], out)
    return out


def forward_kernel(slots, cnt, x, w_in, gain, w_qkv, w_out, pooled, pm_out, normed_out, qkv, prob, a_out, pm_acc):
    tower = pl.program_id(0)
    pairs = pooled.shape[1]
    parts = w_qkv.shape[0]
    per = LANES // slots
    groups = pairs // per
    heads = 2 * parts
    xs = x[0]
    hidden = nn(xs, w_in[0].astype(BF16))
    inverse = lax.rsqrt(jnp.mean(hidden * hidden, -1, keepdims=True) + EPS)
    normed = (hidden * inverse * gain[0]).astype(BF16)
    normed_out[0] = normed
    for c in range(3):
        for m in range(parts):
            qkv[0, c * parts + m] = nn(normed, w_qkv[m, 0, c]).astype(BF16)
    lane = iota((LANES, LANES), 1)
    line = iota((LANES, LANES), 0)
    shift = slots.bit_length() - 1
    pair_r, pair_s = lax.shift_right_logical(lane, shift), lax.shift_right_logical(line, shift)
    same = pair_r == pair_s
    halves = [lane < DH, lane >= DH]
    own_head = iota((per * heads, LANES), 0) & (heads - 1)

    def group(g, carry):
        counts = [cnt[tower * pairs + g * per + k] for k in range(per)]
        live_r = same & ((lane & (slots - 1)) < chain(pair_r, counts))
        live_s = (line & (slots - 1)) < chain(pair_s, counts)
        rows = pl.ds(pl.multiple_of(g * LANES, LANES), LANES)
        sums = []
        for m in range(parts):
            query, key = qkv[0, m, rows, :], qkv[0, parts + m, rows, :]
            for half in range(2):
                scores = nt(jnp.where(halves[half], query, jnp.zeros_like(query)), key) * 0.125
                scores = jnp.where(live_r, scores, -1000000000.0)
                expo = jnp.exp(scores - jnp.max(scores, 1, keepdims=True))
                p = (expo * (1.0 / jnp.sum(expo, 1, keepdims=True))).astype(BF16)
                prob[0, g, 2 * m + half] = p
                sums.append(jnp.sum(jnp.where(live_s, p.astype(F32), 0.0), 0, keepdims=True))
        sums = jnp.concatenate(sums, 0)
        pair_l = lax.shift_right_logical(iota((heads, LANES), 1), shift)
        stack = jnp.concatenate([jnp.where(pair_l == k, sums, 0.0) for k in range(per)], 0).astype(BF16)
        a_out[0, g] = stack
        for m in range(parts):
            mix = nn(stack, qkv[0, 2 * parts + m, rows, :])
            head = iota((per * heads, LANES), 1) // DH + 2 * m
            mix = jnp.where(own_head == head, mix, 0.0)
            pm_acc[g, :, m * LANES : (m + 1) * LANES] = jnp.concatenate(
                [jnp.sum(mix[k * heads : (k + 1) * heads], 0, keepdims=True) for k in range(per)], 0
            )
        return carry

    lax.fori_loop(0, groups, group, 0)
    pm = jnp.concatenate([pm_acc[g] for g in range(groups)], 0).astype(BF16)
    pm_out[0] = pm
    every = [cnt[tower * pairs + k] for k in range(pairs)]
    tokens = iota((pairs, pairs * slots), 1)
    mine = lax.shift_right_logical(tokens, shift) == iota(tokens.shape, 0)
    live = mine & ((tokens & (slots - 1)) < chain(iota(tokens.shape, 0), every))
    high, low = split(nn(live.astype(BF16), xs))
    w = w_in[0].astype(BF16)
    total = nn(high, w) + nn(low, w)
    for m in range(parts):
        total = total + nn(pm[:, m * LANES : (m + 1) * LANES], w_out[m, 0])
    count = chain(iota(total.shape, 0), every).astype(F32)
    pooled[0] = (total / count).astype(BF16)


def backward_kernel(
    slots, cnt, x, w_in, gain, w_qkv, w_out, normed_in, qkv, prob, a_in, pm_in, dpooled, demb, d_in, d_gain, d_qkv, d_out, dqkv
):
    tower = pl.program_id(0)
    pairs, width = dpooled.shape[1:]
    parts = w_qkv.shape[0]
    per = LANES // slots
    groups = pairs // per
    heads = 2 * parts
    shift = slots.bit_length() - 1
    tokens = pairs * slots
    every = [cnt[tower * pairs + k] for k in range(pairs)]
    count = chain(iota((pairs, width), 0), every).astype(F32)
    dsum = dpooled[0].astype(F32) / count
    branch = dsum.astype(BF16)
    dmix = []
    for m in range(parts):
        d_out[0, m] = tn(pm_in[0, :, m * LANES : (m + 1) * LANES], branch).astype(BF16)
        dmix.append(nt(branch, w_out[m, 0]))
    lane = iota((LANES, LANES), 1)
    line = iota((LANES, LANES), 0)
    pair_s = lax.shift_right_logical(line, shift)
    halves = [lane < DH, lane >= DH]
    own_head = iota((per * heads, LANES), 0) & (heads - 1)
    own_pair = lax.shift_right_logical(iota((per * heads, LANES), 0), heads.bit_length() - 1)
    token_pair = lax.shift_right_logical(iota((per * heads, LANES), 1), shift)
    for g in range(groups):
        rows = slice(g * LANES, (g + 1) * LANES)
        live_s = (line & (slots - 1)) < chain(pair_s, every[g * per : (g + 1) * per])
        scale = jnp.where(live_s, 0.125, 0.0)
        dots = jnp.zeros((per * heads, LANES), F32)
        stacks = []
        for m in range(parts):
            cut = dmix[m][g * per : (g + 1) * per]
            spread = jnp.concatenate([jnp.broadcast_to(cut[k : k + 1], (heads, LANES)) for k in range(per)], 0)
            head = iota((per * heads, LANES), 1) // DH + 2 * m
            stack = jnp.where(own_head == head, spread, 0.0).astype(BF16)
            stacks.append(stack)
            dots = dots + nt(stack, qkv[0, 2 * parts + m, rows, :])
        dots = jnp.where(own_pair == token_pair, dots, 0.0)
        pull = dots[0:heads]
        for k in range(1, per):
            pull = pull + dots[k * heads : (k + 1) * heads]
        for m in range(parts):
            query, key = qkv[0, m, rows, :], qkv[0, parts + m, rows, :]
            none = jnp.zeros_like(query)
            dq = jnp.zeros((LANES, LANES), F32)
            dk = jnp.zeros((LANES, LANES), F32)
            for half in range(2):
                h = 2 * m + half
                p = prob[0, g, h].astype(F32)
                t = p * pull[h : h + 1, :]
                ds = ((t - p * jnp.sum(t, 1, keepdims=True)) * scale).astype(BF16)
                dq = dq + nn(ds, jnp.where(halves[half], key, none))
                dk = dk + tn(ds, jnp.where(halves[half], query, none))
            dqkv[m, rows, :] = dq.astype(BF16)
            dqkv[parts + m, rows, :] = dk.astype(BF16)
            dqkv[2 * parts + m, rows, :] = tn(a_in[0, g], stacks[m]).astype(BF16)
    normed = normed_in[0]
    dnormed = jnp.zeros((tokens, width), F32)
    for m in range(parts):
        for c in range(3):
            grad = dqkv[c * parts + m]
            dnormed = dnormed + nt(grad, w_qkv[m, 0, c])
            d_qkv[0, m, c] = tn(normed, grad).astype(BF16)
    dnormed = dnormed.astype(BF16).astype(F32)
    xs = x[0]
    w = w_in[0].astype(BF16)
    hidden = nn(xs, w)
    inverse = lax.rsqrt(jnp.mean(hidden * hidden, -1, keepdims=True) + EPS)
    unit = hidden * inverse
    d_gain[0] = jnp.sum(dnormed * unit, 0, keepdims=True)
    scaled = dnormed * gain[0]
    dh = inverse * (scaled - unit * jnp.mean(scaled * unit, -1, keepdims=True))
    spread = jnp.broadcast_to(dsum[:, None, :], (pairs, slots, width))
    slot = iota((pairs, slots, width), 1)
    counts = chain(iota((pairs, slots, width), 0), every)
    spread = jnp.where(slot < counts, spread, 0.0).reshape(tokens, width)
    dhidden = (spread + dh).astype(BF16)
    d_in[0] = tn(xs, dhidden).astype(BF16)
    demb[0] = nt(dhidden, w).astype(BF16)


def gelu_parts(v):
    c = 0.7978845608028654
    inner = jnp.tanh(c * (v + 0.044715 * (v * v * v)))
    value = 0.5 * v * (1.0 + inner)
    slope = 0.5 * (1.0 + inner) + 0.5 * v * (1.0 - inner * inner) * (c * (1.0 + 3.0 * 0.044715 * (v * v)))
    return value, slope


def upper_kernel(
    plane,
    line,
    pooled,
    w_one,
    w_two,
    w_three,
    prior_row,
    prior_col,
    pos_row,
    pos_own,
    dpooled,
    d_one,
    d_two,
    d_three,
    loss,
    pooled_all,
    second_send,
    second_got,
    vec,
    dsec_send,
    dsec_all,
    dpool_send,
    dpool_got,
    out_sems,
    in_sems,
    vec_out,
    vec_in,
):
    me, part = enter(plane, line)
    towers, own, width = pooled.shape
    rows = own * line
    pairs = rows * plane
    peers = [lax.rem(part + k, line) for k in range(1, line)]

    pooled_all[:, part] = pooled[...]
    first = [
        send(pooled_all.at[:, part], pooled_all.at[:, part], out_sems.at[0, k], in_sems.at[0, k], (me, peers[k]))
        for k in range(line - 1)
    ]
    one = [w_one[t].astype(BF16) for t in range(towers)]
    two = [w_two[t].astype(BF16) for t in range(towers)]
    three = [w_three[t].astype(BF16) for t in range(towers)]
    for copy in first:
        copy.wait()
    act_one, slope_one, pools = [], [], []
    for t in range(towers):
        pools.append(pooled_all[t].reshape(rows, width))
        value, slope = gelu_parts(nn(pools[t], one[t]))
        act_one.append(value.astype(BF16))
        slope_one.append(slope)
        second_send[t] = nn(act_one[t], two[t]).reshape(line, own, -1)
    second = [
        send(
            second_send.at[:, peers[k]], second_got.at[:, part], out_sems.at[1, k], in_sems.at[1, k], (me, peers[k])
        )
        for k in range(line - 1)
    ]
    for copy in second:
        copy.wait()
    act_two, slope_two, third, length, vectors = [], [], [], [], []
    for t in range(towers):
        total = second_send[t, part]
        for peer in peers:
            total = total + second_got[t, peer]
        value, slope = gelu_parts(total)
        act_two.append(value.astype(BF16))
        slope_two.append(slope)
        third.append(nn(act_two[t], three[t]))
        length.append(lax.rsqrt(jnp.sum(third[t] * third[t], -1, keepdims=True) + EPS))
        vectors.append((third[t] * length[t]).astype(BF16))
        vec[t, me, part] = vectors[t]
    along = [
        send(vec.at[:, me, part], vec.at[:, me, part], out_sems.at[2, k], in_sems.at[2, k], (me, peers[k]))
        for k in range(line - 1)
    ]
    for copy in along:
        copy.wait()
    across = [
        send(vec.at[:, me], vec.at[:, me], vec_out.at[k], vec_in.at[k], (lax.rem(me + k, plane), part))
        for k in range(1, plane)
    ]
    for copy in across:
        copy.wait()

    queries = vec[0].reshape(pairs, width)
    items = vec[1].reshape(pairs, width)
    logits = INV_TEMP * nt(items, queries) - prior_col[...]
    peak = jnp.max(logits, 0, keepdims=True)
    log_total = peak + jnp.log(jnp.sum(jnp.exp(logits - peak), 0, keepdims=True))
    picked = jnp.where(iota((pairs, pairs), 0) == pos_row[...], logits, 0.0)
    gap = log_total - jnp.sum(picked, 0, keepdims=True)
    loss[...] = jnp.broadcast_to(jnp.sum(gap, 1, keepdims=True), loss.shape)
    ahead = me * rows + part * own
    mine = INV_TEMP * nt(vectors[0], items) - prior_row[...]
    top = jnp.max(mine, 1, keepdims=True)
    expo = jnp.exp(mine - top)
    chance = expo / jnp.sum(expo, 1, keepdims=True)
    target = (iota(mine.shape, 1) == pos_own[...]).astype(F32)
    dlog = ((chance - target) / pairs).astype(BF16)
    dvec = [(INV_TEMP * nn(dlog, items)).astype(BF16)]
    own_prior = prior_col[pl.ds(pl.multiple_of(ahead, own), own), :]
    theirs = INV_TEMP * nt(vectors[1], queries) - own_prior
    target = (iota(theirs.shape, 0) + ahead == pos_row[...]).astype(F32)
    dlog = ((jnp.exp(theirs - log_total) - target) / pairs).astype(BF16)
    dvec.append((INV_TEMP * nn(dlog, queries)).astype(BF16))

    dthirds = []
    for t in range(towers):
        dv = dvec[t].astype(F32)
        inner = jnp.sum(dv * third[t], -1, keepdims=True)
        dthird = (length[t] * dv - third[t] * (length[t] * length[t] * length[t] * inner)).astype(BF16)
        dact = nt(dthird, three[t]).astype(BF16).astype(F32)
        dsec_all[t, part] = (dact * slope_two[t]).astype(BF16)
        dthirds.append(dthird)
    spread = [
        send(dsec_all.at[:, part], dsec_all.at[:, part], out_sems.at[3, k], in_sems.at[3, k], (me, peers[k]))
        for k in range(line - 1)
    ]
    for t in range(towers):
        d_three[t] = tn(act_two[t], dthirds[t]).astype(BF16)
    for copy in spread:
        copy.wait()
    dfirsts = []
    for t in range(towers):
        dsecond = dsec_all[t].reshape(rows, -1)
        dact = nt(dsecond, two[t]).astype(BF16).astype(F32)
        dfirst = (dact * slope_one[t]).astype(BF16)
        dpool_send[t] = nt(dfirst, one[t]).reshape(line, own, width)
        dfirsts.append(dfirst)
    back = [
        send(dpool_send.at[:, peers[k]], dpool_got.at[:, part], out_sems.at[4, k], in_sems.at[4, k], (me, peers[k]))
        for k in range(line - 1)
    ]
    for t in range(towers):
        dsecond = dsec_all[t].reshape(rows, -1)
        d_two[t] = tn(act_one[t], dsecond).astype(BF16)
        d_one[t] = tn(pools[t], dfirsts[t]).astype(BF16)
    for copy in back:
        copy.wait()
    for t in range(towers):
        total = dpool_send[t, part]
        for peer in peers:
            total = total + dpool_got[t, peer]
        dpooled[t] = total.astype(BF16)


def update(weight, grad, moment, average, factor, rate):
    clipped = grad * factor
    moment_new = MOMENTUM * moment + clipped
    weight_new = weight - rate * (clipped + MOMENTUM * moment_new)
    average_new = AVERAGE_DECAY * average + (1.0 - AVERAGE_DECAY) * weight_new
    return [weight_new, moment_new, average_new]


def shards(
    slot_owner,
    slot_row,
    slot_count,
    item_qid,
    positive,
    log_prior,
    embedding,
    embedding_mom,
    embedding_avg,
    w_in,
    w_in_mom,
    w_in_avg,
    norm_gain,
    norm_gain_mom,
    norm_gain_avg,
    w_qkv,
    w_qkv_mom,
    w_qkv_avg,
    w_out,
    w_out_mom,
    w_out_avg,
    w_one,
    w_one_mom,
    w_one_avg,
    w_two,
    w_two_mom,
    w_two_avg,
    w_three,
    w_three_mom,
    w_three_avg,
):
    plane = lax.axis_size("dp")
    line = lax.axis_size("mp")
    batch, towers, slots = slot_row.shape
    own = batch // line
    requests = batch * towers * slots
    own_requests = requests // line
    tokens = own * slots
    capacity = max(LANES, 2 * requests // plane)
    pairs = batch * plane
    part = lax.axis_index("mp")
    me = lax.axis_index("dp")
    width = w_in.shape[2]
    depth = w_in.shape[1]
    units = w_one.shape[2]
    seconds = w_two.shape[2]

    wide_qkv = lax.all_gather(jnp.transpose(w_qkv.astype(BF16), (0, 2, 1, 3)), "mp", axis=0)
    wide_out = lax.all_gather(w_out.astype(BF16), "mp", axis=0)

    def ordered(value):
        value = value.reshape(line, own, towers, slots)
        return jnp.transpose(value, (0, 2, 1, 3)).reshape(requests // LANES, LANES)

    owner = ordered(slot_owner)
    row = ordered(slot_row)
    own_chunks = own_requests // LANES
    own_owner = lax.dynamic_slice_in_dim(owner, part * own_chunks, own_chunks, 0)
    own_row = lax.dynamic_slice_in_dim(row, part * own_chunks, own_chunks, 0)
    per = capacity // LANES
    lists, inverse, own_place = pl.pallas_call(
        functools.partial(prep_kernel, plane, capacity),
        out_shape=[
            shape((plane, 2 * per, LANES), I32),
            shape((plane * per, LANES), I32),
            shape((own_chunks, LANES), I32),
        ],
        in_specs=[VMEM] * 4,
        out_specs=[VMEM] * 3,
        compiler_params=params(32),
        name="request_lists",
    )(owner, row, own_owner, own_row)
    lone = jnp.pad(positive[None, :], ((0, 7), (0, LANES - batch)))
    got_lists, got_pos = pl.pallas_call(
        functools.partial(asks_kernel, plane),
        out_shape=[shape(lists.shape, I32), shape((plane, 8, LANES), I32)],
        in_specs=[VMEM] * 2,
        out_specs=[VMEM] * 2,
        scratch_shapes=[DMA((2, plane)), DMA((2, plane)), DMA((2,))],
        compiler_params=params(32, collective_id=1, has_side_effects=True),
        name="ask",
    )(lists, lone)
    ids = got_lists[:, per:, :].reshape(plane, capacity)
    embedded = pl.pallas_call(
        functools.partial(fetch_kernel, plane, capacity),
        out_shape=shape((own_requests, depth), BF16),
        in_specs=[SMEM, SMEM, VMEM],
        out_specs=VMEM,
        scratch_shapes=[
            pltpu.VMEM((plane, capacity, depth), BF16),
            pltpu.VMEM((plane, capacity, depth), BF16),
            pltpu.VMEM((plane * capacity, depth), F32),
            DMA((plane,)),
            DMA((plane,)),
        ],
        compiler_params=params(48, collective_id=2, has_side_effects=True),
        name="fetch",
    )(ids, own_place.reshape(own_requests), embedding)
    embedded = embedded.reshape(towers, tokens, depth)

    counts = jnp.transpose(slot_count).reshape(towers, line, own)
    counts = lax.dynamic_index_in_dim(counts, part, 1, keepdims=False).reshape(towers * own)
    heads = 2 * line
    gains = norm_gain.reshape(towers, 1, width)
    groups = tokens // LANES
    per_group = LANES // slots
    lead = lambda *dims: pl.BlockSpec((1,) + dims, lambda t: (t,) + (0,) * len(dims))
    qkv_spec = pl.BlockSpec((line, 1, 3, width, LANES), lambda t: (0, t, 0, 0, 0))
    out_spec = pl.BlockSpec((line, 1, LANES, width), lambda t: (0, t, 0, 0))
    pooled, pm, normed, qkv, prob, spread = pl.pallas_call(
        functools.partial(forward_kernel, slots),
        grid=(towers,),
        out_shape=[
            shape((towers, own, width), BF16),
            shape((towers, own, line * LANES), BF16),
            shape((towers, tokens, width), BF16),
            shape((towers, 3 * line, tokens, LANES), BF16),
            shape((towers, groups, heads, LANES, LANES), BF16),
            shape((towers, groups, per_group * heads, LANES), BF16),
        ],
        in_specs=[SMEM, lead(tokens, depth), lead(depth, width), lead(1, width), qkv_spec, out_spec],
        out_specs=[
            lead(own, width),
            lead(own, line * LANES),
            lead(tokens, width),
            lead(3 * line, tokens, LANES),
            lead(groups, heads, LANES, LANES),
            lead(groups, per_group * heads, LANES),
        ],
        scratch_shapes=[pltpu.VMEM((groups, per_group, line * LANES), F32)],
        compiler_params=params(48),
        name="attention_forward",
    )(counts, embedded, w_in, gains, wide_qkv, wide_out)

    prior = jnp.sum(
        jnp.where(item_qid[:, None] == jnp.arange(log_prior.shape[0])[None, :], log_prior[None, :], 0.0), 1
    )
    positions = got_pos[:, 0, :batch].reshape(1, pairs)
    own_positions = lax.dynamic_slice_in_dim(positive, part * own, own, 0).reshape(own, 1)
    dpooled, d_one, d_two, d_three, loss = pl.pallas_call(
        functools.partial(upper_kernel, plane, line),
        out_shape=[
            shape((towers, own, width), BF16),
            shape((towers, width, units), BF16),
            shape((towers, units, seconds), BF16),
            shape((towers, seconds, width), BF16),
            shape((8, LANES), F32),
        ],
        in_specs=[VMEM] * 8,
        out_specs=[VMEM] * 5,
        scratch_shapes=[
            pltpu.VMEM((towers, line, own, width), BF16),
            pltpu.VMEM((towers, line, own, seconds), F32),
            pltpu.VMEM((towers, line, own, seconds), F32),
            pltpu.VMEM((towers, plane, line, own, width), BF16),
            pltpu.VMEM((towers, line, own, seconds), BF16),
            pltpu.VMEM((towers, line, own, seconds), BF16),
            pltpu.VMEM((towers, line, own, width), F32),
            pltpu.VMEM((towers, line, own, width), F32),
            DMA((5, line)),
            DMA((5, line)),
            DMA((plane,)),
            DMA((plane,)),
        ],
        compiler_params=params(56, collective_id=3, has_side_effects=True),
        name="upper",
    )(pooled, w_one, w_two, w_three, prior.reshape(1, pairs), prior.reshape(pairs, 1), positions, own_positions)

    demb, d_in, d_gain, d_qkv, d_out = pl.pallas_call(
        functools.partial(backward_kernel, slots),
        grid=(towers,),
        out_shape=[
            shape((towers, tokens, depth), BF16),
            shape((towers, depth, width), BF16),
            shape((towers, 1, width), F32),
            shape((towers, line, 3, width, LANES), BF16),
            shape((towers, line, LANES, width), BF16),
        ],
        in_specs=[
            SMEM,
            lead(tokens, depth),
            lead(depth, width),
            lead(1, width),
            qkv_spec,
            out_spec,
            lead(tokens, width),
            lead(3 * line, tokens, LANES),
            lead(groups, heads, LANES, LANES),
            lead(groups, per_group * heads, LANES),
            lead(own, line * LANES),
            lead(own, width),
        ],
        out_specs=[
            lead(tokens, depth),
            lead(depth, width),
            lead(1, width),
            lead(line, 3, width, LANES),
            lead(line, LANES, width),
        ],
        scratch_shapes=[pltpu.VMEM((3 * line, tokens, LANES), BF16)],
        compiler_params=params(56),
        name="attention_backward",
    )(counts, embedded, w_in, gains, wide_qkv, wide_out, normed, qkv, prob, spread, pm, dpooled)

    both = ("dp", "mp")
    d_one = lax.psum(d_one, "dp").astype(F32)
    d_two = lax.psum(d_two, "dp").astype(F32)
    d_three = lax.psum(d_three, both).astype(F32)
    d_in = lax.psum(d_in, both).astype(F32)
    d_gain = lax.psum(d_gain.reshape(towers, width).astype(BF16), both).astype(F32)
    d_qkv = lax.psum(lax.psum_scatter(d_qkv, "mp", scatter_dimension=1, tiled=False), "dp")
    d_qkv = jnp.transpose(d_qkv, (0, 2, 1, 3)).astype(F32)
    d_out = lax.psum(lax.psum_scatter(d_out, "mp", scatter_dimension=1, tiled=False), "dp").astype(F32)

    every = pl.pallas_call(
        functools.partial(slots_kernel, line),
        out_shape=shape((line, own_requests, depth), BF16),
        in_specs=[VMEM],
        out_specs=VMEM,
        scratch_shapes=[DMA((line,)), DMA((line,)), DMA],
        compiler_params=params(32, collective_id=4, has_side_effects=True),
        name="line_slots",
    )(demb.reshape(own_requests, depth))
    incoming = pl.pallas_call(
        functools.partial(return_kernel, plane, capacity),
        out_shape=shape((plane, capacity, depth), BF16),
        in_specs=[SMEM, VMEM],
        out_specs=VMEM,
        scratch_shapes=[
            pltpu.VMEM((requests, depth), F32),
            pltpu.VMEM((plane, capacity, depth), BF16),
            DMA((plane,)),
            DMA((plane,)),
            DMA,
        ],
        compiler_params=params(48, collective_id=5, has_side_effects=True),
        name="return_rows",
    )(inverse.reshape(plane, capacity), every.reshape(requests, depth))
    served = got_lists[:, :per, :].reshape(plane, capacity)
    table_grad, table_sq = pl.pallas_call(
        functools.partial(scatter_kernel, capacity),
        out_shape=[shape(embedding.shape, F32), shape((8, LANES), F32)],
        in_specs=[SMEM, SMEM, VMEM],
        out_specs=[VMEM, VMEM],
        scratch_shapes=[pltpu.VMEM((capacity, depth), F32)],
        compiler_params=params(48),
        name="add_rows",
    )(jnp.maximum(served, 0), jnp.sum((served >= 0).astype(I32), 1), incoming)

    whole_sq = jnp.sum(d_in * d_in) + jnp.sum(d_gain * d_gain) + jnp.sum(d_three * d_three)
    shard_sq = jnp.sum(d_qkv * d_qkv) + jnp.sum(d_out * d_out) + jnp.sum(d_one * d_one) + jnp.sum(d_two * d_two)
    got_table, got_dense = pl.pallas_call(
        functools.partial(norm_kernel, plane, line),
        out_shape=[shape((plane, 8, LANES), F32), shape((line, 8, LANES), F32)],
        in_specs=[VMEM] * 2,
        out_specs=[VMEM] * 2,
        scratch_shapes=[DMA((2, plane)), DMA((2, plane)), DMA((2,))],
        compiler_params=params(32, collective_id=6, has_side_effects=True),
        name="norm_parts",
    )(table_sq, jnp.broadcast_to(shard_sq, (8, LANES)))
    norm = jnp.sqrt(jnp.sum(got_table) + jnp.sum(got_dense[:, 0, 0]) + whole_sq)
    factor = jnp.minimum(1.0, CLIP_NORM / norm)
    done = []
    done.extend(update(embedding, table_grad, embedding_mom, embedding_avg, factor, ROW_RATE))
    done.extend(update(w_in, d_in, w_in_mom, w_in_avg, factor, MATRIX_RATE))
    done.extend(update(norm_gain, d_gain, norm_gain_mom, norm_gain_avg, factor, GAIN_RATE))
    done.extend(update(w_qkv, d_qkv, w_qkv_mom, w_qkv_avg, factor, MATRIX_RATE))
    done.extend(update(w_out, d_out, w_out_mom, w_out_avg, factor, MATRIX_RATE))
    done.extend(update(w_one, d_one, w_one_mom, w_one_avg, factor, MATRIX_RATE))
    done.extend(update(w_two, d_two, w_two_mom, w_two_avg, factor, MATRIX_RATE))
    done.extend(update(w_three, d_three, w_three_mom, w_three_avg, factor, MATRIX_RATE))
    return (loss[0, 0], norm, *done)


def solution(mesh):
    rows = P("dp", None)
    qkv = P(None, None, None, "mp")
    deep = P(None, "mp", None)
    wide = P(None, None, "mp")
    weights = (rows,) * 3 + (P(),) * 6 + (qkv,) * 3 + (deep,) * 3 + (wide,) * 3 + (deep,) * 3 + (P(),) * 3
    inputs = (P("dp", None, None, None), P("dp", None, None), P("dp", None), P(), P("dp"), P())
    return jax.shard_map(
        shards, mesh=mesh, in_specs=inputs + weights, out_specs=(P(), P()) + weights, check_vma=False
    )
```

```python
import functools

import jax
import jax.numpy as jnp
from jax import lax
from jax.experimental import pallas as pl
from jax.experimental.pallas import tpu as pltpu
from jax.sharding import PartitionSpec as P

DH = 64
EPS = 1e-06
INV_TEMP = 20.0
CLIP_NORM = 0.1
ROW_RATE = 150000.0
GAIN_RATE = 8000.0
MATRIX_RATE = 600.0
MOMENTUM = 0.9
AVERAGE_DECAY = 0.6

MESH = pl.DeviceIdType.MESH
LANES = 128
F32 = jnp.float32
BF16 = jnp.bfloat16
I32 = jnp.int32
VMEM = pl.BlockSpec(memory_space=pltpu.VMEM)
SMEM = pl.BlockSpec(memory_space=pltpu.SMEM)
DMA = pltpu.SemaphoreType.DMA


def nn(a, b):
    return lax.dot_general(a, b, (((1,), (0,)), ((), ())), preferred_element_type=F32)


def nt(a, b):
    return lax.dot_general(a, b, (((1,), (1,)), ((), ())), preferred_element_type=F32)


def tn(a, b):
    return lax.dot_general(a, b, (((0,), (0,)), ((), ())), preferred_element_type=F32)


def iota(shape, dim):
    return lax.broadcasted_iota(I32, shape, dim)


def split(value):
    high = value.astype(BF16)
    return high, (value - high.astype(F32)).astype(BF16)


def shape(dims, dtype):
    return jax.ShapeDtypeStruct(tuple(dims), dtype)


def params(limit, **more):
    return pltpu.CompilerParams(vmem_limit_bytes=limit << 20, **more)


def lists_of(owner, row, owners, capacity):
    chunks = owner.shape[0]
    width = owners * capacity
    his = width // LANES
    sub = iota((owners, LANES), 0)
    hot = [(owner[c : c + 1, :] == sub).astype(BF16) for c in range(chunks)]
    hots = jnp.concatenate([h.astype(F32) for h in hot], 0).astype(BF16)
    before = (iota((LANES, LANES), 0) < iota((LANES, LANES), 1)).astype(BF16)
    earlier = nn(hots, before)
    totals = nn(hots, jnp.ones((LANES, LANES), BF16))
    base = (sub * capacity).astype(F32)
    places = []
    for c in range(chunks):
        cut = slice(c * owners, (c + 1) * owners)
        at = hots[cut].astype(F32) * (earlier[cut] + base)
        here = jnp.sum(at, 0, keepdims=True).astype(I32)
        places.append(jnp.where(owner[c : c + 1, :] < owners, here, width))
        base = base + totals[cut]
    acc = jnp.zeros((his, 4 * LANES), F32)
    for c in range(chunks):
        place = places[c]
        value = row[c : c + 1, :]
        token = iota((1, LANES), 1) + c * LANES
        left = (lax.shift_right_logical(place, 7) == iota((his, LANES), 0)).astype(BF16)
        low = (place & 127) == iota((LANES, LANES), 0)
        parts = [lax.shift_right_logical(value, 6), value & 63, lax.shift_right_logical(token, 6), token & 63]
        right = jnp.concatenate([jnp.where(low, part.astype(F32), 0.0) for part in parts], 0)
        acc = acc + nt(left, right.astype(BF16))
    cuts = [acc[:, k * LANES : (k + 1) * LANES].astype(I32) for k in range(4)]
    return places, cuts[0] * 64 + cuts[1], cuts[2] * 64 + cuts[3]


def prep_kernel(owners, capacity, owner, row, own_owner, own_row, lists, inverse, own_place):
    per = capacity // LANES
    _, rows, tokens = lists_of(owner[...], row[...] + 1, owners, capacity)
    places, own_rows, _ = lists_of(own_owner[...], own_row[...], owners, capacity)
    rows = rows - 1
    inverse[...] = tokens
    for d in range(owners):
        lists[d, 0:per, :] = rows[d * per : (d + 1) * per, :]
        lists[d, per : 2 * per, :] = own_rows[d * per : (d + 1) * per, :]
    for c, place in enumerate(places):
        own_place[c : c + 1, :] = jnp.where(place < owners * capacity, place, 0)


def enter(plane, line):
    me, part = lax.axis_index("dp"), lax.axis_index("mp")
    barrier = pltpu.get_barrier_semaphore()
    for k in range(1, plane):
        pl.semaphore_signal(barrier, inc=1, device_id=(lax.rem(me + k, plane), part), device_id_type=MESH)
    for k in range(1, line):
        pl.semaphore_signal(barrier, inc=1, device_id=(me, lax.rem(part + k, line)), device_id_type=MESH)
    pl.semaphore_wait(barrier, max(plane - 1, 0) + max(line - 1, 0))
    return me, part


def send(source, target, out_sem, in_sem, device):
    copy = pltpu.make_async_remote_copy(
        src_ref=source, dst_ref=target, send_sem=out_sem, recv_sem=in_sem, device_id=device, device_id_type=MESH
    )
    copy.start()
    return copy


def gather_rows(ids, table, target):
    per = LANES // 16

    def body(i, carry):
        at = pl.multiple_of(i * 16, 16)
        block = lax.shift_right_logical(i, 3)
        first = (i & (per - 1)) * 16
        rows = [table[pl.ds(ids(block, first + u), 1), :] for u in range(16)]
        target[pl.ds(at, 16), :] = jnp.concatenate(rows, 0).astype(BF16)
        return carry

    lax.fori_loop(0, target.shape[0] // 16, body, 0)


def fetch_kernel(
    plane,
    line,
    capacity,
    lists,
    extra,
    place,
    table,
    w_qkv,
    w_out,
    out,
    got_lists,
    got_extra,
    wide_qkv,
    wide_out,
    ids,
    sent,
    got,
    wide,
    list_out,
    list_in,
    out_sems,
    in_sems,
    far_out,
    far_in,
    near_out,
    near_in,
    own_sems,
):
    me, part = enter(plane, line)
    core = lax.rem(me, 2)
    sibling = me + 1 - 2 * core
    wide_qkv[part] = w_qkv[...].astype(BF16)
    wide_out[part] = w_out[...].astype(BF16)
    far = []
    for k in range(1, line):
        peer = lax.rem(part + k, line)
        for j, block in enumerate((wide_qkv, wide_out)):
            at = block.at[part, core]
            far.append(send(at, at, far_out.at[j, k], far_in.at[j, k], (me, peer)))
    asked = []
    for k in range(1, plane):
        peer = lax.rem(me + k, plane)
        asked.append(send(lists.at[peer], got_lists.at[me], list_out.at[0, k], list_in.at[0, k], (peer, part)))
        asked.append(send(extra, got_extra.at[me], list_out.at[1, k], list_in.at[1, k], (peer, part)))
    mine = [
        pltpu.make_async_copy(lists.at[me], got_lists.at[me], own_sems.at[0]),
        pltpu.make_async_copy(extra, got_extra.at[me], own_sems.at[1]),
    ]
    for copy in mine:
        copy.start()
    for copy in mine + asked:
        copy.wait()
    numbers = pltpu.make_async_copy(got_lists, ids, own_sems.at[2])
    numbers.start()
    numbers.wait()
    half = capacity // LANES
    copies = []
    for k in range(1, plane):
        peer = lax.rem(me + k, plane)
        gather_rows(lambda b, j, peer=peer: ids[peer, half + b, j], table, sent.at[peer])
        copies.append(send(sent.at[peer], got.at[me], out_sems.at[k], in_sems.at[k], (peer, part)))
    gather_rows(lambda b, j: ids[me, half + b, j], table, sent.at[me])
    wide[pl.ds(pl.multiple_of(me * capacity, capacity), capacity), :] = sent[me].astype(F32)
    near = []
    for k in range(1, line):
        peer = lax.rem(part - k + line, line)
        for j, block in enumerate((wide_qkv, wide_out)):
            far[2 * (k - 1) + j].wait_recv()
            at = block.at[peer, core]
            near.append(send(at, at, near_out.at[j, k], near_in.at[j, k], (sibling, part)))
    for k in range(1, plane):
        peer = lax.rem(me - k + plane, plane)
        copies[k - 1].wait_recv()
        wide[pl.ds(pl.multiple_of(peer * capacity, capacity), capacity), :] = got[peer].astype(F32)
    gather_rows(lambda b, j: place[b, j], wide, out)
    for copy in copies + far:
        copy.wait_send()
    for copy in near:
        copy.wait()


def spread_kernel(
    plane,
    line,
    mine,
    d_qkv,
    d_out,
    d_three,
    d_in,
    d_one,
    d_two,
    gain,
    out,
    summed,
    gain_sum,
    near_split,
    near_whole,
    half,
    got,
    gains,
    far_out,
    far_in,
    near_out,
    near_in,
    sum_out,
    sum_in,
    gain_out,
    gain_in,
    own_sem,
):
    me, part = enter(plane, line)
    chips = plane // 2
    core = lax.rem(me, 2)
    chip = me // 2
    sibling = me + 1 - 2 * core
    copies = []
    for k in range(1, line):
        peer = lax.rem(part + k, line)
        copies.append(send(mine, out.at[part], far_out.at[k], far_in.at[k], (me, peer)))
    split_grads, whole_grads = (d_qkv, d_out), (d_three, d_in, d_one, d_two)
    first = []
    for j, grad in enumerate(split_grads):
        first.append(send(grad.at[:, :, 1 - core], near_split[j], near_out.at[j], near_in.at[j], (sibling, part)))
    for j, grad in enumerate(whole_grads, len(split_grads)):
        first.append(send(grad.at[:, 1 - core], near_whole[j - 2], near_out.at[j], near_in.at[j], (sibling, part)))
    for k in range(1, plane):
        peer = lax.rem(me + k, plane)
        copies.append(send(gain, gains.at[me], gain_out.at[k], gain_in.at[k], (peer, part)))
    own = pltpu.make_async_copy(mine, out.at[part], own_sem)
    own.start()
    gains[me] = gain[...]
    for copy in first:
        copy.wait()
    for c in range(chips):
        at = 0
        for j, grad in enumerate(split_grads):
            rows = grad.shape[3]
            for m in range(line):
                total = grad[m, c, core].astype(F32) + near_split[j][m, c].astype(F32)
                half[c, at : at + rows, :] = total.astype(BF16)
                at += rows
        for j, grad in enumerate(whole_grads):
            rows = grad.shape[2]
            total = grad[c, core].astype(F32) + near_whole[j][c].astype(F32)
            half[c, at : at + rows, :] = total.astype(BF16)
            at += rows
    sums = []
    for k in range(1, chips):
        to = lax.rem(chip + k, chips)
        sums.append(send(half.at[to], got.at[k - 1], sum_out.at[k], sum_in.at[k], (2 * to + core, part)))
    for copy in sums:
        copy.wait()
    total = half[chip].astype(F32)
    for k in range(chips - 1):
        total = total + got[k].astype(F32)
    summed[...] = total.astype(BF16)
    own.wait()
    for copy in copies:
        copy.wait()
    total = gains[0]
    for d in range(1, plane):
        total = total + gains[d]
    gain_sum[...] = total


def return_kernel(
    plane,
    line,
    capacity,
    cuts,
    tokens,
    rows,
    summed,
    gain,
    out,
    dense,
    dense_sq,
    gain_all,
    wide,
    sent,
    got,
    gains,
    out_sems,
    in_sems,
    far_out,
    far_in,
    gain_out,
    gain_in,
    own_sem,
):
    me, part = enter(plane, line)
    far = []
    split_cuts, (whole_at, whole_rows), (last_at, last_rows) = cuts
    for k in range(1, line):
        peer = lax.rem(part + k, line)
        to = 0
        for j, (at, count) in enumerate(split_cuts):
            begin = pl.multiple_of(at + peer * count, 16)
            far.append(
                send(summed.at[pl.ds(begin, count)], got.at[part, to : to + count], far_out.at[j, k], far_in.at[j, k], (me, peer))
            )
            to += count
        target = got.at[part, to : to + whole_rows]
        source = summed.at[whole_at : whole_at + whole_rows]
        far.append(send(source, target, far_out.at[2, k], far_in.at[2, k], (me, peer)))
        far.append(send(gain, gains.at[part], gain_out.at[k], gain_in.at[k], (me, peer)))
    gains[part] = gain[...]
    wide[...] = rows[...].astype(F32)
    copies = []
    for k in range(1, plane):
        peer = lax.rem(me + k, plane)
        gather_rows(lambda b, j, peer=peer: tokens[peer, b, j], wide, sent.at[peer])
        copies.append(send(sent.at[peer], out.at[me], out_sems.at[k], in_sems.at[k], (peer, part)))
    gather_rows(lambda b, j: tokens[me, b, j], wide, sent.at[me])
    own = pltpu.make_async_copy(sent.at[me], out.at[me], own_sem)
    own.start()
    to = 0
    for at, count in split_cuts:
        got[part, to : to + count] = summed[pl.ds(pl.multiple_of(at + part * count, 16), count), :]
        to += count
    got[part, to : to + whole_rows] = summed[whole_at : whole_at + whole_rows, :]
    for copy in far:
        copy.wait()
    total = got[0].astype(F32)
    for m in range(1, line):
        total = total + got[m].astype(F32)
    dense[0 : to + whole_rows, :] = total.astype(BF16)
    dense[to + whole_rows :, :] = summed[last_at : last_at + last_rows, :]
    square = jnp.zeros((8, LANES), F32)
    for begin, count, weight in ((0, to, 1.0), (to, whole_rows, 1.0 / line), (to + whole_rows, last_rows, 1.0)):
        block = dense[begin : begin + count, :].astype(F32)
        square = square + weight * jnp.sum((block * block).reshape(count // 8, 8, LANES), 0)
    dense_sq[...] = square
    total = gains[0]
    for m in range(1, line):
        total = total + gains[m]
    gain_all[...] = total
    own.wait()
    for copy in copies:
        copy.wait()


def scatter_kernel(capacity, ids, counts, rows, out, square, wide):
    out[...] = jnp.zeros_like(out)
    for d in range(rows.shape[0]):
        wide[...] = rows[d].astype(F32)
        count = counts[d]

        def one(j):
            at = ids[d, j]
            out[pl.ds(at, 1), :] = out[pl.ds(at, 1), :] + wide[pl.ds(j, 1), :]

        def body(i, carry):
            for u in range(8):
                one(i * 8 + u)
            return carry

        def rest(j, carry):
            one(j)
            return carry

        full = lax.shift_right_logical(count, 3)
        lax.fori_loop(0, full, body, 0)
        lax.fori_loop(full * 8, count, rest, 0)

    def add(i, total):
        block = out[pl.ds(pl.multiple_of(i * 64, 64), 64), :]
        block = block * block
        for r in range(8):
            total = total + block[r * 8 : (r + 1) * 8, :]
        return total

    square[...] = lax.fori_loop(0, out.shape[0] // 64, add, jnp.zeros((8, LANES), F32))


def norm_kernel(
    plane,
    line,
    table_sq,
    dense_sq,
    dense,
    gain,
    norm_sq,
    dense_all,
    along,
    across,
    along_out,
    along_in,
    across_out,
    across_in,
    far_out,
    far_in,
    near_out,
    near_in,
    own_sem,
):
    me, part = enter(plane, line)
    chips = plane // 2
    core = lax.rem(me, 2)
    chip = me // 2
    sibling = me + 1 - 2 * core
    across[me] = dense_sq[...] + table_sq[...] * (1.0 / line)
    tiny = [
        send(across.at[me], across.at[me], across_out.at[k], across_in.at[k], (lax.rem(me + k, plane), part))
        for k in range(1, plane)
    ]
    far = []
    for k in range(1, chips):
        to = lax.rem(chip + k, chips)
        far.append(send(dense, dense_all.at[me], far_out.at[k], far_in.at[k], (2 * to + core, part)))
    near = [send(dense, dense_all.at[me], near_out.at[0], near_in.at[0], (sibling, part))]
    own = pltpu.make_async_copy(dense, dense_all.at[me], own_sem)
    own.start()
    for copy in tiny:
        copy.wait()
    total = across[0]
    for d in range(1, plane):
        total = total + across[d]
    along[part] = total
    peers = [lax.rem(part + k, line) for k in range(1, line)]
    tiny = [
        send(along.at[part], along.at[part], along_out.at[k], along_in.at[k], (me, peer)) for k, peer in enumerate(peers)
    ]
    for k in range(1, chips):
        peer = 2 * lax.rem(chip - k + chips, chips) + core
        far[k - 1].wait_recv()
        near.append(send(dense_all.at[peer], dense_all.at[peer], near_out.at[k], near_in.at[k], (sibling, part)))
    for copy in tiny:
        copy.wait()
    total = along[0]
    for m in range(1, line):
        total = total + along[m]
    gains = gain[...]
    norm_sq[...] = jnp.broadcast_to(jnp.sum(total + gains * gains), norm_sq.shape)
    own.wait()
    for copy in far:
        copy.wait_send()
    for copy in near:
        copy.wait()


def chain(index, values):
    out = jnp.full(index.shape, values[0], values[0].dtype)
    for k in range(1, len(values)):
        out = jnp.where(index >= k, values[k], out)
    return out


def forward_kernel(slots, cnt, x, w_in, gain, w_qkv, w_out, pooled, pm_out, normed_out, qkv, prob, a_out, pm_acc):
    tower = pl.program_id(0)
    pairs = pooled.shape[1]
    parts = w_qkv.shape[0]
    per = LANES // slots
    groups = pairs // per
    heads = 2 * parts
    xs = x[0]
    hidden = nn(xs, w_in[0].astype(BF16))
    inverse = lax.rsqrt(jnp.mean(hidden * hidden, -1, keepdims=True) + EPS)
    normed = (hidden * inverse * gain[0]).astype(BF16)
    normed_out[0] = normed
    for c in range(3):
        for m in range(parts):
            qkv[0, c * parts + m] = nn(normed, w_qkv[m, 0, c]).astype(BF16)
    lane = iota((LANES, LANES), 1)
    line = iota((LANES, LANES), 0)
    shift = slots.bit_length() - 1
    pair_r, pair_s = lax.shift_right_logical(lane, shift), lax.shift_right_logical(line, shift)
    same = pair_r == pair_s
    halves = [lane < DH, lane >= DH]
    own_head = iota((per * heads, LANES), 0) & (heads - 1)

    def group(g, carry):
        counts = [cnt[tower * pairs + g * per + k] for k in range(per)]
        live_r = same & ((lane & (slots - 1)) < chain(pair_r, counts))
        live_s = (line & (slots - 1)) < chain(pair_s, counts)
        rows = pl.ds(pl.multiple_of(g * LANES, LANES), LANES)
        sums = []
        for m in range(parts):
            query, key = qkv[0, m, rows, :], qkv[0, parts + m, rows, :]
            for half in range(2):
                scores = nt(jnp.where(halves[half], query, jnp.zeros_like(query)), key) * 0.125
                scores = jnp.where(live_r, scores, -1000000000.0)
                expo = jnp.exp(scores - jnp.max(scores, 1, keepdims=True))
                p = (expo * (1.0 / jnp.sum(expo, 1, keepdims=True))).astype(BF16)
                prob[0, g, 2 * m + half] = p
                sums.append(jnp.sum(jnp.where(live_s, p.astype(F32), 0.0), 0, keepdims=True))
        sums = jnp.concatenate(sums, 0)
        pair_l = lax.shift_right_logical(iota((heads, LANES), 1), shift)
        stack = jnp.concatenate([jnp.where(pair_l == k, sums, 0.0) for k in range(per)], 0).astype(BF16)
        a_out[0, g] = stack
        for m in range(parts):
            mix = nn(stack, qkv[0, 2 * parts + m, rows, :])
            head = iota((per * heads, LANES), 1) // DH + 2 * m
            mix = jnp.where(own_head == head, mix, 0.0)
            pm_acc[g, :, m * LANES : (m + 1) * LANES] = jnp.concatenate(
                [jnp.sum(mix[k * heads : (k + 1) * heads], 0, keepdims=True) for k in range(per)], 0
            )
        return carry

    lax.fori_loop(0, groups, group, 0)
    pm = jnp.concatenate([pm_acc[g] for g in range(groups)], 0).astype(BF16)
    pm_out[0] = pm
    every = [cnt[tower * pairs + k] for k in range(pairs)]
    tokens = iota((pairs, pairs * slots), 1)
    mine = lax.shift_right_logical(tokens, shift) == iota(tokens.shape, 0)
    live = mine & ((tokens & (slots - 1)) < chain(iota(tokens.shape, 0), every))
    high, low = split(nn(live.astype(BF16), xs))
    w = w_in[0].astype(BF16)
    total = nn(high, w) + nn(low, w)
    for m in range(parts):
        total = total + nn(pm[:, m * LANES : (m + 1) * LANES], w_out[m, 0])
    count = chain(iota(total.shape, 0), every).astype(F32)
    pooled[0] = (total / count).astype(BF16)


def backward_kernel(
    slots, cnt, x, w_in, gain, w_qkv, w_out, normed_in, qkv, prob, a_in, pm_in, dpooled, demb, d_in, d_gain, d_qkv, d_out, dqkv
):
    tower = pl.program_id(0)
    pairs, width = dpooled.shape[1:]
    parts = w_qkv.shape[0]
    per = LANES // slots
    groups = pairs // per
    heads = 2 * parts
    shift = slots.bit_length() - 1
    tokens = pairs * slots
    every = [cnt[tower * pairs + k] for k in range(pairs)]
    count = chain(iota((pairs, width), 0), every).astype(F32)
    dsum = dpooled[0].astype(F32) / count
    branch = dsum.astype(BF16)
    dmix = []
    for m in range(parts):
        grad = tn(pm_in[0, :, m * LANES : (m + 1) * LANES], branch).astype(BF16)
        for j in range(width // LANES):
            d_out[m, 0, j] = grad[:, j * LANES : (j + 1) * LANES]
        dmix.append(nt(branch, w_out[m, 0]))
    lane = iota((LANES, LANES), 1)
    line = iota((LANES, LANES), 0)
    pair_s = lax.shift_right_logical(line, shift)
    halves = [lane < DH, lane >= DH]
    own_head = iota((per * heads, LANES), 0) & (heads - 1)
    own_pair = lax.shift_right_logical(iota((per * heads, LANES), 0), heads.bit_length() - 1)
    token_pair = lax.shift_right_logical(iota((per * heads, LANES), 1), shift)
    for g in range(groups):
        rows = slice(g * LANES, (g + 1) * LANES)
        live_s = (line & (slots - 1)) < chain(pair_s, every[g * per : (g + 1) * per])
        scale = jnp.where(live_s, 0.125, 0.0)
        dots = jnp.zeros((per * heads, LANES), F32)
        stacks = []
        for m in range(parts):
            cut = dmix[m][g * per : (g + 1) * per]
            spread = jnp.concatenate([jnp.broadcast_to(cut[k : k + 1], (heads, LANES)) for k in range(per)], 0)
            head = iota((per * heads, LANES), 1) // DH + 2 * m
            stack = jnp.where(own_head == head, spread, 0.0).astype(BF16)
            stacks.append(stack)
            dots = dots + nt(stack, qkv[0, 2 * parts + m, rows, :])
        dots = jnp.where(own_pair == token_pair, dots, 0.0)
        pull = dots[0:heads]
        for k in range(1, per):
            pull = pull + dots[k * heads : (k + 1) * heads]
        for m in range(parts):
            query, key = qkv[0, m, rows, :], qkv[0, parts + m, rows, :]
            none = jnp.zeros_like(query)
            dq = jnp.zeros((LANES, LANES), F32)
            dk = jnp.zeros((LANES, LANES), F32)
            for half in range(2):
                h = 2 * m + half
                p = prob[0, g, h].astype(F32)
                t = p * pull[h : h + 1, :]
                ds = ((t - p * jnp.sum(t, 1, keepdims=True)) * scale).astype(BF16)
                dq = dq + nn(ds, jnp.where(halves[half], key, none))
                dk = dk + tn(ds, jnp.where(halves[half], query, none))
            dqkv[m, rows, :] = dq.astype(BF16)
            dqkv[parts + m, rows, :] = dk.astype(BF16)
            dqkv[2 * parts + m, rows, :] = tn(a_in[0, g], stacks[m]).astype(BF16)
    normed = normed_in[0]
    dnormed = jnp.zeros((tokens, width), F32)
    for m in range(parts):
        for c in range(3):
            grad = dqkv[c * parts + m]
            dnormed = dnormed + nt(grad, w_qkv[m, 0, c])
            d_qkv[m, 0, c] = tn(normed, grad).astype(BF16)
    dnormed = dnormed.astype(BF16).astype(F32)
    xs = x[0]
    w = w_in[0].astype(BF16)
    hidden = nn(xs, w)
    inverse = lax.rsqrt(jnp.mean(hidden * hidden, -1, keepdims=True) + EPS)
    unit = hidden * inverse
    d_gain[0] = jnp.sum(dnormed * unit, 0, keepdims=True)
    scaled = dnormed * gain[0]
    dh = inverse * (scaled - unit * jnp.mean(scaled * unit, -1, keepdims=True))
    spread = jnp.broadcast_to(dsum[:, None, :], (pairs, slots, width))
    slot = iota((pairs, slots, width), 1)
    counts = chain(iota((pairs, slots, width), 0), every)
    spread = jnp.where(slot < counts, spread, 0.0).reshape(tokens, width)
    dhidden = (spread + dh).astype(BF16)
    grad = tn(xs, dhidden).astype(BF16)
    for j in range(width // LANES):
        d_in[0, j] = grad[:, j * LANES : (j + 1) * LANES]
    demb[0] = nt(dhidden, w).astype(BF16)


def gelu_parts(v):
    c = 0.7978845608028654
    inner = jnp.tanh(c * (v + 0.044715 * (v * v * v)))
    value = 0.5 * v * (1.0 + inner)
    slope = 0.5 * (1.0 + inner) + 0.5 * v * (1.0 - inner * inner) * (c * (1.0 + 3.0 * 0.044715 * (v * v)))
    return value, slope


def upper_kernel(
    plane,
    line,
    pooled,
    w_one,
    w_two,
    w_three,
    prior_row,
    prior_col,
    pos_row,
    pos_own,
    dpooled,
    d_one,
    d_two,
    d_three,
    loss,
    pooled_all,
    second_send,
    second_got,
    vec,
    dsec_send,
    dsec_all,
    dpool_send,
    dpool_got,
    out_sems,
    in_sems,
    vec_out,
    vec_in,
):
    me, part = enter(plane, line)
    towers, own, width = pooled.shape
    rows = own * line
    pairs = rows * plane
    peers = [lax.rem(part + k, line) for k in range(1, line)]

    pooled_all[:, part] = pooled[...]
    first = [
        send(pooled_all.at[:, part], pooled_all.at[:, part], out_sems.at[0, k], in_sems.at[0, k], (me, peers[k]))
        for k in range(line - 1)
    ]
    one = [w_one[t].astype(BF16) for t in range(towers)]
    two = [w_two[t].astype(BF16) for t in range(towers)]
    three = [w_three[t].astype(BF16) for t in range(towers)]
    for copy in first:
        copy.wait()
    act_one, slope_one, pools = [], [], []
    for t in range(towers):
        pools.append(pooled_all[t].reshape(rows, width))
        value, slope = gelu_parts(nn(pools[t], one[t]))
        act_one.append(value.astype(BF16))
        slope_one.append(slope)
        second_send[t] = nn(act_one[t], two[t]).reshape(line, own, -1)
    second = [
        send(
            second_send.at[:, peers[k]], second_got.at[:, part], out_sems.at[1, k], in_sems.at[1, k], (me, peers[k])
        )
        for k in range(line - 1)
    ]
    for copy in second:
        copy.wait()
    act_two, slope_two, third, length, vectors = [], [], [], [], []
    for t in range(towers):
        total = second_send[t, part]
        for peer in peers:
            total = total + second_got[t, peer]
        value, slope = gelu_parts(total)
        act_two.append(value.astype(BF16))
        slope_two.append(slope)
        third.append(nn(act_two[t], three[t]))
        length.append(lax.rsqrt(jnp.sum(third[t] * third[t], -1, keepdims=True) + EPS))
        vectors.append((third[t] * length[t]).astype(BF16))
        vec[t, me, part] = vectors[t]
    along = [
        send(vec.at[:, me, part], vec.at[:, me, part], out_sems.at[2, k], in_sems.at[2, k], (me, peers[k]))
        for k in range(line - 1)
    ]
    for copy in along:
        copy.wait()
    across = [
        send(vec.at[:, me], vec.at[:, me], vec_out.at[k], vec_in.at[k], (lax.rem(me + k, plane), part))
        for k in range(1, plane)
    ]
    for copy in across:
        copy.wait()

    queries = vec[0].reshape(pairs, width)
    items = vec[1].reshape(pairs, width)
    logits = INV_TEMP * nt(items, queries) - prior_col[...]
    peak = jnp.max(logits, 0, keepdims=True)
    log_total = peak + jnp.log(jnp.sum(jnp.exp(logits - peak), 0, keepdims=True))
    picked = jnp.where(iota((pairs, pairs), 0) == pos_row[...], logits, 0.0)
    gap = log_total - jnp.sum(picked, 0, keepdims=True)
    loss[...] = jnp.broadcast_to(jnp.sum(gap, 1, keepdims=True), loss.shape)
    ahead = me * rows + part * own
    mine = INV_TEMP * nt(vectors[0], items) - prior_row[...]
    top = jnp.max(mine, 1, keepdims=True)
    expo = jnp.exp(mine - top)
    chance = expo / jnp.sum(expo, 1, keepdims=True)
    target = (iota(mine.shape, 1) == pos_own[...]).astype(F32)
    dlog = ((chance - target) / pairs).astype(BF16)
    dvec = [(INV_TEMP * nn(dlog, items)).astype(BF16)]
    own_prior = prior_col[pl.ds(pl.multiple_of(ahead, own), own), :]
    theirs = INV_TEMP * nt(vectors[1], queries) - own_prior
    target = (iota(theirs.shape, 0) + ahead == pos_row[...]).astype(F32)
    dlog = ((jnp.exp(theirs - log_total) - target) / pairs).astype(BF16)
    dvec.append((INV_TEMP * nn(dlog, queries)).astype(BF16))

    dthirds = []
    for t in range(towers):
        dv = dvec[t].astype(F32)
        inner = jnp.sum(dv * third[t], -1, keepdims=True)
        dthird = (length[t] * dv - third[t] * (length[t] * length[t] * length[t] * inner)).astype(BF16)
        dact = nt(dthird, three[t]).astype(BF16).astype(F32)
        dsec_all[t, part] = (dact * slope_two[t]).astype(BF16)
        dthirds.append(dthird)
    spread = [
        send(dsec_all.at[:, part], dsec_all.at[:, part], out_sems.at[3, k], in_sems.at[3, k], (me, peers[k]))
        for k in range(line - 1)
    ]
    for t in range(towers):
        grad = tn(act_two[t], dthirds[t]).astype(BF16)
        for j in range(width // LANES):
            d_three[t, j] = grad[:, j * LANES : (j + 1) * LANES]
    for copy in spread:
        copy.wait()
    dfirsts = []
    for t in range(towers):
        dsecond = dsec_all[t].reshape(rows, -1)
        dact = nt(dsecond, two[t]).astype(BF16).astype(F32)
        dfirst = (dact * slope_one[t]).astype(BF16)
        dpool_send[t] = nt(dfirst, one[t]).reshape(line, own, width)
        dfirsts.append(dfirst)
    back = [
        send(dpool_send.at[:, peers[k]], dpool_got.at[:, part], out_sems.at[4, k], in_sems.at[4, k], (me, peers[k]))
        for k in range(line - 1)
    ]
    for t in range(towers):
        dsecond = dsec_all[t].reshape(rows, -1)
        for grads, grad in ((d_two, tn(act_one[t], dsecond)), (d_one, tn(pools[t], dfirsts[t]))):
            grad = grad.astype(BF16)
            for j in range(grad.shape[1] // LANES):
                grads[t, j] = grad[:, j * LANES : (j + 1) * LANES]
    for copy in back:
        copy.wait()
    for t in range(towers):
        total = dpool_send[t, part]
        for peer in peers:
            total = total + dpool_got[t, peer]
        dpooled[t] = total.astype(BF16)


def update(weight, grad, moment, average, factor, rate):
    clipped = grad * factor
    moment_new = MOMENTUM * moment + clipped
    weight_new = weight - rate * (clipped + MOMENTUM * moment_new)
    average_new = AVERAGE_DECAY * average + (1.0 - AVERAGE_DECAY) * weight_new
    return [weight_new, moment_new, average_new]


def shards(
    slot_owner,
    slot_row,
    slot_count,
    item_qid,
    positive,
    log_prior,
    embedding,
    embedding_mom,
    embedding_avg,
    w_in,
    w_in_mom,
    w_in_avg,
    norm_gain,
    norm_gain_mom,
    norm_gain_avg,
    w_qkv,
    w_qkv_mom,
    w_qkv_avg,
    w_out,
    w_out_mom,
    w_out_avg,
    w_one,
    w_one_mom,
    w_one_avg,
    w_two,
    w_two_mom,
    w_two_avg,
    w_three,
    w_three_mom,
    w_three_avg,
):
    plane = lax.axis_size("dp")
    line = lax.axis_size("mp")
    batch, towers, slots = slot_row.shape
    own = batch // line
    requests = batch * towers * slots
    own_requests = requests // line
    tokens = own * slots
    capacity = max(LANES, 2 * requests // plane)
    pairs = batch * plane
    part = lax.axis_index("mp")
    me = lax.axis_index("dp")
    width = w_in.shape[2]
    depth = w_in.shape[1]
    units = w_one.shape[2]
    seconds = w_two.shape[2]

    def ordered(value):
        value = value.reshape(line, own, towers, slots)
        return jnp.transpose(value, (0, 2, 1, 3)).reshape(requests // LANES, LANES)

    owner = ordered(slot_owner)
    row = ordered(slot_row)
    own_chunks = own_requests // LANES
    own_owner = lax.dynamic_slice_in_dim(owner, part * own_chunks, own_chunks, 0)
    own_row = lax.dynamic_slice_in_dim(row, part * own_chunks, own_chunks, 0)
    per = capacity // LANES
    lists, inverse, own_place = pl.pallas_call(
        functools.partial(prep_kernel, plane, capacity),
        out_shape=[
            shape((plane, 2 * per, LANES), I32),
            shape((plane * per, LANES), I32),
            shape((own_chunks, LANES), I32),
        ],
        in_specs=[VMEM] * 4,
        out_specs=[VMEM] * 3,
        compiler_params=params(32),
        name="request_lists",
    )(owner, row, own_owner, own_row)
    lone = jnp.pad(positive[None, :], ((0, 7), (0, LANES - batch)))
    embedded, got_lists, got_pos, wide_qkv, wide_out = pl.pallas_call(
        functools.partial(fetch_kernel, plane, line, capacity),
        out_shape=[
            shape((own_requests, depth), BF16),
            shape(lists.shape, I32),
            shape((plane, 8, LANES), I32),
            shape((line, towers, 3, width, LANES), BF16),
            shape((line, towers, LANES, width), BF16),
        ],
        in_specs=[VMEM, VMEM, SMEM, VMEM, VMEM, VMEM],
        out_specs=[VMEM] * 5,
        scratch_shapes=[
            pltpu.SMEM(lists.shape, I32),
            pltpu.VMEM((plane, capacity, depth), BF16),
            pltpu.VMEM((plane, capacity, depth), BF16),
            pltpu.VMEM((plane * capacity, depth), F32),
            DMA((2, plane)),
            DMA((2, plane)),
            DMA((plane,)),
            DMA((plane,)),
            DMA((2, line)),
            DMA((2, line)),
            DMA((2, line)),
            DMA((2, line)),
            DMA((3,)),
        ],
        compiler_params=params(56, collective_id=2, has_side_effects=True),
        name="fetch",
    )(lists, lone, own_place, embedding, jnp.transpose(w_qkv, (0, 2, 1, 3)), w_out)
    embedded = embedded.reshape(towers, tokens, depth)

    counts = jnp.transpose(slot_count).reshape(towers, line, own)
    counts = lax.dynamic_index_in_dim(counts, part, 1, keepdims=False).reshape(towers * own)
    heads = 2 * line
    gains = norm_gain.reshape(towers, 1, width)
    groups = tokens // LANES
    per_group = LANES // slots
    lead = lambda *dims: pl.BlockSpec((1,) + dims, lambda t: (t,) + (0,) * len(dims))
    qkv_spec = pl.BlockSpec((line, 1, 3, width, LANES), lambda t: (0, t, 0, 0, 0))
    out_spec = pl.BlockSpec((line, 1, LANES, width), lambda t: (0, t, 0, 0))
    pooled, pm, normed, qkv, prob, spread = pl.pallas_call(
        functools.partial(forward_kernel, slots),
        grid=(towers,),
        out_shape=[
            shape((towers, own, width), BF16),
            shape((towers, own, line * LANES), BF16),
            shape((towers, tokens, width), BF16),
            shape((towers, 3 * line, tokens, LANES), BF16),
            shape((towers, groups, heads, LANES, LANES), BF16),
            shape((towers, groups, per_group * heads, LANES), BF16),
        ],
        in_specs=[SMEM, lead(tokens, depth), lead(depth, width), lead(1, width), qkv_spec, out_spec],
        out_specs=[
            lead(own, width),
            lead(own, line * LANES),
            lead(tokens, width),
            lead(3 * line, tokens, LANES),
            lead(groups, heads, LANES, LANES),
            lead(groups, per_group * heads, LANES),
        ],
        scratch_shapes=[pltpu.VMEM((groups, per_group, line * LANES), F32)],
        compiler_params=params(48),
        name="attention_forward",
    )(counts, embedded, w_in, gains, wide_qkv, wide_out)

    prior = jnp.sum(
        jnp.where(item_qid[:, None] == jnp.arange(log_prior.shape[0])[None, :], log_prior[None, :], 0.0), 1
    )
    positions = got_pos[:, 0, :batch].reshape(1, pairs)
    own_positions = lax.dynamic_slice_in_dim(positive, part * own, own, 0).reshape(own, 1)
    dpooled, d_one, d_two, d_three, loss = pl.pallas_call(
        functools.partial(upper_kernel, plane, line),
        out_shape=[
            shape((towers, own, width), BF16),
            shape((towers, units // LANES, width, LANES), BF16),
            shape((towers, seconds // LANES, units, LANES), BF16),
            shape((towers, width // LANES, seconds, LANES), BF16),
            shape((8, LANES), F32),
        ],
        in_specs=[VMEM] * 8,
        out_specs=[VMEM] * 5,
        scratch_shapes=[
            pltpu.VMEM((towers, line, own, width), BF16),
            pltpu.VMEM((towers, line, own, seconds), F32),
            pltpu.VMEM((towers, line, own, seconds), F32),
            pltpu.VMEM((towers, plane, line, own, width), BF16),
            pltpu.VMEM((towers, line, own, seconds), BF16),
            pltpu.VMEM((towers, line, own, seconds), BF16),
            pltpu.VMEM((towers, line, own, width), F32),
            pltpu.VMEM((towers, line, own, width), F32),
            DMA((5, line)),
            DMA((5, line)),
            DMA((plane,)),
            DMA((plane,)),
        ],
        compiler_params=params(56, collective_id=3, has_side_effects=True),
        name="upper",
    )(pooled, w_one, w_two, w_three, prior.reshape(1, pairs), prior.reshape(pairs, 1), positions, own_positions)

    demb, d_in, d_gain, d_qkv, d_out = pl.pallas_call(
        functools.partial(backward_kernel, slots),
        grid=(towers,),
        out_shape=[
            shape((towers, tokens, depth), BF16),
            shape((towers, width // LANES, depth, LANES), BF16),
            shape((towers, 1, width), F32),
            shape((line, towers, 3, width, LANES), BF16),
            shape((line, towers, width // LANES, LANES, LANES), BF16),
        ],
        in_specs=[
            SMEM,
            lead(tokens, depth),
            lead(depth, width),
            lead(1, width),
            qkv_spec,
            out_spec,
            lead(tokens, width),
            lead(3 * line, tokens, LANES),
            lead(groups, heads, LANES, LANES),
            lead(groups, per_group * heads, LANES),
            lead(own, line * LANES),
            lead(own, width),
        ],
        out_specs=[
            lead(tokens, depth),
            lead(width // LANES, depth, LANES),
            lead(1, width),
            qkv_spec,
            pl.BlockSpec((line, 1, width // LANES, LANES, LANES), lambda t: (0, t, 0, 0, 0)),
        ],
        scratch_shapes=[pltpu.VMEM((3 * line, tokens, LANES), BF16)],
        compiler_params=params(56),
        name="attention_backward",
    )(counts, embedded, w_in, gains, wide_qkv, wide_out, normed, qkv, prob, spread, pm, dpooled)

    def shares(grad, lead=()):
        rows = grad.size // (LANES * plane * (lead[0] if lead else 1))
        return grad.reshape(*lead, plane // 2, 2, rows, LANES)

    grads = [shares(d_qkv, (line,)), shares(d_out, (line,))] + [shares(g) for g in (d_three, d_in, d_one, d_two)]
    sizes = [g.shape[-2] for g in grads]
    share = line * (sizes[0] + sizes[1]) + sum(sizes[2:])
    gain_rows = jnp.pad(d_gain.reshape(-1, LANES), ((0, 8 - d_gain.size // LANES), (0, 0)))
    every, summed, gain_sum = pl.pallas_call(
        functools.partial(spread_kernel, plane, line),
        out_shape=[
            shape((line, own_requests, depth), BF16),
            shape((share, LANES), BF16),
            shape((8, LANES), F32),
        ],
        in_specs=[VMEM] * 8,
        out_specs=[VMEM] * 3,
        scratch_shapes=[
            [pltpu.VMEM((line, plane // 2, size, LANES), BF16) for size in sizes[:2]],
            [pltpu.VMEM((plane // 2, size, LANES), BF16) for size in sizes[2:]],
            pltpu.VMEM((plane // 2, share, LANES), BF16),
            pltpu.VMEM((plane // 2 - 1, share, LANES), BF16),
            pltpu.VMEM((plane, 8, LANES), F32),
            DMA((line,)),
            DMA((line,)),
            DMA((6,)),
            DMA((6,)),
            DMA((plane // 2,)),
            DMA((plane // 2,)),
            DMA((plane,)),
            DMA((plane,)),
            DMA,
        ],
        compiler_params=params(48, collective_id=4, has_side_effects=True),
        name="spread",
    )(demb.reshape(own_requests, depth), *grads, gain_rows)
    whole_at = line * (sizes[0] + sizes[1])
    whole_rows = sizes[2] + sizes[3]
    last_rows = sizes[4] + sizes[5]
    cuts = (
        ((0, sizes[0]), (line * sizes[0], sizes[1])),
        (whole_at, whole_rows),
        (whole_at + whole_rows, last_rows),
    )
    line_rows = sizes[0] + sizes[1] + whole_rows
    incoming, dense, dense_sq, gain_all = pl.pallas_call(
        functools.partial(return_kernel, plane, line, capacity, cuts),
        out_shape=[
            shape((plane, capacity, depth), BF16),
            shape((line_rows + last_rows, LANES), BF16),
            shape((8, LANES), F32),
            shape((8, LANES), F32),
        ],
        in_specs=[SMEM, VMEM, VMEM, VMEM],
        out_specs=[VMEM] * 4,
        scratch_shapes=[
            pltpu.VMEM((requests, depth), F32),
            pltpu.VMEM((plane, capacity, depth), BF16),
            pltpu.VMEM((line, line_rows, LANES), BF16),
            pltpu.VMEM((line, 8, LANES), F32),
            DMA((plane,)),
            DMA((plane,)),
            DMA((3, line)),
            DMA((3, line)),
            DMA((line,)),
            DMA((line,)),
            DMA,
        ],
        compiler_params=params(48, collective_id=5, has_side_effects=True),
        name="return_rows",
    )(inverse.reshape(plane, per, LANES), every.reshape(requests, depth), summed, gain_sum)
    served = got_lists[:, :per, :].reshape(plane, capacity)
    table_grad, table_sq = pl.pallas_call(
        functools.partial(scatter_kernel, capacity),
        out_shape=[shape(embedding.shape, F32), shape((8, LANES), F32)],
        in_specs=[SMEM, SMEM, VMEM],
        out_specs=[VMEM, VMEM],
        scratch_shapes=[pltpu.VMEM((capacity, depth), F32)],
        compiler_params=params(48),
        name="add_rows",
    )(jnp.maximum(served, 0), jnp.sum((served >= 0).astype(I32), 1), incoming)

    norm_sq, dense_all = pl.pallas_call(
        functools.partial(norm_kernel, plane, line),
        out_shape=[shape((8, LANES), F32), shape((plane, *dense.shape), BF16)],
        in_specs=[VMEM] * 4,
        out_specs=[VMEM] * 2,
        scratch_shapes=[
            pltpu.VMEM((line, 8, LANES), F32),
            pltpu.VMEM((plane, 8, LANES), F32),
            DMA((line,)),
            DMA((line,)),
            DMA((plane,)),
            DMA((plane,)),
            DMA((plane // 2,)),
            DMA((plane // 2,)),
            DMA((plane // 2,)),
            DMA((plane // 2,)),
            DMA,
        ],
        compiler_params=params(32, collective_id=6, has_side_effects=True),
        name="norm_parts",
    )(table_sq, dense_sq, dense, gain_all)
    norm = jnp.sqrt(norm_sq[0, 0])
    factor = jnp.minimum(1.0, CLIP_NORM / norm)
    found, at = [], 0
    for size in sizes:
        found.append(dense_all[:, at : at + size].astype(F32))
        at += size
    d_qkv = jnp.transpose(found[0].reshape(towers, 3, width, LANES), (0, 2, 1, 3))
    side = lambda grad, rows: jnp.transpose(grad.reshape(towers, -1, rows, LANES), (0, 2, 1, 3)).reshape(towers, rows, -1)
    d_out, d_three, d_in = side(found[1], LANES), side(found[2], seconds), side(found[3], depth)
    d_one, d_two = side(found[4], width), side(found[5], units)
    d_gain = gain_all[: d_gain.size // LANES].reshape(towers, width)
    done = []
    done.extend(update(embedding, table_grad, embedding_mom, embedding_avg, factor, ROW_RATE))
    done.extend(update(w_in, d_in, w_in_mom, w_in_avg, factor, MATRIX_RATE))
    done.extend(update(norm_gain, d_gain, norm_gain_mom, norm_gain_avg, factor, GAIN_RATE))
    done.extend(update(w_qkv, d_qkv, w_qkv_mom, w_qkv_avg, factor, MATRIX_RATE))
    done.extend(update(w_out, d_out, w_out_mom, w_out_avg, factor, MATRIX_RATE))
    done.extend(update(w_one, d_one, w_one_mom, w_one_avg, factor, MATRIX_RATE))
    done.extend(update(w_two, d_two, w_two_mom, w_two_avg, factor, MATRIX_RATE))
    done.extend(update(w_three, d_three, w_three_mom, w_three_avg, factor, MATRIX_RATE))
    return (loss[0, 0], norm, *done)


def solution(mesh):
    rows = P("dp", None)
    qkv = P(None, None, None, "mp")
    deep = P(None, "mp", None)
    wide = P(None, None, "mp")
    weights = (rows,) * 3 + (P(),) * 6 + (qkv,) * 3 + (deep,) * 3 + (wide,) * 3 + (deep,) * 3 + (P(),) * 3
    inputs = (P("dp", None, None, None), P("dp", None, None), P("dp", None), P(), P("dp"), P())
    return jax.shard_map(
        shards, mesh=mesh, in_specs=inputs + weights, out_specs=(P(), P()) + weights, check_vma=False
    )
```

```python
import functools

import jax
import jax.numpy as jnp
from jax import lax
from jax.experimental import pallas as pl
from jax.experimental.pallas import tpu as pltpu
from jax.sharding import PartitionSpec as P

DH = 64
EPS = 1e-06
INV_TEMP = 20.0
CLIP_NORM = 0.1
ROW_RATE = 150000.0
GAIN_RATE = 8000.0
MATRIX_RATE = 600.0
MOMENTUM = 0.9
AVERAGE_DECAY = 0.6

MESH = pl.DeviceIdType.MESH
LANES = 128
F32 = jnp.float32
BF16 = jnp.bfloat16
I32 = jnp.int32
VMEM = pl.BlockSpec(memory_space=pltpu.VMEM)
HBM = pl.BlockSpec(memory_space=pltpu.HBM)
SMEM = pl.BlockSpec(memory_space=pltpu.SMEM)
DMA = pltpu.SemaphoreType.DMA


def nn(a, b):
    return lax.dot_general(a, b, (((1,), (0,)), ((), ())), preferred_element_type=F32)


def nt(a, b):
    return lax.dot_general(a, b, (((1,), (1,)), ((), ())), preferred_element_type=F32)


def tn(a, b):
    return lax.dot_general(a, b, (((0,), (0,)), ((), ())), preferred_element_type=F32)


def iota(shape, dim):
    return lax.broadcasted_iota(I32, shape, dim)


def split(value):
    high = value.astype(BF16)
    return high, (value - high.astype(F32)).astype(BF16)


def shape(dims, dtype):
    return jax.ShapeDtypeStruct(tuple(dims), dtype)


def params(limit, **more):
    return pltpu.CompilerParams(vmem_limit_bytes=limit << 20, **more)


def lists_of(owner, row, owners, capacity):
    chunks = owner.shape[0]
    width = owners * capacity
    his = width // LANES
    sub = iota((owners, LANES), 0)
    hots = jnp.concatenate([(owner[c : c + 1, :] == sub).astype(F32) for c in range(chunks)], 0).astype(BF16)
    before = (iota((LANES, LANES), 0) < iota((LANES, LANES), 1)).astype(BF16)
    earlier = nn(hots, before)
    totals = nn(hots, jnp.ones((LANES, LANES), BF16))
    base = (sub * capacity).astype(F32)
    places = []
    for c in range(chunks):
        cut = slice(c * owners, (c + 1) * owners)
        at = hots[cut].astype(F32) * (earlier[cut] + base)
        here = jnp.sum(at, 0, keepdims=True).astype(I32)
        places.append(jnp.where(owner[c : c + 1, :] < owners, here, width))
        base = base + totals[cut]
    acc = jnp.zeros((his, 4 * LANES), F32)
    for c in range(chunks):
        place = places[c]
        value = row[c : c + 1, :]
        token = iota((1, LANES), 1) + c * LANES
        left = (lax.shift_right_logical(place, 7) == iota((his, LANES), 0)).astype(BF16)
        low = (place & 127) == iota((LANES, LANES), 0)
        parts = [lax.shift_right_logical(value, 6), value & 63, lax.shift_right_logical(token, 6), token & 63]
        right = jnp.concatenate([jnp.where(low, part.astype(F32), 0.0) for part in parts], 0)
        acc = acc + nt(left, right.astype(BF16))
    cuts = [acc[:, k * LANES : (k + 1) * LANES].astype(I32) for k in range(4)]
    totals = [totals[c * owners : (c + 1) * owners] for c in range(chunks)]
    return places, cuts[0] * 64 + cuts[1], cuts[2] * 64 + cuts[3], totals


def prep_kernel(owners, capacity, small, line, owner, row, own_owner, own_row, positive, lists, inverse, own_place, own_small, extra):
    per = capacity // LANES
    _, rows, tokens, totals = lists_of(owner[...], row[...] + 1, owners, capacity)
    places, own_rows, _, _ = lists_of(own_owner[...], own_row[...], owners, capacity)
    rows = rows - 1
    inverse[...] = tokens
    for d in range(owners):
        lists[d, 0:per, :] = rows[d * per : (d + 1) * per, :]
        lists[d, per : 2 * per, :] = own_rows[d * per : (d + 1) * per, :]
    bits = capacity.bit_length() - 1
    for c, place in enumerate(places):
        place = jnp.where(place < owners * capacity, place, 0)
        own_place[c : c + 1, :] = place
        rank = jnp.minimum(place & (capacity - 1), small - 1)
        own_small[c : c + 1, :] = lax.shift_right_logical(place, bits) * small + rank
    cut = len(totals) // line
    blocks = [sum(totals[m * cut + 1 : (m + 1) * cut], totals[m * cut]) for m in range(line)]
    most = jnp.zeros((1, LANES), F32)
    for block in blocks:
        most = jnp.maximum(most, jnp.max(block, 0, keepdims=True))
    every = jnp.max(sum(blocks[1:], blocks[0]), 0, keepdims=True)
    extra[...] = jnp.zeros_like(extra)
    extra[0:1, 0 : positive.shape[1]] = positive[...]
    extra[1:2, :] = most.astype(I32)
    extra[2:3, :] = every.astype(I32)


def enter(plane, line):
    me, part = lax.axis_index("dp"), lax.axis_index("mp")
    barrier = pltpu.get_barrier_semaphore()
    for k in range(1, plane):
        pl.semaphore_signal(barrier, inc=1, device_id=(lax.rem(me + k, plane), part), device_id_type=MESH)
    for k in range(1, line):
        pl.semaphore_signal(barrier, inc=1, device_id=(me, lax.rem(part + k, line)), device_id_type=MESH)
    pl.semaphore_wait(barrier, max(plane - 1, 0) + max(line - 1, 0))
    return me, part


def send(source, target, out_sem, in_sem, device):
    copy = pltpu.make_async_remote_copy(
        src_ref=source, dst_ref=target, send_sem=out_sem, recv_sem=in_sem, device_id=device, device_id_type=MESH
    )
    copy.start()
    return copy


def gather_rows(ids, table, target):
    per = LANES // 16

    def body(i, carry):
        at = pl.multiple_of(i * 16, 16)
        block = lax.shift_right_logical(i, 3)
        first = (i & (per - 1)) * 16
        rows = [table[pl.ds(ids(block, first + u), 1), :] for u in range(16)]
        target[pl.ds(at, 16), :] = jnp.concatenate(rows, 0).astype(BF16)
        return carry

    lax.fori_loop(0, target.shape[0] // 16, body, 0)


def send_rows(plane, me, part, ids, table, sent, got, wide, out_sems, in_sems):
    capacity = sent.shape[1]
    half = ids.shape[1] // 2
    copies = []
    for k in range(1, plane):
        peer = lax.rem(me + k, plane)
        gather_rows(lambda b, j, peer=peer: ids[peer, half + b, j], table, sent.at[peer])
        copies.append(send(sent.at[peer], got.at[me], out_sems.at[k], in_sems.at[k], (peer, part)))
    gather_rows(lambda b, j: ids[me, half + b, j], table, sent.at[me])
    wide[pl.ds(pl.multiple_of(me * capacity, capacity), capacity), :] = sent[me].astype(F32)
    return copies


def take_rows(plane, me, copies, place, got, wide, out):
    capacity = got.shape[1]
    for k in range(1, plane):
        peer = lax.rem(me - k + plane, plane)
        copies[k - 1].wait_recv()
        wide[pl.ds(pl.multiple_of(peer * capacity, capacity), capacity), :] = got[peer].astype(F32)
    gather_rows(lambda b, j: place[b, j], wide, out)


def refetch_kernel(plane, ids, place, table, out, sent, got, wide, out_sems, in_sems):
    me, part = enter(plane, 0)
    copies = send_rows(plane, me, part, ids, table, sent, got, wide, out_sems, in_sems)
    take_rows(plane, me, copies, place, got, wide, out)
    for copy in copies:
        copy.wait_send()


def fetch_kernel(
    plane,
    line,
    lists,
    extra,
    place,
    table,
    w_qkv,
    w_out,
    out,
    got_lists,
    got_extra,
    wide_qkv,
    wide_out,
    ids,
    sent,
    got,
    wide,
    list_out,
    list_in,
    out_sems,
    in_sems,
    far_out,
    far_in,
    near_out,
    near_in,
    own_sems,
):
    me, part = enter(plane, line)
    core = lax.rem(me, 2)
    sibling = me + 1 - 2 * core
    wide_qkv[part] = w_qkv[...].astype(BF16)
    wide_out[part] = w_out[...].astype(BF16)
    far = []
    for k in range(1, line):
        peer = lax.rem(part + k, line)
        for j, block in enumerate((wide_qkv, wide_out)):
            at = block.at[part, core]
            far.append(send(at, at, far_out.at[j, k], far_in.at[j, k], (me, peer)))
    asked = []
    for k in range(1, plane):
        peer = lax.rem(me + k, plane)
        asked.append(send(lists.at[peer], got_lists.at[me], list_out.at[0, k], list_in.at[0, k], (peer, part)))
        asked.append(send(extra, got_extra.at[me], list_out.at[1, k], list_in.at[1, k], (peer, part)))
    mine = [
        pltpu.make_async_copy(lists.at[me], got_lists.at[me], own_sems.at[0]),
        pltpu.make_async_copy(extra, got_extra.at[me], own_sems.at[1]),
    ]
    for copy in mine:
        copy.start()
    for copy in mine + asked:
        copy.wait()
    numbers = pltpu.make_async_copy(got_lists, ids, own_sems.at[2])
    numbers.start()
    numbers.wait()
    copies = send_rows(plane, me, part, ids, table, sent, got, wide, out_sems, in_sems)
    near = []
    for k in range(1, line):
        peer = lax.rem(part - k + line, line)
        for j, block in enumerate((wide_qkv, wide_out)):
            far[2 * (k - 1) + j].wait_recv()
            at = block.at[peer, core]
            near.append(send(at, at, near_out.at[j, k], near_in.at[j, k], (sibling, part)))
    take_rows(plane, me, copies, place, got, wide, out)
    for copy in copies + far:
        copy.wait_send()
    for copy in near:
        copy.wait()


def spread_kernel(
    plane,
    line,
    mine,
    d_qkv,
    d_out,
    d_three,
    d_in,
    d_one,
    d_two,
    gain,
    out,
    summed,
    gain_sum,
    near_split,
    near_whole,
    half,
    got,
    gains,
    far_out,
    far_in,
    near_out,
    near_in,
    sum_out,
    sum_in,
    gain_out,
    gain_in,
    own_sem,
):
    me, part = enter(plane, line)
    chips = plane // 2
    core = lax.rem(me, 2)
    chip = me // 2
    sibling = me + 1 - 2 * core
    copies = []
    for k in range(1, line):
        peer = lax.rem(part + k, line)
        copies.append(send(mine, out.at[part], far_out.at[k], far_in.at[k], (me, peer)))
    split_grads, whole_grads = (d_qkv, d_out), (d_three, d_in, d_one, d_two)
    first = []
    for j, grad in enumerate(split_grads):
        first.append(send(grad.at[:, :, 1 - core], near_split[j], near_out.at[j], near_in.at[j], (sibling, part)))
    for j, grad in enumerate(whole_grads, len(split_grads)):
        first.append(send(grad.at[:, 1 - core], near_whole[j - 2], near_out.at[j], near_in.at[j], (sibling, part)))
    for k in range(1, plane):
        peer = lax.rem(me + k, plane)
        copies.append(send(gain, gains.at[me], gain_out.at[k], gain_in.at[k], (peer, part)))
    own = pltpu.make_async_copy(mine, out.at[part], own_sem)
    own.start()
    gains[me] = gain[...]
    for copy in first:
        copy.wait()
    for c in range(chips):
        at = 0
        for j, grad in enumerate(split_grads):
            rows = grad.shape[3]
            for m in range(line):
                total = grad[m, c, core].astype(F32) + near_split[j][m, c].astype(F32)
                half[c, at : at + rows, :] = total.astype(BF16)
                at += rows
        for j, grad in enumerate(whole_grads):
            rows = grad.shape[2]
            total = grad[c, core].astype(F32) + near_whole[j][c].astype(F32)
            half[c, at : at + rows, :] = total.astype(BF16)
            at += rows
    sums = []
    for k in range(1, chips):
        to = lax.rem(chip + k, chips)
        sums.append(send(half.at[to], got.at[k - 1], sum_out.at[k], sum_in.at[k], (2 * to + core, part)))
    for copy in sums:
        copy.wait()
    total = half[chip].astype(F32)
    for k in range(chips - 1):
        total = total + got[k].astype(F32)
    summed[...] = total.astype(BF16)
    own.wait()
    for copy in copies:
        copy.wait()
    total = gains[0]
    for d in range(1, plane):
        total = total + gains[d]
    gain_sum[...] = total


def return_kernel(
    plane,
    line,
    capacity,
    cuts,
    tokens,
    rows,
    summed,
    gain,
    out,
    dense,
    dense_sq,
    gain_all,
    wide,
    sent,
    got,
    gains,
    out_sems,
    in_sems,
    far_out,
    far_in,
    gain_out,
    gain_in,
    own_sem,
):
    me, part = enter(plane, line)
    far = []
    split_cuts, (whole_at, whole_rows), (last_at, last_rows) = cuts
    for k in range(1, line):
        peer = lax.rem(part + k, line)
        to = 0
        for j, (at, count) in enumerate(split_cuts):
            begin = pl.multiple_of(at + peer * count, 16)
            far.append(
                send(summed.at[pl.ds(begin, count)], got.at[part, to : to + count], far_out.at[j, k], far_in.at[j, k], (me, peer))
            )
            to += count
        target = got.at[part, to : to + whole_rows]
        source = summed.at[whole_at : whole_at + whole_rows]
        far.append(send(source, target, far_out.at[2, k], far_in.at[2, k], (me, peer)))
        far.append(send(gain, gains.at[part], gain_out.at[k], gain_in.at[k], (me, peer)))
    gains[part] = gain[...]
    wide[...] = rows[...].astype(F32)
    copies = []
    for k in range(1, plane):
        peer = lax.rem(me + k, plane)
        gather_rows(lambda b, j, peer=peer: tokens[peer, b, j], wide, sent.at[peer])
        target = out.at[me, 0:capacity]
        copies.append(send(sent.at[peer], target, out_sems.at[k], in_sems.at[k], (peer, part)))
    gather_rows(lambda b, j: tokens[me, b, j], wide, sent.at[me])
    own = pltpu.make_async_copy(sent.at[me], out.at[me, 0:capacity], own_sem)
    own.start()
    to = 0
    for at, count in split_cuts:
        got[part, to : to + count] = summed[pl.ds(pl.multiple_of(at + part * count, 16), count), :]
        to += count
    got[part, to : to + whole_rows] = summed[whole_at : whole_at + whole_rows, :]
    for copy in far:
        copy.wait()
    total = got[0].astype(F32)
    for m in range(1, line):
        total = total + got[m].astype(F32)
    dense[0 : to + whole_rows, :] = total.astype(BF16)
    dense[to + whole_rows :, :] = summed[last_at : last_at + last_rows, :]
    square = jnp.zeros((8, LANES), F32)
    for begin, count, weight in ((0, to, 1.0), (to, whole_rows, 1.0 / line), (to + whole_rows, last_rows, 1.0)):
        block = dense[begin : begin + count, :].astype(F32)
        square = square + weight * jnp.sum((block * block).reshape(count // 8, 8, LANES), 0)
    dense_sq[...] = square
    total = gains[0]
    for m in range(1, line):
        total = total + gains[m]
    gain_all[...] = total
    own.wait()
    for copy in copies:
        copy.wait()


def scatter_kernel(ids, counts, rows, out, square, wide, *others):
    tables = (out, *others)
    ways = len(tables)
    for table in tables:
        table[...] = jnp.zeros_like(table)
    step = 4 * ways

    for d in range(rows.shape[0]):
        count = counts[d]

        def widen(i, carry):
            at = pl.ds(pl.multiple_of(i * 64, 64), 64)
            wide[at, :] = rows[d, at, :].astype(F32)
            return carry

        lax.fori_loop(0, lax.shift_right_logical(count + 63, 6), widen, 0)

        def body(i, carry):
            for u in range(0, step, ways):
                first = i * step + u
                at = [ids[d, first + n] for n in range(ways)]
                sums = [
                    table[pl.ds(at[n], 1), :] + wide[pl.ds(first + n, 1), :] for n, table in enumerate(tables)
                ]
                for n, table in enumerate(tables):
                    table[pl.ds(at[n], 1), :] = sums[n]
            return carry

        def rest(j, carry):
            at = ids[d, j]
            out[pl.ds(at, 1), :] = out[pl.ds(at, 1), :] + wide[pl.ds(j, 1), :]
            return carry

        full = lax.div(count, step)
        lax.fori_loop(0, full, body, 0)
        lax.fori_loop(full * step, count, rest, 0)

    def add(i, total):
        at = pl.ds(pl.multiple_of(i * 32, 32), 32)
        block = out[at, :]
        for table in others:
            block = block + table[at, :]
        out[at, :] = block
        block = block * block
        for r in range(4):
            total = total + block[r * 8 : (r + 1) * 8, :]
        return total

    square[...] = lax.fori_loop(0, out.shape[0] // 32, add, jnp.zeros((8, LANES), F32))


def norm_kernel(
    plane,
    line,
    table_sq,
    dense_sq,
    dense,
    gain,
    norm_sq,
    dense_all,
    along,
    across,
    along_out,
    along_in,
    across_out,
    across_in,
    far_out,
    far_in,
    near_out,
    near_in,
    own_sem,
):
    me, part = enter(plane, line)
    chips = plane // 2
    core = lax.rem(me, 2)
    chip = me // 2
    sibling = me + 1 - 2 * core
    across[me] = dense_sq[...] + table_sq[...] * (1.0 / line)
    tiny = [
        send(across.at[me], across.at[me], across_out.at[k], across_in.at[k], (lax.rem(me + k, plane), part))
        for k in range(1, plane)
    ]
    far = []
    for k in range(1, chips):
        to = lax.rem(chip + k, chips)
        far.append(send(dense, dense_all.at[me], far_out.at[k], far_in.at[k], (2 * to + core, part)))
    near = [send(dense, dense_all.at[me], near_out.at[0], near_in.at[0], (sibling, part))]
    own = pltpu.make_async_copy(dense, dense_all.at[me], own_sem)
    own.start()
    for copy in tiny:
        copy.wait()
    total = across[0]
    for d in range(1, plane):
        total = total + across[d]
    along[part] = total
    peers = [lax.rem(part + k, line) for k in range(1, line)]
    tiny = [
        send(along.at[part], along.at[part], along_out.at[k], along_in.at[k], (me, peer)) for k, peer in enumerate(peers)
    ]
    for k in range(1, chips):
        peer = 2 * lax.rem(chip - k + chips, chips) + core
        far[k - 1].wait_recv()
        near.append(send(dense_all.at[peer], dense_all.at[peer], near_out.at[k], near_in.at[k], (sibling, part)))
    for copy in tiny:
        copy.wait()
    total = along[0]
    for m in range(1, line):
        total = total + along[m]
    gains = gain[...]
    norm_sq[...] = jnp.broadcast_to(jnp.sum(total + gains * gains), norm_sq.shape)
    own.wait()
    for copy in far:
        copy.wait_send()
    for copy in near:
        copy.wait()


def chain(index, values):
    out = jnp.full(index.shape, values[0], values[0].dtype)
    for k in range(1, len(values)):
        out = jnp.where(index >= k, values[k], out)
    return out


def forward_kernel(slots, cnt, x, w_in, gain, w_qkv, w_out, pooled, pm_out, normed_out, qkv, prob, a_out, pm_acc):
    tower = pl.program_id(0)
    pairs = pooled.shape[1]
    parts = w_qkv.shape[0]
    per = LANES // slots
    groups = pairs // per
    heads = 2 * parts
    xs = x[0]
    hidden = nn(xs, w_in[0].astype(BF16))
    inverse = lax.rsqrt(jnp.mean(hidden * hidden, -1, keepdims=True) + EPS)
    normed = (hidden * inverse * gain[0]).astype(BF16)
    normed_out[0] = normed
    for c in range(3):
        for m in range(parts):
            qkv[0, c * parts + m] = nn(normed, w_qkv[m, 0, c]).astype(BF16)
    lane = iota((LANES, LANES), 1)
    line = iota((LANES, LANES), 0)
    shift = slots.bit_length() - 1
    pair_r, pair_s = lax.shift_right_logical(lane, shift), lax.shift_right_logical(line, shift)
    same = pair_r == pair_s
    halves = [lane < DH, lane >= DH]
    own_head = iota((per * heads, LANES), 0) & (heads - 1)

    def group(g, carry):
        counts = [cnt[tower * pairs + g * per + k] for k in range(per)]
        live_r = same & ((lane & (slots - 1)) < chain(pair_r, counts))
        live_s = (line & (slots - 1)) < chain(pair_s, counts)
        rows = pl.ds(pl.multiple_of(g * LANES, LANES), LANES)
        sums = []
        for m in range(parts):
            query, key = qkv[0, m, rows, :], qkv[0, parts + m, rows, :]
            for half in range(2):
                scores = nt(jnp.where(halves[half], query, jnp.zeros_like(query)), key) * 0.125
                scores = jnp.where(live_r, scores, -1000000000.0)
                expo = jnp.exp(scores - jnp.max(scores, 1, keepdims=True))
                p = (expo * (1.0 / jnp.sum(expo, 1, keepdims=True))).astype(BF16)
                prob[0, g, 2 * m + half] = p
                sums.append(jnp.sum(jnp.where(live_s, p.astype(F32), 0.0), 0, keepdims=True))
        sums = jnp.concatenate(sums, 0)
        pair_l = lax.shift_right_logical(iota((heads, LANES), 1), shift)
        stack = jnp.concatenate([jnp.where(pair_l == k, sums, 0.0) for k in range(per)], 0).astype(BF16)
        a_out[0, g] = stack
        for m in range(parts):
            mix = nn(stack, qkv[0, 2 * parts + m, rows, :])
            head = iota((per * heads, LANES), 1) // DH + 2 * m
            mix = jnp.where(own_head == head, mix, 0.0)
            pm_acc[g, :, m * LANES : (m + 1) * LANES] = jnp.concatenate(
                [jnp.sum(mix[k * heads : (k + 1) * heads], 0, keepdims=True) for k in range(per)], 0
            )
        return carry

    lax.fori_loop(0, groups, group, 0)
    pm = jnp.concatenate([pm_acc[g] for g in range(groups)], 0).astype(BF16)
    pm_out[0] = pm
    every = [cnt[tower * pairs + k] for k in range(pairs)]
    tokens = iota((pairs, pairs * slots), 1)
    mine = lax.shift_right_logical(tokens, shift) == iota(tokens.shape, 0)
    live = mine & ((tokens & (slots - 1)) < chain(iota(tokens.shape, 0), every))
    high, low = split(nn(live.astype(BF16), xs))
    w = w_in[0].astype(BF16)
    total = nn(high, w) + nn(low, w)
    for m in range(parts):
        total = total + nn(pm[:, m * LANES : (m + 1) * LANES], w_out[m, 0])
    count = chain(iota(total.shape, 0), every).astype(F32)
    pooled[0] = (total / count).astype(BF16)


def backward_kernel(
    slots, cnt, x, w_in, gain, w_qkv, w_out, normed_in, qkv, prob, a_in, pm_in, dpooled, demb, d_in, d_gain, d_qkv, d_out, dqkv
):
    tower = pl.program_id(0)
    pairs, width = dpooled.shape[1:]
    parts = w_qkv.shape[0]
    per = LANES // slots
    groups = pairs // per
    heads = 2 * parts
    shift = slots.bit_length() - 1
    tokens = pairs * slots
    every = [cnt[tower * pairs + k] for k in range(pairs)]
    count = chain(iota((pairs, width), 0), every).astype(F32)
    dsum = dpooled[0].astype(F32) / count
    branch = dsum.astype(BF16)
    dmix = []
    for m in range(parts):
        grad = tn(pm_in[0, :, m * LANES : (m + 1) * LANES], branch).astype(BF16)
        for j in range(width // LANES):
            d_out[m, 0, j] = grad[:, j * LANES : (j + 1) * LANES]
        dmix.append(nt(branch, w_out[m, 0]))
    lane = iota((LANES, LANES), 1)
    line = iota((LANES, LANES), 0)
    pair_s = lax.shift_right_logical(line, shift)
    halves = [lane < DH, lane >= DH]
    own_head = iota((per * heads, LANES), 0) & (heads - 1)
    own_pair = lax.shift_right_logical(iota((per * heads, LANES), 0), heads.bit_length() - 1)
    token_pair = lax.shift_right_logical(iota((per * heads, LANES), 1), shift)
    for g in range(groups):
        rows = slice(g * LANES, (g + 1) * LANES)
        live_s = (line & (slots - 1)) < chain(pair_s, every[g * per : (g + 1) * per])
        scale = jnp.where(live_s, 0.125, 0.0)
        dots = jnp.zeros((per * heads, LANES), F32)
        stacks = []
        for m in range(parts):
            cut = dmix[m][g * per : (g + 1) * per]
            spread = jnp.concatenate([jnp.broadcast_to(cut[k : k + 1], (heads, LANES)) for k in range(per)], 0)
            head = iota((per * heads, LANES), 1) // DH + 2 * m
            stack = jnp.where(own_head == head, spread, 0.0).astype(BF16)
            stacks.append(stack)
            dots = dots + nt(stack, qkv[0, 2 * parts + m, rows, :])
        dots = jnp.where(own_pair == token_pair, dots, 0.0)
        pull = dots[0:heads]
        for k in range(1, per):
            pull = pull + dots[k * heads : (k + 1) * heads]
        for m in range(parts):
            query, key = qkv[0, m, rows, :], qkv[0, parts + m, rows, :]
            none = jnp.zeros_like(query)
            dq = jnp.zeros((LANES, LANES), F32)
            dk = jnp.zeros((LANES, LANES), F32)
            for half in range(2):
                h = 2 * m + half
                p = prob[0, g, h].astype(F32)
                t = p * pull[h : h + 1, :]
                ds = ((t - p * jnp.sum(t, 1, keepdims=True)) * scale).astype(BF16)
                dq = dq + nn(ds, jnp.where(halves[half], key, none))
                dk = dk + tn(ds, jnp.where(halves[half], query, none))
            dqkv[m, rows, :] = dq.astype(BF16)
            dqkv[parts + m, rows, :] = dk.astype(BF16)
            dqkv[2 * parts + m, rows, :] = tn(a_in[0, g], stacks[m]).astype(BF16)
    normed = normed_in[0]
    dnormed = jnp.zeros((tokens, width), F32)
    for m in range(parts):
        for c in range(3):
            grad = dqkv[c * parts + m]
            dnormed = dnormed + nt(grad, w_qkv[m, 0, c])
            d_qkv[m, 0, c] = tn(normed, grad).astype(BF16)
    dnormed = dnormed.astype(BF16).astype(F32)
    xs = x[0]
    w = w_in[0].astype(BF16)
    hidden = nn(xs, w)
    inverse = lax.rsqrt(jnp.mean(hidden * hidden, -1, keepdims=True) + EPS)
    unit = hidden * inverse
    d_gain[0] = jnp.sum(dnormed * unit, 0, keepdims=True)
    scaled = dnormed * gain[0]
    dh = inverse * (scaled - unit * jnp.mean(scaled * unit, -1, keepdims=True))
    spread = jnp.broadcast_to(dsum[:, None, :], (pairs, slots, width))
    slot = iota((pairs, slots, width), 1)
    counts = chain(iota((pairs, slots, width), 0), every)
    spread = jnp.where(slot < counts, spread, 0.0).reshape(tokens, width)
    dhidden = (spread + dh).astype(BF16)
    grad = tn(xs, dhidden).astype(BF16)
    for j in range(width // LANES):
        d_in[0, j] = grad[:, j * LANES : (j + 1) * LANES]
    demb[0] = nt(dhidden, w).astype(BF16)


def gelu_parts(v):
    c = 0.7978845608028654
    inner = jnp.tanh(c * (v + 0.044715 * (v * v * v)))
    value = 0.5 * v * (1.0 + inner)
    slope = 0.5 * (1.0 + inner) + 0.5 * v * (1.0 - inner * inner) * (c * (1.0 + 3.0 * 0.044715 * (v * v)))
    return value, slope


def upper_kernel(
    plane,
    line,
    pooled,
    far_one,
    far_two,
    far_three,
    prior_row,
    prior_col,
    pos_row,
    pos_own,
    dpooled,
    d_one,
    d_two,
    d_three,
    loss,
    pooled_all,
    second_send,
    second_got,
    vec,
    dsec_send,
    dsec_all,
    dpool_send,
    dpool_got,
    out_sems,
    in_sems,
    vec_out,
    vec_in,
    w_one,
    w_two,
    w_three,
    load_sems,
):
    loads = [
        pltpu.make_async_copy(source, target, load_sems.at[j])
        for j, (source, target) in enumerate(((far_one, w_one), (far_two, w_two), (far_three, w_three)))
    ]
    for copy in loads:
        copy.start()
    me, part = enter(plane, line)
    towers, own, width = pooled.shape
    rows = own * line
    pairs = rows * plane
    peers = [lax.rem(part + k, line) for k in range(1, line)]

    pooled_all[:, part] = pooled[...]
    first = [
        send(pooled_all.at[:, part], pooled_all.at[:, part], out_sems.at[0, k], in_sems.at[0, k], (me, peers[k]))
        for k in range(line - 1)
    ]
    for copy in loads:
        copy.wait()
    one = [w_one[t].astype(BF16) for t in range(towers)]
    two = [w_two[t].astype(BF16) for t in range(towers)]
    three = [w_three[t].astype(BF16) for t in range(towers)]
    for copy in first:
        copy.wait()
    act_one, slope_one, pools = [], [], []
    for t in range(towers):
        pools.append(pooled_all[t].reshape(rows, width))
        value, slope = gelu_parts(nn(pools[t], one[t]))
        act_one.append(value.astype(BF16))
        slope_one.append(slope)
        second_send[t] = nn(act_one[t], two[t]).reshape(line, own, -1)
    second = [
        send(
            second_send.at[:, peers[k]], second_got.at[:, part], out_sems.at[1, k], in_sems.at[1, k], (me, peers[k])
        )
        for k in range(line - 1)
    ]
    for copy in second:
        copy.wait()
    act_two, slope_two, third, length, vectors = [], [], [], [], []
    for t in range(towers):
        total = second_send[t, part]
        for peer in peers:
            total = total + second_got[t, peer]
        value, slope = gelu_parts(total)
        act_two.append(value.astype(BF16))
        slope_two.append(slope)
        third.append(nn(act_two[t], three[t]))
        length.append(lax.rsqrt(jnp.sum(third[t] * third[t], -1, keepdims=True) + EPS))
        vectors.append((third[t] * length[t]).astype(BF16))
        vec[t, me, part] = vectors[t]
    along = [
        send(vec.at[:, me, part], vec.at[:, me, part], out_sems.at[2, k], in_sems.at[2, k], (me, peers[k]))
        for k in range(line - 1)
    ]
    for copy in along:
        copy.wait()
    across = [
        send(vec.at[:, me], vec.at[:, me], vec_out.at[k], vec_in.at[k], (lax.rem(me + k, plane), part))
        for k in range(1, plane)
    ]
    for copy in across:
        copy.wait()

    queries = vec[0].reshape(pairs, width)
    items = vec[1].reshape(pairs, width)
    logits = INV_TEMP * nt(items, queries) - prior_col[...]
    peak = jnp.max(logits, 0, keepdims=True)
    log_total = peak + jnp.log(jnp.sum(jnp.exp(logits - peak), 0, keepdims=True))
    picked = jnp.where(iota((pairs, pairs), 0) == pos_row[...], logits, 0.0)
    gap = log_total - jnp.sum(picked, 0, keepdims=True)
    loss[...] = jnp.broadcast_to(jnp.sum(gap, 1, keepdims=True), loss.shape)
    ahead = me * rows + part * own
    mine = INV_TEMP * nt(vectors[0], items) - prior_row[...]
    top = jnp.max(mine, 1, keepdims=True)
    expo = jnp.exp(mine - top)
    chance = expo / jnp.sum(expo, 1, keepdims=True)
    target = (iota(mine.shape, 1) == pos_own[...]).astype(F32)
    dlog = ((chance - target) / pairs).astype(BF16)
    dvec = [(INV_TEMP * nn(dlog, items)).astype(BF16)]
    own_prior = prior_col[pl.ds(pl.multiple_of(ahead, own), own), :]
    theirs = INV_TEMP * nt(vectors[1], queries) - own_prior
    target = (iota(theirs.shape, 0) + ahead == pos_row[...]).astype(F32)
    dlog = ((jnp.exp(theirs - log_total) - target) / pairs).astype(BF16)
    dvec.append((INV_TEMP * nn(dlog, queries)).astype(BF16))

    dthirds = []
    for t in range(towers):
        dv = dvec[t].astype(F32)
        inner = jnp.sum(dv * third[t], -1, keepdims=True)
        dthird = (length[t] * dv - third[t] * (length[t] * length[t] * length[t] * inner)).astype(BF16)
        dact = nt(dthird, three[t]).astype(BF16).astype(F32)
        dsec_all[t, part] = (dact * slope_two[t]).astype(BF16)
        dthirds.append(dthird)
    spread = [
        send(dsec_all.at[:, part], dsec_all.at[:, part], out_sems.at[3, k], in_sems.at[3, k], (me, peers[k]))
        for k in range(line - 1)
    ]
    for t in range(towers):
        grad = tn(act_two[t], dthirds[t]).astype(BF16)
        for j in range(width // LANES):
            d_three[t, j] = grad[:, j * LANES : (j + 1) * LANES]
    for copy in spread:
        copy.wait()
    dfirsts = []
    for t in range(towers):
        dsecond = dsec_all[t].reshape(rows, -1)
        dact = nt(dsecond, two[t]).astype(BF16).astype(F32)
        dfirst = (dact * slope_one[t]).astype(BF16)
        dpool_send[t] = nt(dfirst, one[t]).reshape(line, own, width)
        dfirsts.append(dfirst)
    back = [
        send(dpool_send.at[:, peers[k]], dpool_got.at[:, part], out_sems.at[4, k], in_sems.at[4, k], (me, peers[k]))
        for k in range(line - 1)
    ]
    for t in range(towers):
        dsecond = dsec_all[t].reshape(rows, -1)
        for grads, grad in ((d_two, tn(act_one[t], dsecond)), (d_one, tn(pools[t], dfirsts[t]))):
            grad = grad.astype(BF16)
            for j in range(grad.shape[1] // LANES):
                grads[t, j] = grad[:, j * LANES : (j + 1) * LANES]
    for copy in back:
        copy.wait()
    for t in range(towers):
        total = dpool_send[t, part]
        for peer in peers:
            total = total + dpool_got[t, peer]
        dpooled[t] = total.astype(BF16)


def update(weight, grad, moment, average, factor, rate):
    clipped = grad * factor
    moment_new = MOMENTUM * moment + clipped
    weight_new = weight - rate * (clipped + MOMENTUM * moment_new)
    average_new = AVERAGE_DECAY * average + (1.0 - AVERAGE_DECAY) * weight_new
    return [weight_new, moment_new, average_new]


def update_kernel(blocks, norm_sq, table_grad, dense, gain, *refs):
    arrays = 3 * 8
    sources, targets, norm = refs[:arrays], refs[arrays : 2 * arrays], refs[2 * arrays]
    held, in_sems, out_sems = refs[2 * arrays + 1 : 3 * arrays + 1], refs[-2], refs[-1]
    loads = [pltpu.make_async_copy(sources[k], held[k], in_sems.at[k]) for k in range(arrays)]
    for copy in loads:
        copy.start()
    norm[...] = jnp.sqrt(norm_sq[...])
    factor = jnp.minimum(1.0, CLIP_NORM / norm[0:1, :])
    stores = []

    def finish(k):
        for j in range(3 * k, 3 * k + 3):
            copy = pltpu.make_async_copy(held[j], targets[j], out_sems.at[j])
            copy.start()
            stores.append(copy)

    def apply(k, rows, lanes, grad, rate):
        cells = [ref.at[rows, lanes] for ref in held[3 * k : 3 * k + 3]]
        new = update(cells[0][...], grad, cells[1][...], cells[2][...], factor, rate)
        for cell, value in zip(cells, new):
            cell[...] = value

    def wait(k):
        for copy in loads[3 * k : 3 * k + 3]:
            copy.wait()

    wait(0)

    def rows(i, carry):
        at = pl.ds(pl.multiple_of(i * 32, 32), 32)
        apply(0, at, slice(0, LANES), table_grad[at, :], ROW_RATE)
        return carry

    lax.fori_loop(0, table_grad.shape[0] // 32, rows, 0, unroll=2)
    finish(0)
    at = 0
    for k, size, height, wide in blocks:
        wait(k)
        total = dense.shape[0] * size
        step = 32 if size % 32 == 0 else 16
        for first in range(0, total, min(size, height)):
            count = min(size, height)
            share, inside = first // size, first % size
            block, begin = first // height, first % height
            t, j = block // wide, block % wide
            top = t * height + begin

            def piece(i, carry):
                take = pl.ds(pl.multiple_of(at + inside + i * step, 16), step)
                rows = pl.ds(pl.multiple_of(top + i * step, 16), step)
                grad = dense[share, take, :].astype(F32)
                apply(k, rows, slice(j * LANES, (j + 1) * LANES), grad, MATRIX_RATE)
                return carry

            lax.fori_loop(0, count // step, piece, 0, unroll=2)
        at += size
        finish(k)
    last = 7
    wait(last)
    for t in range(held[3 * last].shape[0]):
        for j in range(held[3 * last].shape[1] // LANES):
            r = t * (held[3 * last].shape[1] // LANES) + j
            apply(last, slice(t, t + 1), slice(j * LANES, (j + 1) * LANES), gain[r : r + 1, :], GAIN_RATE)
    finish(last)
    for copy in stores:
        copy.wait()


def shards(
    slot_owner,
    slot_row,
    slot_count,
    item_qid,
    positive,
    log_prior,
    embedding,
    embedding_mom,
    embedding_avg,
    w_in,
    w_in_mom,
    w_in_avg,
    norm_gain,
    norm_gain_mom,
    norm_gain_avg,
    w_qkv,
    w_qkv_mom,
    w_qkv_avg,
    w_out,
    w_out_mom,
    w_out_avg,
    w_one,
    w_one_mom,
    w_one_avg,
    w_two,
    w_two_mom,
    w_two_avg,
    w_three,
    w_three_mom,
    w_three_avg,
):
    plane = lax.axis_size("dp")
    line = lax.axis_size("mp")
    batch, towers, slots = slot_row.shape
    own = batch // line
    requests = batch * towers * slots
    own_requests = requests // line
    tokens = own * slots
    capacity = max(LANES, 2 * requests // plane)
    pairs = batch * plane
    part = lax.axis_index("mp")
    me = lax.axis_index("dp")
    width = w_in.shape[2]
    depth = w_in.shape[1]
    units = w_one.shape[2]
    seconds = w_two.shape[2]

    def ordered(value):
        value = value.reshape(line, own, towers, slots)
        return jnp.transpose(value, (0, 2, 1, 3)).reshape(requests // LANES, LANES)

    live = jnp.arange(slots)[None, None, :] < slot_count[:, :, None]
    owner = ordered(jnp.where(live, slot_owner[..., 0], plane))
    row = ordered(slot_row)
    own_chunks = own_requests // LANES
    own_owner = lax.dynamic_slice_in_dim(owner, part * own_chunks, own_chunks, 0)
    own_row = lax.dynamic_slice_in_dim(row, part * own_chunks, own_chunks, 0)
    per = capacity // LANES
    small = capacity // 4
    lists, inverse, own_place, own_small, extra = pl.pallas_call(
        functools.partial(prep_kernel, plane, capacity, small, line),
        out_shape=[
            shape((plane, 2 * per, LANES), I32),
            shape((plane * per, LANES), I32),
            shape((own_chunks, LANES), I32),
            shape((own_chunks, LANES), I32),
            shape((8, LANES), I32),
        ],
        in_specs=[VMEM] * 5,
        out_specs=[VMEM] * 5,
        compiler_params=params(16),
        name="request_lists",
    )(owner, row, own_owner, own_row, positive.reshape(1, batch))

    def row_scratch(count):
        return [
            pltpu.VMEM((plane, count, depth), BF16),
            pltpu.VMEM((plane, count, depth), BF16),
            pltpu.VMEM((plane * count, depth), F32),
        ]

    embedded, got_lists, got_extra, wide_qkv, wide_out = pl.pallas_call(
        functools.partial(fetch_kernel, plane, line),
        out_shape=[
            shape((own_requests, depth), BF16),
            shape(lists.shape, I32),
            shape((plane, 8, LANES), I32),
            shape((line, towers, 3, width, LANES), BF16),
            shape((line, towers, LANES, width), BF16),
        ],
        in_specs=[VMEM, VMEM, SMEM, VMEM, VMEM, VMEM],
        out_specs=[VMEM] * 5,
        scratch_shapes=[
            pltpu.SMEM(lists.shape, I32),
            *row_scratch(small),
            DMA((2, plane)),
            DMA((2, plane)),
            DMA((plane,)),
            DMA((plane,)),
            DMA((2, line)),
            DMA((2, line)),
            DMA((2, line)),
            DMA((2, line)),
            DMA((3,)),
        ],
        compiler_params=params(16, collective_id=2, has_side_effects=True),
        name="fetch",
    )(lists, extra, own_small, embedding, jnp.transpose(w_qkv, (0, 2, 1, 3)), w_out)
    most = jnp.max(got_extra[:, 1:3, 0], 0)

    def refetch(ids, place, table, _):
        return pl.pallas_call(
            functools.partial(refetch_kernel, plane),
            out_shape=shape((own_requests, depth), BF16),
            in_specs=[SMEM, SMEM, VMEM],
            out_specs=VMEM,
            scratch_shapes=[*row_scratch(capacity), DMA((plane,)), DMA((plane,))],
            compiler_params=params(16, collective_id=7, has_side_effects=True),
            name="refetch",
        )(ids, place, table)

    embedded = lax.cond(most[0] > small, refetch, lambda *given: given[3], got_lists, own_place, embedding, embedded)
    embedded = embedded.reshape(towers, tokens, depth)

    counts = jnp.transpose(slot_count).reshape(towers, line, own)
    counts = lax.dynamic_index_in_dim(counts, part, 1, keepdims=False).reshape(towers * own)
    heads = 2 * line
    gains = norm_gain.reshape(towers, 1, width)
    groups = tokens // LANES
    per_group = LANES // slots
    lead = lambda *dims: pl.BlockSpec((1,) + dims, lambda t: (t,) + (0,) * len(dims))
    qkv_spec = pl.BlockSpec((line, 1, 3, width, LANES), lambda t: (0, t, 0, 0, 0))
    out_spec = pl.BlockSpec((line, 1, LANES, width), lambda t: (0, t, 0, 0))
    pooled, pm, normed, qkv, prob, spread = pl.pallas_call(
        functools.partial(forward_kernel, slots),
        grid=(towers,),
        out_shape=[
            shape((towers, own, width), BF16),
            shape((towers, own, line * LANES), BF16),
            shape((towers, tokens, width), BF16),
            shape((towers, 3 * line, tokens, LANES), BF16),
            shape((towers, groups, heads, LANES, LANES), BF16),
            shape((towers, groups, per_group * heads, LANES), BF16),
        ],
        in_specs=[SMEM, lead(tokens, depth), lead(depth, width), lead(1, width), qkv_spec, out_spec],
        out_specs=[
            lead(own, width),
            lead(own, line * LANES),
            lead(tokens, width),
            lead(3 * line, tokens, LANES),
            lead(groups, heads, LANES, LANES),
            lead(groups, per_group * heads, LANES),
        ],
        scratch_shapes=[pltpu.VMEM((groups, per_group, line * LANES), F32)],
        compiler_params=params(20),
        name="attention_forward",
    )(counts, embedded, w_in, gains, wide_qkv, wide_out)

    prior = jnp.sum(
        jnp.where(item_qid[:, None] == jnp.arange(log_prior.shape[0])[None, :], log_prior[None, :], 0.0), 1
    )
    positions = got_extra[:, 0, :batch].reshape(1, pairs)
    own_positions = lax.dynamic_slice_in_dim(positive, part * own, own, 0).reshape(own, 1)
    dpooled, d_one, d_two, d_three, loss = pl.pallas_call(
        functools.partial(upper_kernel, plane, line),
        out_shape=[
            shape((towers, own, width), BF16),
            shape((towers, units // LANES, width, LANES), BF16),
            shape((towers, seconds // LANES, units, LANES), BF16),
            shape((towers, width // LANES, seconds, LANES), BF16),
            shape((8, LANES), F32),
        ],
        in_specs=[VMEM] + [HBM] * 3 + [VMEM] * 4,
        out_specs=[VMEM] * 5,
        scratch_shapes=[
            pltpu.VMEM((towers, line, own, width), BF16),
            pltpu.VMEM((towers, line, own, seconds), F32),
            pltpu.VMEM((towers, line, own, seconds), F32),
            pltpu.VMEM((towers, plane, line, own, width), BF16),
            pltpu.VMEM((towers, line, own, seconds), BF16),
            pltpu.VMEM((towers, line, own, seconds), BF16),
            pltpu.VMEM((towers, line, own, width), F32),
            pltpu.VMEM((towers, line, own, width), F32),
            DMA((5, line)),
            DMA((5, line)),
            DMA((plane,)),
            DMA((plane,)),
            pltpu.VMEM(w_one.shape, F32),
            pltpu.VMEM(w_two.shape, F32),
            pltpu.VMEM(w_three.shape, F32),
            DMA((3,)),
        ],
        compiler_params=params(22 + 2 * (pairs * pairs >> 18), collective_id=3, has_side_effects=True),
        name="upper",
    )(pooled, w_one, w_two, w_three, prior.reshape(1, pairs), prior.reshape(pairs, 1), positions, own_positions)

    demb, d_in, d_gain, d_qkv, d_out = pl.pallas_call(
        functools.partial(backward_kernel, slots),
        grid=(towers,),
        out_shape=[
            shape((towers, tokens, depth), BF16),
            shape((towers, width // LANES, depth, LANES), BF16),
            shape((towers, 1, width), F32),
            shape((line, towers, 3, width, LANES), BF16),
            shape((line, towers, width // LANES, LANES, LANES), BF16),
        ],
        in_specs=[
            SMEM,
            lead(tokens, depth),
            lead(depth, width),
            lead(1, width),
            qkv_spec,
            out_spec,
            lead(tokens, width),
            lead(3 * line, tokens, LANES),
            lead(groups, heads, LANES, LANES),
            lead(groups, per_group * heads, LANES),
            lead(own, line * LANES),
            lead(own, width),
        ],
        out_specs=[
            lead(tokens, depth),
            lead(width // LANES, depth, LANES),
            lead(1, width),
            qkv_spec,
            pl.BlockSpec((line, 1, width // LANES, LANES, LANES), lambda t: (0, t, 0, 0, 0)),
        ],
        scratch_shapes=[pltpu.VMEM((3 * line, tokens, LANES), BF16)],
        compiler_params=params(24),
        name="attention_backward",
    )(counts, embedded, w_in, gains, wide_qkv, wide_out, normed, qkv, prob, spread, pm, dpooled)

    def shares(grad, lead=()):
        rows = grad.size // (LANES * plane * (lead[0] if lead else 1))
        return grad.reshape(*lead, plane // 2, 2, rows, LANES)

    grads = [shares(d_qkv, (line,)), shares(d_out, (line,))] + [shares(g) for g in (d_three, d_in, d_one, d_two)]
    sizes = [g.shape[-2] for g in grads]
    share = line * (sizes[0] + sizes[1]) + sum(sizes[2:])
    gain_rows = jnp.pad(d_gain.reshape(-1, LANES), ((0, 8 - d_gain.size // LANES), (0, 0)))
    every, summed, gain_sum = pl.pallas_call(
        functools.partial(spread_kernel, plane, line),
        out_shape=[
            shape((line, own_requests, depth), BF16),
            shape((share, LANES), BF16),
            shape((8, LANES), F32),
        ],
        in_specs=[VMEM] * 8,
        out_specs=[VMEM] * 3,
        scratch_shapes=[
            [pltpu.VMEM((line, plane // 2, size, LANES), BF16) for size in sizes[:2]],
            [pltpu.VMEM((plane // 2, size, LANES), BF16) for size in sizes[2:]],
            pltpu.VMEM((plane // 2, share, LANES), BF16),
            pltpu.VMEM((plane // 2 - 1, share, LANES), BF16),
            pltpu.VMEM((plane, 8, LANES), F32),
            DMA((line,)),
            DMA((line,)),
            DMA((6,)),
            DMA((6,)),
            DMA((plane // 2,)),
            DMA((plane // 2,)),
            DMA((plane,)),
            DMA((plane,)),
            DMA,
        ],
        compiler_params=params(20, collective_id=4, has_side_effects=True),
        name="spread",
    )(demb.reshape(own_requests, depth), *grads, gain_rows)
    whole_at = line * (sizes[0] + sizes[1])
    whole_rows = sizes[2] + sizes[3]
    last_rows = sizes[4] + sizes[5]
    cuts = (
        ((0, sizes[0]), (line * sizes[0], sizes[1])),
        (whole_at, whole_rows),
        (whole_at + whole_rows, last_rows),
    )
    line_rows = sizes[0] + sizes[1] + whole_rows

    def give_back(count, number):
        return lambda *given: pl.pallas_call(
            functools.partial(return_kernel, plane, line, count, cuts),
            out_shape=[
                shape((plane, capacity, depth), BF16),
                shape((line_rows + last_rows, LANES), BF16),
                shape((8, LANES), F32),
                shape((8, LANES), F32),
            ],
            in_specs=[SMEM, VMEM, VMEM, VMEM],
            out_specs=[VMEM] * 4,
            scratch_shapes=[
                pltpu.VMEM((requests, depth), F32),
                pltpu.VMEM((plane, count, depth), BF16),
                pltpu.VMEM((line, line_rows, LANES), BF16),
                pltpu.VMEM((line, 8, LANES), F32),
                DMA((plane,)),
                DMA((plane,)),
                DMA((3, line)),
                DMA((3, line)),
                DMA((line,)),
                DMA((line,)),
                DMA,
            ],
            compiler_params=params(16, collective_id=number, has_side_effects=True),
            name="return_rows",
        )(*given)

    medium = capacity * 5 // 8
    incoming, dense, dense_sq, gain_all = lax.cond(
        most[1] > medium,
        give_back(capacity, 8),
        give_back(medium, 5),
        inverse.reshape(plane, per, LANES),
        every.reshape(requests, depth),
        summed,
        gain_sum,
    )
    served = got_lists[:, :per, :].reshape(plane, capacity)
    table_grad, table_sq = pl.pallas_call(
        scatter_kernel,
        out_shape=[shape(embedding.shape, F32), shape((8, LANES), F32)],
        in_specs=[SMEM, SMEM, VMEM],
        out_specs=[VMEM, VMEM],
        scratch_shapes=[pltpu.VMEM((capacity, depth), F32)] + [pltpu.VMEM(embedding.shape, F32)] * 3,
        compiler_params=params(20),
        name="add_rows",
    )(jnp.maximum(served, 0), jnp.sum((served >= 0).astype(I32), 1), incoming)

    norm_sq, dense_all = pl.pallas_call(
        functools.partial(norm_kernel, plane, line),
        out_shape=[shape((8, LANES), F32), shape((plane, *dense.shape), BF16)],
        in_specs=[VMEM] * 4,
        out_specs=[VMEM] * 2,
        scratch_shapes=[
            pltpu.VMEM((line, 8, LANES), F32),
            pltpu.VMEM((plane, 8, LANES), F32),
            DMA((line,)),
            DMA((line,)),
            DMA((plane,)),
            DMA((plane,)),
            DMA((plane // 2,)),
            DMA((plane // 2,)),
            DMA((plane // 2,)),
            DMA((plane // 2,)),
            DMA,
        ],
        compiler_params=params(12, collective_id=6, has_side_effects=True),
        name="norm_parts",
    )(table_sq, dense_sq, dense, gain_all)
    flat = lambda w: w.reshape(-1, w.shape[-1])
    turn = lambda w: flat(jnp.transpose(w, (0, 2, 1, 3)))
    given = [embedding, embedding_mom, embedding_avg]
    given += [turn(w) for w in (w_qkv, w_qkv_mom, w_qkv_avg)]
    rest = (w_out, w_out_mom, w_out_avg, w_three, w_three_mom, w_three_avg, w_in, w_in_mom, w_in_avg)
    rest += (w_one, w_one_mom, w_one_avg, w_two, w_two_mom, w_two_avg)
    given += [flat(w) for w in rest]
    given += [norm_gain, norm_gain_mom, norm_gain_avg]
    heights = (towers * 3 * width, LANES, seconds, depth, width, units)
    wides = (1, width // LANES, width // LANES, width // LANES, units // LANES, seconds // LANES)
    blocks = tuple((k + 1, size, height, wide) for k, (size, height, wide) in enumerate(zip(sizes, heights, wides)))
    *done, norm = pl.pallas_call(
        functools.partial(update_kernel, blocks),
        out_shape=[shape(w.shape, F32) for w in given] + [shape((8, LANES), F32)],
        in_specs=[VMEM] * 4 + [HBM] * len(given),
        out_specs=[HBM] * len(given) + [VMEM],
        scratch_shapes=[pltpu.VMEM(w.shape, F32) for w in given] + [DMA((len(given),))] * 2,
        compiler_params=params(57),
        name="update",
    )(norm_sq, table_grad, dense_all, gain_all, *given)
    back = lambda k, w: [done[3 * k + j].reshape(w.shape) for j in range(3)]
    unturned = [
        jnp.transpose(w.reshape(towers, 3, width, LANES), (0, 2, 1, 3)) for w in done[3:6]
    ]
    new = done[:3] + back(4, w_in) + done[21:24] + unturned + back(2, w_out) + back(5, w_one) + back(6, w_two)
    return (loss[0, 0], norm[0, 0], *new, *back(3, w_three))


def solution(mesh):
    rows = P("dp", None)
    qkv = P(None, None, None, "mp")
    deep = P(None, "mp", None)
    wide = P(None, None, "mp")
    weights = (rows,) * 3 + (P(),) * 6 + (qkv,) * 3 + (deep,) * 3 + (wide,) * 3 + (deep,) * 3 + (P(),) * 3
    inputs = (P("dp", None, None, None), P("dp", None, None), P("dp", None), P(), P("dp"), P())
    return jax.shard_map(
        shards, mesh=mesh, in_specs=inputs + weights, out_specs=(P(), P()) + weights, check_vma=False
    )
```

```python
import functools

import jax
import jax.numpy as jnp
from jax import lax
from jax.experimental import pallas as pl
from jax.experimental.pallas import tpu as pltpu
from jax.sharding import PartitionSpec as P

DH = 64
EPS = 1e-06
INV_TEMP = 20.0
CLIP_NORM = 0.1
ROW_RATE = 150000.0
GAIN_RATE = 8000.0
MATRIX_RATE = 600.0
MOMENTUM = 0.9
AVERAGE_DECAY = 0.6

MESH = pl.DeviceIdType.MESH
LANES = 128
F32 = jnp.float32
BF16 = jnp.bfloat16
I32 = jnp.int32
VMEM = pl.BlockSpec(memory_space=pltpu.VMEM)
HBM = pl.BlockSpec(memory_space=pltpu.HBM)
SMEM = pl.BlockSpec(memory_space=pltpu.SMEM)
DMA = pltpu.SemaphoreType.DMA


def nn(a, b):
    return lax.dot_general(a, b, (((1,), (0,)), ((), ())), preferred_element_type=F32)


def nt(a, b):
    return lax.dot_general(a, b, (((1,), (1,)), ((), ())), preferred_element_type=F32)


def tn(a, b):
    return lax.dot_general(a, b, (((0,), (0,)), ((), ())), preferred_element_type=F32)


def iota(shape, dim):
    return lax.broadcasted_iota(I32, shape, dim)


def split(value):
    high = value.astype(BF16)
    return high, (value - high.astype(F32)).astype(BF16)


def shape(dims, dtype):
    return jax.ShapeDtypeStruct(tuple(dims), dtype)


def params(limit, **more):
    return pltpu.CompilerParams(vmem_limit_bytes=limit << 20, **more)


def lists_of(owner, values, owners, capacity):
    chunks = owner.shape[0]
    width = owners * capacity
    his = width // LANES
    sub = iota((owners, LANES), 0)
    hot = [(owner[c : c + 1, :] == sub).astype(F32) for c in range(chunks)]
    hots = jnp.concatenate(hot, 0).astype(BF16)
    before = (iota((LANES, LANES), 0) < iota((LANES, LANES), 1)).astype(BF16)
    earlier = nn(hots, before)
    totals = nn(hots, jnp.ones((LANES, LANES), BF16))
    base = (sub * capacity).astype(F32)
    places = []
    for c in range(chunks):
        cut = slice(c * owners, (c + 1) * owners)
        here = jnp.sum(hot[c] * (earlier[cut] + base), 0, keepdims=True).astype(I32)
        places.append(jnp.where(owner[c : c + 1, :] < owners, here, width))
        base = base + totals[cut]
    parts = 2 * len(values)
    acc = jnp.zeros((his, parts * LANES), F32)
    for c in range(chunks):
        place = places[c]
        left = (lax.shift_right_logical(place, 7) == iota((his, LANES), 0)).astype(BF16)
        low = (place & 127) == iota((LANES, LANES), 0)
        cuts = []
        for value in values:
            value = value[c : c + 1, :]
            cuts += [lax.shift_right_logical(value, 6), value & 63]
        right = jnp.concatenate([jnp.where(low, cut.astype(F32), 0.0) for cut in cuts], 0)
        acc = acc + nt(left, right.astype(BF16))
    cuts = [acc[:, k * LANES : (k + 1) * LANES].astype(I32) for k in range(parts)]
    lists = [cuts[2 * k] * 64 + cuts[2 * k + 1] for k in range(len(values))]
    return places, lists, hot


def log2(value):
    return value.bit_length() - 1


def prep_kernel(
    owners, capacity, small, line, owner_in, row_in, count, positive, lists, inverse, own_place, own_small, extra
):
    towers, slots, batch = owner_in.shape
    own = batch // line
    per = capacity // LANES
    side = lambda ref: jnp.concatenate([ref[t] for t in range(towers)], 1)
    counts = jnp.concatenate([count[t : t + 1, :] for t in range(towers)], 1)
    row = side(row_in)
    slot, lane = iota((slots, LANES), 0), iota((slots, LANES), 1)
    owner = jnp.where(slot < counts, side(owner_in), owners)
    tower = lax.shift_right_logical(lane, log2(batch))
    block = lax.shift_right_logical(lane & (batch - 1), log2(own))
    token = ((block * towers + tower) * own + (lane & (own - 1))) * slots + slot
    _, (rows, tokens), hot = lists_of(owner, (row + 1, token), owners, capacity)
    own_owner = jnp.where(block == lax.axis_index("mp"), owner, owners)
    places, (own_rows,), _ = lists_of(own_owner, (row,), owners, capacity)
    rows = rows - 1
    inverse[...] = tokens
    for d in range(owners):
        lists[d, 0:per, :] = rows[d * per : (d + 1) * per, :]
        lists[d, per : 2 * per, :] = own_rows[d * per : (d + 1) * per, :]
    place = jnp.concatenate(places, 0)
    place = jnp.where(place < owners * capacity, place, 0)
    own_place[...] = place
    rank = jnp.minimum(place & (capacity - 1), small - 1)
    own_small[...] = lax.shift_right_logical(place, log2(capacity)) * small + rank
    asked = hot[0]
    for more in hot[1:]:
        asked = asked + more
    near = lax.shift_right_logical(iota((LANES, LANES), 0) & (batch - 1), log2(own)) == iota((LANES, LANES), 1)
    asked = asked.astype(BF16)
    most = jnp.max(jnp.max(nn(asked, near.astype(BF16)), 0, keepdims=True), 1, keepdims=True)
    every = jnp.max(nn(asked, jnp.ones((LANES, LANES), BF16)), 0, keepdims=True)
    extra[...] = jnp.zeros_like(extra)
    extra[0:1, 0:batch] = positive[...]
    extra[1:2, :] = jnp.broadcast_to(most, (1, LANES)).astype(I32)
    extra[2:3, :] = every.astype(I32)


def enter(plane, line):
    me, part = lax.axis_index("dp"), lax.axis_index("mp")
    barrier = pltpu.get_barrier_semaphore()
    for k in range(1, plane):
        pl.semaphore_signal(barrier, inc=1, device_id=(lax.rem(me + k, plane), part), device_id_type=MESH)
    for k in range(1, line):
        pl.semaphore_signal(barrier, inc=1, device_id=(me, lax.rem(part + k, line)), device_id_type=MESH)
    pl.semaphore_wait(barrier, max(plane - 1, 0) + max(line - 1, 0))
    return me, part


def send(source, target, out_sem, in_sem, device):
    copy = pltpu.make_async_remote_copy(
        src_ref=source, dst_ref=target, send_sem=out_sem, recv_sem=in_sem, device_id=device, device_id_type=MESH
    )
    copy.start()
    return copy


def gather_rows(ids, table, target):
    def body(i, carry):
        at = ids(i)
        rows = [table[pl.ds(at(u), 1), :] for u in range(16)]
        target[pl.ds(pl.multiple_of(i * 16, 16), 16), :] = jnp.concatenate(rows, 0).astype(BF16)
        return carry

    lax.fori_loop(0, target.shape[0] // 16, body, 0)


def listed(ids, first):
    def at(i):
        block = first + lax.shift_right_logical(i, 3)
        start = (i & 7) * 16
        return lambda u: ids[block, start + u]

    return at


def placed(place, part, towers, own, slots):
    per = slots // 16

    def at(i):
        pair = lax.shift_right_logical(i, log2(per))
        tower = lax.shift_right_logical(pair, log2(own))
        lane = tower * (LANES // towers) + part * own + (pair & (own - 1))
        start = (i & (per - 1)) * 16
        return lambda u: place[start + u, lane]

    return at


def send_rows(plane, me, part, ids, table, sent, got, wide, out_sems, in_sems):
    capacity = sent.shape[1]
    half = ids.shape[1] // 2
    copies = []
    for k in range(1, plane):
        peer = lax.rem(me + k, plane)
        gather_rows(listed(ids.at[peer], half), table, sent.at[peer])
        copies.append(send(sent.at[peer], got.at[me], out_sems.at[k], in_sems.at[k], (peer, part)))
    gather_rows(listed(ids.at[me], half), table, sent.at[me])
    wide[pl.ds(pl.multiple_of(me * capacity, capacity), capacity), :] = sent[me].astype(F32)
    return copies


def take_rows(plane, me, part, dims, copies, place, got, wide, out):
    capacity = got.shape[1]
    for k in range(1, plane):
        peer = lax.rem(me - k + plane, plane)
        copies[k - 1].wait_recv()
        wide[pl.ds(pl.multiple_of(peer * capacity, capacity), capacity), :] = got[peer].astype(F32)
    gather_rows(placed(place, part, *dims), wide, out)


def refetch_kernel(plane, dims, ids, place, table, out, sent, got, wide, out_sems, in_sems):
    me, part = enter(plane, 0)
    copies = send_rows(plane, me, part, ids, table, sent, got, wide, out_sems, in_sems)
    take_rows(plane, me, part, dims, copies, place, got, wide, out)
    for copy in copies:
        copy.wait_send()


def fetch_kernel(
    plane,
    line,
    dims,
    lists,
    extra,
    place,
    table,
    w_qkv,
    w_out,
    out,
    got_lists,
    got_extra,
    wide_qkv,
    wide_out,
    ids,
    sent,
    got,
    wide,
    list_out,
    list_in,
    out_sems,
    in_sems,
    far_out,
    far_in,
    near_out,
    near_in,
    own_sems,
):
    me, part = enter(plane, line)
    core = lax.rem(me, 2)
    sibling = me + 1 - 2 * core
    wide_qkv[part] = w_qkv[...].astype(BF16)
    wide_out[part] = w_out[...].astype(BF16)
    far = []
    for k in range(1, line):
        peer = lax.rem(part + k, line)
        for j, block in enumerate((wide_qkv, wide_out)):
            at = block.at[part, core]
            far.append(send(at, at, far_out.at[j, k], far_in.at[j, k], (me, peer)))
    asked = []
    for k in range(1, plane):
        peer = lax.rem(me + k, plane)
        asked.append(send(lists.at[peer], got_lists.at[me], list_out.at[0, k], list_in.at[0, k], (peer, part)))
        asked.append(send(extra, got_extra.at[me], list_out.at[1, k], list_in.at[1, k], (peer, part)))
    mine = [
        pltpu.make_async_copy(lists.at[me], got_lists.at[me], own_sems.at[0]),
        pltpu.make_async_copy(extra, got_extra.at[me], own_sems.at[1]),
    ]
    for copy in mine:
        copy.start()
    for copy in mine + asked:
        copy.wait()
    numbers = pltpu.make_async_copy(got_lists, ids, own_sems.at[2])
    numbers.start()
    numbers.wait()
    copies = send_rows(plane, me, part, ids, table, sent, got, wide, out_sems, in_sems)
    near = []
    for k in range(1, line):
        peer = lax.rem(part - k + line, line)
        for j, block in enumerate((wide_qkv, wide_out)):
            far[2 * (k - 1) + j].wait_recv()
            at = block.at[peer, core]
            near.append(send(at, at, near_out.at[j, k], near_in.at[j, k], (sibling, part)))
    take_rows(plane, me, part, dims, copies, place, got, wide, out)
    for copy in copies + far:
        copy.wait_send()
    for copy in near:
        copy.wait()


def spread_kernel(
    plane,
    line,
    mine,
    d_qkv,
    d_out,
    d_three,
    d_in,
    d_one,
    d_two,
    gain,
    out,
    summed,
    gain_sum,
    near_split,
    near_whole,
    half,
    got,
    gains,
    far_out,
    far_in,
    near_out,
    near_in,
    sum_out,
    sum_in,
    gain_out,
    gain_in,
    own_sem,
):
    me, part = enter(plane, line)
    chips = plane // 2
    core = lax.rem(me, 2)
    chip = me // 2
    sibling = me + 1 - 2 * core
    copies = []
    for k in range(1, line):
        peer = lax.rem(part + k, line)
        copies.append(send(mine, out.at[part], far_out.at[k], far_in.at[k], (me, peer)))
    split_grads, whole_grads = (d_qkv, d_out), (d_three, d_in, d_one, d_two)
    first = []
    for j, grad in enumerate(split_grads):
        first.append(send(grad.at[:, :, 1 - core], near_split[j], near_out.at[j], near_in.at[j], (sibling, part)))
    for j, grad in enumerate(whole_grads, len(split_grads)):
        first.append(send(grad.at[:, 1 - core], near_whole[j - 2], near_out.at[j], near_in.at[j], (sibling, part)))
    for k in range(1, plane):
        peer = lax.rem(me + k, plane)
        copies.append(send(gain, gains.at[me], gain_out.at[k], gain_in.at[k], (peer, part)))
    own = pltpu.make_async_copy(mine, out.at[part], own_sem)
    own.start()
    gains[me] = gain[...]
    for copy in first:
        copy.wait()
    for c in range(chips):
        at = 0
        for j, grad in enumerate(split_grads):
            rows = grad.shape[3]
            for m in range(line):
                total = grad[m, c, core].astype(F32) + near_split[j][m, c].astype(F32)
                half[c, at : at + rows, :] = total.astype(BF16)
                at += rows
        for j, grad in enumerate(whole_grads):
            rows = grad.shape[2]
            total = grad[c, core].astype(F32) + near_whole[j][c].astype(F32)
            half[c, at : at + rows, :] = total.astype(BF16)
            at += rows
    sums = []
    for k in range(1, chips):
        to = lax.rem(chip + k, chips)
        sums.append(send(half.at[to], got.at[k - 1], sum_out.at[k], sum_in.at[k], (2 * to + core, part)))
    for copy in sums:
        copy.wait()
    total = half[chip].astype(F32)
    for k in range(chips - 1):
        total = total + got[k].astype(F32)
    summed[...] = total.astype(BF16)
    own.wait()
    for copy in copies:
        copy.wait()
    total = gains[0]
    for d in range(1, plane):
        total = total + gains[d]
    gain_sum[...] = total


def add_rows(ids, count, blocks, grads, total, fresh):
    height = total.shape[0]
    rows = []
    for block in blocks:
        for r in range(-(-count // LANES)):
            rows.append(ids[block, r : r + 1, 0 : min(LANES, count - r * LANES)])
    numbers = jnp.concatenate(rows, 1)
    values = jnp.concatenate([ref[...] for ref in grads], 0)
    turned = jnp.transpose(jnp.broadcast_to(numbers.astype(F32), (8, numbers.shape[1])), (1, 0))[:, 0:1]
    upper = turned >= height
    none = jnp.zeros_like(values)
    values = jnp.concatenate([jnp.where(upper, none, values), jnp.where(upper, values, none)], 1)
    low = jnp.where(numbers >= 0, numbers & (height - 1), -1)
    step = min(height, 1024)

    def body(i, carry):
        at = pl.multiple_of(i * step, step)
        hot = jnp.where(low - at == iota((step, low.shape[1]), 0), 1.0, 0.0).astype(BF16)
        part = nn(hot, values)
        at = pl.ds(at, step)
        total[at, :] = part if fresh else total[at, :] + part
        return carry

    lax.fori_loop(0, height // step, body, 0)


def tail_kernel(
    plane,
    line,
    capacity,
    cuts,
    tokens,
    ids,
    rows,
    summed,
    gain,
    table,
    dense_all,
    norm_sq,
    gain_all,
    wide,
    sent,
    back,
    total,
    got,
    gains,
    along,
    across,
    out_sems,
    in_sems,
    far_out,
    far_in,
    gain_out,
    gain_in,
    along_out,
    along_in,
    across_out,
    across_in,
    chip_out,
    chip_in,
    near_out,
    near_in,
):
    me, part = enter(plane, line)
    chips = plane // 2
    core = lax.rem(me, 2)
    chip = me // 2
    sibling = me + 1 - 2 * core
    far = []
    split_cuts, (whole_at, whole_rows), (last_at, last_rows) = cuts
    for k in range(1, line):
        peer = lax.rem(part + k, line)
        to = 0
        for j, (at, count) in enumerate(split_cuts):
            begin = pl.multiple_of(at + peer * count, 16)
            far.append(
                send(summed.at[pl.ds(begin, count)], got.at[part, to : to + count], far_out.at[j, k], far_in.at[j, k], (me, peer))
            )
            to += count
        target = got.at[part, to : to + whole_rows]
        source = summed.at[whole_at : whole_at + whole_rows]
        far.append(send(source, target, far_out.at[2, k], far_in.at[2, k], (me, peer)))
        far.append(send(gain, gains.at[part], gain_out.at[k], gain_in.at[k], (me, peer)))
    gains[part] = gain[...]
    wide[...] = rows[...].astype(F32)
    copies = []
    for k in range(1, plane):
        peer = lax.rem(me + k, plane)
        gather_rows(listed(tokens.at[peer], 0), wide, sent.at[peer])
        copies.append(send(sent.at[peer], back.at[me], out_sems.at[k], in_sems.at[k], (peer, part)))
    gather_rows(listed(tokens.at[me], 0), wide, sent.at[me])
    to = 0
    for at, count in split_cuts:
        got[part, to : to + count] = summed[pl.ds(pl.multiple_of(at + part * count, 16), count), :]
        to += count
    got[part, to : to + whole_rows] = summed[whole_at : whole_at + whole_rows, :]
    for copy in far:
        copy.wait()
    share = got[0].astype(F32)
    for m in range(1, line):
        share = share + got[m].astype(F32)
    dense_all[me, 0 : to + whole_rows, :] = share.astype(BF16)
    dense_all[me, to + whole_rows :, :] = summed[last_at : last_at + last_rows, :]
    dense = dense_all.at[me]
    spread = []
    for k in range(1, chips):
        other = lax.rem(chip + k, chips)
        spread.append(send(dense, dense, chip_out.at[k], chip_in.at[k], (2 * other + core, part)))
    near = [send(dense, dense, near_out.at[0], near_in.at[0], (sibling, part))]

    group = max(1, 1280 // capacity)
    order = [me] + [lax.rem(me - k + plane, plane) for k in range(1, plane)]
    for first in range(0, plane, group):
        blocks = order[first : first + group]
        grads = [sent.at[blocks[0]] if first == 0 else back.at[blocks[0]]] + [back.at[block] for block in blocks[1:]]
        for k in range(max(first, 1), min(first + group, plane)):
            copies[k - 1].wait_recv()
        add_rows(ids, capacity, blocks, grads, total, first == 0)
    for k in range(1, chips):
        peer = 2 * lax.rem(chip - k + chips, chips) + core
        spread[k - 1].wait_recv()
        near.append(send(dense_all.at[peer], dense_all.at[peer], near_out.at[k], near_in.at[k], (sibling, part)))

    square = jnp.zeros((8, LANES), F32)
    for begin, count, weight in ((0, to, 1.0), (to, whole_rows, 1.0 / line), (to + whole_rows, last_rows, 1.0)):
        block = dense_all[me, begin : begin + count, :].astype(F32)
        square = square + weight * jnp.sum((block * block).reshape(count // 8, 8, LANES), 0)
    height = total.shape[0]

    def settle(i, carry):
        at = pl.multiple_of(i * 32, 32)
        for half in range(2):
            block = total[pl.ds(at, 32), half * LANES : (half + 1) * LANES]
            table[pl.ds(at + half * height, 32), :] = block
            block = block * block
            for r in range(4):
                carry = carry + block[r * 8 : (r + 1) * 8, :]
        return carry

    table_sq = lax.fori_loop(0, height // 32, settle, jnp.zeros((8, LANES), F32))
    across[me] = square + table_sq * (1.0 / line)
    tiny = [
        send(across.at[me], across.at[me], across_out.at[k], across_in.at[k], (lax.rem(me + k, plane), part))
        for k in range(1, plane)
    ]
    for copy in tiny:
        copy.wait()
    sums = across[0]
    for d in range(1, plane):
        sums = sums + across[d]
    along[part] = sums
    peers = [lax.rem(part + k, line) for k in range(1, line)]
    tiny = [
        send(along.at[part], along.at[part], along_out.at[k], along_in.at[k], (me, peer)) for k, peer in enumerate(peers)
    ]
    gain_sum = gains[0]
    for m in range(1, line):
        gain_sum = gain_sum + gains[m]
    gain_all[...] = gain_sum
    for copy in tiny:
        copy.wait()
    sums = along[0]
    for m in range(1, line):
        sums = sums + along[m]
    norm_sq[...] = jnp.broadcast_to(jnp.sum(sums + gain_sum * gain_sum), norm_sq.shape)
    for copy in copies + spread:
        copy.wait_send()
    for copy in near:
        copy.wait()


def chain(index, values):
    out = jnp.full(index.shape, values[0], values[0].dtype)
    for k in range(1, len(values)):
        out = jnp.where(index >= k, values[k], out)
    return out


def forward_kernel(slots, cnt, x, w_in, gain, w_qkv, w_out, pooled, pm_out, normed_out, qkv, prob, a_out, pm_acc):
    tower = pl.program_id(0)
    pairs = pooled.shape[1]
    first = lax.axis_index("mp") * pairs
    parts = w_qkv.shape[0]
    per = LANES // slots
    groups = pairs // per
    heads = 2 * parts
    xs = x[0]
    hidden = nn(xs, w_in[0].astype(BF16))
    inverse = lax.rsqrt(jnp.mean(hidden * hidden, -1, keepdims=True) + EPS)
    normed = (hidden * inverse * gain[pl.ds(tower, 1), :]).astype(BF16)
    normed_out[0] = normed
    for c in range(3):
        for m in range(parts):
            qkv[0, c * parts + m] = nn(normed, w_qkv[m, 0, c]).astype(BF16)
    lane = iota((LANES, LANES), 1)
    line = iota((LANES, LANES), 0)
    shift = slots.bit_length() - 1
    pair_r, pair_s = lax.shift_right_logical(lane, shift), lax.shift_right_logical(line, shift)
    same = pair_r == pair_s
    halves = [lane < DH, lane >= DH]
    own_head = iota((per * heads, LANES), 0) & (heads - 1)

    def group(g, carry):
        counts = [cnt[tower, first + g * per + k] for k in range(per)]
        live_r = same & ((lane & (slots - 1)) < chain(pair_r, counts))
        live_s = (line & (slots - 1)) < chain(pair_s, counts)
        rows = pl.ds(pl.multiple_of(g * LANES, LANES), LANES)
        sums = []
        for m in range(parts):
            query, key = qkv[0, m, rows, :], qkv[0, parts + m, rows, :]
            for half in range(2):
                scores = nt(jnp.where(halves[half], query, jnp.zeros_like(query)), key) * 0.125
                scores = jnp.where(live_r, scores, -1000000000.0)
                expo = jnp.exp(scores - jnp.max(scores, 1, keepdims=True))
                p = (expo * (1.0 / jnp.sum(expo, 1, keepdims=True))).astype(BF16)
                prob[0, g, 2 * m + half] = p
                sums.append(jnp.sum(jnp.where(live_s, p.astype(F32), 0.0), 0, keepdims=True))
        sums = jnp.concatenate(sums, 0)
        pair_l = lax.shift_right_logical(iota((heads, LANES), 1), shift)
        stack = jnp.concatenate([jnp.where(pair_l == k, sums, 0.0) for k in range(per)], 0).astype(BF16)
        a_out[0, g] = stack
        for m in range(parts):
            mix = nn(stack, qkv[0, 2 * parts + m, rows, :])
            head = iota((per * heads, LANES), 1) // DH + 2 * m
            mix = jnp.where(own_head == head, mix, 0.0)
            pm_acc[g, :, m * LANES : (m + 1) * LANES] = jnp.concatenate(
                [jnp.sum(mix[k * heads : (k + 1) * heads], 0, keepdims=True) for k in range(per)], 0
            )
        return carry

    lax.fori_loop(0, groups, group, 0)
    pm = jnp.concatenate([pm_acc[g] for g in range(groups)], 0).astype(BF16)
    pm_out[0] = pm
    every = [cnt[tower, first + k] for k in range(pairs)]
    tokens = iota((pairs, pairs * slots), 1)
    mine = lax.shift_right_logical(tokens, shift) == iota(tokens.shape, 0)
    live = mine & ((tokens & (slots - 1)) < chain(iota(tokens.shape, 0), every))
    high, low = split(nn(live.astype(BF16), xs))
    w = w_in[0].astype(BF16)
    total = nn(high, w) + nn(low, w)
    for m in range(parts):
        total = total + nn(pm[:, m * LANES : (m + 1) * LANES], w_out[m, 0])
    count = chain(iota(total.shape, 0), every).astype(F32)
    pooled[0] = (total / count).astype(BF16)


def backward_kernel(
    slots, cnt, x, w_in, gain, w_qkv, w_out, normed_in, qkv, prob, a_in, pm_in, dpooled, demb, d_in, d_gain, d_qkv, d_out, dqkv
):
    tower = pl.program_id(0)
    pairs, width = dpooled.shape[1:]
    parts = w_qkv.shape[0]
    per = LANES // slots
    groups = pairs // per
    heads = 2 * parts
    shift = slots.bit_length() - 1
    tokens = pairs * slots
    first = lax.axis_index("mp") * pairs
    every = [cnt[tower, first + k] for k in range(pairs)]
    count = chain(iota((pairs, width), 0), every).astype(F32)
    dsum = dpooled[0].astype(F32) / count
    branch = dsum.astype(BF16)
    dmix = []
    for m in range(parts):
        grad = tn(pm_in[0, :, m * LANES : (m + 1) * LANES], branch).astype(BF16)
        for j in range(width // LANES):
            d_out[m, 0, j] = grad[:, j * LANES : (j + 1) * LANES]
        dmix.append(nt(branch, w_out[m, 0]))
    lane = iota((LANES, LANES), 1)
    line = iota((LANES, LANES), 0)
    pair_s = lax.shift_right_logical(line, shift)
    halves = [lane < DH, lane >= DH]
    own_head = iota((per * heads, LANES), 0) & (heads - 1)
    own_pair = lax.shift_right_logical(iota((per * heads, LANES), 0), heads.bit_length() - 1)
    token_pair = lax.shift_right_logical(iota((per * heads, LANES), 1), shift)
    for g in range(groups):
        rows = slice(g * LANES, (g + 1) * LANES)
        live_s = (line & (slots - 1)) < chain(pair_s, every[g * per : (g + 1) * per])
        scale = jnp.where(live_s, 0.125, 0.0)
        dots = jnp.zeros((per * heads, LANES), F32)
        stacks = []
        for m in range(parts):
            cut = dmix[m][g * per : (g + 1) * per]
            spread = jnp.concatenate([jnp.broadcast_to(cut[k : k + 1], (heads, LANES)) for k in range(per)], 0)
            head = iota((per * heads, LANES), 1) // DH + 2 * m
            stack = jnp.where(own_head == head, spread, 0.0).astype(BF16)
            stacks.append(stack)
            dots = dots + nt(stack, qkv[0, 2 * parts + m, rows, :])
        dots = jnp.where(own_pair == token_pair, dots, 0.0)
        pull = dots[0:heads]
        for k in range(1, per):
            pull = pull + dots[k * heads : (k + 1) * heads]
        for m in range(parts):
            query, key = qkv[0, m, rows, :], qkv[0, parts + m, rows, :]
            none = jnp.zeros_like(query)
            dq = jnp.zeros((LANES, LANES), F32)
            dk = jnp.zeros((LANES, LANES), F32)
            for half in range(2):
                h = 2 * m + half
                p = prob[0, g, h].astype(F32)
                t = p * pull[h : h + 1, :]
                ds = ((t - p * jnp.sum(t, 1, keepdims=True)) * scale).astype(BF16)
                dq = dq + nn(ds, jnp.where(halves[half], key, none))
                dk = dk + tn(ds, jnp.where(halves[half], query, none))
            dqkv[m, rows, :] = dq.astype(BF16)
            dqkv[parts + m, rows, :] = dk.astype(BF16)
            dqkv[2 * parts + m, rows, :] = tn(a_in[0, g], stacks[m]).astype(BF16)
    normed = normed_in[0]
    dnormed = jnp.zeros((tokens, width), F32)
    for m in range(parts):
        for c in range(3):
            grad = dqkv[c * parts + m]
            dnormed = dnormed + nt(grad, w_qkv[m, 0, c])
            d_qkv[m, 0, c] = tn(normed, grad).astype(BF16)
    dnormed = dnormed.astype(BF16).astype(F32)
    xs = x[0]
    w = w_in[0].astype(BF16)
    hidden = nn(xs, w)
    inverse = lax.rsqrt(jnp.mean(hidden * hidden, -1, keepdims=True) + EPS)
    unit = hidden * inverse
    grad = jnp.sum(dnormed * unit, 0, keepdims=True)

    @pl.when(tower == 0)
    def _():
        d_gain[...] = jnp.zeros_like(d_gain)

    for j in range(width // LANES):
        d_gain[pl.ds(tower * (width // LANES) + j, 1), :] = grad[:, j * LANES : (j + 1) * LANES]
    scaled = dnormed * gain[pl.ds(tower, 1), :]
    dh = inverse * (scaled - unit * jnp.mean(scaled * unit, -1, keepdims=True))
    spread = jnp.broadcast_to(dsum[:, None, :], (pairs, slots, width))
    slot = iota((pairs, slots, width), 1)
    counts = chain(iota((pairs, slots, width), 0), every)
    spread = jnp.where(slot < counts, spread, 0.0).reshape(tokens, width)
    dhidden = (spread + dh).astype(BF16)
    grad = tn(xs, dhidden).astype(BF16)
    for j in range(width // LANES):
        d_in[0, j] = grad[:, j * LANES : (j + 1) * LANES]
    demb[0] = nt(dhidden, w).astype(BF16)


def gelu_parts(v):
    c = 0.7978845608028654
    inner = jnp.tanh(c * (v + 0.044715 * (v * v * v)))
    value = 0.5 * v * (1.0 + inner)
    slope = 0.5 * (1.0 + inner) + 0.5 * v * (1.0 - inner * inner) * (c * (1.0 + 3.0 * 0.044715 * (v * v)))
    return value, slope


def upper_kernel(
    plane,
    line,
    pooled,
    far_one,
    far_two,
    far_three,
    log_prior,
    item_qid,
    extra,
    positive,
    dpooled,
    d_one,
    d_two,
    d_three,
    loss,
    pooled_all,
    second_send,
    second_got,
    vec,
    dsec_send,
    dsec_all,
    dpool_send,
    dpool_got,
    out_sems,
    in_sems,
    vec_out,
    vec_in,
    w_one,
    w_two,
    w_three,
    load_sems,
    second_mine,
    dpool_mine,
    prior_col,
):
    loads = [
        pltpu.make_async_copy(source, target, load_sems.at[j])
        for j, (source, target) in enumerate(((far_one, w_one), (far_two, w_two), (far_three, w_three)))
    ]
    for copy in loads:
        copy.start()
    me, part = enter(plane, line)
    towers, own, width = pooled.shape
    rows = own * line
    pairs = rows * plane
    peers = [lax.rem(part + k, line) for k in range(1, line)]

    pooled_all[:, part] = pooled[...]
    first = [
        send(pooled_all.at[:, part], pooled_all.at[:, part], out_sems.at[0, k], in_sems.at[0, k], (me, peers[k]))
        for k in range(line - 1)
    ]
    for copy in loads:
        copy.wait()
    one = [w_one[t].astype(BF16) for t in range(towers)]
    two = [w_two[t].astype(BF16) for t in range(towers)]
    three = [w_three[t].astype(BF16) for t in range(towers)]
    qid = item_qid[...]
    hot = (lax.shift_right_logical(qid, 7) == iota((log_prior.shape[0], pairs), 0)).astype(BF16)
    high, rest = log_prior[...].astype(BF16), log_prior[...]
    rest = rest - high.astype(F32)
    middle, low = split(rest)
    table = tn(high, hot) + tn(middle, hot) + tn(low, hot)
    prior_row = jnp.sum(jnp.where((qid & 127) == iota((LANES, pairs), 0), table, 0.0), 0, keepdims=True)
    prior_col[...] = jnp.transpose(jnp.broadcast_to(prior_row, (8, pairs)), (1, 0))
    pos_row = jnp.concatenate([extra[d, 0:1, 0:rows] for d in range(plane)], 1)
    pos_own = chain(iota((own, pairs), 0), [positive[part * own + k] for k in range(own)])
    for copy in first:
        copy.wait()
    act_one, slope_one, pools = [], [], []
    for t in range(towers):
        pools.append(pooled_all[t].reshape(rows, width))
        value, slope = gelu_parts(nn(pools[t], one[t]))
        act_one.append(value.astype(BF16))
        slope_one.append(slope)
        partial = nn(act_one[t], two[t]).reshape(line, own, -1)
        second_mine[t] = partial
        second_send[t] = partial.astype(BF16)
    second = [
        send(
            second_send.at[:, peers[k]], second_got.at[:, part], out_sems.at[1, k], in_sems.at[1, k], (me, peers[k])
        )
        for k in range(line - 1)
    ]
    for copy in second:
        copy.wait()
    act_two, slope_two, third, length, vectors = [], [], [], [], []
    for t in range(towers):
        total = second_mine[t, part]
        for peer in peers:
            total = total + second_got[t, peer].astype(F32)
        value, slope = gelu_parts(total)
        act_two.append(value.astype(BF16))
        slope_two.append(slope)
        third.append(nn(act_two[t], three[t]))
        length.append(lax.rsqrt(jnp.sum(third[t] * third[t], -1, keepdims=True) + EPS))
        vectors.append((third[t] * length[t]).astype(BF16))
        vec[t, me, part] = vectors[t]
    along = [
        send(vec.at[:, me, part], vec.at[:, me, part], out_sems.at[2, k], in_sems.at[2, k], (me, peers[k]))
        for k in range(line - 1)
    ]
    for copy in along:
        copy.wait()
    chips = plane // 2
    core = lax.rem(me, 2)
    chip = me // 2
    sibling = me + 1 - 2 * core
    near = [send(vec.at[:, me], vec.at[:, me], vec_out.at[0], vec_in.at[0], (sibling, part))]
    across = []
    for k in range(1, chips):
        other = 2 * lax.rem(chip + k, chips) + core
        across.append(send(vec.at[:, me], vec.at[:, me], vec_out.at[k], vec_in.at[k], (other, part)))
    for k in range(1, chips):
        peer = 2 * lax.rem(chip - k + chips, chips) + core
        across[k - 1].wait_recv()
        sems = vec_out.at[chips + k], vec_in.at[chips + k]
        near.append(send(vec.at[:, peer], vec.at[:, peer], *sems, (sibling, part)))
    for copy in across:
        copy.wait_send()
    for copy in near:
        copy.wait()

    queries = vec[0].reshape(pairs, width)
    items = vec[1].reshape(pairs, width)
    logits = INV_TEMP * nt(items, queries) - prior_col[:, 0:1]
    peak = jnp.max(logits, 0, keepdims=True)
    log_total = peak + jnp.log(jnp.sum(jnp.exp(logits - peak), 0, keepdims=True))
    picked = jnp.where(iota((pairs, pairs), 0) == pos_row, logits, 0.0)
    gap = log_total - jnp.sum(picked, 0, keepdims=True)
    loss[...] = jnp.broadcast_to(jnp.sum(gap, 1, keepdims=True), loss.shape)
    ahead = me * rows + part * own
    mine = INV_TEMP * nt(vectors[0], items) - prior_row
    top = jnp.max(mine, 1, keepdims=True)
    expo = jnp.exp(mine - top)
    chance = expo / jnp.sum(expo, 1, keepdims=True)
    target = (iota(mine.shape, 1) == pos_own).astype(F32)
    dlog = ((chance - target) / pairs).astype(BF16)
    dvec = [(INV_TEMP * nn(dlog, items)).astype(BF16)]
    own_prior = prior_col[pl.ds(pl.multiple_of(ahead, own), own), 0:1]
    theirs = INV_TEMP * nt(vectors[1], queries) - own_prior
    target = (iota(theirs.shape, 0) + ahead == pos_row).astype(F32)
    dlog = ((jnp.exp(theirs - log_total) - target) / pairs).astype(BF16)
    dvec.append((INV_TEMP * nn(dlog, queries)).astype(BF16))

    dthirds = []
    for t in range(towers):
        dv = dvec[t].astype(F32)
        inner = jnp.sum(dv * third[t], -1, keepdims=True)
        dthird = (length[t] * dv - third[t] * (length[t] * length[t] * length[t] * inner)).astype(BF16)
        dact = nt(dthird, three[t]).astype(BF16).astype(F32)
        dsec_all[t, part] = (dact * slope_two[t]).astype(BF16)
        dthirds.append(dthird)
    spread = [
        send(dsec_all.at[:, part], dsec_all.at[:, part], out_sems.at[3, k], in_sems.at[3, k], (me, peers[k]))
        for k in range(line - 1)
    ]
    for t in range(towers):
        grad = tn(act_two[t], dthirds[t]).astype(BF16)
        for j in range(width // LANES):
            d_three[t, j] = grad[:, j * LANES : (j + 1) * LANES]
    for copy in spread:
        copy.wait()
    dfirsts = []
    for t in range(towers):
        dsecond = dsec_all[t].reshape(rows, -1)
        dact = nt(dsecond, two[t]).astype(BF16).astype(F32)
        dfirst = (dact * slope_one[t]).astype(BF16)
        partial = nt(dfirst, one[t]).reshape(line, own, width)
        dpool_mine[t] = partial
        dpool_send[t] = partial.astype(BF16)
        dfirsts.append(dfirst)
    back = [
        send(dpool_send.at[:, peers[k]], dpool_got.at[:, part], out_sems.at[4, k], in_sems.at[4, k], (me, peers[k]))
        for k in range(line - 1)
    ]
    for t in range(towers):
        dsecond = dsec_all[t].reshape(rows, -1)
        for grads, grad in ((d_two, tn(act_one[t], dsecond)), (d_one, tn(pools[t], dfirsts[t]))):
            grad = grad.astype(BF16)
            for j in range(grad.shape[1] // LANES):
                grads[t, j] = grad[:, j * LANES : (j + 1) * LANES]
    for copy in back:
        copy.wait()
    for t in range(towers):
        total = dpool_mine[t, part]
        for peer in peers:
            total = total + dpool_got[t, peer].astype(F32)
        dpooled[t] = total.astype(BF16)


def update(weight, grad, moment, average, factor, rate):
    clipped = grad * factor
    moment_new = MOMENTUM * moment + clipped
    weight_new = weight - rate * (clipped + MOMENTUM * moment_new)
    average_new = AVERAGE_DECAY * average + (1.0 - AVERAGE_DECAY) * weight_new
    return [weight_new, moment_new, average_new]


def update_kernel(blocks, norm_sq, table_grad, dense, gain, *refs):
    arrays = 3 * 8
    sources, targets, norm = refs[:arrays], refs[arrays : 2 * arrays], refs[2 * arrays]
    held, in_sems, out_sems = refs[2 * arrays + 1 : 3 * arrays + 1], refs[-2], refs[-1]
    loads = [pltpu.make_async_copy(sources[k], held[k], in_sems.at[k]) for k in range(arrays)]
    for copy in loads:
        copy.start()
    norm[...] = jnp.sqrt(norm_sq[...])
    factor = jnp.minimum(1.0, CLIP_NORM / norm[0:1, :])
    stores = []

    def finish(k):
        for j in range(3 * k, 3 * k + 3):
            copy = pltpu.make_async_copy(held[j], targets[j], out_sems.at[j])
            copy.start()
            stores.append(copy)

    def apply(k, rows, lanes, grad, rate):
        cells = [ref.at[rows, lanes] for ref in held[3 * k : 3 * k + 3]]
        new = update(cells[0][...], grad, cells[1][...], cells[2][...], factor, rate)
        for cell, value in zip(cells, new):
            cell[...] = value

    def wait(k):
        for copy in loads[3 * k : 3 * k + 3]:
            copy.wait()

    wait(0)

    def rows(i, carry):
        at = pl.ds(pl.multiple_of(i * 32, 32), 32)
        apply(0, at, slice(0, LANES), table_grad[at, :], ROW_RATE)
        return carry

    lax.fori_loop(0, table_grad.shape[0] // 32, rows, 0, unroll=2)
    finish(0)
    at = 0
    for k, size, height, wide in blocks:
        wait(k)
        total = dense.shape[0] * size
        step = 32 if size % 32 == 0 else 16
        for first in range(0, total, min(size, height)):
            count = min(size, height)
            share, inside = first // size, first % size
            block, begin = first // height, first % height
            t, j = block // wide, block % wide
            top = t * height + begin

            def piece(i, carry):
                take = pl.ds(pl.multiple_of(at + inside + i * step, 16), step)
                rows = pl.ds(pl.multiple_of(top + i * step, 16), step)
                grad = dense[share, take, :].astype(F32)
                apply(k, rows, slice(j * LANES, (j + 1) * LANES), grad, MATRIX_RATE)
                return carry

            lax.fori_loop(0, count // step, piece, 0, unroll=2)
        at += size
        finish(k)
    last = 7
    wait(last)
    for t in range(held[3 * last].shape[0]):
        for j in range(held[3 * last].shape[1] // LANES):
            r = t * (held[3 * last].shape[1] // LANES) + j
            apply(last, slice(t, t + 1), slice(j * LANES, (j + 1) * LANES), gain[r : r + 1, :], GAIN_RATE)
    finish(last)
    for copy in stores:
        copy.wait()


def shards(
    slot_owner,
    slot_row,
    slot_count,
    item_qid,
    positive,
    log_prior,
    embedding,
    embedding_mom,
    embedding_avg,
    w_in,
    w_in_mom,
    w_in_avg,
    norm_gain,
    norm_gain_mom,
    norm_gain_avg,
    w_qkv,
    w_qkv_mom,
    w_qkv_avg,
    w_out,
    w_out_mom,
    w_out_avg,
    w_one,
    w_one_mom,
    w_one_avg,
    w_two,
    w_two_mom,
    w_two_avg,
    w_three,
    w_three_mom,
    w_three_avg,
):
    plane = lax.axis_size("dp")
    line = lax.axis_size("mp")
    batch, towers, slots = slot_row.shape
    own = batch // line
    requests = batch * towers * slots
    own_requests = requests // line
    tokens = own * slots
    capacity = max(LANES, 2 * requests // plane)
    pairs = batch * plane
    part = lax.axis_index("mp")
    me = lax.axis_index("dp")
    width = w_in.shape[2]
    depth = w_in.shape[1]
    units = w_one.shape[2]
    seconds = w_two.shape[2]

    per = capacity // LANES
    small = capacity // 4
    lists, inverse, own_place, own_small, extra = pl.pallas_call(
        functools.partial(prep_kernel, plane, capacity, small, line),
        out_shape=[
            shape((plane, 2 * per, LANES), I32),
            shape((plane * per, LANES), I32),
            shape((slots, LANES), I32),
            shape((slots, LANES), I32),
            shape((8, LANES), I32),
        ],
        in_specs=[VMEM] * 4,
        out_specs=[VMEM] * 5,
        compiler_params=params(16),
        name="request_lists",
    )(
        jnp.transpose(slot_owner[..., 0], (1, 2, 0)),
        jnp.transpose(slot_row, (1, 2, 0)),
        jnp.transpose(slot_count),
        positive.reshape(1, batch),
    )
    dims = (towers, own, slots)

    def row_scratch(count):
        return [
            pltpu.VMEM((plane, count, depth), BF16),
            pltpu.VMEM((plane, count, depth), BF16),
            pltpu.VMEM((plane * count, depth), F32),
        ]

    embedded, got_lists, got_extra, wide_qkv, wide_out = pl.pallas_call(
        functools.partial(fetch_kernel, plane, line, dims),
        out_shape=[
            shape((own_requests, depth), BF16),
            shape(lists.shape, I32),
            shape((plane, 8, LANES), I32),
            shape((line, towers, 3, width, LANES), BF16),
            shape((line, towers, LANES, width), BF16),
        ],
        in_specs=[VMEM, VMEM, SMEM, VMEM, VMEM, VMEM],
        out_specs=[VMEM] * 5,
        scratch_shapes=[
            pltpu.SMEM(lists.shape, I32),
            *row_scratch(small),
            DMA((2, plane)),
            DMA((2, plane)),
            DMA((plane,)),
            DMA((plane,)),
            DMA((2, line)),
            DMA((2, line)),
            DMA((2, line)),
            DMA((2, line)),
            DMA((3,)),
        ],
        compiler_params=params(16, collective_id=2, has_side_effects=True),
        name="fetch",
    )(lists, extra, own_small, embedding, jnp.transpose(w_qkv, (0, 2, 1, 3)), w_out)
    most = jnp.max(got_extra[:, 1:3, 0], 0)

    def refetch(ids, place, table, _):
        return pl.pallas_call(
            functools.partial(refetch_kernel, plane, dims),
            out_shape=shape((own_requests, depth), BF16),
            in_specs=[SMEM, SMEM, VMEM],
            out_specs=VMEM,
            scratch_shapes=[*row_scratch(capacity), DMA((plane,)), DMA((plane,))],
            compiler_params=params(16, collective_id=7, has_side_effects=True),
            name="refetch",
        )(ids, place, table)

    embedded = lax.cond(most[0] > small, refetch, lambda *given: given[3], got_lists, own_place, embedding, embedded)
    embedded = embedded.reshape(towers, tokens, depth)

    counts = jnp.transpose(slot_count)
    heads = 2 * line
    groups = tokens // LANES
    per_group = LANES // slots
    lead = lambda *dims: pl.BlockSpec((1,) + dims, lambda t: (t,) + (0,) * len(dims))
    qkv_spec = pl.BlockSpec((line, 1, 3, width, LANES), lambda t: (0, t, 0, 0, 0))
    out_spec = pl.BlockSpec((line, 1, LANES, width), lambda t: (0, t, 0, 0))
    pooled, pm, normed, qkv, prob, spread = pl.pallas_call(
        functools.partial(forward_kernel, slots),
        grid=(towers,),
        out_shape=[
            shape((towers, own, width), BF16),
            shape((towers, own, line * LANES), BF16),
            shape((towers, tokens, width), BF16),
            shape((towers, 3 * line, tokens, LANES), BF16),
            shape((towers, groups, heads, LANES, LANES), BF16),
            shape((towers, groups, per_group * heads, LANES), BF16),
        ],
        in_specs=[SMEM, lead(tokens, depth), lead(depth, width), VMEM, qkv_spec, out_spec],
        out_specs=[
            lead(own, width),
            lead(own, line * LANES),
            lead(tokens, width),
            lead(3 * line, tokens, LANES),
            lead(groups, heads, LANES, LANES),
            lead(groups, per_group * heads, LANES),
        ],
        scratch_shapes=[pltpu.VMEM((groups, per_group, line * LANES), F32)],
        compiler_params=params(20),
        name="attention_forward",
    )(counts, embedded, w_in, norm_gain, wide_qkv, wide_out)

    dpooled, d_one, d_two, d_three, loss = pl.pallas_call(
        functools.partial(upper_kernel, plane, line),
        out_shape=[
            shape((towers, own, width), BF16),
            shape((towers, units // LANES, width, LANES), BF16),
            shape((towers, seconds // LANES, units, LANES), BF16),
            shape((towers, width // LANES, seconds, LANES), BF16),
            shape((8, LANES), F32),
        ],
        in_specs=[VMEM] + [HBM] * 3 + [VMEM] * 3 + [SMEM],
        out_specs=[VMEM] * 5,
        scratch_shapes=[
            pltpu.VMEM((towers, line, own, width), BF16),
            pltpu.VMEM((towers, line, own, seconds), BF16),
            pltpu.VMEM((towers, line, own, seconds), BF16),
            pltpu.VMEM((towers, plane, line, own, width), BF16),
            pltpu.VMEM((towers, line, own, seconds), BF16),
            pltpu.VMEM((towers, line, own, seconds), BF16),
            pltpu.VMEM((towers, line, own, width), BF16),
            pltpu.VMEM((towers, line, own, width), BF16),
            DMA((5, line)),
            DMA((5, line)),
            DMA((plane,)),
            DMA((plane,)),
            pltpu.VMEM(w_one.shape, F32),
            pltpu.VMEM(w_two.shape, F32),
            pltpu.VMEM(w_three.shape, F32),
            DMA((3,)),
            pltpu.VMEM((towers, line, own, seconds), F32),
            pltpu.VMEM((towers, line, own, width), F32),
            pltpu.VMEM((pairs, 8), F32),
        ],
        compiler_params=params(22 + 2 * (pairs * pairs >> 18), collective_id=3, has_side_effects=True),
        name="upper",
    )(
        pooled,
        w_one,
        w_two,
        w_three,
        log_prior.reshape(-1, LANES),
        item_qid.reshape(1, pairs),
        got_extra,
        positive,
    )

    demb, d_in, d_gain, d_qkv, d_out = pl.pallas_call(
        functools.partial(backward_kernel, slots),
        grid=(towers,),
        out_shape=[
            shape((towers, tokens, depth), BF16),
            shape((towers, width // LANES, depth, LANES), BF16),
            shape((8, LANES), F32),
            shape((line, towers, 3, width, LANES), BF16),
            shape((line, towers, width // LANES, LANES, LANES), BF16),
        ],
        in_specs=[
            SMEM,
            lead(tokens, depth),
            lead(depth, width),
            VMEM,
            qkv_spec,
            out_spec,
            lead(tokens, width),
            lead(3 * line, tokens, LANES),
            lead(groups, heads, LANES, LANES),
            lead(groups, per_group * heads, LANES),
            lead(own, line * LANES),
            lead(own, width),
        ],
        out_specs=[
            lead(tokens, depth),
            lead(width // LANES, depth, LANES),
            pl.BlockSpec((8, LANES), lambda t: (0, 0)),
            qkv_spec,
            pl.BlockSpec((line, 1, width // LANES, LANES, LANES), lambda t: (0, t, 0, 0, 0)),
        ],
        scratch_shapes=[pltpu.VMEM((3 * line, tokens, LANES), BF16)],
        compiler_params=params(24),
        name="attention_backward",
    )(counts, embedded, w_in, norm_gain, wide_qkv, wide_out, normed, qkv, prob, spread, pm, dpooled)

    def shares(grad, lead=()):
        rows = grad.size // (LANES * plane * (lead[0] if lead else 1))
        return grad.reshape(*lead, plane // 2, 2, rows, LANES)

    grads = [shares(d_qkv, (line,)), shares(d_out, (line,))] + [shares(g) for g in (d_three, d_in, d_one, d_two)]
    sizes = [g.shape[-2] for g in grads]
    share = line * (sizes[0] + sizes[1]) + sum(sizes[2:])
    every, summed, gain_sum = pl.pallas_call(
        functools.partial(spread_kernel, plane, line),
        out_shape=[
            shape((line, own_requests, depth), BF16),
            shape((share, LANES), BF16),
            shape((8, LANES), F32),
        ],
        in_specs=[VMEM] * 8,
        out_specs=[VMEM] * 3,
        scratch_shapes=[
            [pltpu.VMEM((line, plane // 2, size, LANES), BF16) for size in sizes[:2]],
            [pltpu.VMEM((plane // 2, size, LANES), BF16) for size in sizes[2:]],
            pltpu.VMEM((plane // 2, share, LANES), BF16),
            pltpu.VMEM((plane // 2 - 1, share, LANES), BF16),
            pltpu.VMEM((plane, 8, LANES), F32),
            DMA((line,)),
            DMA((line,)),
            DMA((6,)),
            DMA((6,)),
            DMA((plane // 2,)),
            DMA((plane // 2,)),
            DMA((plane,)),
            DMA((plane,)),
            DMA,
        ],
        compiler_params=params(20, collective_id=4, has_side_effects=True),
        name="spread",
    )(demb.reshape(own_requests, depth), *grads, d_gain)
    whole_at = line * (sizes[0] + sizes[1])
    whole_rows = sizes[2] + sizes[3]
    last_rows = sizes[4] + sizes[5]
    cuts = (
        ((0, sizes[0]), (line * sizes[0], sizes[1])),
        (whole_at, whole_rows),
        (whole_at + whole_rows, last_rows),
    )
    line_rows = sizes[0] + sizes[1] + whole_rows

    def tail(count, number):
        return lambda *given: pl.pallas_call(
            functools.partial(tail_kernel, plane, line, count, cuts),
            out_shape=[
                shape(embedding.shape, F32),
                shape((plane, line_rows + last_rows, LANES), BF16),
                shape((8, LANES), F32),
                shape((8, LANES), F32),
            ],
            in_specs=[SMEM] + [VMEM] * 4,
            out_specs=[VMEM] * 4,
            scratch_shapes=[
                pltpu.VMEM((requests, depth), F32),
                pltpu.VMEM((plane, count, depth), BF16),
                pltpu.VMEM((plane, count, depth), BF16),
                pltpu.VMEM((embedding.shape[0] // 2, 2 * depth), F32),
                pltpu.VMEM((line, line_rows, LANES), BF16),
                pltpu.VMEM((line, 8, LANES), F32),
                pltpu.VMEM((line, 8, LANES), F32),
                pltpu.VMEM((plane, 8, LANES), F32),
                DMA((plane,)),
                DMA((plane,)),
                DMA((3, line)),
                DMA((3, line)),
                DMA((line,)),
                DMA((line,)),
                DMA((line,)),
                DMA((line,)),
                DMA((plane,)),
                DMA((plane,)),
                DMA((plane // 2,)),
                DMA((plane // 2,)),
                DMA((plane // 2,)),
                DMA((plane // 2,)),
            ],
            compiler_params=params(36, collective_id=number, has_side_effects=True),
            name="tail",
        )(*given)

    medium = capacity * 5 // 8
    table_grad, dense_all, norm_sq, gain_all = lax.cond(
        most[1] > medium,
        tail(capacity, 8),
        tail(medium, 5),
        inverse.reshape(plane, per, LANES),
        got_lists,
        every.reshape(requests, depth),
        summed,
        gain_sum,
    )
    flat = lambda w: w.reshape(-1, w.shape[-1])
    turn = lambda w: flat(jnp.transpose(w, (0, 2, 1, 3)))
    given = [embedding, embedding_mom, embedding_avg]
    given += [turn(w) for w in (w_qkv, w_qkv_mom, w_qkv_avg)]
    rest = (w_out, w_out_mom, w_out_avg, w_three, w_three_mom, w_three_avg, w_in, w_in_mom, w_in_avg)
    rest += (w_one, w_one_mom, w_one_avg, w_two, w_two_mom, w_two_avg)
    given += [flat(w) for w in rest]
    given += [norm_gain, norm_gain_mom, norm_gain_avg]
    heights = (towers * 3 * width, LANES, seconds, depth, width, units)
    wides = (1, width // LANES, width // LANES, width // LANES, units // LANES, seconds // LANES)
    blocks = tuple((k + 1, size, height, wide) for k, (size, height, wide) in enumerate(zip(sizes, heights, wides)))
    *done, norm = pl.pallas_call(
        functools.partial(update_kernel, blocks),
        out_shape=[shape(w.shape, F32) for w in given] + [shape((8, LANES), F32)],
        in_specs=[VMEM] * 4 + [HBM] * len(given),
        out_specs=[HBM] * len(given) + [VMEM],
        scratch_shapes=[pltpu.VMEM(w.shape, F32) for w in given] + [DMA((len(given),))] * 2,
        compiler_params=params(57),
        name="update",
    )(norm_sq, table_grad, dense_all, gain_all, *given)
    back = lambda k, w: [done[3 * k + j].reshape(w.shape) for j in range(3)]
    unturned = [
        jnp.transpose(w.reshape(towers, 3, width, LANES), (0, 2, 1, 3)) for w in done[3:6]
    ]
    new = done[:3] + back(4, w_in) + done[21:24] + unturned + back(2, w_out) + back(5, w_one) + back(6, w_two)
    return (loss[0, 0], norm[0, 0], *new, *back(3, w_three))


def solution(mesh):
    rows = P("dp", None)
    qkv = P(None, None, None, "mp")
    deep = P(None, "mp", None)
    wide = P(None, None, "mp")
    weights = (rows,) * 3 + (P(),) * 6 + (qkv,) * 3 + (deep,) * 3 + (wide,) * 3 + (deep,) * 3 + (P(),) * 3
    inputs = (P("dp", None, None, None), P("dp", None, None), P("dp", None), P(), P("dp"), P())
    return jax.shard_map(
        shards, mesh=mesh, in_specs=inputs + weights, out_specs=(P(), P()) + weights, check_vma=False
    )
```

```python
import functools

import jax
import jax.numpy as jnp
from jax import lax
from jax.experimental import pallas as pl
from jax.experimental.pallas import tpu as pltpu
from jax.sharding import PartitionSpec as P

DH = 64
EPS = 1e-06
INV_TEMP = 20.0
CLIP_NORM = 0.1
ROW_RATE = 150000.0
GAIN_RATE = 8000.0
MATRIX_RATE = 600.0
MOMENTUM = 0.9
AVERAGE_DECAY = 0.6

MESH = pl.DeviceIdType.MESH
LANES = 128
F32 = jnp.float32
BF16 = jnp.bfloat16
I32 = jnp.int32
VMEM = pl.BlockSpec(memory_space=pltpu.VMEM)
HBM = pl.BlockSpec(memory_space=pltpu.HBM)
SMEM = pl.BlockSpec(memory_space=pltpu.SMEM)
DMA = pltpu.SemaphoreType.DMA


def nn(a, b):
    return lax.dot_general(a, b, (((1,), (0,)), ((), ())), preferred_element_type=F32)


def nt(a, b):
    return lax.dot_general(a, b, (((1,), (1,)), ((), ())), preferred_element_type=F32)


def tn(a, b):
    return lax.dot_general(a, b, (((0,), (0,)), ((), ())), preferred_element_type=F32)


def iota(shape, dim):
    return lax.broadcasted_iota(I32, shape, dim)


def split(value):
    high = value.astype(BF16)
    return high, (value - high.astype(F32)).astype(BF16)


def shape(dims, dtype):
    return jax.ShapeDtypeStruct(tuple(dims), dtype)


def params(limit, **more):
    return pltpu.CompilerParams(vmem_limit_bytes=limit << 20, **more)


def log2(value):
    return value.bit_length() - 1


def lists_of(owner, values, owners, capacity):
    chunks = owner.shape[0]
    width = owners * capacity
    his = width // LANES
    sub = iota((owners, LANES), 0)
    hot = [(owner[c : c + 1, :] == sub).astype(F32) for c in range(chunks)]
    hots = jnp.concatenate(hot, 0).astype(BF16)
    before = (iota((LANES, LANES), 0) < iota((LANES, LANES), 1)).astype(BF16)
    earlier = nn(hots, before)
    totals = nn(hots, jnp.ones((LANES, LANES), BF16))
    base = (sub * capacity).astype(F32)
    places = []
    for c in range(chunks):
        cut = slice(c * owners, (c + 1) * owners)
        here = jnp.sum(hot[c] * (earlier[cut] + base), 0, keepdims=True).astype(I32)
        places.append(jnp.where(owner[c : c + 1, :] < owners, here, width))
        base = base + totals[cut]
    parts = 2 * len(values)
    acc = jnp.zeros((his, parts * LANES), F32)
    for c in range(chunks):
        place = places[c]
        left = (lax.shift_right_logical(place, 7) == iota((his, LANES), 0)).astype(BF16)
        low = (place & 127) == iota((LANES, LANES), 0)
        cuts = []
        for value in values:
            value = value[c : c + 1, :]
            cuts += [lax.shift_right_logical(value, 6), value & 63]
        right = jnp.concatenate([jnp.where(low, cut.astype(F32), 0.0) for cut in cuts], 0)
        acc = acc + nt(left, right.astype(BF16))
    cuts = [acc[:, k * LANES : (k + 1) * LANES].astype(I32) for k in range(parts)]
    lists = [cuts[2 * k] * 64 + cuts[2 * k + 1] for k in range(len(values))]
    return places, lists, hot


class Slots:
    def __init__(self, owners, line, owner, row, count):
        towers, slots, batch = owner.shape
        own = batch // line
        side = lambda ref: jnp.concatenate([ref[t] for t in range(towers)], 1)
        counts = jnp.concatenate([count[t : t + 1, :] for t in range(towers)], 1)
        slot, lane = iota((slots, LANES), 0), iota((slots, LANES), 1)
        tower = lax.shift_right_logical(lane, log2(batch))
        self.row = side(row)
        self.owner = jnp.where(slot < counts, side(owner), owners)
        self.block = lax.shift_right_logical(lane & (batch - 1), log2(own))
        self.token = ((self.block * towers + tower) * own + (lane & (own - 1))) * slots + slot


def make_own_lists(slots, owners, capacity, small, height, own_lists, own_place, own_small):
    per = capacity // LANES
    owner = jnp.where(slots.block == lax.axis_index("mp"), slots.owner, owners)
    places, (rows,), _ = lists_of(owner, (slots.row,), owners, capacity)
    rows = jnp.minimum(jnp.maximum(rows, 0), height - 1)
    for d in range(owners):
        own_lists[d] = rows[d * per : (d + 1) * per, :]
    place = jnp.concatenate(places, 0)
    place = jnp.maximum(jnp.where(place < owners * capacity, place, 0), 0)
    own_place[...] = place
    rank = jnp.minimum(place & (capacity - 1), small - 1)
    own_small[...] = lax.shift_right_logical(place, log2(capacity)) * small + rank


def make_lists(slots, owners, capacity, batch, line, positive, lists, inverse):
    per = capacity // LANES
    _, (rows, tokens), hot = lists_of(slots.owner, (slots.row + 1, slots.token), owners, capacity)
    rows = rows - 1
    inverse[...] = tokens
    asked = hot[0]
    for more in hot[1:]:
        asked = asked + more
    own = batch // line
    near = lax.shift_right_logical(iota((LANES, LANES), 0) & (batch - 1), log2(own)) == iota((LANES, LANES), 1)
    asked = asked.astype(BF16)
    most = jnp.max(jnp.max(nn(asked, near.astype(BF16)), 0, keepdims=True), 1, keepdims=True)
    every = jnp.max(nn(asked, jnp.ones((LANES, LANES), BF16)), 0, keepdims=True)
    most = jnp.broadcast_to(most, (1, LANES))
    for d in range(owners):
        lists[d, 0:per, :] = rows[d * per : (d + 1) * per, :]
        lists[d, per : per + 1, 0:batch] = positive[...]
        lists[d, per + 1 : per + 2, :] = most.astype(I32)
        lists[d, per + 2 : per + 3, :] = every.astype(I32)


def announce(plane, line):
    me, part = lax.axis_index("dp"), lax.axis_index("mp")
    barrier = pltpu.get_barrier_semaphore()
    for k in range(1, plane):
        pl.semaphore_signal(barrier, inc=1, device_id=(lax.rem(me + k, plane), part), device_id_type=MESH)
    for k in range(1, line):
        pl.semaphore_signal(barrier, inc=1, device_id=(me, lax.rem(part + k, line)), device_id_type=MESH)
    return me, part


def await_others(plane, line):
    pl.semaphore_wait(pltpu.get_barrier_semaphore(), max(plane - 1, 0) + max(line - 1, 0))


def enter(plane, line):
    me, part = announce(plane, line)
    await_others(plane, line)
    return me, part


def partners(me, count):
    order = sorted(range(1, count), key=lambda k: (-bin(k >> 1).count("1"), k & 1, k))
    bits = [lax.rem(me // (1 << b), 2) for b in range(log2(count))]
    return [sum((1 << b) * (1 - bit if k >> b & 1 else bit) for b, bit in enumerate(bits)) for k in order]


def send(source, target, out_sem, in_sem, device):
    copy = pltpu.make_async_remote_copy(
        src_ref=source, dst_ref=target, send_sem=out_sem, recv_sem=in_sem, device_id=device, device_id_type=MESH
    )
    copy.start()
    return copy


def gather_rows(ids, table, target):
    def body(i, carry):
        at = ids(i)
        rows = [table[pl.ds(at(u), 1), :] for u in range(16)]
        target[pl.ds(pl.multiple_of(i * 16, 16), 16), :] = jnp.concatenate(rows, 0).astype(BF16)
        return carry

    lax.fori_loop(0, target.shape[0] // 16, body, 0)


def listed(ids, first):
    def at(i):
        block = first + lax.shift_right_logical(i, 3)
        start = (i & 7) * 16
        return lambda u: ids[block, start + u]

    return at


def placed(place, part, towers, own, slots):
    per = slots // 16

    def at(i):
        pair = lax.shift_right_logical(i, log2(per))
        tower = lax.shift_right_logical(pair, log2(own))
        lane = tower * (LANES // towers) + part * own + (pair & (own - 1))
        start = (i & (per - 1)) * 16
        return lambda u: place[start + u, lane]

    return at


def send_rows(plane, me, part, ids, table, sent, got, wide, out_sems, in_sems):
    capacity = sent.shape[1]
    copies = []
    for k, peer in enumerate(partners(me, plane)):
        gather_rows(listed(ids.at[peer], 0), table, sent.at[peer])
        copies.append(send(sent.at[peer], got.at[me], out_sems.at[k], in_sems.at[k], (peer, part)))
    gather_rows(listed(ids.at[me], 0), table, sent.at[me])
    wide[pl.ds(pl.multiple_of(me * capacity, capacity), capacity), :] = sent[me].astype(F32)
    return copies


def take_rows(plane, me, part, dims, copies, place, got, wide, out):
    capacity = got.shape[1]
    for copy, peer in zip(copies, partners(me, plane)):
        copy.wait_recv()
        wide[pl.ds(pl.multiple_of(peer * capacity, capacity), capacity), :] = got[peer].astype(F32)
    gather_rows(placed(place, part, *dims), wide, out)


def refetch_kernel(plane, dims, ids, place, table, out, sent, got, wide, out_sems, in_sems):
    me, part = enter(plane, 0)
    copies = send_rows(plane, me, part, ids, table, sent, got, wide, out_sems, in_sems)
    take_rows(plane, me, part, dims, copies, place, got, wide, out)
    for copy in copies:
        copy.wait_send()


def fetch_kernel(
    plane,
    line,
    dims,
    capacity,
    owner_in,
    row_in,
    count,
    positive,
    far_table,
    far_qkv,
    far_wout,
    out,
    got_own,
    got_lists,
    weights,
    inverse,
    own_place,
    own_lists,
    own_small,
    lists,
    table,
    w_qkv,
    w_out,
    place,
    ids,
    sent,
    got,
    wide,
    list_out,
    list_in,
    out_sems,
    in_sems,
    far_out,
    far_in,
    side_out,
    side_in,
    near_out,
    near_in,
    own_sems,
    load_sems,
):
    loads = [
        pltpu.make_async_copy(source, target, load_sems.at[j])
        for j, (source, target) in enumerate(((far_qkv, w_qkv), (far_wout, w_out), (far_table, table)))
    ]
    for copy in loads:
        copy.start()
    me, part = announce(plane, line)
    core = lax.rem(me, 2)
    half = lax.rem(me // 2, 2)
    sibling = me + 1 - 2 * core
    partner = me + 2 - 4 * half
    batch = positive.shape[1]
    slots = Slots(plane, line, owner_in, row_in, count)
    make_own_lists(slots, plane, capacity, sent.shape[1], table.shape[0], own_lists, own_place, own_small)
    places = pltpu.make_async_copy(own_small, place, own_sems.at[0])
    places.start()
    for copy in loads[:2]:
        copy.wait()
    rows = weights.shape[3] // 2
    for c in range(3):
        weights[part, :, c] = w_qkv[:, c].astype(BF16)
    for j in range(2):
        weights[part, :, 3, j * LANES : (j + 1) * LANES, :] = w_out[:, :, j * LANES : (j + 1) * LANES].astype(BF16)
    quarter = lambda m, h: weights.at[m, core, :, pl.ds(pl.multiple_of(h * rows, rows), rows), :]
    await_others(plane, line)
    far, asked, told = [], [], []
    for k in range(1, line):
        peer = lax.rem(part + k, line)
        far.append(send(quarter(part, half), quarter(part, half), far_out.at[k], far_in.at[k], (me, peer)))
    for k in range(1, plane):
        peer = lax.rem(me + k, plane)
        asked.append(send(own_lists.at[peer], got_own.at[me], list_out.at[0, k], list_in.at[0, k], (peer, part)))
    make_lists(slots, plane, capacity, batch, line, positive, lists, inverse)
    for k in range(1, plane):
        peer = lax.rem(me + k, plane)
        told.append(send(lists.at[peer], got_lists.at[me], list_out.at[1, k], list_in.at[1, k], (peer, part)))
    mine = [
        pltpu.make_async_copy(own_lists.at[me], got_own.at[me], own_sems.at[1]),
        pltpu.make_async_copy(lists.at[me], got_lists.at[me], own_sems.at[2]),
    ]
    for copy in mine:
        copy.start()
    for copy in asked:
        copy.wait()
    mine[0].wait()
    numbers = pltpu.make_async_copy(got_own.at[:, 0 : ids.shape[1]], ids, own_sems.at[3])
    numbers.start()
    for copy in (numbers, places, loads[2]):
        copy.wait()
    copies = send_rows(plane, me, part, ids, table, sent, got, wide, out_sems, in_sems)
    sides, near = [], []
    for k in range(1, line):
        peer = lax.rem(part - k + line, line)
        far[k - 1].wait_recv()
        at = quarter(peer, half)
        sides.append(send(at, at, side_out.at[k], side_in.at[k], (partner, part)))
        near.append(send(at, at, near_out.at[0, k], near_in.at[0, k], (sibling, part)))
    take_rows(plane, me, part, dims, copies, place, got, wide, out)
    for k in range(1, line):
        peer = lax.rem(part - k + line, line)
        sides[k - 1].wait_recv()
        at = quarter(peer, 1 - half)
        near.append(send(at, at, near_out.at[1, k], near_in.at[1, k], (sibling, part)))
    mine[1].wait()
    for copy in copies + far + sides:
        copy.wait_send()
    for copy in told + near:
        copy.wait()


def spread_kernel(
    plane,
    line,
    mine,
    d_qkv,
    d_out,
    d_three,
    d_in,
    d_one,
    d_two,
    gain,
    out,
    summed,
    gain_sum,
    near_split,
    near_whole,
    half,
    got,
    gains,
    far_out,
    far_in,
    near_out,
    near_in,
    sum_out,
    sum_in,
    gain_out,
    gain_in,
    own_sem,
):
    me, part = enter(plane, line)
    chips = plane // 2
    core = lax.rem(me, 2)
    chip = me // 2
    sibling = me + 1 - 2 * core
    copies = []
    for k in range(1, line):
        peer = lax.rem(part + k, line)
        copies.append(send(mine, out.at[part], far_out.at[k], far_in.at[k], (me, peer)))
    split_grads, whole_grads = (d_qkv, d_out), (d_three, d_in, d_one, d_two)
    first = []
    for j, grad in enumerate(split_grads):
        first.append(send(grad.at[:, :, 1 - core], near_split[j], near_out.at[j], near_in.at[j], (sibling, part)))
    for j, grad in enumerate(whole_grads, len(split_grads)):
        first.append(send(grad.at[:, 1 - core], near_whole[j - 2], near_out.at[j], near_in.at[j], (sibling, part)))
    for k in range(1, plane):
        peer = lax.rem(me + k, plane)
        copies.append(send(gain, gains.at[me], gain_out.at[k], gain_in.at[k], (peer, part)))
    own = pltpu.make_async_copy(mine, out.at[part], own_sem)
    own.start()
    gains[me] = gain[...]
    for copy in first:
        copy.wait()
    for c in range(chips):
        at = 0
        for j, grad in enumerate(split_grads):
            rows = grad.shape[3]
            for m in range(line):
                total = grad[m, c, core].astype(F32) + near_split[j][m, c].astype(F32)
                half[c, at : at + rows, :] = total.astype(BF16)
                at += rows
        for j, grad in enumerate(whole_grads):
            rows = grad.shape[2]
            total = grad[c, core].astype(F32) + near_whole[j][c].astype(F32)
            half[c, at : at + rows, :] = total.astype(BF16)
            at += rows
    sums = []
    for k in range(1, chips):
        to = lax.rem(chip + k, chips)
        sums.append(send(half.at[to], got.at[k - 1], sum_out.at[k], sum_in.at[k], (2 * to + core, part)))
    for copy in sums:
        copy.wait()
    total = half[chip].astype(F32)
    for k in range(chips - 1):
        total = total + got[k].astype(F32)
    summed[...] = total.astype(BF16)
    own.wait()
    for copy in copies:
        copy.wait()
    total = gains[0]
    for d in range(1, plane):
        total = total + gains[d]
    gain_sum[...] = total


def add_rows(ids, count, blocks, grads, total, fresh):
    height = total.shape[0]
    rows = []
    for block in blocks:
        for r in range(-(-count // LANES)):
            rows.append(ids[block, r : r + 1, 0 : min(LANES, count - r * LANES)])
    numbers = jnp.concatenate(rows, 1)
    values = jnp.concatenate([ref[...] for ref in grads], 0)
    turned = jnp.transpose(jnp.broadcast_to(numbers.astype(F32), (8, numbers.shape[1])), (1, 0))[:, 0:1]
    upper = turned >= height
    none = jnp.zeros_like(values)
    values = jnp.concatenate([jnp.where(upper, none, values), jnp.where(upper, values, none)], 1)
    low = jnp.where(numbers >= 0, numbers & (height - 1), -1)
    step = min(height, 1024)

    def body(i, carry):
        at = pl.multiple_of(i * step, step)
        hot = jnp.where(low - at == iota((step, low.shape[1]), 0), 1.0, 0.0).astype(BF16)
        part = nn(hot, values)
        at = pl.ds(at, step)
        total[at, :] = part if fresh else total[at, :] + part
        return carry

    lax.fori_loop(0, height // step, body, 0)


def tail_kernel(
    plane,
    line,
    capacity,
    cuts,
    tokens,
    ids,
    rows,
    summed,
    gain,
    table,
    dense_all,
    norm_sq,
    gain_all,
    wide,
    sent,
    back,
    total,
    got,
    gains,
    along,
    across,
    out_sems,
    in_sems,
    far_out,
    far_in,
    gain_out,
    gain_in,
    along_out,
    along_in,
    across_out,
    across_in,
    chip_out,
    chip_in,
    near_out,
    near_in,
):
    me, part = enter(plane, line)
    chips = plane // 2
    core = lax.rem(me, 2)
    chip = me // 2
    sibling = me + 1 - 2 * core
    far = []
    split_cuts, (whole_at, whole_rows), (last_at, last_rows) = cuts
    for k in range(1, line):
        peer = lax.rem(part + k, line)
        to = 0
        for j, (at, count) in enumerate(split_cuts):
            begin = pl.multiple_of(at + peer * count, 16)
            far.append(
                send(summed.at[pl.ds(begin, count)], got.at[part, to : to + count], far_out.at[j, k], far_in.at[j, k], (me, peer))
            )
            to += count
        target = got.at[part, to : to + whole_rows]
        source = summed.at[whole_at : whole_at + whole_rows]
        far.append(send(source, target, far_out.at[2, k], far_in.at[2, k], (me, peer)))
        far.append(send(gain, gains.at[part], gain_out.at[k], gain_in.at[k], (me, peer)))
    gains[part] = gain[...]
    wide[...] = rows[...].astype(F32)
    copies = []
    others = partners(me, plane)
    for k, peer in enumerate(others):
        gather_rows(listed(tokens.at[peer], 0), wide, sent.at[peer])
        copies.append(send(sent.at[peer], back.at[me], out_sems.at[k], in_sems.at[k], (peer, part)))
    gather_rows(listed(tokens.at[me], 0), wide, sent.at[me])
    to = 0
    for at, count in split_cuts:
        got[part, to : to + count] = summed[pl.ds(pl.multiple_of(at + part * count, 16), count), :]
        to += count
    got[part, to : to + whole_rows] = summed[whole_at : whole_at + whole_rows, :]
    for copy in far:
        copy.wait()
    share = got[0].astype(F32)
    for m in range(1, line):
        share = share + got[m].astype(F32)
    dense_all[me, 0 : to + whole_rows, :] = share.astype(BF16)
    dense_all[me, to + whole_rows :, :] = summed[last_at : last_at + last_rows, :]
    dense = dense_all.at[me]
    spread, near = [], []
    group = max(1, 1280 // capacity)
    order = [me] + others
    for first in range(0, plane, group):
        blocks = order[first : first + group]
        grads = [sent.at[blocks[0]] if first == 0 else back.at[blocks[0]]] + [back.at[block] for block in blocks[1:]]
        for k in range(max(first, 1), min(first + group, plane)):
            copies[k - 1].wait_recv()
        if first + group >= plane:
            for k in range(1, chips):
                other = lax.rem(chip + k, chips)
                spread.append(send(dense, dense, chip_out.at[k], chip_in.at[k], (2 * other + core, part)))
            near.append(send(dense, dense, near_out.at[0], near_in.at[0], (sibling, part)))
        add_rows(ids, capacity, blocks, grads, total, first == 0)
    square = jnp.zeros((8, LANES), F32)
    for begin, count, weight in ((0, to, 1.0), (to, whole_rows, 1.0 / line), (to + whole_rows, last_rows, 1.0)):
        block = dense_all[me, begin : begin + count, :].astype(F32)
        square = square + weight * jnp.sum((block * block).reshape(count // 8, 8, LANES), 0)
    height = total.shape[0]

    def settle(i, carry):
        at = pl.multiple_of(i * 32, 32)
        for half in range(2):
            block = total[pl.ds(at, 32), half * LANES : (half + 1) * LANES]
            table[pl.ds(at + half * height, 32), :] = block
            block = block * block
            for r in range(4):
                carry = carry + block[r * 8 : (r + 1) * 8, :]
        return carry

    table_sq = lax.fori_loop(0, height // 32, settle, jnp.zeros((8, LANES), F32))
    across[me] = square + table_sq * (1.0 / line)
    tiny = [
        send(across.at[me], across.at[me], across_out.at[k], across_in.at[k], (lax.rem(me + k, plane), part))
        for k in range(1, plane)
    ]
    for copy in tiny:
        copy.wait()
    sums = across[0]
    for d in range(1, plane):
        sums = sums + across[d]
    along[part] = sums
    peers = [lax.rem(part + k, line) for k in range(1, line)]
    tiny = [
        send(along.at[part], along.at[part], along_out.at[k], along_in.at[k], (me, peer)) for k, peer in enumerate(peers)
    ]
    for k in range(1, chips):
        peer = 2 * lax.rem(chip - k + chips, chips) + core
        spread[k - 1].wait_recv()
        near.append(send(dense_all.at[peer], dense_all.at[peer], near_out.at[k], near_in.at[k], (sibling, part)))
    gain_sum = gains[0]
    for m in range(1, line):
        gain_sum = gain_sum + gains[m]
    gain_all[...] = gain_sum
    for copy in tiny:
        copy.wait()
    sums = along[0]
    for m in range(1, line):
        sums = sums + along[m]
    norm_sq[...] = jnp.broadcast_to(jnp.sum(sums + gain_sum * gain_sum), norm_sq.shape)
    for copy in copies + spread:
        copy.wait_send()
    for copy in near:
        copy.wait()


def chain(index, values):
    out = jnp.full(index.shape, values[0], values[0].dtype)
    for k in range(1, len(values)):
        out = jnp.where(index >= k, values[k], out)
    return out


def forward_kernel(slots, cnt, x, w_in, gain, w_all, pooled, pm_out, normed_out, qkv, prob, a_out, pm_acc):
    tower = pl.program_id(0)
    pairs = pooled.shape[1]
    first = lax.axis_index("mp") * pairs
    parts = w_all.shape[0]
    per = LANES // slots
    groups = pairs // per
    heads = 2 * parts
    xs = x[0]
    hidden = nn(xs, w_in[0].astype(BF16))
    inverse = lax.rsqrt(jnp.mean(hidden * hidden, -1, keepdims=True) + EPS)
    normed = (hidden * inverse * gain[pl.ds(tower, 1), :]).astype(BF16)
    normed_out[0] = normed
    for c in range(3):
        for m in range(parts):
            qkv[0, c * parts + m] = nn(normed, w_all[m, 0, c]).astype(BF16)
    lane = iota((LANES, LANES), 1)
    line = iota((LANES, LANES), 0)
    shift = slots.bit_length() - 1
    pair_r, pair_s = lax.shift_right_logical(lane, shift), lax.shift_right_logical(line, shift)
    same = pair_r == pair_s
    halves = [lane < DH, lane >= DH]
    own_head = iota((per * heads, LANES), 0) & (heads - 1)

    def group(g, carry):
        counts = [cnt[tower, first + g * per + k] for k in range(per)]
        live_r = same & ((lane & (slots - 1)) < chain(pair_r, counts))
        live_s = (line & (slots - 1)) < chain(pair_s, counts)
        rows = pl.ds(pl.multiple_of(g * LANES, LANES), LANES)
        sums = []
        for m in range(parts):
            query, key = qkv[0, m, rows, :], qkv[0, parts + m, rows, :]
            for half in range(2):
                scores = nt(jnp.where(halves[half], query, jnp.zeros_like(query)), key) * 0.125
                scores = jnp.where(live_r, scores, -1000000000.0)
                expo = jnp.exp(scores - jnp.max(scores, 1, keepdims=True))
                p = (expo * (1.0 / jnp.sum(expo, 1, keepdims=True))).astype(BF16)
                prob[0, g, 2 * m + half] = p
                sums.append(jnp.sum(jnp.where(live_s, p.astype(F32), 0.0), 0, keepdims=True))
        sums = jnp.concatenate(sums, 0)
        pair_l = lax.shift_right_logical(iota((heads, LANES), 1), shift)
        stack = jnp.concatenate([jnp.where(pair_l == k, sums, 0.0) for k in range(per)], 0).astype(BF16)
        a_out[0, g] = stack
        for m in range(parts):
            mix = nn(stack, qkv[0, 2 * parts + m, rows, :])
            head = iota((per * heads, LANES), 1) // DH + 2 * m
            mix = jnp.where(own_head == head, mix, 0.0)
            pm_acc[g, :, m * LANES : (m + 1) * LANES] = jnp.concatenate(
                [jnp.sum(mix[k * heads : (k + 1) * heads], 0, keepdims=True) for k in range(per)], 0
            )
        return carry

    lax.fori_loop(0, groups, group, 0)
    pm = jnp.concatenate([pm_acc[g] for g in range(groups)], 0).astype(BF16)
    pm_out[0] = pm
    every = [cnt[tower, first + k] for k in range(pairs)]
    tokens = iota((pairs, pairs * slots), 1)
    mine = lax.shift_right_logical(tokens, shift) == iota(tokens.shape, 0)
    live = mine & ((tokens & (slots - 1)) < chain(iota(tokens.shape, 0), every))
    high, low = split(nn(live.astype(BF16), xs))
    w = w_in[0].astype(BF16)
    total = nn(high, w) + nn(low, w)
    sides = []
    for j in range(2):
        side = total[:, j * LANES : (j + 1) * LANES]
        for m in range(parts):
            side = side + nn(pm[:, m * LANES : (m + 1) * LANES], w_all[m, 0, 3, j * LANES : (j + 1) * LANES, :])
        sides.append(side)
    total = jnp.concatenate(sides, 1)
    count = chain(iota(total.shape, 0), every).astype(F32)
    pooled[0] = (total / count).astype(BF16)


def backward_kernel(
    slots, cnt, x, w_in, gain, w_all, normed_in, qkv, prob, a_in, pm_in, dpooled, demb, d_in, d_gain, d_qkv, d_out, dqkv
):
    tower = pl.program_id(0)
    pairs, width = dpooled.shape[1:]
    parts = w_all.shape[0]
    per = LANES // slots
    groups = pairs // per
    heads = 2 * parts
    shift = slots.bit_length() - 1
    tokens = pairs * slots
    first = lax.axis_index("mp") * pairs
    every = [cnt[tower, first + k] for k in range(pairs)]
    count = chain(iota((pairs, width), 0), every).astype(F32)
    dsum = dpooled[0].astype(F32) / count
    branch = dsum.astype(BF16)
    dmix = []
    for m in range(parts):
        grad = tn(pm_in[0, :, m * LANES : (m + 1) * LANES], branch).astype(BF16)
        for j in range(width // LANES):
            d_out[m, 0, j] = grad[:, j * LANES : (j + 1) * LANES]
        mix = 0.0
        for j in range(2):
            cut = slice(j * LANES, (j + 1) * LANES)
            mix = mix + nt(branch[:, cut], w_all[m, 0, 3, cut, :])
        dmix.append(mix)
    lane = iota((LANES, LANES), 1)
    line = iota((LANES, LANES), 0)
    pair_s = lax.shift_right_logical(line, shift)
    halves = [lane < DH, lane >= DH]
    own_head = iota((per * heads, LANES), 0) & (heads - 1)
    own_pair = lax.shift_right_logical(iota((per * heads, LANES), 0), heads.bit_length() - 1)
    token_pair = lax.shift_right_logical(iota((per * heads, LANES), 1), shift)
    for g in range(groups):
        rows = slice(g * LANES, (g + 1) * LANES)
        live_s = (line & (slots - 1)) < chain(pair_s, every[g * per : (g + 1) * per])
        scale = jnp.where(live_s, 0.125, 0.0)
        dots = jnp.zeros((per * heads, LANES), F32)
        stacks = []
        for m in range(parts):
            cut = dmix[m][g * per : (g + 1) * per]
            spread = jnp.concatenate([jnp.broadcast_to(cut[k : k + 1], (heads, LANES)) for k in range(per)], 0)
            head = iota((per * heads, LANES), 1) // DH + 2 * m
            stack = jnp.where(own_head == head, spread, 0.0).astype(BF16)
            stacks.append(stack)
            dots = dots + nt(stack, qkv[0, 2 * parts + m, rows, :])
        dots = jnp.where(own_pair == token_pair, dots, 0.0)
        pull = dots[0:heads]
        for k in range(1, per):
            pull = pull + dots[k * heads : (k + 1) * heads]
        for m in range(parts):
            query, key = qkv[0, m, rows, :], qkv[0, parts + m, rows, :]
            none = jnp.zeros_like(query)
            dq = jnp.zeros((LANES, LANES), F32)
            dk = jnp.zeros((LANES, LANES), F32)
            for half in range(2):
                h = 2 * m + half
                p = prob[0, g, h].astype(F32)
                t = p * pull[h : h + 1, :]
                ds = ((t - p * jnp.sum(t, 1, keepdims=True)) * scale).astype(BF16)
                dq = dq + nn(ds, jnp.where(halves[half], key, none))
                dk = dk + tn(ds, jnp.where(halves[half], query, none))
            dqkv[m, rows, :] = dq.astype(BF16)
            dqkv[parts + m, rows, :] = dk.astype(BF16)
            dqkv[2 * parts + m, rows, :] = tn(a_in[0, g], stacks[m]).astype(BF16)
    normed = normed_in[0]
    dnormed = jnp.zeros((tokens, width), F32)
    for m in range(parts):
        for c in range(3):
            grad = dqkv[c * parts + m]
            dnormed = dnormed + nt(grad, w_all[m, 0, c])
            d_qkv[m, 0, c] = tn(normed, grad).astype(BF16)
    dnormed = dnormed.astype(BF16).astype(F32)
    xs = x[0]
    w = w_in[0].astype(BF16)
    hidden = nn(xs, w)
    inverse = lax.rsqrt(jnp.mean(hidden * hidden, -1, keepdims=True) + EPS)
    unit = hidden * inverse
    grad = jnp.sum(dnormed * unit, 0, keepdims=True)

    @pl.when(tower == 0)
    def _():
        d_gain[...] = jnp.zeros_like(d_gain)

    for j in range(width // LANES):
        d_gain[pl.ds(tower * (width // LANES) + j, 1), :] = grad[:, j * LANES : (j + 1) * LANES]
    scaled = dnormed * gain[pl.ds(tower, 1), :]
    dh = inverse * (scaled - unit * jnp.mean(scaled * unit, -1, keepdims=True))
    spread = jnp.broadcast_to(dsum[:, None, :], (pairs, slots, width))
    slot = iota((pairs, slots, width), 1)
    counts = chain(iota((pairs, slots, width), 0), every)
    spread = jnp.where(slot < counts, spread, 0.0).reshape(tokens, width)
    dhidden = (spread + dh).astype(BF16)
    grad = tn(xs, dhidden).astype(BF16)
    for j in range(width // LANES):
        d_in[0, j] = grad[:, j * LANES : (j + 1) * LANES]
    demb[0] = nt(dhidden, w).astype(BF16)


def gelu_parts(v):
    c = 0.7978845608028654
    inner = jnp.tanh(c * (v + 0.044715 * (v * v * v)))
    value = 0.5 * v * (1.0 + inner)
    slope = 0.5 * (1.0 + inner) + 0.5 * v * (1.0 - inner * inner) * (c * (1.0 + 3.0 * 0.044715 * (v * v)))
    return value, slope


def upper_kernel(
    plane,
    line,
    pooled,
    far_one,
    far_two,
    far_three,
    log_prior,
    item_qid,
    lists,
    positive,
    dpooled,
    d_one,
    d_two,
    d_three,
    loss,
    pooled_all,
    second_send,
    second_got,
    vec,
    dsec_send,
    dsec_all,
    dpool_send,
    dpool_got,
    out_sems,
    in_sems,
    vec_out,
    vec_in,
    w_one,
    w_two,
    w_three,
    load_sems,
    second_mine,
    dpool_mine,
    prior_col,
):
    loads = [
        pltpu.make_async_copy(source, target, load_sems.at[j])
        for j, (source, target) in enumerate(((far_one, w_one), (far_two, w_two), (far_three, w_three)))
    ]
    for copy in loads:
        copy.start()
    me, part = enter(plane, line)
    towers, own, width = pooled.shape
    per = lists.shape[1] - 8
    rows = own * line
    pairs = rows * plane
    peers = [lax.rem(part + k, line) for k in range(1, line)]

    pooled_all[:, part] = pooled[...]
    first = [
        send(pooled_all.at[:, part], pooled_all.at[:, part], out_sems.at[0, k], in_sems.at[0, k], (me, peers[k]))
        for k in range(line - 1)
    ]
    for copy in loads:
        copy.wait()
    one = [w_one[t].astype(BF16) for t in range(towers)]
    two = [w_two[t].astype(BF16) for t in range(towers)]
    three = [w_three[t].astype(BF16) for t in range(towers)]
    qid = item_qid[...]
    hot = (lax.shift_right_logical(qid, 7) == iota((log_prior.shape[0], pairs), 0)).astype(BF16)
    high, rest = log_prior[...].astype(BF16), log_prior[...]
    rest = rest - high.astype(F32)
    middle, low = split(rest)
    table = tn(high, hot) + tn(middle, hot) + tn(low, hot)
    prior_row = jnp.sum(jnp.where((qid & 127) == iota((LANES, pairs), 0), table, 0.0), 0, keepdims=True)
    prior_col[...] = jnp.transpose(jnp.broadcast_to(prior_row, (8, pairs)), (1, 0))
    pos_row = jnp.concatenate([lists[d, per : per + 1, 0:rows] for d in range(plane)], 1)
    pos_own = chain(iota((own, pairs), 0), [positive[part * own + k] for k in range(own)])
    for copy in first:
        copy.wait()
    act_one, slope_one, pools = [], [], []
    for t in range(towers):
        pools.append(pooled_all[t].reshape(rows, width))
        value, slope = gelu_parts(nn(pools[t], one[t]))
        act_one.append(value.astype(BF16))
        slope_one.append(slope)
        partial = nn(act_one[t], two[t]).reshape(line, own, -1)
        second_mine[t] = partial
        second_send[t] = partial.astype(BF16)
    second = [
        send(
            second_send.at[:, peers[k]], second_got.at[:, part], out_sems.at[1, k], in_sems.at[1, k], (me, peers[k])
        )
        for k in range(line - 1)
    ]
    for copy in second:
        copy.wait()
    act_two, slope_two, third, length, vectors = [], [], [], [], []
    for t in range(towers):
        total = second_mine[t, part]
        for peer in peers:
            total = total + second_got[t, peer].astype(F32)
        value, slope = gelu_parts(total)
        act_two.append(value.astype(BF16))
        slope_two.append(slope)
        third.append(nn(act_two[t], three[t]))
        length.append(lax.rsqrt(jnp.sum(third[t] * third[t], -1, keepdims=True) + EPS))
        vectors.append((third[t] * length[t]).astype(BF16))
        vec[t, me, part] = vectors[t]
    along = [
        send(vec.at[:, me, part], vec.at[:, me, part], out_sems.at[2, k], in_sems.at[2, k], (me, peers[k]))
        for k in range(line - 1)
    ]
    for copy in along:
        copy.wait()
    chips = plane // 2
    core = lax.rem(me, 2)
    chip = me // 2
    sibling = me + 1 - 2 * core
    near = [send(vec.at[:, me], vec.at[:, me], vec_out.at[0], vec_in.at[0], (sibling, part))]
    across = []
    for k in range(1, chips):
        other = 2 * lax.rem(chip + k, chips) + core
        across.append(send(vec.at[:, me], vec.at[:, me], vec_out.at[k], vec_in.at[k], (other, part)))
    for k in range(1, chips):
        peer = 2 * lax.rem(chip - k + chips, chips) + core
        across[k - 1].wait_recv()
        sems = vec_out.at[chips + k], vec_in.at[chips + k]
        near.append(send(vec.at[:, peer], vec.at[:, peer], *sems, (sibling, part)))
    for copy in across:
        copy.wait_send()
    for copy in near:
        copy.wait()

    queries = vec[0].reshape(pairs, width)
    items = vec[1].reshape(pairs, width)
    logits = INV_TEMP * nt(items, queries) - prior_col[:, 0:1]
    peak = jnp.max(logits, 0, keepdims=True)
    log_total = peak + jnp.log(jnp.sum(jnp.exp(logits - peak), 0, keepdims=True))
    picked = jnp.where(iota((pairs, pairs), 0) == pos_row, logits, 0.0)
    gap = log_total - jnp.sum(picked, 0, keepdims=True)
    loss[0, 0] = jnp.sum(gap)
    ahead = me * rows + part * own
    mine = INV_TEMP * nt(vectors[0], items) - prior_row
    top = jnp.max(mine, 1, keepdims=True)
    expo = jnp.exp(mine - top)
    chance = expo / jnp.sum(expo, 1, keepdims=True)
    target = (iota(mine.shape, 1) == pos_own).astype(F32)
    dlog = ((chance - target) / pairs).astype(BF16)
    dvec = [(INV_TEMP * nn(dlog, items)).astype(BF16)]
    own_prior = prior_col[pl.ds(pl.multiple_of(ahead, own), own), 0:1]
    theirs = INV_TEMP * nt(vectors[1], queries) - own_prior
    target = (iota(theirs.shape, 0) + ahead == pos_row).astype(F32)
    dlog = ((jnp.exp(theirs - log_total) - target) / pairs).astype(BF16)
    dvec.append((INV_TEMP * nn(dlog, queries)).astype(BF16))

    dthirds = []
    for t in range(towers):
        dv = dvec[t].astype(F32)
        inner = jnp.sum(dv * third[t], -1, keepdims=True)
        dthird = (length[t] * dv - third[t] * (length[t] * length[t] * length[t] * inner)).astype(BF16)
        dact = nt(dthird, three[t]).astype(BF16).astype(F32)
        dsec_all[t, part] = (dact * slope_two[t]).astype(BF16)
        dthirds.append(dthird)
    spread = [
        send(dsec_all.at[:, part], dsec_all.at[:, part], out_sems.at[3, k], in_sems.at[3, k], (me, peers[k]))
        for k in range(line - 1)
    ]
    for t in range(towers):
        grad = tn(act_two[t], dthirds[t]).astype(BF16)
        for j in range(width // LANES):
            d_three[t, j] = grad[:, j * LANES : (j + 1) * LANES]
    for copy in spread:
        copy.wait()
    dfirsts = []
    for t in range(towers):
        dsecond = dsec_all[t].reshape(rows, -1)
        dact = nt(dsecond, two[t]).astype(BF16).astype(F32)
        dfirst = (dact * slope_one[t]).astype(BF16)
        partial = nt(dfirst, one[t]).reshape(line, own, width)
        dpool_mine[t] = partial
        dpool_send[t] = partial.astype(BF16)
        dfirsts.append(dfirst)
    back = [
        send(dpool_send.at[:, peers[k]], dpool_got.at[:, part], out_sems.at[4, k], in_sems.at[4, k], (me, peers[k]))
        for k in range(line - 1)
    ]
    for t in range(towers):
        dsecond = dsec_all[t].reshape(rows, -1)
        for grads, grad in ((d_two, tn(act_one[t], dsecond)), (d_one, tn(pools[t], dfirsts[t]))):
            grad = grad.astype(BF16)
            for j in range(grad.shape[1] // LANES):
                grads[t, j] = grad[:, j * LANES : (j + 1) * LANES]
    for copy in back:
        copy.wait()
    for t in range(towers):
        total = dpool_mine[t, part]
        for peer in peers:
            total = total + dpool_got[t, peer].astype(F32)
        dpooled[t] = total.astype(BF16)


def update(weight, grad, moment, average, factor, rate):
    clipped = grad * factor
    moment_new = MOMENTUM * moment + clipped
    weight_new = weight - rate * (clipped + MOMENTUM * moment_new)
    average_new = AVERAGE_DECAY * average + (1.0 - AVERAGE_DECAY) * weight_new
    return [weight_new, moment_new, average_new]


def update_kernel(blocks, norm_sq, table_grad, dense, gain, *refs):
    arrays = 3 * 8
    sources, targets, norm = refs[:arrays], refs[arrays : 2 * arrays], refs[2 * arrays]
    held, in_sems, out_sems = refs[2 * arrays + 1 : 3 * arrays + 1], refs[-2], refs[-1]
    loads = [pltpu.make_async_copy(sources[k], held[k], in_sems.at[k]) for k in range(arrays)]
    ahead = 8

    def load(k):
        if k < arrays // 3:
            for copy in loads[3 * k : 3 * k + 3]:
                copy.start()

    for k in range(ahead):
        load(k)
    root = jnp.sqrt(norm_sq[...])
    norm[0, 0] = jnp.max(root)
    factor = jnp.minimum(1.0, CLIP_NORM / root[0:1, :])
    stores = []

    def finish(k):
        for j in range(3 * k, 3 * k + 3):
            copy = pltpu.make_async_copy(held[j], targets[j], out_sems.at[j])
            copy.start()
            stores.append(copy)

    def apply(k, rows, lanes, grad, rate):
        cells = [ref.at[rows, lanes] for ref in held[3 * k : 3 * k + 3]]
        new = update(cells[0][...], grad, cells[1][...], cells[2][...], factor, rate)
        for cell, value in zip(cells, new):
            cell[...] = value

    def wait(k):
        for copy in loads[3 * k : 3 * k + 3]:
            copy.wait()
        load(k + ahead)

    wait(0)

    def rows(i, carry):
        at = pl.ds(pl.multiple_of(i * 32, 32), 32)
        apply(0, at, slice(0, LANES), table_grad[at, :], ROW_RATE)
        return carry

    lax.fori_loop(0, table_grad.shape[0] // 32, rows, 0, unroll=2)
    finish(0)
    at = 0
    for k, size, height, wide in blocks:
        wait(k)
        total = dense.shape[0] * size
        step = 32 if size % 32 == 0 else 16
        for first in range(0, total, min(size, height)):
            count = min(size, height)
            share, inside = first // size, first % size
            block, begin = first // height, first % height
            t, j = block // wide, block % wide
            top = t * height + begin

            def piece(i, carry):
                take = pl.ds(pl.multiple_of(at + inside + i * step, 16), step)
                rows = pl.ds(pl.multiple_of(top + i * step, 16), step)
                grad = dense[share, take, :].astype(F32)
                apply(k, rows, slice(j * LANES, (j + 1) * LANES), grad, MATRIX_RATE)
                return carry

            lax.fori_loop(0, count // step, piece, 0, unroll=2)
        at += size
        finish(k)
    last = 7
    wait(last)
    for t in range(held[3 * last].shape[0]):
        for j in range(held[3 * last].shape[1] // LANES):
            r = t * (held[3 * last].shape[1] // LANES) + j
            apply(last, slice(t, t + 1), slice(j * LANES, (j + 1) * LANES), gain[r : r + 1, :], GAIN_RATE)
    finish(last)
    for copy in stores:
        copy.wait()


def shards(
    slot_owner,
    slot_row,
    slot_count,
    item_qid,
    positive,
    log_prior,
    embedding,
    embedding_mom,
    embedding_avg,
    w_in,
    w_in_mom,
    w_in_avg,
    norm_gain,
    norm_gain_mom,
    norm_gain_avg,
    w_qkv,
    w_qkv_mom,
    w_qkv_avg,
    w_out,
    w_out_mom,
    w_out_avg,
    w_one,
    w_one_mom,
    w_one_avg,
    w_two,
    w_two_mom,
    w_two_avg,
    w_three,
    w_three_mom,
    w_three_avg,
):
    plane = lax.axis_size("dp")
    line = lax.axis_size("mp")
    batch, towers, slots = slot_row.shape
    own = batch // line
    requests = batch * towers * slots
    own_requests = requests // line
    tokens = own * slots
    capacity = max(LANES, 2 * requests // plane)
    pairs = batch * plane
    part = lax.axis_index("mp")
    me = lax.axis_index("dp")
    width = w_in.shape[2]
    depth = w_in.shape[1]
    units = w_one.shape[2]
    seconds = w_two.shape[2]

    per = capacity // LANES
    small = capacity // 4
    dims = (towers, own, slots)

    def row_scratch(count):
        return [
            pltpu.VMEM((plane, count, depth), BF16),
            pltpu.VMEM((plane, count, depth), BF16),
            pltpu.VMEM((plane * count, depth), F32),
        ]

    turned = jnp.transpose(w_qkv, (0, 2, 1, 3))
    embedded, got_own, got_lists, weights, inverse, own_place = pl.pallas_call(
        functools.partial(fetch_kernel, plane, line, dims, capacity),
        out_shape=[
            shape((own_requests, depth), BF16),
            shape((plane, per, LANES), I32),
            shape((plane, per + 8, LANES), I32),
            shape((line, towers, 4, width, LANES), BF16),
            shape((plane * per, LANES), I32),
            shape((slots, LANES), I32),
        ],
        in_specs=[VMEM] * 4 + [HBM] * 3,
        out_specs=[VMEM] * 6,
        scratch_shapes=[
            pltpu.VMEM((plane, per, LANES), I32),
            pltpu.VMEM((slots, LANES), I32),
            pltpu.VMEM((plane, per + 8, LANES), I32),
            pltpu.VMEM(embedding.shape, F32),
            pltpu.VMEM(turned.shape, F32),
            pltpu.VMEM(w_out.shape, F32),
            pltpu.SMEM((slots, LANES), I32),
            pltpu.SMEM((plane, -(-small // LANES), LANES), I32),
            *row_scratch(small),
            DMA((2, plane)),
            DMA((2, plane)),
            DMA((plane,)),
            DMA((plane,)),
            DMA((line,)),
            DMA((line,)),
            DMA((line,)),
            DMA((line,)),
            DMA((2, line)),
            DMA((2, line)),
            DMA((4,)),
            DMA((3,)),
        ],
        compiler_params=params(60, collective_id=2, has_side_effects=True),
        name="fetch",
    )(
        jnp.transpose(slot_owner[..., 0], (1, 2, 0)),
        jnp.transpose(slot_row, (1, 2, 0)),
        jnp.transpose(slot_count),
        positive.reshape(1, batch),
        embedding,
        turned,
        w_out,
    )
    most = jnp.max(got_lists[:, per + 1 : per + 3, 0], 0)

    def refetch(ids, place, table, _):
        return pl.pallas_call(
            functools.partial(refetch_kernel, plane, dims),
            out_shape=shape((own_requests, depth), BF16),
            in_specs=[SMEM, SMEM, VMEM],
            out_specs=VMEM,
            scratch_shapes=[*row_scratch(capacity), DMA((plane,)), DMA((plane,))],
            compiler_params=params(16, collective_id=7, has_side_effects=True),
            name="refetch",
        )(ids, place, table)

    embedded = lax.cond(most[0] > small, refetch, lambda *given: given[3], got_own, own_place, embedding, embedded)
    embedded = embedded.reshape(towers, tokens, depth)

    counts = jnp.transpose(slot_count)
    heads = 2 * line
    groups = tokens // LANES
    per_group = LANES // slots
    lead = lambda *dims: pl.BlockSpec((1,) + dims, lambda t: (t,) + (0,) * len(dims))
    qkv_spec = pl.BlockSpec((line, 1, 3, width, LANES), lambda t: (0, t, 0, 0, 0))
    all_spec = pl.BlockSpec((line, 1, 4, width, LANES), lambda t: (0, t, 0, 0, 0))
    pooled, pm, normed, qkv, prob, spread = pl.pallas_call(
        functools.partial(forward_kernel, slots),
        grid=(towers,),
        out_shape=[
            shape((towers, own, width), BF16),
            shape((towers, own, line * LANES), BF16),
            shape((towers, tokens, width), BF16),
            shape((towers, 3 * line, tokens, LANES), BF16),
            shape((towers, groups, heads, LANES, LANES), BF16),
            shape((towers, groups, per_group * heads, LANES), BF16),
        ],
        in_specs=[SMEM, lead(tokens, depth), lead(depth, width), VMEM, all_spec],
        out_specs=[
            lead(own, width),
            lead(own, line * LANES),
            lead(tokens, width),
            lead(3 * line, tokens, LANES),
            lead(groups, heads, LANES, LANES),
            lead(groups, per_group * heads, LANES),
        ],
        scratch_shapes=[pltpu.VMEM((groups, per_group, line * LANES), F32)],
        compiler_params=params(20),
        name="attention_forward",
    )(counts, embedded, w_in, norm_gain, weights)

    dpooled, d_one, d_two, d_three, loss = pl.pallas_call(
        functools.partial(upper_kernel, plane, line),
        out_shape=[
            shape((towers, own, width), BF16),
            shape((towers, units // LANES, width, LANES), BF16),
            shape((towers, seconds // LANES, units, LANES), BF16),
            shape((towers, width // LANES, seconds, LANES), BF16),
            shape((1, 1), F32),
        ],
        in_specs=[VMEM] + [HBM] * 3 + [VMEM] * 3 + [SMEM],
        out_specs=[VMEM] * 4 + [SMEM],
        scratch_shapes=[
            pltpu.VMEM((towers, line, own, width), BF16),
            pltpu.VMEM((towers, line, own, seconds), BF16),
            pltpu.VMEM((towers, line, own, seconds), BF16),
            pltpu.VMEM((towers, plane, line, own, width), BF16),
            pltpu.VMEM((towers, line, own, seconds), BF16),
            pltpu.VMEM((towers, line, own, seconds), BF16),
            pltpu.VMEM((towers, line, own, width), BF16),
            pltpu.VMEM((towers, line, own, width), BF16),
            DMA((5, line)),
            DMA((5, line)),
            DMA((plane,)),
            DMA((plane,)),
            pltpu.VMEM(w_one.shape, F32),
            pltpu.VMEM(w_two.shape, F32),
            pltpu.VMEM(w_three.shape, F32),
            DMA((3,)),
            pltpu.VMEM((towers, line, own, seconds), F32),
            pltpu.VMEM((towers, line, own, width), F32),
            pltpu.VMEM((pairs, 8), F32),
        ],
        compiler_params=params(22 + 2 * (pairs * pairs >> 18), collective_id=3, has_side_effects=True),
        name="upper",
    )(
        pooled,
        w_one,
        w_two,
        w_three,
        log_prior.reshape(-1, LANES),
        item_qid.reshape(1, pairs),
        got_lists,
        positive,
    )

    demb, d_in, d_gain, d_qkv, d_out = pl.pallas_call(
        functools.partial(backward_kernel, slots),
        grid=(towers,),
        out_shape=[
            shape((towers, tokens, depth), BF16),
            shape((towers, width // LANES, depth, LANES), BF16),
            shape((8, LANES), F32),
            shape((line, towers, 3, width, LANES), BF16),
            shape((line, towers, width // LANES, LANES, LANES), BF16),
        ],
        in_specs=[
            SMEM,
            lead(tokens, depth),
            lead(depth, width),
            VMEM,
            all_spec,
            lead(tokens, width),
            lead(3 * line, tokens, LANES),
            lead(groups, heads, LANES, LANES),
            lead(groups, per_group * heads, LANES),
            lead(own, line * LANES),
            lead(own, width),
        ],
        out_specs=[
            lead(tokens, depth),
            lead(width // LANES, depth, LANES),
            pl.BlockSpec((8, LANES), lambda t: (0, 0)),
            qkv_spec,
            pl.BlockSpec((line, 1, width // LANES, LANES, LANES), lambda t: (0, t, 0, 0, 0)),
        ],
        scratch_shapes=[pltpu.VMEM((3 * line, tokens, LANES), BF16)],
        compiler_params=params(24),
        name="attention_backward",
    )(counts, embedded, w_in, norm_gain, weights, normed, qkv, prob, spread, pm, dpooled)

    def shares(grad, lead=()):
        rows = grad.size // (LANES * plane * (lead[0] if lead else 1))
        return grad.reshape(*lead, plane // 2, 2, rows, LANES)

    grads = [shares(d_qkv, (line,)), shares(d_out, (line,))] + [shares(g) for g in (d_three, d_in, d_one, d_two)]
    sizes = [g.shape[-2] for g in grads]
    share = line * (sizes[0] + sizes[1]) + sum(sizes[2:])
    every, summed, gain_sum = pl.pallas_call(
        functools.partial(spread_kernel, plane, line),
        out_shape=[
            shape((line, own_requests, depth), BF16),
            shape((share, LANES), BF16),
            shape((8, LANES), F32),
        ],
        in_specs=[VMEM] * 8,
        out_specs=[VMEM] * 3,
        scratch_shapes=[
            [pltpu.VMEM((line, plane // 2, size, LANES), BF16) for size in sizes[:2]],
            [pltpu.VMEM((plane // 2, size, LANES), BF16) for size in sizes[2:]],
            pltpu.VMEM((plane // 2, share, LANES), BF16),
            pltpu.VMEM((plane // 2 - 1, share, LANES), BF16),
            pltpu.VMEM((plane, 8, LANES), F32),
            DMA((line,)),
            DMA((line,)),
            DMA((6,)),
            DMA((6,)),
            DMA((plane // 2,)),
            DMA((plane // 2,)),
            DMA((plane,)),
            DMA((plane,)),
            DMA,
        ],
        compiler_params=params(20, collective_id=4, has_side_effects=True),
        name="spread",
    )(demb.reshape(own_requests, depth), *grads, d_gain)
    whole_at = line * (sizes[0] + sizes[1])
    whole_rows = sizes[2] + sizes[3]
    last_rows = sizes[4] + sizes[5]
    cuts = (
        ((0, sizes[0]), (line * sizes[0], sizes[1])),
        (whole_at, whole_rows),
        (whole_at + whole_rows, last_rows),
    )
    line_rows = sizes[0] + sizes[1] + whole_rows

    def tail(count, number):
        return lambda *given: pl.pallas_call(
            functools.partial(tail_kernel, plane, line, count, cuts),
            out_shape=[
                shape(embedding.shape, F32),
                shape((plane, line_rows + last_rows, LANES), BF16),
                shape((8, LANES), F32),
                shape((8, LANES), F32),
            ],
            in_specs=[SMEM] + [VMEM] * 4,
            out_specs=[VMEM] * 4,
            scratch_shapes=[
                pltpu.VMEM((requests, depth), F32),
                pltpu.VMEM((plane, count, depth), BF16),
                pltpu.VMEM((plane, count, depth), BF16),
                pltpu.VMEM((embedding.shape[0] // 2, 2 * depth), F32),
                pltpu.VMEM((line, line_rows, LANES), BF16),
                pltpu.VMEM((line, 8, LANES), F32),
                pltpu.VMEM((line, 8, LANES), F32),
                pltpu.VMEM((plane, 8, LANES), F32),
                DMA((plane,)),
                DMA((plane,)),
                DMA((3, line)),
                DMA((3, line)),
                DMA((line,)),
                DMA((line,)),
                DMA((line,)),
                DMA((line,)),
                DMA((plane,)),
                DMA((plane,)),
                DMA((plane // 2,)),
                DMA((plane // 2,)),
                DMA((plane // 2,)),
                DMA((plane // 2,)),
            ],
            compiler_params=params(36, collective_id=number, has_side_effects=True),
            name="tail",
        )(given[0][:, : -(-count // LANES)], *given[1:])

    medium = capacity * 5 // 8
    table_grad, dense_all, norm_sq, gain_all = lax.cond(
        most[1] > medium,
        tail(capacity, 8),
        tail(medium, 5),
        inverse.reshape(plane, per, LANES),
        got_lists,
        every.reshape(requests, depth),
        summed,
        gain_sum,
    )
    flat = lambda w: w.reshape(-1, w.shape[-1])
    turn = lambda w: flat(jnp.transpose(w, (0, 2, 1, 3)))
    given = [embedding, embedding_mom, embedding_avg]
    given += [turn(w) for w in (w_qkv, w_qkv_mom, w_qkv_avg)]
    rest = (w_out, w_out_mom, w_out_avg, w_three, w_three_mom, w_three_avg, w_in, w_in_mom, w_in_avg)
    rest += (w_one, w_one_mom, w_one_avg, w_two, w_two_mom, w_two_avg)
    given += [flat(w) for w in rest]
    given += [norm_gain, norm_gain_mom, norm_gain_avg]
    heights = (towers * 3 * width, LANES, seconds, depth, width, units)
    wides = (1, width // LANES, width // LANES, width // LANES, units // LANES, seconds // LANES)
    blocks = tuple((k + 1, size, height, wide) for k, (size, height, wide) in enumerate(zip(sizes, heights, wides)))
    *done, norm = pl.pallas_call(
        functools.partial(update_kernel, blocks),
        out_shape=[shape(w.shape, F32) for w in given] + [shape((1, 1), F32)],
        in_specs=[VMEM] * 4 + [HBM] * len(given),
        out_specs=[HBM] * len(given) + [SMEM],
        scratch_shapes=[pltpu.VMEM(w.shape, F32) for w in given] + [DMA((len(given),))] * 2,
        compiler_params=params(57),
        name="update",
    )(norm_sq, table_grad, dense_all, gain_all, *given)
    back = lambda k, w: [done[3 * k + j].reshape(w.shape) for j in range(3)]
    unturned = [
        jnp.transpose(w.reshape(towers, 3, width, LANES), (0, 2, 1, 3)) for w in done[3:6]
    ]
    new = done[:3] + back(4, w_in) + done[21:24] + unturned + back(2, w_out) + back(5, w_one) + back(6, w_two)
    return (loss.reshape(()), norm.reshape(()), *new, *back(3, w_three))


def solution(mesh):
    rows = P("dp", None)
    qkv = P(None, None, None, "mp")
    deep = P(None, "mp", None)
    wide = P(None, None, "mp")
    weights = (rows,) * 3 + (P(),) * 6 + (qkv,) * 3 + (deep,) * 3 + (wide,) * 3 + (deep,) * 3 + (P(),) * 3
    inputs = (P("dp", None, None, None), P("dp", None, None), P("dp", None), P(), P("dp"), P())
    return jax.shard_map(
        shards, mesh=mesh, in_specs=inputs + weights, out_specs=(P(), P()) + weights, check_vma=False
    )
```

```python
import functools

import jax
import jax.numpy as jnp
from jax import lax
from jax.experimental import pallas as pl
from jax.experimental.pallas import tpu as pltpu
from jax.sharding import PartitionSpec as P

DH = 64
EPS = 1e-06
INV_TEMP = 20.0
CLIP_NORM = 0.1
ROW_RATE = 150000.0
GAIN_RATE = 8000.0
MATRIX_RATE = 600.0
MOMENTUM = 0.9
AVERAGE_DECAY = 0.6

MESH = pl.DeviceIdType.MESH
LANES = 128
F32 = jnp.float32
BF16 = jnp.bfloat16
I32 = jnp.int32
VMEM = pl.BlockSpec(memory_space=pltpu.VMEM)
HBM = pl.BlockSpec(memory_space=pltpu.HBM)
SMEM = pl.BlockSpec(memory_space=pltpu.SMEM)
DMA = pltpu.SemaphoreType.DMA


def nn(a, b):
    return lax.dot_general(a, b, (((1,), (0,)), ((), ())), preferred_element_type=F32)


def nt(a, b):
    return lax.dot_general(a, b, (((1,), (1,)), ((), ())), preferred_element_type=F32)


def tn(a, b):
    return lax.dot_general(a, b, (((0,), (0,)), ((), ())), preferred_element_type=F32)


def iota(shape, dim):
    return lax.broadcasted_iota(I32, shape, dim)


def split(value):
    high = value.astype(BF16)
    return high, (value - high.astype(F32)).astype(BF16)


def shape(dims, dtype):
    return jax.ShapeDtypeStruct(tuple(dims), dtype)


def params(limit, **more):
    return pltpu.CompilerParams(vmem_limit_bytes=limit << 20, **more)


def log2(value):
    return value.bit_length() - 1


def lists_of(owner, values, owners, capacity):
    chunks = owner.shape[0]
    width = owners * capacity
    his = width // LANES
    sub = iota((owners, LANES), 0)
    hot = [(owner[c : c + 1, :] == sub).astype(F32) for c in range(chunks)]
    hots = jnp.concatenate(hot, 0).astype(BF16)
    before = (iota((LANES, LANES), 0) < iota((LANES, LANES), 1)).astype(BF16)
    earlier = nn(hots, before)
    totals = nn(hots, jnp.ones((LANES, LANES), BF16))
    base = (sub * capacity).astype(F32)
    places = []
    for c in range(chunks):
        cut = slice(c * owners, (c + 1) * owners)
        here = jnp.sum(hot[c] * (earlier[cut] + base), 0, keepdims=True).astype(I32)
        places.append(jnp.where(owner[c : c + 1, :] < owners, here, width))
        base = base + totals[cut]
    parts = 2 * len(values)
    acc = jnp.zeros((his, parts * LANES), F32)
    for c in range(chunks):
        place = places[c]
        left = (lax.shift_right_logical(place, 7) == iota((his, LANES), 0)).astype(BF16)
        low = (place & 127) == iota((LANES, LANES), 0)
        cuts = []
        for value in values:
            value = value[c : c + 1, :]
            cuts += [lax.shift_right_logical(value, 6), value & 63]
        right = jnp.concatenate([jnp.where(low, cut.astype(F32), 0.0) for cut in cuts], 0)
        acc = acc + nt(left, right.astype(BF16))
    cuts = [acc[:, k * LANES : (k + 1) * LANES].astype(I32) for k in range(parts)]
    lists = [cuts[2 * k] * 64 + cuts[2 * k + 1] for k in range(len(values))]
    return places, lists, hot


class Slots:
    def __init__(self, owners, line, owner, row, count):
        towers, slots, batch = owner.shape
        own = batch // line
        side = lambda ref: jnp.concatenate([ref[t] for t in range(towers)], 1)
        counts = jnp.concatenate([count[t : t + 1, :] for t in range(towers)], 1)
        slot, lane = iota((slots, LANES), 0), iota((slots, LANES), 1)
        tower = lax.shift_right_logical(lane, log2(batch))
        self.row = side(row)
        self.owner = jnp.where(slot < counts, side(owner), owners)
        self.block = lax.shift_right_logical(lane & (batch - 1), log2(own))
        self.token = ((self.block * towers + tower) * own + (lane & (own - 1))) * slots + slot


def make_own_lists(slots, owners, capacity, small, height, own_lists, own_place, own_small):
    per = capacity // LANES
    owner = jnp.where(slots.block == lax.axis_index("mp"), slots.owner, owners)
    places, (rows,), _ = lists_of(owner, (slots.row,), owners, capacity)
    rows = jnp.minimum(jnp.maximum(rows, 0), height - 1)
    for d in range(owners):
        own_lists[d] = rows[d * per : (d + 1) * per, :]
    place = jnp.concatenate(places, 0)
    place = jnp.maximum(jnp.where(place < owners * capacity, place, 0), 0)
    own_place[...] = place
    rank = jnp.minimum(place & (capacity - 1), small - 1)
    own_small[...] = lax.shift_right_logical(place, log2(capacity)) * small + rank


def make_lists(slots, owners, capacity, batch, line, positive, lists, inverse):
    per = capacity // LANES
    _, (rows, tokens), hot = lists_of(slots.owner, (slots.row + 1, slots.token), owners, capacity)
    rows = rows - 1
    inverse[...] = tokens
    asked = hot[0]
    for more in hot[1:]:
        asked = asked + more
    own = batch // line
    near = lax.shift_right_logical(iota((LANES, LANES), 0) & (batch - 1), log2(own)) == iota((LANES, LANES), 1)
    asked = asked.astype(BF16)
    most = jnp.max(jnp.max(nn(asked, near.astype(BF16)), 0, keepdims=True), 1, keepdims=True)
    every = jnp.max(nn(asked, jnp.ones((LANES, LANES), BF16)), 0, keepdims=True)
    most = jnp.broadcast_to(most, (1, LANES))
    for d in range(owners):
        lists[d, 0:per, :] = rows[d * per : (d + 1) * per, :]
        lists[d, per : per + 1, 0:batch] = positive[...]
        lists[d, per + 1 : per + 2, :] = most.astype(I32)
        lists[d, per + 2 : per + 3, :] = every.astype(I32)


def announce(plane, line):
    me, part = lax.axis_index("dp"), lax.axis_index("mp")
    barrier = pltpu.get_barrier_semaphore()
    for k in range(1, plane):
        pl.semaphore_signal(barrier, inc=1, device_id=(lax.rem(me + k, plane), part), device_id_type=MESH)
    for k in range(1, line):
        pl.semaphore_signal(barrier, inc=1, device_id=(me, lax.rem(part + k, line)), device_id_type=MESH)
    return me, part


def await_others(plane, line):
    pl.semaphore_wait(pltpu.get_barrier_semaphore(), max(plane - 1, 0) + max(line - 1, 0))


def enter(plane, line):
    me, part = announce(plane, line)
    await_others(plane, line)
    return me, part


def partners(me, count):
    order = sorted(range(1, count), key=lambda k: (-bin(k >> 1).count("1"), k & 1, k))
    bits = [lax.rem(me // (1 << b), 2) for b in range(log2(count))]
    return [sum((1 << b) * (1 - bit if k >> b & 1 else bit) for b, bit in enumerate(bits)) for k in order]


def send(source, target, out_sem, in_sem, device):
    copy = pltpu.make_async_remote_copy(
        src_ref=source, dst_ref=target, send_sem=out_sem, recv_sem=in_sem, device_id=device, device_id_type=MESH
    )
    copy.start()
    return copy


def gather_rows(ids, table, target):
    def body(i, carry):
        at = ids(i)
        rows = [table[pl.ds(at(u), 1), :] for u in range(16)]
        target[pl.ds(pl.multiple_of(i * 16, 16), 16), :] = jnp.concatenate(rows, 0).astype(BF16)
        return carry

    lax.fori_loop(0, target.shape[0] // 16, body, 0)


def listed(ids, first):
    def at(i):
        block = first + lax.shift_right_logical(i, 3)
        start = (i & 7) * 16
        return lambda u: ids[block, start + u]

    return at


def placed(place, part, towers, own, slots):
    per = slots // 16

    def at(i):
        pair = lax.shift_right_logical(i, log2(per))
        tower = lax.shift_right_logical(pair, log2(own))
        lane = tower * (LANES // towers) + part * own + (pair & (own - 1))
        start = (i & (per - 1)) * 16
        return lambda u: place[start + u, lane]

    return at


def send_rows(plane, me, part, ids, table, sent, got, wide, out_sems, in_sems):
    capacity = sent.shape[1]
    copies = []
    for k, peer in enumerate(partners(me, plane)):
        gather_rows(listed(ids.at[peer], 0), table, sent.at[peer])
        copies.append(send(sent.at[peer], got.at[me], out_sems.at[k], in_sems.at[k], (peer, part)))
    gather_rows(listed(ids.at[me], 0), table, sent.at[me])
    wide[pl.ds(pl.multiple_of(me * capacity, capacity), capacity), :] = sent[me].astype(F32)
    return copies


def take_rows(plane, me, part, dims, copies, place, got, wide, out):
    capacity = got.shape[1]
    for copy, peer in zip(copies, partners(me, plane)):
        copy.wait_recv()
        wide[pl.ds(pl.multiple_of(peer * capacity, capacity), capacity), :] = got[peer].astype(F32)
    gather_rows(placed(place, part, *dims), wide, out)


def refetch_kernel(plane, dims, ids, place, table, out, sent, got, wide, out_sems, in_sems):
    me, part = enter(plane, 0)
    copies = send_rows(plane, me, part, ids, table, sent, got, wide, out_sems, in_sems)
    take_rows(plane, me, part, dims, copies, place, got, wide, out)
    for copy in copies:
        copy.wait_send()


def fetch_kernel(
    plane,
    line,
    dims,
    capacity,
    owner_in,
    row_in,
    count,
    positive,
    far_table,
    far_qkv,
    far_wout,
    out,
    got_own,
    got_lists,
    weights,
    inverse,
    own_place,
    own_lists,
    own_small,
    lists,
    table,
    w_qkv,
    w_out,
    place,
    ids,
    sent,
    got,
    wide,
    list_out,
    list_in,
    out_sems,
    in_sems,
    far_out,
    far_in,
    side_out,
    side_in,
    near_out,
    near_in,
    own_sems,
    load_sems,
):
    loads = [
        pltpu.make_async_copy(source, target, load_sems.at[j])
        for j, (source, target) in enumerate(((far_qkv, w_qkv), (far_wout, w_out), (far_table, table)))
    ]
    for copy in loads:
        copy.start()
    me, part = announce(plane, line)
    core = lax.rem(me, 2)
    half = lax.rem(me // 2, 2)
    sibling = me + 1 - 2 * core
    partner = me + 2 - 4 * half
    batch = positive.shape[1]
    slots = Slots(plane, line, owner_in, row_in, count)
    make_own_lists(slots, plane, capacity, sent.shape[1], table.shape[0], own_lists, own_place, own_small)
    places = pltpu.make_async_copy(own_small, place, own_sems.at[0])
    places.start()
    for copy in loads[:2]:
        copy.wait()
    rows = weights.shape[3] // 2
    for c in range(3):
        weights[part, :, c] = w_qkv[:, c].astype(BF16)
    for j in range(2):
        weights[part, :, 3, j * LANES : (j + 1) * LANES, :] = w_out[:, :, j * LANES : (j + 1) * LANES].astype(BF16)
    quarter = lambda m, h: weights.at[m, core, :, pl.ds(pl.multiple_of(h * rows, rows), rows), :]
    await_others(plane, line)
    far, asked, told = [], [], []
    for k in range(1, line):
        peer = lax.rem(part + k, line)
        far.append(send(quarter(part, half), quarter(part, half), far_out.at[k], far_in.at[k], (me, peer)))
    for k in range(1, plane):
        peer = lax.rem(me + k, plane)
        asked.append(send(own_lists.at[peer], got_own.at[me], list_out.at[0, k], list_in.at[0, k], (peer, part)))
    make_lists(slots, plane, capacity, batch, line, positive, lists, inverse)
    for k in range(1, plane):
        peer = lax.rem(me + k, plane)
        told.append(send(lists.at[peer], got_lists.at[me], list_out.at[1, k], list_in.at[1, k], (peer, part)))
    mine = [
        pltpu.make_async_copy(own_lists.at[me], got_own.at[me], own_sems.at[1]),
        pltpu.make_async_copy(lists.at[me], got_lists.at[me], own_sems.at[2]),
    ]
    for copy in mine:
        copy.start()
    for copy in asked:
        copy.wait()
    mine[0].wait()
    numbers = pltpu.make_async_copy(got_own.at[:, 0 : ids.shape[1]], ids, own_sems.at[3])
    numbers.start()
    for copy in (numbers, places, loads[2]):
        copy.wait()
    copies = send_rows(plane, me, part, ids, table, sent, got, wide, out_sems, in_sems)
    sides, near = [], []
    for k in range(1, line):
        peer = lax.rem(part - k + line, line)
        far[k - 1].wait_recv()
        at = quarter(peer, half)
        sides.append(send(at, at, side_out.at[k], side_in.at[k], (partner, part)))
        near.append(send(at, at, near_out.at[0, k], near_in.at[0, k], (sibling, part)))
    take_rows(plane, me, part, dims, copies, place, got, wide, out)
    for k in range(1, line):
        peer = lax.rem(part - k + line, line)
        sides[k - 1].wait_recv()
        at = quarter(peer, 1 - half)
        near.append(send(at, at, near_out.at[1, k], near_in.at[1, k], (sibling, part)))
    mine[1].wait()
    for copy in copies + far + sides:
        copy.wait_send()
    for copy in told + near:
        copy.wait()


def add_rows(ids, count, blocks, grads, total, fresh):
    height = total.shape[0]
    rows = []
    for block in blocks:
        for r in range(-(-count // LANES)):
            rows.append(ids[block, r : r + 1, 0 : min(LANES, count - r * LANES)])
    numbers = jnp.concatenate(rows, 1)
    values = jnp.concatenate([ref[...] for ref in grads], 0)
    turned = jnp.transpose(jnp.broadcast_to(numbers.astype(F32), (8, numbers.shape[1])), (1, 0))[:, 0:1]
    upper = turned >= height
    none = jnp.zeros_like(values)
    values = jnp.concatenate([jnp.where(upper, none, values), jnp.where(upper, values, none)], 1)
    low = jnp.where(numbers >= 0, numbers & (height - 1), -1)
    step = min(height, 1024)

    def body(i, carry):
        at = pl.multiple_of(i * step, step)
        hot = jnp.where(low - at == iota((step, low.shape[1]), 0), 1.0, 0.0).astype(BF16)
        part = nn(hot, values)
        at = pl.ds(at, step)
        total[at, :] = part if fresh else total[at, :] + part
        return carry

    lax.fori_loop(0, height // step, body, 0)


def tail_kernel(
    plane,
    line,
    capacity,
    cuts,
    tokens,
    ids,
    rows,
    summed,
    gain,
    table,
    dense_all,
    norm_sq,
    gain_all,
    wide,
    sent,
    back,
    total,
    got,
    gains,
    along,
    across,
    out_sems,
    in_sems,
    far_out,
    far_in,
    gain_out,
    gain_in,
    along_out,
    along_in,
    across_out,
    across_in,
    chip_out,
    chip_in,
    near_out,
    near_in,
):
    me, part = enter(plane, line)
    chips = plane // 2
    core = lax.rem(me, 2)
    chip = me // 2
    sibling = me + 1 - 2 * core
    far = []
    split_cuts, (whole_at, whole_rows), (last_at, last_rows) = cuts
    for k in range(1, line):
        peer = lax.rem(part + k, line)
        to = 0
        for j, (at, count) in enumerate(split_cuts):
            begin = pl.multiple_of(at + peer * count, 16)
            far.append(
                send(summed.at[pl.ds(begin, count)], got.at[part, to : to + count], far_out.at[j, k], far_in.at[j, k], (me, peer))
            )
            to += count
        target = got.at[part, to : to + whole_rows]
        source = summed.at[whole_at : whole_at + whole_rows]
        far.append(send(source, target, far_out.at[2, k], far_in.at[2, k], (me, peer)))
        far.append(send(gain, gains.at[part], gain_out.at[k], gain_in.at[k], (me, peer)))
    gains[part] = gain[...]
    wide[...] = rows[...].astype(F32)
    copies = []
    others = partners(me, plane)
    for k, peer in enumerate(others):
        gather_rows(listed(tokens.at[peer], 0), wide, sent.at[peer])
        copies.append(send(sent.at[peer], back.at[me], out_sems.at[k], in_sems.at[k], (peer, part)))
    gather_rows(listed(tokens.at[me], 0), wide, sent.at[me])
    to = 0
    for at, count in split_cuts:
        got[part, to : to + count] = summed[pl.ds(pl.multiple_of(at + part * count, 16), count), :]
        to += count
    got[part, to : to + whole_rows] = summed[whole_at : whole_at + whole_rows, :]
    for copy in far:
        copy.wait()
    share = got[0].astype(F32)
    for m in range(1, line):
        share = share + got[m].astype(F32)
    dense_all[me, 0 : to + whole_rows, :] = share.astype(BF16)
    dense_all[me, to + whole_rows :, :] = summed[last_at : last_at + last_rows, :]
    dense = dense_all.at[me]
    spread, near = [], []
    group = max(1, 1280 // capacity)
    order = [me] + others
    for first in range(0, plane, group):
        blocks = order[first : first + group]
        grads = [sent.at[blocks[0]] if first == 0 else back.at[blocks[0]]] + [back.at[block] for block in blocks[1:]]
        for k in range(max(first, 1), min(first + group, plane)):
            copies[k - 1].wait_recv()
        if first + group >= plane:
            for k in range(1, chips):
                other = lax.rem(chip + k, chips)
                spread.append(send(dense, dense, chip_out.at[k], chip_in.at[k], (2 * other + core, part)))
            near.append(send(dense, dense, near_out.at[0], near_in.at[0], (sibling, part)))
        add_rows(ids, capacity, blocks, grads, total, first == 0)
    square = jnp.zeros((8, LANES), F32)
    for begin, count, weight in ((0, to, 1.0), (to, whole_rows, 1.0 / line), (to + whole_rows, last_rows, 1.0)):
        block = dense_all[me, begin : begin + count, :].astype(F32)
        square = square + weight * jnp.sum((block * block).reshape(count // 8, 8, LANES), 0)
    height = total.shape[0]

    def settle(i, carry):
        at = pl.multiple_of(i * 32, 32)
        for half in range(2):
            block = total[pl.ds(at, 32), half * LANES : (half + 1) * LANES]
            table[pl.ds(at + half * height, 32), :] = block
            block = block * block
            for r in range(4):
                carry = carry + block[r * 8 : (r + 1) * 8, :]
        return carry

    table_sq = lax.fori_loop(0, height // 32, settle, jnp.zeros((8, LANES), F32))
    across[me] = square + table_sq * (1.0 / line)
    tiny = [
        send(across.at[me], across.at[me], across_out.at[k], across_in.at[k], (lax.rem(me + k, plane), part))
        for k in range(1, plane)
    ]
    for copy in tiny:
        copy.wait()
    sums = across[0]
    for d in range(1, plane):
        sums = sums + across[d]
    along[part] = sums
    peers = [lax.rem(part + k, line) for k in range(1, line)]
    tiny = [
        send(along.at[part], along.at[part], along_out.at[k], along_in.at[k], (me, peer)) for k, peer in enumerate(peers)
    ]
    for k in range(1, chips):
        peer = 2 * lax.rem(chip - k + chips, chips) + core
        spread[k - 1].wait_recv()
        near.append(send(dense_all.at[peer], dense_all.at[peer], near_out.at[k], near_in.at[k], (sibling, part)))
    gain_sum = gains[0]
    for m in range(1, line):
        gain_sum = gain_sum + gains[m]
    gain_all[...] = gain_sum
    for copy in tiny:
        copy.wait()
    sums = along[0]
    for m in range(1, line):
        sums = sums + along[m]
    norm_sq[...] = jnp.broadcast_to(jnp.sum(sums + gain_sum * gain_sum), norm_sq.shape)
    for copy in copies + spread:
        copy.wait_send()
    for copy in near:
        copy.wait()


def chain(index, values):
    out = jnp.full(index.shape, values[0], values[0].dtype)
    for k in range(1, len(values)):
        out = jnp.where(index >= k, values[k], out)
    return out


def forward_kernel(slots, cnt, x, w_in, gain, w_all, pooled, pm_out, normed_out, qkv, prob, a_out, pm_acc):
    tower = pl.program_id(0)
    pairs = pooled.shape[1]
    first = lax.axis_index("mp") * pairs
    parts = w_all.shape[0]
    per = LANES // slots
    groups = pairs // per
    heads = 2 * parts
    xs = x[0]
    hidden = nn(xs, w_in[0].astype(BF16))
    inverse = lax.rsqrt(jnp.mean(hidden * hidden, -1, keepdims=True) + EPS)
    normed = (hidden * inverse * gain[pl.ds(tower, 1), :]).astype(BF16)
    normed_out[0] = normed
    for c in range(3):
        for m in range(parts):
            qkv[0, c * parts + m] = nn(normed, w_all[m, 0, c]).astype(BF16)
    lane = iota((LANES, LANES), 1)
    line = iota((LANES, LANES), 0)
    shift = slots.bit_length() - 1
    pair_r, pair_s = lax.shift_right_logical(lane, shift), lax.shift_right_logical(line, shift)
    same = pair_r == pair_s
    halves = [lane < DH, lane >= DH]
    own_head = iota((per * heads, LANES), 0) & (heads - 1)

    def group(g, carry):
        counts = [cnt[tower, first + g * per + k] for k in range(per)]
        live_r = same & ((lane & (slots - 1)) < chain(pair_r, counts))
        live_s = (line & (slots - 1)) < chain(pair_s, counts)
        rows = pl.ds(pl.multiple_of(g * LANES, LANES), LANES)
        sums = []
        for m in range(parts):
            query, key = qkv[0, m, rows, :], qkv[0, parts + m, rows, :]
            for half in range(2):
                scores = nt(jnp.where(halves[half], query, jnp.zeros_like(query)), key) * 0.125
                scores = jnp.where(live_r, scores, -1000000000.0)
                expo = jnp.exp(scores - jnp.max(scores, 1, keepdims=True))
                p = (expo * (1.0 / jnp.sum(expo, 1, keepdims=True))).astype(BF16)
                prob[0, g, 2 * m + half] = p
                sums.append(jnp.sum(jnp.where(live_s, p.astype(F32), 0.0), 0, keepdims=True))
        sums = jnp.concatenate(sums, 0)
        pair_l = lax.shift_right_logical(iota((heads, LANES), 1), shift)
        stack = jnp.concatenate([jnp.where(pair_l == k, sums, 0.0) for k in range(per)], 0).astype(BF16)
        a_out[0, g] = stack
        for m in range(parts):
            mix = nn(stack, qkv[0, 2 * parts + m, rows, :])
            head = iota((per * heads, LANES), 1) // DH + 2 * m
            mix = jnp.where(own_head == head, mix, 0.0)
            pm_acc[g, :, m * LANES : (m + 1) * LANES] = jnp.concatenate(
                [jnp.sum(mix[k * heads : (k + 1) * heads], 0, keepdims=True) for k in range(per)], 0
            )
        return carry

    lax.fori_loop(0, groups, group, 0)
    pm = jnp.concatenate([pm_acc[g] for g in range(groups)], 0).astype(BF16)
    pm_out[0] = pm
    every = [cnt[tower, first + k] for k in range(pairs)]
    tokens = iota((pairs, pairs * slots), 1)
    mine = lax.shift_right_logical(tokens, shift) == iota(tokens.shape, 0)
    live = mine & ((tokens & (slots - 1)) < chain(iota(tokens.shape, 0), every))
    high, low = split(nn(live.astype(BF16), xs))
    w = w_in[0].astype(BF16)
    total = nn(high, w) + nn(low, w)
    sides = []
    for j in range(2):
        side = total[:, j * LANES : (j + 1) * LANES]
        for m in range(parts):
            side = side + nn(pm[:, m * LANES : (m + 1) * LANES], w_all[m, 0, 3, j * LANES : (j + 1) * LANES, :])
        sides.append(side)
    total = jnp.concatenate(sides, 1)
    count = chain(iota(total.shape, 0), every).astype(F32)
    pooled[0] = (total / count).astype(BF16)


def put(target, size, first, value):
    done = 0
    while done < value.shape[0]:
        share, inside = divmod(first + done, size)
        count = min(size - inside, value.shape[0] - done)
        target[share // 2, share % 2, inside : inside + count, :] = value[done : done + count]
        done += count


def backward_tower(
    tower, slots, cnt, x, w_in, gain, w_all, normed_in, qkv, prob, a_in, pm_in, dpooled, demb, d_in, d_gain, d_qkv, d_out, dqkv
):
    pairs, width = dpooled.shape[1:]
    parts = w_all.shape[0]
    per = LANES // slots
    groups = pairs // per
    heads = 2 * parts
    shift = slots.bit_length() - 1
    tokens = pairs * slots
    first = lax.axis_index("mp") * pairs
    every = [cnt[tower, first + k] for k in range(pairs)]
    count = chain(iota((pairs, width), 0), every).astype(F32)
    dsum = dpooled[tower].astype(F32) / count
    branch = dsum.astype(BF16)
    dmix = []
    for m in range(parts):
        grad = tn(pm_in[tower, :, m * LANES : (m + 1) * LANES], branch).astype(BF16)
        for j in range(width // LANES):
            begin = (tower * (width // LANES) + j) * LANES
            put(d_out.at[m], d_out.shape[3], begin, grad[:, j * LANES : (j + 1) * LANES])
        mix = 0.0
        for j in range(2):
            cut = slice(j * LANES, (j + 1) * LANES)
            mix = mix + nt(branch[:, cut], w_all[m, tower, 3, cut, :])
        dmix.append(mix)
    lane = iota((LANES, LANES), 1)
    line = iota((LANES, LANES), 0)
    pair_s = lax.shift_right_logical(line, shift)
    halves = [lane < DH, lane >= DH]
    own_head = iota((per * heads, LANES), 0) & (heads - 1)
    own_pair = lax.shift_right_logical(iota((per * heads, LANES), 0), heads.bit_length() - 1)
    token_pair = lax.shift_right_logical(iota((per * heads, LANES), 1), shift)
    for g in range(groups):
        rows = slice(g * LANES, (g + 1) * LANES)
        live_s = (line & (slots - 1)) < chain(pair_s, every[g * per : (g + 1) * per])
        scale = jnp.where(live_s, 0.125, 0.0)
        dots = jnp.zeros((per * heads, LANES), F32)
        stacks = []
        for m in range(parts):
            cut = dmix[m][g * per : (g + 1) * per]
            spread = jnp.concatenate([jnp.broadcast_to(cut[k : k + 1], (heads, LANES)) for k in range(per)], 0)
            head = iota((per * heads, LANES), 1) // DH + 2 * m
            stack = jnp.where(own_head == head, spread, 0.0).astype(BF16)
            stacks.append(stack)
            dots = dots + nt(stack, qkv[tower, 2 * parts + m, rows, :])
        dots = jnp.where(own_pair == token_pair, dots, 0.0)
        pull = dots[0:heads]
        for k in range(1, per):
            pull = pull + dots[k * heads : (k + 1) * heads]
        for m in range(parts):
            query, key = qkv[tower, m, rows, :], qkv[tower, parts + m, rows, :]
            none = jnp.zeros_like(query)
            dq = jnp.zeros((LANES, LANES), F32)
            dk = jnp.zeros((LANES, LANES), F32)
            for half in range(2):
                h = 2 * m + half
                p = prob[tower, g, h].astype(F32)
                t = p * pull[h : h + 1, :]
                ds = ((t - p * jnp.sum(t, 1, keepdims=True)) * scale).astype(BF16)
                dq = dq + nn(ds, jnp.where(halves[half], key, none))
                dk = dk + tn(ds, jnp.where(halves[half], query, none))
            dqkv[m, rows, :] = dq.astype(BF16)
            dqkv[parts + m, rows, :] = dk.astype(BF16)
            dqkv[2 * parts + m, rows, :] = tn(a_in[tower, g], stacks[m]).astype(BF16)
    normed = normed_in[tower]
    dnormed = jnp.zeros((tokens, width), F32)
    for m in range(parts):
        for c in range(3):
            grad = dqkv[c * parts + m]
            dnormed = dnormed + nt(grad, w_all[m, tower, c])
            put(d_qkv.at[m], d_qkv.shape[3], (tower * 3 + c) * width, tn(normed, grad).astype(BF16))
    dnormed = dnormed.astype(BF16).astype(F32)
    xs = x[tower]
    w = w_in[tower].astype(BF16)
    hidden = nn(xs, w)
    inverse = lax.rsqrt(jnp.mean(hidden * hidden, -1, keepdims=True) + EPS)
    unit = hidden * inverse
    grad = jnp.sum(dnormed * unit, 0, keepdims=True)
    for j in range(width // LANES):
        r = tower * (width // LANES) + j
        d_gain[r : r + 1, :] = grad[:, j * LANES : (j + 1) * LANES]
    scaled = dnormed * gain[tower : tower + 1, :]
    dh = inverse * (scaled - unit * jnp.mean(scaled * unit, -1, keepdims=True))
    spread = jnp.broadcast_to(dsum[:, None, :], (pairs, slots, width))
    slot = iota((pairs, slots, width), 1)
    counts = chain(iota((pairs, slots, width), 0), every)
    spread = jnp.where(slot < counts, spread, 0.0).reshape(tokens, width)
    dhidden = (spread + dh).astype(BF16)
    grad = tn(xs, dhidden).astype(BF16)
    for j in range(width // LANES):
        begin = (tower * (width // LANES) + j) * xs.shape[1]
        put(d_in, d_in.shape[2], begin, grad[:, j * LANES : (j + 1) * LANES])
    demb[...] = nt(dhidden, w).astype(BF16)


def backward_kernel(
    plane,
    line,
    slots,
    cnt,
    x,
    w_in,
    gain,
    w_all,
    normed,
    qkv,
    prob,
    a_in,
    pm,
    dpooled,
    d_three,
    d_one,
    d_two,
    out,
    summed,
    gain_sum,
    d_qkv,
    d_out,
    d_in,
    d_gain,
    dqkv,
    near_split,
    near_whole,
    half,
    got,
    got_late,
    gains,
    far_out,
    far_in,
    near_out,
    near_in,
    sum_out,
    sum_in,
    gain_out,
    gain_in,
):
    me, part = enter(plane, line)
    chips = plane // 2
    core = lax.rem(me, 2)
    chip = me // 2
    sibling = me + 1 - 2 * core
    towers, tokens = x.shape[:2]
    late, early = (d_in,), (d_three, d_one, d_two)
    nears = [send(grad.at[:, 1 - core], near_whole[1 + j], near_out.at[j], near_in.at[j], (sibling, part)) for j, grad in enumerate(early)]
    copies = []

    def tower(t):
        demb = out.at[part, t * tokens : (t + 1) * tokens]
        backward_tower(
            t, slots, cnt, x, w_in, gain, w_all, normed, qkv, prob, a_in, pm, dpooled, demb, d_in, d_gain, d_qkv, d_out, dqkv
        )
        for k in range(1, line):
            peer = lax.rem(part + k, line)
            copies.append(send(demb, demb, far_out.at[t, k], far_in.at[t, k], (me, peer)))

    def whole(c, at, grad, near):
        rows = grad.shape[2]
        half[c, at : at + rows, :] = (grad[c, core].astype(F32) + near[c].astype(F32)).astype(BF16)
        return at + rows

    def exchange(begin, end, target, sems):
        sums = []
        for k in range(1, chips):
            to = lax.rem(chip + k, chips)
            source = half.at[to, begin:end]
            sums.append(send(source, target.at[k - 1], sum_out.at[sems, k], sum_in.at[sems, k], (2 * to + core, part)))
        return sums

    def collect(begin, end, target, sums):
        for copy in sums:
            copy.wait()
        total = half[chip, begin:end, :].astype(F32)
        for k in range(chips - 1):
            total = total + target[k].astype(F32)
        summed[begin:end, :] = total.astype(BF16)

    first = line * (d_qkv.shape[3] + d_out.shape[3]) + d_in.shape[2]
    d_gain[...] = jnp.zeros_like(d_gain)
    tower(0)
    for copy in nears:
        copy.wait()
    for c in range(chips):
        at = first
        for j, grad in enumerate(early):
            at = whole(c, at, grad, near_whole[1 + j])
    last = at
    sums = exchange(first, last, got, 0)
    for t in range(1, towers):
        tower(t)
    nears = []
    for j, grad in enumerate((d_qkv, d_out)):
        nears.append(send(grad.at[:, :, 1 - core], near_split[j], near_out.at[3 + j], near_in.at[3 + j], (sibling, part)))
    nears.append(send(d_in.at[:, 1 - core], near_whole[0], near_out.at[5], near_in.at[5], (sibling, part)))
    for k in range(1, plane):
        peer = lax.rem(me + k, plane)
        copies.append(send(d_gain, gains.at[me], gain_out.at[k], gain_in.at[k], (peer, part)))
    gains[me] = d_gain[...]
    for copy in nears:
        copy.wait()
    for c in range(chips):
        at = 0
        for grad, near in zip((d_qkv, d_out), near_split):
            rows = grad.shape[3]
            for m in range(line):
                total = grad[m, c, core].astype(F32) + near[m, c].astype(F32)
                half[c, at : at + rows, :] = total.astype(BF16)
                at += rows
        whole(c, at, d_in, near_whole[0])
    late_sums = exchange(0, first, got_late, 1)
    collect(first, last, got, sums)
    collect(0, first, got_late, late_sums)
    for copy in copies:
        copy.wait()
    total = gains[0]
    for d in range(1, plane):
        total = total + gains[d]
    gain_sum[...] = total


def gelu_parts(v):
    c = 0.7978845608028654
    inner = jnp.tanh(c * (v + 0.044715 * (v * v * v)))
    value = 0.5 * v * (1.0 + inner)
    slope = 0.5 * (1.0 + inner) + 0.5 * v * (1.0 - inner * inner) * (c * (1.0 + 3.0 * 0.044715 * (v * v)))
    return value, slope


def upper_kernel(
    plane,
    line,
    pooled,
    far_one,
    far_two,
    far_three,
    log_prior,
    item_qid,
    lists,
    positive,
    dpooled,
    d_one,
    d_two,
    d_three,
    loss,
    pooled_all,
    second_send,
    second_got,
    vec,
    dsec_send,
    dsec_all,
    dpool_send,
    dpool_got,
    out_sems,
    in_sems,
    vec_out,
    vec_in,
    w_one,
    w_two,
    w_three,
    load_sems,
    second_mine,
    dpool_mine,
    prior_col,
):
    loads = [
        pltpu.make_async_copy(source, target, load_sems.at[j])
        for j, (source, target) in enumerate(((far_one, w_one), (far_two, w_two), (far_three, w_three)))
    ]
    for copy in loads:
        copy.start()
    me, part = enter(plane, line)
    towers, own, width = pooled.shape
    per = lists.shape[1] - 8
    rows = own * line
    pairs = rows * plane
    peers = [lax.rem(part + k, line) for k in range(1, line)]

    pooled_all[:, part] = pooled[...]
    first = [
        send(pooled_all.at[:, part], pooled_all.at[:, part], out_sems.at[0, k], in_sems.at[0, k], (me, peers[k]))
        for k in range(line - 1)
    ]
    for copy in loads:
        copy.wait()
    one = [w_one[t].astype(BF16) for t in range(towers)]
    two = [w_two[t].astype(BF16) for t in range(towers)]
    three = [w_three[t].astype(BF16) for t in range(towers)]
    qid = item_qid[...]
    hot = (lax.shift_right_logical(qid, 7) == iota((log_prior.shape[0], pairs), 0)).astype(BF16)
    high, rest = log_prior[...].astype(BF16), log_prior[...]
    rest = rest - high.astype(F32)
    middle, low = split(rest)
    table = tn(high, hot) + tn(middle, hot) + tn(low, hot)
    prior_row = jnp.sum(jnp.where((qid & 127) == iota((LANES, pairs), 0), table, 0.0), 0, keepdims=True)
    prior_col[...] = jnp.transpose(jnp.broadcast_to(prior_row, (8, pairs)), (1, 0))
    pos_row = jnp.concatenate([lists[d, per : per + 1, 0:rows] for d in range(plane)], 1)
    pos_own = chain(iota((own, pairs), 0), [positive[part * own + k] for k in range(own)])
    for copy in first:
        copy.wait()
    act_one, slope_one, pools = [], [], []
    for t in range(towers):
        pools.append(pooled_all[t].reshape(rows, width))
        value, slope = gelu_parts(nn(pools[t], one[t]))
        act_one.append(value.astype(BF16))
        slope_one.append(slope)
        partial = nn(act_one[t], two[t]).reshape(line, own, -1)
        second_mine[t] = partial
        second_send[t] = partial.astype(BF16)
    second = [
        send(
            second_send.at[:, peers[k]], second_got.at[:, part], out_sems.at[1, k], in_sems.at[1, k], (me, peers[k])
        )
        for k in range(line - 1)
    ]
    for copy in second:
        copy.wait()
    act_two, slope_two, third, length, vectors = [], [], [], [], []
    for t in range(towers):
        total = second_mine[t, part]
        for peer in peers:
            total = total + second_got[t, peer].astype(F32)
        value, slope = gelu_parts(total)
        act_two.append(value.astype(BF16))
        slope_two.append(slope)
        third.append(nn(act_two[t], three[t]))
        length.append(lax.rsqrt(jnp.sum(third[t] * third[t], -1, keepdims=True) + EPS))
        vectors.append((third[t] * length[t]).astype(BF16))
        vec[t, me, part] = vectors[t]
    along = [
        send(vec.at[:, me, part], vec.at[:, me, part], out_sems.at[2, k], in_sems.at[2, k], (me, peers[k]))
        for k in range(line - 1)
    ]
    for copy in along:
        copy.wait()
    chips = plane // 2
    core = lax.rem(me, 2)
    chip = me // 2
    sibling = me + 1 - 2 * core
    near = [send(vec.at[:, me], vec.at[:, me], vec_out.at[0], vec_in.at[0], (sibling, part))]
    across = []
    for k in range(1, chips):
        other = 2 * lax.rem(chip + k, chips) + core
        across.append(send(vec.at[:, me], vec.at[:, me], vec_out.at[k], vec_in.at[k], (other, part)))
    for k in range(1, chips):
        peer = 2 * lax.rem(chip - k + chips, chips) + core
        across[k - 1].wait_recv()
        sems = vec_out.at[chips + k], vec_in.at[chips + k]
        near.append(send(vec.at[:, peer], vec.at[:, peer], *sems, (sibling, part)))
    for copy in across:
        copy.wait_send()
    for copy in near:
        copy.wait()

    queries = vec[0].reshape(pairs, width)
    items = vec[1].reshape(pairs, width)
    logits = INV_TEMP * nt(items, queries) - prior_col[:, 0:1]
    peak = jnp.max(logits, 0, keepdims=True)
    log_total = peak + jnp.log(jnp.sum(jnp.exp(logits - peak), 0, keepdims=True))
    picked = jnp.where(iota((pairs, pairs), 0) == pos_row, logits, 0.0)
    gap = log_total - jnp.sum(picked, 0, keepdims=True)
    loss[0, 0] = jnp.sum(gap)
    ahead = me * rows + part * own
    mine = INV_TEMP * nt(vectors[0], items) - prior_row
    top = jnp.max(mine, 1, keepdims=True)
    expo = jnp.exp(mine - top)
    chance = expo / jnp.sum(expo, 1, keepdims=True)
    target = (iota(mine.shape, 1) == pos_own).astype(F32)
    dlog = ((chance - target) / pairs).astype(BF16)
    dvec = [(INV_TEMP * nn(dlog, items)).astype(BF16)]
    own_prior = prior_col[pl.ds(pl.multiple_of(ahead, own), own), 0:1]
    theirs = INV_TEMP * nt(vectors[1], queries) - own_prior
    target = (iota(theirs.shape, 0) + ahead == pos_row).astype(F32)
    dlog = ((jnp.exp(theirs - log_total) - target) / pairs).astype(BF16)
    dvec.append((INV_TEMP * nn(dlog, queries)).astype(BF16))

    dthirds = []
    for t in range(towers):
        dv = dvec[t].astype(F32)
        inner = jnp.sum(dv * third[t], -1, keepdims=True)
        dthird = (length[t] * dv - third[t] * (length[t] * length[t] * length[t] * inner)).astype(BF16)
        dact = nt(dthird, three[t]).astype(BF16).astype(F32)
        dsec_all[t, part] = (dact * slope_two[t]).astype(BF16)
        dthirds.append(dthird)
    spread = [
        send(dsec_all.at[:, part], dsec_all.at[:, part], out_sems.at[3, k], in_sems.at[3, k], (me, peers[k]))
        for k in range(line - 1)
    ]
    for t in range(towers):
        grad = tn(act_two[t], dthirds[t]).astype(BF16)
        for j in range(width // LANES):
            d_three[t, j] = grad[:, j * LANES : (j + 1) * LANES]
    for copy in spread:
        copy.wait()
    dfirsts = []
    for t in range(towers):
        dsecond = dsec_all[t].reshape(rows, -1)
        dact = nt(dsecond, two[t]).astype(BF16).astype(F32)
        dfirst = (dact * slope_one[t]).astype(BF16)
        partial = nt(dfirst, one[t]).reshape(line, own, width)
        dpool_mine[t] = partial
        dpool_send[t] = partial.astype(BF16)
        dfirsts.append(dfirst)
    back = [
        send(dpool_send.at[:, peers[k]], dpool_got.at[:, part], out_sems.at[4, k], in_sems.at[4, k], (me, peers[k]))
        for k in range(line - 1)
    ]
    for t in range(towers):
        dsecond = dsec_all[t].reshape(rows, -1)
        for grads, grad in ((d_two, tn(act_one[t], dsecond)), (d_one, tn(pools[t], dfirsts[t]))):
            grad = grad.astype(BF16)
            for j in range(grad.shape[1] // LANES):
                grads[t, j] = grad[:, j * LANES : (j + 1) * LANES]
    for copy in back:
        copy.wait()
    for t in range(towers):
        total = dpool_mine[t, part]
        for peer in peers:
            total = total + dpool_got[t, peer].astype(F32)
        dpooled[t] = total.astype(BF16)


def update(weight, grad, moment, average, factor, rate):
    clipped = grad * factor
    moment_new = MOMENTUM * moment + clipped
    weight_new = weight - rate * (clipped + MOMENTUM * moment_new)
    average_new = AVERAGE_DECAY * average + (1.0 - AVERAGE_DECAY) * weight_new
    return [weight_new, moment_new, average_new]


def update_kernel(blocks, norm_sq, table_grad, dense, gain, *refs):
    arrays = 3 * 8
    sources, targets, norm = refs[:arrays], refs[arrays : 2 * arrays], refs[2 * arrays]
    held, in_sems, out_sems = refs[2 * arrays + 1 : 3 * arrays + 1], refs[-2], refs[-1]
    loads = [pltpu.make_async_copy(sources[k], held[k], in_sems.at[k]) for k in range(arrays)]
    ahead = 8

    def load(k):
        if k < arrays // 3:
            for copy in loads[3 * k : 3 * k + 3]:
                copy.start()

    for k in range(ahead):
        load(k)
    root = jnp.sqrt(norm_sq[...])
    norm[0, 0] = jnp.max(root)
    factor = jnp.minimum(1.0, CLIP_NORM / root[0:1, :])
    stores = []

    def finish(k):
        for j in range(3 * k, 3 * k + 3):
            copy = pltpu.make_async_copy(held[j], targets[j], out_sems.at[j])
            copy.start()
            stores.append(copy)

    def apply(k, rows, lanes, grad, rate):
        cells = [ref.at[rows, lanes] for ref in held[3 * k : 3 * k + 3]]
        new = update(cells[0][...], grad, cells[1][...], cells[2][...], factor, rate)
        for cell, value in zip(cells, new):
            cell[...] = value

    def wait(k):
        for copy in loads[3 * k : 3 * k + 3]:
            copy.wait()
        load(k + ahead)

    wait(0)

    def rows(i, carry):
        at = pl.ds(pl.multiple_of(i * 32, 32), 32)
        apply(0, at, slice(0, LANES), table_grad[at, :], ROW_RATE)
        return carry

    lax.fori_loop(0, table_grad.shape[0] // 32, rows, 0, unroll=2)
    finish(0)
    at = 0
    for k, size, height, wide in blocks:
        wait(k)
        total = dense.shape[0] * size
        step = 32 if size % 32 == 0 else 16
        for first in range(0, total, min(size, height)):
            count = min(size, height)
            share, inside = first // size, first % size
            block, begin = first // height, first % height
            t, j = block // wide, block % wide
            top = t * height + begin

            def piece(i, carry):
                take = pl.ds(pl.multiple_of(at + inside + i * step, 16), step)
                rows = pl.ds(pl.multiple_of(top + i * step, 16), step)
                grad = dense[share, take, :].astype(F32)
                apply(k, rows, slice(j * LANES, (j + 1) * LANES), grad, MATRIX_RATE)
                return carry

            lax.fori_loop(0, count // step, piece, 0, unroll=2)
        at += size
        finish(k)
    last = 7
    wait(last)
    for t in range(held[3 * last].shape[0]):
        for j in range(held[3 * last].shape[1] // LANES):
            r = t * (held[3 * last].shape[1] // LANES) + j
            apply(last, slice(t, t + 1), slice(j * LANES, (j + 1) * LANES), gain[r : r + 1, :], GAIN_RATE)
    finish(last)
    for copy in stores:
        copy.wait()


def shards(
    slot_owner,
    slot_row,
    slot_count,
    item_qid,
    positive,
    log_prior,
    embedding,
    embedding_mom,
    embedding_avg,
    w_in,
    w_in_mom,
    w_in_avg,
    norm_gain,
    norm_gain_mom,
    norm_gain_avg,
    w_qkv,
    w_qkv_mom,
    w_qkv_avg,
    w_out,
    w_out_mom,
    w_out_avg,
    w_one,
    w_one_mom,
    w_one_avg,
    w_two,
    w_two_mom,
    w_two_avg,
    w_three,
    w_three_mom,
    w_three_avg,
):
    plane = lax.axis_size("dp")
    line = lax.axis_size("mp")
    batch, towers, slots = slot_row.shape
    own = batch // line
    requests = batch * towers * slots
    own_requests = requests // line
    tokens = own * slots
    capacity = max(LANES, 2 * requests // plane)
    pairs = batch * plane
    part = lax.axis_index("mp")
    me = lax.axis_index("dp")
    width = w_in.shape[2]
    depth = w_in.shape[1]
    units = w_one.shape[2]
    seconds = w_two.shape[2]

    per = capacity // LANES
    small = capacity // 4
    dims = (towers, own, slots)

    def row_scratch(count):
        return [
            pltpu.VMEM((plane, count, depth), BF16),
            pltpu.VMEM((plane, count, depth), BF16),
            pltpu.VMEM((plane * count, depth), F32),
        ]

    turned = jnp.transpose(w_qkv, (0, 2, 1, 3))
    embedded, got_own, got_lists, weights, inverse, own_place = pl.pallas_call(
        functools.partial(fetch_kernel, plane, line, dims, capacity),
        out_shape=[
            shape((own_requests, depth), BF16),
            shape((plane, per, LANES), I32),
            shape((plane, per + 8, LANES), I32),
            shape((line, towers, 4, width, LANES), BF16),
            shape((plane * per, LANES), I32),
            shape((slots, LANES), I32),
        ],
        in_specs=[VMEM] * 4 + [HBM] * 3,
        out_specs=[VMEM] * 6,
        scratch_shapes=[
            pltpu.VMEM((plane, per, LANES), I32),
            pltpu.VMEM((slots, LANES), I32),
            pltpu.VMEM((plane, per + 8, LANES), I32),
            pltpu.VMEM(embedding.shape, F32),
            pltpu.VMEM(turned.shape, F32),
            pltpu.VMEM(w_out.shape, F32),
            pltpu.SMEM((slots, LANES), I32),
            pltpu.SMEM((plane, -(-small // LANES), LANES), I32),
            *row_scratch(small),
            DMA((2, plane)),
            DMA((2, plane)),
            DMA((plane,)),
            DMA((plane,)),
            DMA((line,)),
            DMA((line,)),
            DMA((line,)),
            DMA((line,)),
            DMA((2, line)),
            DMA((2, line)),
            DMA((4,)),
            DMA((3,)),
        ],
        compiler_params=params(60, collective_id=2, has_side_effects=True),
        name="fetch",
    )(
        jnp.transpose(slot_owner[..., 0], (1, 2, 0)),
        jnp.transpose(slot_row, (1, 2, 0)),
        jnp.transpose(slot_count),
        positive.reshape(1, batch),
        embedding,
        turned,
        w_out,
    )
    most = jnp.max(got_lists[:, per + 1 : per + 3, 0], 0)

    def refetch(ids, place, table, _):
        return pl.pallas_call(
            functools.partial(refetch_kernel, plane, dims),
            out_shape=shape((own_requests, depth), BF16),
            in_specs=[SMEM, SMEM, VMEM],
            out_specs=VMEM,
            scratch_shapes=[*row_scratch(capacity), DMA((plane,)), DMA((plane,))],
            compiler_params=params(16, collective_id=7, has_side_effects=True),
            name="refetch",
        )(ids, place, table)

    embedded = lax.cond(most[0] > small, refetch, lambda *given: given[3], got_own, own_place, embedding, embedded)
    embedded = embedded.reshape(towers, tokens, depth)

    counts = jnp.transpose(slot_count)
    heads = 2 * line
    groups = tokens // LANES
    per_group = LANES // slots
    lead = lambda *dims: pl.BlockSpec((1,) + dims, lambda t: (t,) + (0,) * len(dims))
    all_spec = pl.BlockSpec((line, 1, 4, width, LANES), lambda t: (0, t, 0, 0, 0))
    pooled, pm, normed, qkv, prob, spread = pl.pallas_call(
        functools.partial(forward_kernel, slots),
        grid=(towers,),
        out_shape=[
            shape((towers, own, width), BF16),
            shape((towers, own, line * LANES), BF16),
            shape((towers, tokens, width), BF16),
            shape((towers, 3 * line, tokens, LANES), BF16),
            shape((towers, groups, heads, LANES, LANES), BF16),
            shape((towers, groups, per_group * heads, LANES), BF16),
        ],
        in_specs=[SMEM, lead(tokens, depth), lead(depth, width), VMEM, all_spec],
        out_specs=[
            lead(own, width),
            lead(own, line * LANES),
            lead(tokens, width),
            lead(3 * line, tokens, LANES),
            lead(groups, heads, LANES, LANES),
            lead(groups, per_group * heads, LANES),
        ],
        scratch_shapes=[pltpu.VMEM((groups, per_group, line * LANES), F32)],
        compiler_params=params(20),
        name="attention_forward",
    )(counts, embedded, w_in, norm_gain, weights)

    dpooled, d_one, d_two, d_three, loss = pl.pallas_call(
        functools.partial(upper_kernel, plane, line),
        out_shape=[
            shape((towers, own, width), BF16),
            shape((towers, units // LANES, width, LANES), BF16),
            shape((towers, seconds // LANES, units, LANES), BF16),
            shape((towers, width // LANES, seconds, LANES), BF16),
            shape((1, 1), F32),
        ],
        in_specs=[VMEM] + [HBM] * 3 + [VMEM] * 3 + [SMEM],
        out_specs=[VMEM] * 4 + [SMEM],
        scratch_shapes=[
            pltpu.VMEM((towers, line, own, width), BF16),
            pltpu.VMEM((towers, line, own, seconds), BF16),
            pltpu.VMEM((towers, line, own, seconds), BF16),
            pltpu.VMEM((towers, plane, line, own, width), BF16),
            pltpu.VMEM((towers, line, own, seconds), BF16),
            pltpu.VMEM((towers, line, own, seconds), BF16),
            pltpu.VMEM((towers, line, own, width), BF16),
            pltpu.VMEM((towers, line, own, width), BF16),
            DMA((5, line)),
            DMA((5, line)),
            DMA((plane,)),
            DMA((plane,)),
            pltpu.VMEM(w_one.shape, F32),
            pltpu.VMEM(w_two.shape, F32),
            pltpu.VMEM(w_three.shape, F32),
            DMA((3,)),
            pltpu.VMEM((towers, line, own, seconds), F32),
            pltpu.VMEM((towers, line, own, width), F32),
            pltpu.VMEM((pairs, 8), F32),
        ],
        compiler_params=params(22 + 2 * (pairs * pairs >> 18), collective_id=3, has_side_effects=True),
        name="upper",
    )(
        pooled,
        w_one,
        w_two,
        w_three,
        log_prior.reshape(-1, LANES),
        item_qid.reshape(1, pairs),
        got_lists,
        positive,
    )

    totals = (towers * 3 * width, towers * width, towers * depth * width // LANES)
    totals += tuple(grad.size // LANES for grad in (d_three, d_one, d_two))
    sizes = [total // plane for total in totals]
    shares = lambda grad: grad.reshape(plane // 2, 2, -1, LANES)
    share = line * (sizes[0] + sizes[1]) + sum(sizes[2:])
    early = sum(sizes[3:])
    every, summed, gain_sum = pl.pallas_call(
        functools.partial(backward_kernel, plane, line, slots),
        out_shape=[
            shape((line, own_requests, depth), BF16),
            shape((share, LANES), BF16),
            shape((8, LANES), F32),
        ],
        in_specs=[SMEM] + [VMEM] * 13,
        out_specs=[VMEM] * 3,
        scratch_shapes=[
            pltpu.VMEM((line, plane // 2, 2, sizes[0], LANES), BF16),
            pltpu.VMEM((line, plane // 2, 2, sizes[1], LANES), BF16),
            pltpu.VMEM((plane // 2, 2, sizes[2], LANES), BF16),
            pltpu.VMEM((8, LANES), F32),
            pltpu.VMEM((3 * line, tokens, LANES), BF16),
            [pltpu.VMEM((line, plane // 2, size, LANES), BF16) for size in sizes[:2]],
            [pltpu.VMEM((plane // 2, size, LANES), BF16) for size in sizes[2:]],
            pltpu.VMEM((plane // 2, share, LANES), BF16),
            pltpu.VMEM((plane // 2 - 1, early, LANES), BF16),
            pltpu.VMEM((plane // 2 - 1, share - early, LANES), BF16),
            pltpu.VMEM((plane, 8, LANES), F32),
            DMA((towers, line)),
            DMA((towers, line)),
            DMA((6,)),
            DMA((6,)),
            DMA((2, plane // 2)),
            DMA((2, plane // 2)),
            DMA((plane,)),
            DMA((plane,)),
        ],
        compiler_params=params(40, collective_id=4, has_side_effects=True),
        name="attention_backward",
    )(
        counts,
        embedded,
        w_in,
        norm_gain,
        weights,
        normed,
        qkv,
        prob,
        spread,
        pm,
        dpooled,
        shares(d_three),
        shares(d_one),
        shares(d_two),
    )
    whole_at = line * (sizes[0] + sizes[1])
    whole_rows = sizes[2] + sizes[3]
    last_rows = sizes[4] + sizes[5]
    cuts = (
        ((0, sizes[0]), (line * sizes[0], sizes[1])),
        (whole_at, whole_rows),
        (whole_at + whole_rows, last_rows),
    )
    line_rows = sizes[0] + sizes[1] + whole_rows

    def tail(count, number):
        return lambda *given: pl.pallas_call(
            functools.partial(tail_kernel, plane, line, count, cuts),
            out_shape=[
                shape(embedding.shape, F32),
                shape((plane, line_rows + last_rows, LANES), BF16),
                shape((8, LANES), F32),
                shape((8, LANES), F32),
            ],
            in_specs=[SMEM] + [VMEM] * 4,
            out_specs=[VMEM] * 4,
            scratch_shapes=[
                pltpu.VMEM((requests, depth), F32),
                pltpu.VMEM((plane, count, depth), BF16),
                pltpu.VMEM((plane, count, depth), BF16),
                pltpu.VMEM((embedding.shape[0] // 2, 2 * depth), F32),
                pltpu.VMEM((line, line_rows, LANES), BF16),
                pltpu.VMEM((line, 8, LANES), F32),
                pltpu.VMEM((line, 8, LANES), F32),
                pltpu.VMEM((plane, 8, LANES), F32),
                DMA((plane,)),
                DMA((plane,)),
                DMA((3, line)),
                DMA((3, line)),
                DMA((line,)),
                DMA((line,)),
                DMA((line,)),
                DMA((line,)),
                DMA((plane,)),
                DMA((plane,)),
                DMA((plane // 2,)),
                DMA((plane // 2,)),
                DMA((plane // 2,)),
                DMA((plane // 2,)),
            ],
            compiler_params=params(36, collective_id=number, has_side_effects=True),
            name="tail",
        )(given[0][:, : -(-count // LANES)], *given[1:])

    medium = capacity * 5 // 8
    table_grad, dense_all, norm_sq, gain_all = lax.cond(
        most[1] > medium,
        tail(capacity, 8),
        tail(medium, 5),
        inverse.reshape(plane, per, LANES),
        got_lists,
        every.reshape(requests, depth),
        summed,
        gain_sum,
    )
    flat = lambda w: w.reshape(-1, w.shape[-1])
    turn = lambda w: flat(jnp.transpose(w, (0, 2, 1, 3)))
    given = [embedding, embedding_mom, embedding_avg]
    given += [turn(w) for w in (w_qkv, w_qkv_mom, w_qkv_avg)]
    rest = (w_out, w_out_mom, w_out_avg, w_in, w_in_mom, w_in_avg, w_three, w_three_mom, w_three_avg)
    rest += (w_one, w_one_mom, w_one_avg, w_two, w_two_mom, w_two_avg)
    given += [flat(w) for w in rest]
    given += [norm_gain, norm_gain_mom, norm_gain_avg]
    heights = (towers * 3 * width, LANES, depth, seconds, width, units)
    wides = (1, width // LANES, width // LANES, width // LANES, units // LANES, seconds // LANES)
    blocks = tuple((k + 1, size, height, wide) for k, (size, height, wide) in enumerate(zip(sizes, heights, wides)))
    *done, norm = pl.pallas_call(
        functools.partial(update_kernel, blocks),
        out_shape=[shape(w.shape, F32) for w in given] + [shape((1, 1), F32)],
        in_specs=[VMEM] * 4 + [HBM] * len(given),
        out_specs=[HBM] * len(given) + [SMEM],
        scratch_shapes=[pltpu.VMEM(w.shape, F32) for w in given] + [DMA((len(given),))] * 2,
        compiler_params=params(57),
        name="update",
    )(norm_sq, table_grad, dense_all, gain_all, *given)
    back = lambda k, w: [done[3 * k + j].reshape(w.shape) for j in range(3)]
    unturned = [
        jnp.transpose(w.reshape(towers, 3, width, LANES), (0, 2, 1, 3)) for w in done[3:6]
    ]
    new = done[:3] + back(3, w_in) + done[21:24] + unturned + back(2, w_out) + back(5, w_one) + back(6, w_two)
    return (loss.reshape(()), norm.reshape(()), *new, *back(4, w_three))


def solution(mesh):
    rows = P("dp", None)
    qkv = P(None, None, None, "mp")
    deep = P(None, "mp", None)
    wide = P(None, None, "mp")
    weights = (rows,) * 3 + (P(),) * 6 + (qkv,) * 3 + (deep,) * 3 + (wide,) * 3 + (deep,) * 3 + (P(),) * 3
    inputs = (P("dp", None, None, None), P("dp", None, None), P("dp", None), P(), P("dp"), P())
    return jax.shard_map(
        shards, mesh=mesh, in_specs=inputs + weights, out_specs=(P(), P()) + weights, check_vma=False
    )
```

```python
import functools

import jax
import jax.numpy as jnp
from jax import lax
from jax.experimental import pallas as pl
from jax.experimental.pallas import tpu as pltpu
from jax.sharding import PartitionSpec as P

DH = 64
EPS = 1e-06
INV_TEMP = 20.0
CLIP_NORM = 0.1
ROW_RATE = 150000.0
GAIN_RATE = 8000.0
MATRIX_RATE = 600.0
MOMENTUM = 0.9
AVERAGE_DECAY = 0.6

MESH = pl.DeviceIdType.MESH
LANES = 128
F32 = jnp.float32
BF16 = jnp.bfloat16
I32 = jnp.int32
VMEM = pl.BlockSpec(memory_space=pltpu.VMEM)
HBM = pl.BlockSpec(memory_space=pltpu.HBM)
SMEM = pl.BlockSpec(memory_space=pltpu.SMEM)
DMA = pltpu.SemaphoreType.DMA


def nn(a, b):
    return lax.dot_general(a, b, (((1,), (0,)), ((), ())), preferred_element_type=F32)


def nt(a, b):
    return lax.dot_general(a, b, (((1,), (1,)), ((), ())), preferred_element_type=F32)


def tn(a, b):
    return lax.dot_general(a, b, (((0,), (0,)), ((), ())), preferred_element_type=F32)


def iota(shape, dim):
    return lax.broadcasted_iota(I32, shape, dim)


def split(value):
    high = value.astype(BF16)
    return high, (value - high.astype(F32)).astype(BF16)


def shape(dims, dtype):
    return jax.ShapeDtypeStruct(tuple(dims), dtype)


def params(limit, **more):
    return pltpu.CompilerParams(vmem_limit_bytes=limit << 20, **more)


def log2(value):
    return value.bit_length() - 1


def lists_of(owner, values, owners, capacity):
    chunks = owner.shape[0]
    width = owners * capacity
    his = width // LANES
    sub = iota((owners, LANES), 0)
    hot = [(owner[c : c + 1, :] == sub).astype(F32) for c in range(chunks)]
    hots = jnp.concatenate(hot, 0).astype(BF16)
    before = (iota((LANES, LANES), 0) < iota((LANES, LANES), 1)).astype(BF16)
    earlier = nn(hots, before)
    totals = nn(hots, jnp.ones((LANES, LANES), BF16))
    base = (sub * capacity).astype(F32)
    places = []
    for c in range(chunks):
        cut = slice(c * owners, (c + 1) * owners)
        here = jnp.sum(hot[c] * (earlier[cut] + base), 0, keepdims=True).astype(I32)
        places.append(jnp.where(owner[c : c + 1, :] < owners, here, width))
        base = base + totals[cut]
    parts = 2 * len(values)
    acc = jnp.zeros((his, parts * LANES), F32)
    for c in range(chunks):
        place = places[c]
        left = (lax.shift_right_logical(place, 7) == iota((his, LANES), 0)).astype(BF16)
        low = (place & 127) == iota((LANES, LANES), 0)
        cuts = []
        for value in values:
            value = value[c : c + 1, :]
            cuts += [lax.shift_right_logical(value, 6), value & 63]
        right = jnp.concatenate([jnp.where(low, cut.astype(F32), 0.0) for cut in cuts], 0)
        acc = acc + nt(left, right.astype(BF16))
    cuts = [acc[:, k * LANES : (k + 1) * LANES].astype(I32) for k in range(parts)]
    lists = [cuts[2 * k] * 64 + cuts[2 * k + 1] for k in range(len(values))]
    return places, lists, hot


class Slots:
    def __init__(self, owners, line, owner, row, count):
        towers, slots, batch = owner.shape
        own = batch // line
        side = lambda ref: jnp.concatenate([ref[t] for t in range(towers)], 1)
        counts = jnp.concatenate([count[t : t + 1, :] for t in range(towers)], 1)
        slot, lane = iota((slots, LANES), 0), iota((slots, LANES), 1)
        tower = lax.shift_right_logical(lane, log2(batch))
        self.row = side(row)
        self.owner = jnp.where(slot < counts, side(owner), owners)
        self.block = lax.shift_right_logical(lane & (batch - 1), log2(own))
        self.token = ((self.block * towers + tower) * own + (lane & (own - 1))) * slots + slot


def make_own_lists(slots, owners, capacity, small, height, own_lists, own_place, own_small):
    per = capacity // LANES
    owner = jnp.where(slots.block == lax.axis_index("mp"), slots.owner, owners)
    places, (rows,), _ = lists_of(owner, (slots.row,), owners, capacity)
    rows = jnp.minimum(jnp.maximum(rows, 0), height - 1)
    for d in range(owners):
        own_lists[d] = rows[d * per : (d + 1) * per, :]
    place = jnp.concatenate(places, 0)
    place = jnp.maximum(jnp.where(place < owners * capacity, place, 0), 0)
    own_place[...] = place
    rank = jnp.minimum(place & (capacity - 1), small - 1)
    own_small[...] = lax.shift_right_logical(place, log2(capacity)) * small + rank


def make_lists(slots, owners, capacity, batch, line, positive, lists, inverse):
    per = capacity // LANES
    _, (rows, tokens), hot = lists_of(slots.owner, (slots.row + 1, slots.token), owners, capacity)
    rows = rows - 1
    inverse[...] = tokens
    asked = hot[0]
    for more in hot[1:]:
        asked = asked + more
    own = batch // line
    near = lax.shift_right_logical(iota((LANES, LANES), 0) & (batch - 1), log2(own)) == iota((LANES, LANES), 1)
    asked = asked.astype(BF16)
    most = jnp.max(jnp.max(nn(asked, near.astype(BF16)), 0, keepdims=True), 1, keepdims=True)
    every = jnp.max(nn(asked, jnp.ones((LANES, LANES), BF16)), 0, keepdims=True)
    most = jnp.broadcast_to(most, (1, LANES))
    for d in range(owners):
        lists[d, 0:per, :] = rows[d * per : (d + 1) * per, :]
        lists[d, per : per + 1, 0:batch] = positive[...]
        lists[d, per + 1 : per + 2, :] = most.astype(I32)
        lists[d, per + 2 : per + 3, :] = every.astype(I32)


def announce(plane, line):
    me, part = lax.axis_index("dp"), lax.axis_index("mp")
    barrier = pltpu.get_barrier_semaphore()
    for k in range(1, plane):
        pl.semaphore_signal(barrier, inc=1, device_id=(lax.rem(me + k, plane), part), device_id_type=MESH)
    for k in range(1, line):
        pl.semaphore_signal(barrier, inc=1, device_id=(me, lax.rem(part + k, line)), device_id_type=MESH)
    return me, part


def await_others(plane, line):
    pl.semaphore_wait(pltpu.get_barrier_semaphore(), max(plane - 1, 0) + max(line - 1, 0))


def enter(plane, line):
    me, part = announce(plane, line)
    await_others(plane, line)
    return me, part


def partners(me, count):
    order = sorted(range(1, count), key=lambda k: (-bin(k >> 1).count("1"), k & 1, k))
    bits = [lax.rem(me // (1 << b), 2) for b in range(log2(count))]
    return [sum((1 << b) * (1 - bit if k >> b & 1 else bit) for b, bit in enumerate(bits)) for k in order]


def send(source, target, out_sem, in_sem, device):
    copy = pltpu.make_async_remote_copy(
        src_ref=source, dst_ref=target, send_sem=out_sem, recv_sem=in_sem, device_id=device, device_id_type=MESH
    )
    copy.start()
    return copy


def gather_rows(ids, table, target):
    def body(i, carry):
        at = ids(i)
        rows = [table[pl.ds(at(u), 1), :] for u in range(16)]
        target[pl.ds(pl.multiple_of(i * 16, 16), 16), :] = jnp.concatenate(rows, 0).astype(BF16)
        return carry

    lax.fori_loop(0, target.shape[0] // 16, body, 0)


def listed(ids, first):
    def at(i):
        block = first + lax.shift_right_logical(i, 3)
        start = (i & 7) * 16
        return lambda u: ids[block, start + u]

    return at


def placed(place, part, towers, own, slots):
    per = slots // 16

    def at(i):
        pair = lax.shift_right_logical(i, log2(per))
        tower = lax.shift_right_logical(pair, log2(own))
        lane = tower * (LANES // towers) + part * own + (pair & (own - 1))
        start = (i & (per - 1)) * 16
        return lambda u: place[start + u, lane]

    return at


def send_rows(plane, me, part, ids, table, sent, got, wide, out_sems, in_sems):
    capacity = sent.shape[1]
    copies = []
    for k, peer in enumerate(partners(me, plane)):
        gather_rows(listed(ids.at[peer], 0), table, sent.at[peer])
        copies.append(send(sent.at[peer], got.at[me], out_sems.at[k], in_sems.at[k], (peer, part)))
    gather_rows(listed(ids.at[me], 0), table, sent.at[me])
    wide[pl.ds(pl.multiple_of(me * capacity, capacity), capacity), :] = sent[me].astype(F32)
    return copies


def take_rows(plane, me, part, dims, copies, place, got, wide, out):
    capacity = got.shape[1]
    for copy, peer in zip(copies, partners(me, plane)):
        copy.wait_recv()
        wide[pl.ds(pl.multiple_of(peer * capacity, capacity), capacity), :] = got[peer].astype(F32)
    gather_rows(placed(place, part, *dims), wide, out)


def refetch_kernel(plane, dims, ids, place, table, out, sent, got, wide, out_sems, in_sems):
    me, part = enter(plane, 0)
    copies = send_rows(plane, me, part, ids, table, sent, got, wide, out_sems, in_sems)
    take_rows(plane, me, part, dims, copies, place, got, wide, out)
    for copy in copies:
        copy.wait_send()


def fetch_kernel(
    plane,
    line,
    dims,
    capacity,
    owner_in,
    row_in,
    count,
    positive,
    far_table,
    far_qkv,
    far_wout,
    out,
    got_own,
    got_lists,
    weights,
    inverse,
    own_place,
    own_lists,
    own_small,
    lists,
    table,
    w_qkv,
    w_out,
    place,
    ids,
    sent,
    got,
    wide,
    list_out,
    list_in,
    out_sems,
    in_sems,
    far_out,
    far_in,
    side_out,
    side_in,
    near_out,
    near_in,
    own_sems,
    load_sems,
):
    loads = [
        pltpu.make_async_copy(source, target, load_sems.at[j])
        for j, (source, target) in enumerate(((far_qkv, w_qkv), (far_wout, w_out), (far_table, table)))
    ]
    for copy in loads:
        copy.start()
    me, part = announce(plane, line)
    core = lax.rem(me, 2)
    half = lax.rem(me // 2, 2)
    sibling = me + 1 - 2 * core
    partner = me + 2 - 4 * half
    batch = positive.shape[1]
    slots = Slots(plane, line, owner_in, row_in, count)
    make_own_lists(slots, plane, capacity, sent.shape[1], table.shape[0], own_lists, own_place, own_small)
    places = pltpu.make_async_copy(own_small, place, own_sems.at[0])
    places.start()
    for copy in loads[:2]:
        copy.wait()
    rows = weights.shape[3] // 2
    for c in range(3):
        weights[part, :, c] = w_qkv[:, c].astype(BF16)
    for j in range(2):
        weights[part, :, 3, j * LANES : (j + 1) * LANES, :] = w_out[:, :, j * LANES : (j + 1) * LANES].astype(BF16)
    quarter = lambda m, h: weights.at[m, core, :, pl.ds(pl.multiple_of(h * rows, rows), rows), :]
    await_others(plane, line)
    far, asked, told = [], [], []
    for k in range(1, line):
        peer = lax.rem(part + k, line)
        far.append(send(quarter(part, half), quarter(part, half), far_out.at[k], far_in.at[k], (me, peer)))
    for k in range(1, plane):
        peer = lax.rem(me + k, plane)
        asked.append(send(own_lists.at[peer], got_own.at[me], list_out.at[0, k], list_in.at[0, k], (peer, part)))
    make_lists(slots, plane, capacity, batch, line, positive, lists, inverse)
    for k in range(1, plane):
        peer = lax.rem(me + k, plane)
        told.append(send(lists.at[peer], got_lists.at[me], list_out.at[1, k], list_in.at[1, k], (peer, part)))
    mine = [
        pltpu.make_async_copy(own_lists.at[me], got_own.at[me], own_sems.at[1]),
        pltpu.make_async_copy(lists.at[me], got_lists.at[me], own_sems.at[2]),
    ]
    for copy in mine:
        copy.start()
    for copy in asked:
        copy.wait()
    mine[0].wait()
    numbers = pltpu.make_async_copy(got_own.at[:, 0 : ids.shape[1]], ids, own_sems.at[3])
    numbers.start()
    for copy in (numbers, places, loads[2]):
        copy.wait()
    copies = send_rows(plane, me, part, ids, table, sent, got, wide, out_sems, in_sems)
    sides, near = [], []
    for k in range(1, line):
        peer = lax.rem(part - k + line, line)
        far[k - 1].wait_recv()
        at = quarter(peer, half)
        sides.append(send(at, at, side_out.at[k], side_in.at[k], (partner, part)))
        near.append(send(at, at, near_out.at[0, k], near_in.at[0, k], (sibling, part)))
    take_rows(plane, me, part, dims, copies, place, got, wide, out)
    for k in range(1, line):
        peer = lax.rem(part - k + line, line)
        sides[k - 1].wait_recv()
        at = quarter(peer, 1 - half)
        near.append(send(at, at, near_out.at[1, k], near_in.at[1, k], (sibling, part)))
    mine[1].wait()
    for copy in copies + far + sides:
        copy.wait_send()
    for copy in told + near:
        copy.wait()


def add_rows(ids, count, blocks, grads, total, fresh):
    height = total.shape[0]
    rows = []
    for block in blocks:
        for r in range(-(-count // LANES)):
            rows.append(ids[block, r : r + 1, 0 : min(LANES, count - r * LANES)])
    numbers = jnp.concatenate(rows, 1)
    values = jnp.concatenate([ref[...] for ref in grads], 0)
    turned = jnp.transpose(jnp.broadcast_to(numbers.astype(F32), (8, numbers.shape[1])), (1, 0))[:, 0:1]
    upper = turned >= height
    none = jnp.zeros_like(values)
    values = jnp.concatenate([jnp.where(upper, none, values), jnp.where(upper, values, none)], 1)
    low = jnp.where(numbers >= 0, numbers & (height - 1), -1)
    step = min(height, 1024)

    def body(i, carry):
        at = pl.multiple_of(i * step, step)
        hot = jnp.where(low - at == iota((step, low.shape[1]), 0), 1.0, 0.0).astype(BF16)
        part = nn(hot, values)
        at = pl.ds(at, step)
        total[at, :] = part if fresh else total[at, :] + part
        return carry

    lax.fori_loop(0, height // step, body, 0)


def tail_kernel(
    plane,
    line,
    capacity,
    cuts,
    tokens,
    ids,
    rows,
    summed,
    gain,
    table,
    dense_all,
    norm_sq,
    gain_all,
    wide,
    sent,
    back,
    total,
    got,
    gains,
    along,
    across,
    out_sems,
    in_sems,
    far_out,
    far_in,
    gain_out,
    gain_in,
    along_out,
    along_in,
    across_out,
    across_in,
    chip_out,
    chip_in,
    near_out,
    near_in,
):
    me, part = enter(plane, line)
    chips = plane // 2
    core = lax.rem(me, 2)
    chip = me // 2
    sibling = me + 1 - 2 * core
    far = []
    split_cuts, (whole_at, whole_rows), (last_at, last_rows) = cuts
    for k in range(1, line):
        peer = lax.rem(part + k, line)
        to = 0
        for j, (at, count) in enumerate(split_cuts):
            begin = pl.multiple_of(at + peer * count, 16)
            far.append(
                send(summed.at[pl.ds(begin, count)], got.at[part, to : to + count], far_out.at[j, k], far_in.at[j, k], (me, peer))
            )
            to += count
        target = got.at[part, to : to + whole_rows]
        source = summed.at[whole_at : whole_at + whole_rows]
        far.append(send(source, target, far_out.at[2, k], far_in.at[2, k], (me, peer)))
        far.append(send(gain, gains.at[part], gain_out.at[k], gain_in.at[k], (me, peer)))
    gains[part] = gain[...]
    wide[...] = rows[...].astype(F32)
    copies = []
    others = partners(me, plane)
    for k, peer in enumerate(others):
        gather_rows(listed(tokens.at[peer], 0), wide, sent.at[peer])
        copies.append(send(sent.at[peer], back.at[me], out_sems.at[k], in_sems.at[k], (peer, part)))
    gather_rows(listed(tokens.at[me], 0), wide, sent.at[me])
    to = 0
    for at, count in split_cuts:
        got[part, to : to + count] = summed[pl.ds(pl.multiple_of(at + part * count, 16), count), :]
        to += count
    got[part, to : to + whole_rows] = summed[whole_at : whole_at + whole_rows, :]
    for copy in far:
        copy.wait()
    share = got[0].astype(F32)
    for m in range(1, line):
        share = share + got[m].astype(F32)
    dense_all[me, 0 : to + whole_rows, :] = share.astype(BF16)
    dense_all[me, to + whole_rows :, :] = summed[last_at : last_at + last_rows, :]
    dense = dense_all.at[me]
    spread, near = [], []
    group = max(1, 1280 // capacity)
    order = [me] + others
    for first in range(0, plane, group):
        blocks = order[first : first + group]
        grads = [sent.at[blocks[0]] if first == 0 else back.at[blocks[0]]] + [back.at[block] for block in blocks[1:]]
        for k in range(max(first, 1), min(first + group, plane)):
            copies[k - 1].wait_recv()
        if first + group >= plane:
            for k in range(1, chips):
                other = lax.rem(chip + k, chips)
                spread.append(send(dense, dense, chip_out.at[k], chip_in.at[k], (2 * other + core, part)))
            near.append(send(dense, dense, near_out.at[0], near_in.at[0], (sibling, part)))
        add_rows(ids, capacity, blocks, grads, total, first == 0)
    square = jnp.zeros((8, LANES), F32)
    for begin, count, weight in ((0, to, 1.0), (to, whole_rows, 1.0 / line), (to + whole_rows, last_rows, 1.0)):
        block = dense_all[me, begin : begin + count, :].astype(F32)
        square = square + weight * jnp.sum((block * block).reshape(count // 8, 8, LANES), 0)
    height = total.shape[0]

    def settle(i, carry):
        at = pl.multiple_of(i * 32, 32)
        for half in range(2):
            block = total[pl.ds(at, 32), half * LANES : (half + 1) * LANES]
            table[pl.ds(at + half * height, 32), :] = block
            block = block * block
            for r in range(4):
                carry = carry + block[r * 8 : (r + 1) * 8, :]
        return carry

    table_sq = lax.fori_loop(0, height // 32, settle, jnp.zeros((8, LANES), F32))
    across[me] = square + table_sq * (1.0 / line)
    tiny = [
        send(across.at[me], across.at[me], across_out.at[k], across_in.at[k], (lax.rem(me + k, plane), part))
        for k in range(1, plane)
    ]
    for copy in tiny:
        copy.wait()
    sums = across[0]
    for d in range(1, plane):
        sums = sums + across[d]
    along[part] = sums
    peers = [lax.rem(part + k, line) for k in range(1, line)]
    tiny = [
        send(along.at[part], along.at[part], along_out.at[k], along_in.at[k], (me, peer)) for k, peer in enumerate(peers)
    ]
    for k in range(1, chips):
        peer = 2 * lax.rem(chip - k + chips, chips) + core
        spread[k - 1].wait_recv()
        near.append(send(dense_all.at[peer], dense_all.at[peer], near_out.at[k], near_in.at[k], (sibling, part)))
    gain_sum = gains[0]
    for m in range(1, line):
        gain_sum = gain_sum + gains[m]
    gain_all[...] = gain_sum
    for copy in tiny:
        copy.wait()
    sums = along[0]
    for m in range(1, line):
        sums = sums + along[m]
    norm_sq[...] = jnp.broadcast_to(jnp.sum(sums + gain_sum * gain_sum), norm_sq.shape)
    for copy in copies + spread:
        copy.wait_send()
    for copy in near:
        copy.wait()


def chain(index, values):
    out = jnp.full(index.shape, values[0], values[0].dtype)
    for k in range(1, len(values)):
        out = jnp.where(index >= k, values[k], out)
    return out


def forward_tower(tower, slots, cnt, x, w_in, gain, w_all, pooled, pm_out, normed_out, qkv, prob, a_out, pm_acc):
    pairs = pooled.shape[1]
    first = lax.axis_index("mp") * pairs
    parts = w_all.shape[0]
    per = LANES // slots
    groups = pairs // per
    heads = 2 * parts
    xs = x[tower]
    hidden = nn(xs, w_in[tower].astype(BF16))
    inverse = lax.rsqrt(jnp.mean(hidden * hidden, -1, keepdims=True) + EPS)
    normed = (hidden * inverse * gain[tower : tower + 1, :]).astype(BF16)
    normed_out[tower] = normed
    for c in range(3):
        for m in range(parts):
            qkv[tower, c * parts + m] = nn(normed, w_all[m, tower, c]).astype(BF16)
    lane = iota((LANES, LANES), 1)
    line = iota((LANES, LANES), 0)
    shift = slots.bit_length() - 1
    pair_r, pair_s = lax.shift_right_logical(lane, shift), lax.shift_right_logical(line, shift)
    same = pair_r == pair_s
    halves = [lane < DH, lane >= DH]
    own_head = iota((per * heads, LANES), 0) & (heads - 1)

    def group(g, carry):
        counts = [cnt[tower, first + g * per + k] for k in range(per)]
        live_r = same & ((lane & (slots - 1)) < chain(pair_r, counts))
        live_s = (line & (slots - 1)) < chain(pair_s, counts)
        rows = pl.ds(pl.multiple_of(g * LANES, LANES), LANES)
        sums = []
        for m in range(parts):
            query, key = qkv[tower, m, rows, :], qkv[tower, parts + m, rows, :]
            for half in range(2):
                scores = nt(jnp.where(halves[half], query, jnp.zeros_like(query)), key) * 0.125
                scores = jnp.where(live_r, scores, -1000000000.0)
                expo = jnp.exp(scores - jnp.max(scores, 1, keepdims=True))
                p = (expo * (1.0 / jnp.sum(expo, 1, keepdims=True))).astype(BF16)
                prob[tower, g, 2 * m + half] = p
                sums.append(jnp.sum(jnp.where(live_s, p.astype(F32), 0.0), 0, keepdims=True))
        sums = jnp.concatenate(sums, 0)
        pair_l = lax.shift_right_logical(iota((heads, LANES), 1), shift)
        stack = jnp.concatenate([jnp.where(pair_l == k, sums, 0.0) for k in range(per)], 0).astype(BF16)
        a_out[tower, g] = stack
        for m in range(parts):
            mix = nn(stack, qkv[tower, 2 * parts + m, rows, :])
            head = iota((per * heads, LANES), 1) // DH + 2 * m
            mix = jnp.where(own_head == head, mix, 0.0)
            pm_acc[g, :, m * LANES : (m + 1) * LANES] = jnp.concatenate(
                [jnp.sum(mix[k * heads : (k + 1) * heads], 0, keepdims=True) for k in range(per)], 0
            )
        return carry

    lax.fori_loop(0, groups, group, 0)
    pm = jnp.concatenate([pm_acc[g] for g in range(groups)], 0).astype(BF16)
    pm_out[tower] = pm
    every = [cnt[tower, first + k] for k in range(pairs)]
    tokens = iota((pairs, pairs * slots), 1)
    mine = lax.shift_right_logical(tokens, shift) == iota(tokens.shape, 0)
    live = mine & ((tokens & (slots - 1)) < chain(iota(tokens.shape, 0), every))
    high, low = split(nn(live.astype(BF16), xs))
    w = w_in[tower].astype(BF16)
    total = nn(high, w) + nn(low, w)
    sides = []
    for j in range(2):
        side = total[:, j * LANES : (j + 1) * LANES]
        for m in range(parts):
            side = side + nn(pm[:, m * LANES : (m + 1) * LANES], w_all[m, tower, 3, j * LANES : (j + 1) * LANES, :])
        sides.append(side)
    total = jnp.concatenate(sides, 1)
    count = chain(iota(total.shape, 0), every).astype(F32)
    pooled[tower] = (total / count).astype(BF16)


def put(target, size, first, value):
    done = 0
    while done < value.shape[0]:
        share, inside = divmod(first + done, size)
        count = min(size - inside, value.shape[0] - done)
        target[share // 2, share % 2, inside : inside + count, :] = value[done : done + count]
        done += count


def backward_tower(
    tower, slots, cnt, x, w_in, gain, w_all, normed_in, qkv, prob, a_in, pm_in, dpooled, demb, d_in, d_gain, d_qkv, d_out, dqkv
):
    pairs, width = dpooled.shape[1:]
    parts = w_all.shape[0]
    per = LANES // slots
    groups = pairs // per
    heads = 2 * parts
    shift = slots.bit_length() - 1
    tokens = pairs * slots
    first = lax.axis_index("mp") * pairs
    every = [cnt[tower, first + k] for k in range(pairs)]
    count = chain(iota((pairs, width), 0), every).astype(F32)
    dsum = dpooled[tower].astype(F32) / count
    branch = dsum.astype(BF16)
    dmix = []
    for m in range(parts):
        grad = tn(pm_in[tower, :, m * LANES : (m + 1) * LANES], branch).astype(BF16)
        for j in range(width // LANES):
            begin = (tower * (width // LANES) + j) * LANES
            put(d_out.at[m], d_out.shape[3], begin, grad[:, j * LANES : (j + 1) * LANES])
        mix = 0.0
        for j in range(2):
            cut = slice(j * LANES, (j + 1) * LANES)
            mix = mix + nt(branch[:, cut], w_all[m, tower, 3, cut, :])
        dmix.append(mix)
    lane = iota((LANES, LANES), 1)
    line = iota((LANES, LANES), 0)
    pair_s = lax.shift_right_logical(line, shift)
    halves = [lane < DH, lane >= DH]
    own_head = iota((per * heads, LANES), 0) & (heads - 1)
    own_pair = lax.shift_right_logical(iota((per * heads, LANES), 0), heads.bit_length() - 1)
    token_pair = lax.shift_right_logical(iota((per * heads, LANES), 1), shift)
    for g in range(groups):
        rows = slice(g * LANES, (g + 1) * LANES)
        live_s = (line & (slots - 1)) < chain(pair_s, every[g * per : (g + 1) * per])
        scale = jnp.where(live_s, 0.125, 0.0)
        dots = jnp.zeros((per * heads, LANES), F32)
        stacks = []
        for m in range(parts):
            cut = dmix[m][g * per : (g + 1) * per]
            spread = jnp.concatenate([jnp.broadcast_to(cut[k : k + 1], (heads, LANES)) for k in range(per)], 0)
            head = iota((per * heads, LANES), 1) // DH + 2 * m
            stack = jnp.where(own_head == head, spread, 0.0).astype(BF16)
            stacks.append(stack)
            dots = dots + nt(stack, qkv[tower, 2 * parts + m, rows, :])
        dots = jnp.where(own_pair == token_pair, dots, 0.0)
        pull = dots[0:heads]
        for k in range(1, per):
            pull = pull + dots[k * heads : (k + 1) * heads]
        for m in range(parts):
            query, key = qkv[tower, m, rows, :], qkv[tower, parts + m, rows, :]
            none = jnp.zeros_like(query)
            dq = jnp.zeros((LANES, LANES), F32)
            dk = jnp.zeros((LANES, LANES), F32)
            for half in range(2):
                h = 2 * m + half
                p = prob[tower, g, h].astype(F32)
                t = p * pull[h : h + 1, :]
                ds = ((t - p * jnp.sum(t, 1, keepdims=True)) * scale).astype(BF16)
                dq = dq + nn(ds, jnp.where(halves[half], key, none))
                dk = dk + tn(ds, jnp.where(halves[half], query, none))
            dqkv[m, rows, :] = dq.astype(BF16)
            dqkv[parts + m, rows, :] = dk.astype(BF16)
            dqkv[2 * parts + m, rows, :] = tn(a_in[tower, g], stacks[m]).astype(BF16)
    normed = normed_in[tower]
    dnormed = jnp.zeros((tokens, width), F32)
    for m in range(parts):
        for c in range(3):
            grad = dqkv[c * parts + m]
            dnormed = dnormed + nt(grad, w_all[m, tower, c])
            put(d_qkv.at[m], d_qkv.shape[3], (tower * 3 + c) * width, tn(normed, grad).astype(BF16))
    dnormed = dnormed.astype(BF16).astype(F32)
    xs = x[tower]
    w = w_in[tower].astype(BF16)
    hidden = nn(xs, w)
    inverse = lax.rsqrt(jnp.mean(hidden * hidden, -1, keepdims=True) + EPS)
    unit = hidden * inverse
    grad = jnp.sum(dnormed * unit, 0, keepdims=True)
    for j in range(width // LANES):
        r = tower * (width // LANES) + j
        d_gain[r : r + 1, :] = grad[:, j * LANES : (j + 1) * LANES]
    scaled = dnormed * gain[tower : tower + 1, :]
    dh = inverse * (scaled - unit * jnp.mean(scaled * unit, -1, keepdims=True))
    spread = jnp.broadcast_to(dsum[:, None, :], (pairs, slots, width))
    slot = iota((pairs, slots, width), 1)
    counts = chain(iota((pairs, slots, width), 0), every)
    spread = jnp.where(slot < counts, spread, 0.0).reshape(tokens, width)
    dhidden = (spread + dh).astype(BF16)
    grad = tn(xs, dhidden).astype(BF16)
    for j in range(width // LANES):
        begin = (tower * (width // LANES) + j) * xs.shape[1]
        put(d_in, d_in.shape[2], begin, grad[:, j * LANES : (j + 1) * LANES])
    demb[...] = nt(dhidden, w).astype(BF16)


def gelu_parts(v):
    c = 0.7978845608028654
    inner = jnp.tanh(c * (v + 0.044715 * (v * v * v)))
    value = 0.5 * v * (1.0 + inner)
    slope = 0.5 * (1.0 + inner) + 0.5 * v * (1.0 - inner * inner) * (c * (1.0 + 3.0 * 0.044715 * (v * v)))
    return value, slope


def upper_layers(
    me,
    part,
    plane,
    line,
    pooled,
    log_prior,
    item_qid,
    lists,
    positive,
    dpooled,
    d_one,
    d_two,
    d_three,
    loss,
    pooled_all,
    second_send,
    second_got,
    vec,
    dsec_send,
    dsec_all,
    dpool_send,
    dpool_got,
    out_sems,
    in_sems,
    vec_out,
    vec_in,
    w_one,
    w_two,
    w_three,
    loads,
    second_mine,
    dpool_mine,
    prior_col,
):
    towers, own, width = pooled.shape
    per = lists.shape[1] - 8
    rows = own * line
    pairs = rows * plane
    peers = [lax.rem(part + k, line) for k in range(1, line)]

    pooled_all[:, part] = pooled[...]
    first = [
        send(pooled_all.at[:, part], pooled_all.at[:, part], out_sems.at[0, k], in_sems.at[0, k], (me, peers[k]))
        for k in range(line - 1)
    ]
    for copy in loads:
        copy.wait()
    one = [w_one[t].astype(BF16) for t in range(towers)]
    two = [w_two[t].astype(BF16) for t in range(towers)]
    three = [w_three[t].astype(BF16) for t in range(towers)]
    qid = item_qid[...]
    hot = (lax.shift_right_logical(qid, 7) == iota((log_prior.shape[0], pairs), 0)).astype(BF16)
    high, rest = log_prior[...].astype(BF16), log_prior[...]
    rest = rest - high.astype(F32)
    middle, low = split(rest)
    table = tn(high, hot) + tn(middle, hot) + tn(low, hot)
    prior_row = jnp.sum(jnp.where((qid & 127) == iota((LANES, pairs), 0), table, 0.0), 0, keepdims=True)
    prior_col[...] = jnp.transpose(jnp.broadcast_to(prior_row, (8, pairs)), (1, 0))
    pos_row = jnp.concatenate([lists[d, per : per + 1, 0:rows] for d in range(plane)], 1)
    pos_own = chain(iota((own, pairs), 0), [positive[part * own + k] for k in range(own)])
    for copy in first:
        copy.wait()
    act_one, slope_one, pools = [], [], []
    for t in range(towers):
        pools.append(pooled_all[t].reshape(rows, width))
        value, slope = gelu_parts(nn(pools[t], one[t]))
        act_one.append(value.astype(BF16))
        slope_one.append(slope)
        partial = nn(act_one[t], two[t]).reshape(line, own, -1)
        second_mine[t] = partial
        second_send[t] = partial.astype(BF16)
    second = [
        send(
            second_send.at[:, peers[k]], second_got.at[:, part], out_sems.at[1, k], in_sems.at[1, k], (me, peers[k])
        )
        for k in range(line - 1)
    ]
    for copy in second:
        copy.wait()
    act_two, slope_two, third, length, vectors = [], [], [], [], []
    for t in range(towers):
        total = second_mine[t, part]
        for peer in peers:
            total = total + second_got[t, peer].astype(F32)
        value, slope = gelu_parts(total)
        act_two.append(value.astype(BF16))
        slope_two.append(slope)
        third.append(nn(act_two[t], three[t]))
        length.append(lax.rsqrt(jnp.sum(third[t] * third[t], -1, keepdims=True) + EPS))
        vectors.append((third[t] * length[t]).astype(BF16))
        vec[t, me, part] = vectors[t]
    along = [
        send(vec.at[:, me, part], vec.at[:, me, part], out_sems.at[2, k], in_sems.at[2, k], (me, peers[k]))
        for k in range(line - 1)
    ]
    for copy in along:
        copy.wait()
    chips = plane // 2
    core = lax.rem(me, 2)
    chip = me // 2
    sibling = me + 1 - 2 * core
    near = [send(vec.at[:, me], vec.at[:, me], vec_out.at[0], vec_in.at[0], (sibling, part))]
    across = []
    for k in range(1, chips):
        other = 2 * lax.rem(chip + k, chips) + core
        across.append(send(vec.at[:, me], vec.at[:, me], vec_out.at[k], vec_in.at[k], (other, part)))
    for k in range(1, chips):
        peer = 2 * lax.rem(chip - k + chips, chips) + core
        across[k - 1].wait_recv()
        sems = vec_out.at[chips + k], vec_in.at[chips + k]
        near.append(send(vec.at[:, peer], vec.at[:, peer], *sems, (sibling, part)))
    for copy in across:
        copy.wait_send()
    for copy in near:
        copy.wait()

    queries = vec[0].reshape(pairs, width)
    items = vec[1].reshape(pairs, width)
    logits = INV_TEMP * nt(items, queries) - prior_col[:, 0:1]
    peak = jnp.max(logits, 0, keepdims=True)
    log_total = peak + jnp.log(jnp.sum(jnp.exp(logits - peak), 0, keepdims=True))
    picked = jnp.where(iota((pairs, pairs), 0) == pos_row, logits, 0.0)
    gap = log_total - jnp.sum(picked, 0, keepdims=True)
    loss[0, 0] = jnp.sum(gap)
    ahead = me * rows + part * own
    mine = INV_TEMP * nt(vectors[0], items) - prior_row
    top = jnp.max(mine, 1, keepdims=True)
    expo = jnp.exp(mine - top)
    chance = expo / jnp.sum(expo, 1, keepdims=True)
    target = (iota(mine.shape, 1) == pos_own).astype(F32)
    dlog = ((chance - target) / pairs).astype(BF16)
    dvec = [(INV_TEMP * nn(dlog, items)).astype(BF16)]
    own_prior = prior_col[pl.ds(pl.multiple_of(ahead, own), own), 0:1]
    theirs = INV_TEMP * nt(vectors[1], queries) - own_prior
    target = (iota(theirs.shape, 0) + ahead == pos_row).astype(F32)
    dlog = ((jnp.exp(theirs - log_total) - target) / pairs).astype(BF16)
    dvec.append((INV_TEMP * nn(dlog, queries)).astype(BF16))

    dthirds = []
    for t in range(towers):
        dv = dvec[t].astype(F32)
        inner = jnp.sum(dv * third[t], -1, keepdims=True)
        dthird = (length[t] * dv - third[t] * (length[t] * length[t] * length[t] * inner)).astype(BF16)
        dact = nt(dthird, three[t]).astype(BF16).astype(F32)
        dsec_all[t, part] = (dact * slope_two[t]).astype(BF16)
        dthirds.append(dthird)
    spread = [
        send(dsec_all.at[:, part], dsec_all.at[:, part], out_sems.at[3, k], in_sems.at[3, k], (me, peers[k]))
        for k in range(line - 1)
    ]
    for t in range(towers):
        grad = tn(act_two[t], dthirds[t]).astype(BF16)
        for j in range(width // LANES):
            put(d_three, d_three.shape[2], (t * (width // LANES) + j) * grad.shape[0], grad[:, j * LANES : (j + 1) * LANES])
    for copy in spread:
        copy.wait()
    dfirsts = []
    for t in range(towers):
        dsecond = dsec_all[t].reshape(rows, -1)
        dact = nt(dsecond, two[t]).astype(BF16).astype(F32)
        dfirst = (dact * slope_one[t]).astype(BF16)
        partial = nt(dfirst, one[t]).reshape(line, own, width)
        dpool_mine[t] = partial
        dpool_send[t] = partial.astype(BF16)
        dfirsts.append(dfirst)
    back = [
        send(dpool_send.at[:, peers[k]], dpool_got.at[:, part], out_sems.at[4, k], in_sems.at[4, k], (me, peers[k]))
        for k in range(line - 1)
    ]
    for t in range(towers):
        dsecond = dsec_all[t].reshape(rows, -1)
        for grads, grad in ((d_two, tn(act_one[t], dsecond)), (d_one, tn(pools[t], dfirsts[t]))):
            grad = grad.astype(BF16)
            wide = grad.shape[1] // LANES
            for j in range(wide):
                begin = (t * wide + j) * grad.shape[0]
                put(grads, grads.shape[2], begin, grad[:, j * LANES : (j + 1) * LANES])
    for copy in back:
        copy.wait()
    for t in range(towers):
        total = dpool_mine[t, part]
        for peer in peers:
            total = total + dpool_got[t, peer].astype(F32)
        dpooled[t] = total.astype(BF16)


def towers_kernel(
    plane,
    line,
    slots,
    cnt,
    x,
    w_in,
    gain,
    w_all,
    far_one,
    far_two,
    far_three,
    log_prior,
    item_qid,
    lists,
    positive,
    out,
    summed,
    gain_sum,
    loss,
    pooled,
    pm,
    normed,
    qkv,
    prob,
    a_in,
    pm_acc,
    upper_scratch,
    w_one,
    w_two,
    w_three,
    load_sems,
    dpooled,
    d_three,
    d_one,
    d_two,
    d_qkv,
    d_out,
    d_in,
    d_gain,
    dqkv,
    near_split,
    near_whole,
    half,
    got,
    got_late,
    gains,
    far_out,
    far_in,
    near_out,
    near_in,
    sum_out,
    sum_in,
    gain_out,
    gain_in,
):
    loads = [
        pltpu.make_async_copy(source, target, load_sems.at[j])
        for j, (source, target) in enumerate(((far_one, w_one), (far_two, w_two), (far_three, w_three)))
    ]
    for copy in loads:
        copy.start()
    me, part = announce(plane, line)
    for t in range(x.shape[0]):
        forward_tower(t, slots, cnt, x, w_in, gain, w_all, pooled, pm, normed, qkv, prob, a_in, pm_acc)
    await_others(plane, line)
    upper_layers(
        me,
        part,
        plane,
        line,
        pooled,
        log_prior,
        item_qid,
        lists,
        positive,
        dpooled,
        d_one,
        d_two,
        d_three,
        loss,
        *upper_scratch[:-3],
        w_one,
        w_two,
        w_three,
        loads,
        *upper_scratch[-3:],
    )
    chips = plane // 2
    core = lax.rem(me, 2)
    chip = me // 2
    sibling = me + 1 - 2 * core
    towers, tokens = x.shape[:2]
    late, early = (d_in,), (d_three, d_one, d_two)
    nears = [send(grad.at[:, 1 - core], near_whole[1 + j], near_out.at[j], near_in.at[j], (sibling, part)) for j, grad in enumerate(early)]
    copies = []

    def tower(t):
        demb = out.at[part, t * tokens : (t + 1) * tokens]
        backward_tower(
            t, slots, cnt, x, w_in, gain, w_all, normed, qkv, prob, a_in, pm, dpooled, demb, d_in, d_gain, d_qkv, d_out, dqkv
        )
        for k in range(1, line):
            peer = lax.rem(part + k, line)
            copies.append(send(demb, demb, far_out.at[t, k], far_in.at[t, k], (me, peer)))

    def whole(c, at, grad, near):
        rows = grad.shape[2]
        half[c, at : at + rows, :] = (grad[c, core].astype(F32) + near[c].astype(F32)).astype(BF16)
        return at + rows

    def exchange(begin, end, target, sems):
        sums = []
        for k in range(1, chips):
            to = lax.rem(chip + k, chips)
            source = half.at[to, begin:end]
            sums.append(send(source, target.at[k - 1], sum_out.at[sems, k], sum_in.at[sems, k], (2 * to + core, part)))
        return sums

    def collect(begin, end, target, sums):
        for copy in sums:
            copy.wait()
        total = half[chip, begin:end, :].astype(F32)
        for k in range(chips - 1):
            total = total + target[k].astype(F32)
        summed[begin:end, :] = total.astype(BF16)

    first = line * (d_qkv.shape[3] + d_out.shape[3]) + d_in.shape[2]
    d_gain[...] = jnp.zeros_like(d_gain)
    tower(0)
    for copy in nears:
        copy.wait()
    for c in range(chips):
        at = first
        for j, grad in enumerate(early):
            at = whole(c, at, grad, near_whole[1 + j])
    last = at
    sums = exchange(first, last, got, 0)
    for t in range(1, towers):
        tower(t)
    nears = []
    for j, grad in enumerate((d_qkv, d_out)):
        nears.append(send(grad.at[:, :, 1 - core], near_split[j], near_out.at[3 + j], near_in.at[3 + j], (sibling, part)))
    nears.append(send(d_in.at[:, 1 - core], near_whole[0], near_out.at[5], near_in.at[5], (sibling, part)))
    for k in range(1, plane):
        peer = lax.rem(me + k, plane)
        copies.append(send(d_gain, gains.at[me], gain_out.at[k], gain_in.at[k], (peer, part)))
    gains[me] = d_gain[...]
    for copy in nears:
        copy.wait()
    for c in range(chips):
        at = 0
        for grad, near in zip((d_qkv, d_out), near_split):
            rows = grad.shape[3]
            for m in range(line):
                total = grad[m, c, core].astype(F32) + near[m, c].astype(F32)
                half[c, at : at + rows, :] = total.astype(BF16)
                at += rows
        whole(c, at, d_in, near_whole[0])
    late_sums = exchange(0, first, got_late, 1)
    collect(first, last, got, sums)
    collect(0, first, got_late, late_sums)
    for copy in copies:
        copy.wait()
    total = gains[0]
    for d in range(1, plane):
        total = total + gains[d]
    gain_sum[...] = total


def update(weight, grad, moment, average, factor, rate):
    clipped = grad * factor
    moment_new = MOMENTUM * moment + clipped
    weight_new = weight - rate * (clipped + MOMENTUM * moment_new)
    average_new = AVERAGE_DECAY * average + (1.0 - AVERAGE_DECAY) * weight_new
    return [weight_new, moment_new, average_new]


def update_kernel(blocks, norm_sq, table_grad, dense, gain, *refs):
    arrays = 3 * 8
    sources, targets, norm = refs[:arrays], refs[arrays : 2 * arrays], refs[2 * arrays]
    held, in_sems, out_sems = refs[2 * arrays + 1 : 3 * arrays + 1], refs[-2], refs[-1]
    loads = [pltpu.make_async_copy(sources[k], held[k], in_sems.at[k]) for k in range(arrays)]
    ahead = 8

    def load(k):
        if k < arrays // 3:
            for copy in loads[3 * k : 3 * k + 3]:
                copy.start()

    for k in range(ahead):
        load(k)
    root = jnp.sqrt(norm_sq[...])
    norm[0, 0] = jnp.max(root)
    factor = jnp.minimum(1.0, CLIP_NORM / root[0:1, :])
    stores = []

    def finish(k):
        for j in range(3 * k, 3 * k + 3):
            copy = pltpu.make_async_copy(held[j], targets[j], out_sems.at[j])
            copy.start()
            stores.append(copy)

    def apply(k, rows, lanes, grad, rate):
        cells = [ref.at[rows, lanes] for ref in held[3 * k : 3 * k + 3]]
        new = update(cells[0][...], grad, cells[1][...], cells[2][...], factor, rate)
        for cell, value in zip(cells, new):
            cell[...] = value

    def wait(k):
        for copy in loads[3 * k : 3 * k + 3]:
            copy.wait()
        load(k + ahead)

    wait(0)

    def rows(i, carry):
        at = pl.ds(pl.multiple_of(i * 32, 32), 32)
        apply(0, at, slice(0, LANES), table_grad[at, :], ROW_RATE)
        return carry

    lax.fori_loop(0, table_grad.shape[0] // 32, rows, 0, unroll=2)
    finish(0)
    at = 0
    for k, size, height, wide in blocks:
        wait(k)
        total = dense.shape[0] * size
        step = 32 if size % 32 == 0 else 16
        for first in range(0, total, min(size, height)):
            count = min(size, height)
            share, inside = first // size, first % size
            block, begin = first // height, first % height
            t, j = block // wide, block % wide
            top = t * height + begin

            def piece(i, carry):
                take = pl.ds(pl.multiple_of(at + inside + i * step, 16), step)
                rows = pl.ds(pl.multiple_of(top + i * step, 16), step)
                grad = dense[share, take, :].astype(F32)
                apply(k, rows, slice(j * LANES, (j + 1) * LANES), grad, MATRIX_RATE)
                return carry

            lax.fori_loop(0, count // step, piece, 0, unroll=2)
        at += size
        finish(k)
    last = 7
    wait(last)
    for t in range(held[3 * last].shape[0]):
        for j in range(held[3 * last].shape[1] // LANES):
            r = t * (held[3 * last].shape[1] // LANES) + j
            apply(last, slice(t, t + 1), slice(j * LANES, (j + 1) * LANES), gain[r : r + 1, :], GAIN_RATE)
    finish(last)
    for copy in stores:
        copy.wait()


def shards(
    slot_owner,
    slot_row,
    slot_count,
    item_qid,
    positive,
    log_prior,
    embedding,
    embedding_mom,
    embedding_avg,
    w_in,
    w_in_mom,
    w_in_avg,
    norm_gain,
    norm_gain_mom,
    norm_gain_avg,
    w_qkv,
    w_qkv_mom,
    w_qkv_avg,
    w_out,
    w_out_mom,
    w_out_avg,
    w_one,
    w_one_mom,
    w_one_avg,
    w_two,
    w_two_mom,
    w_two_avg,
    w_three,
    w_three_mom,
    w_three_avg,
):
    plane = lax.axis_size("dp")
    line = lax.axis_size("mp")
    batch, towers, slots = slot_row.shape
    own = batch // line
    requests = batch * towers * slots
    own_requests = requests // line
    tokens = own * slots
    capacity = max(LANES, 2 * requests // plane)
    pairs = batch * plane
    part = lax.axis_index("mp")
    me = lax.axis_index("dp")
    width = w_in.shape[2]
    depth = w_in.shape[1]
    units = w_one.shape[2]
    seconds = w_two.shape[2]

    per = capacity // LANES
    small = capacity // 4
    dims = (towers, own, slots)

    def row_scratch(count):
        return [
            pltpu.VMEM((plane, count, depth), BF16),
            pltpu.VMEM((plane, count, depth), BF16),
            pltpu.VMEM((plane * count, depth), F32),
        ]

    turned = jnp.transpose(w_qkv, (0, 2, 1, 3))
    embedded, got_own, got_lists, weights, inverse, own_place = pl.pallas_call(
        functools.partial(fetch_kernel, plane, line, dims, capacity),
        out_shape=[
            shape((own_requests, depth), BF16),
            shape((plane, per, LANES), I32),
            shape((plane, per + 8, LANES), I32),
            shape((line, towers, 4, width, LANES), BF16),
            shape((plane * per, LANES), I32),
            shape((slots, LANES), I32),
        ],
        in_specs=[VMEM] * 4 + [HBM] * 3,
        out_specs=[VMEM] * 6,
        scratch_shapes=[
            pltpu.VMEM((plane, per, LANES), I32),
            pltpu.VMEM((slots, LANES), I32),
            pltpu.VMEM((plane, per + 8, LANES), I32),
            pltpu.VMEM(embedding.shape, F32),
            pltpu.VMEM(turned.shape, F32),
            pltpu.VMEM(w_out.shape, F32),
            pltpu.SMEM((slots, LANES), I32),
            pltpu.SMEM((plane, -(-small // LANES), LANES), I32),
            *row_scratch(small),
            DMA((2, plane)),
            DMA((2, plane)),
            DMA((plane,)),
            DMA((plane,)),
            DMA((line,)),
            DMA((line,)),
            DMA((line,)),
            DMA((line,)),
            DMA((2, line)),
            DMA((2, line)),
            DMA((4,)),
            DMA((3,)),
        ],
        compiler_params=params(60, collective_id=2, has_side_effects=True),
        name="fetch",
    )(
        jnp.transpose(slot_owner[..., 0], (1, 2, 0)),
        jnp.transpose(slot_row, (1, 2, 0)),
        jnp.transpose(slot_count),
        positive.reshape(1, batch),
        embedding,
        turned,
        w_out,
    )
    most = jnp.max(got_lists[:, per + 1 : per + 3, 0], 0)

    def refetch(ids, place, table, _):
        return pl.pallas_call(
            functools.partial(refetch_kernel, plane, dims),
            out_shape=shape((own_requests, depth), BF16),
            in_specs=[SMEM, SMEM, VMEM],
            out_specs=VMEM,
            scratch_shapes=[*row_scratch(capacity), DMA((plane,)), DMA((plane,))],
            compiler_params=params(16, collective_id=7, has_side_effects=True),
            name="refetch",
        )(ids, place, table)

    embedded = lax.cond(most[0] > small, refetch, lambda *given: given[3], got_own, own_place, embedding, embedded)
    embedded = embedded.reshape(towers, tokens, depth)

    counts = jnp.transpose(slot_count)
    heads = 2 * line
    groups = tokens // LANES
    per_group = LANES // slots
    totals = (towers * 3 * width, towers * width, towers * depth * width // LANES)
    totals += tuple(towers * size // LANES for size in (seconds * width, width * units, units * seconds))
    sizes = [total // plane for total in totals]
    held = lambda size: pltpu.VMEM((plane // 2, 2, size, LANES), BF16)
    share = line * (sizes[0] + sizes[1]) + sum(sizes[2:])
    early = sum(sizes[3:])
    every, summed, gain_sum, loss = pl.pallas_call(
        functools.partial(towers_kernel, plane, line, slots),
        out_shape=[
            shape((line, own_requests, depth), BF16),
            shape((share, LANES), BF16),
            shape((8, LANES), F32),
            shape((1, 1), F32),
        ],
        in_specs=[SMEM] + [VMEM] * 4 + [HBM] * 3 + [VMEM] * 3 + [SMEM],
        out_specs=[VMEM] * 3 + [SMEM],
        scratch_shapes=[
            pltpu.VMEM((towers, own, width), BF16),
            pltpu.VMEM((towers, own, line * LANES), BF16),
            pltpu.VMEM((towers, tokens, width), BF16),
            pltpu.VMEM((towers, 3 * line, tokens, LANES), BF16),
            pltpu.VMEM((towers, groups, heads, LANES, LANES), BF16),
            pltpu.VMEM((towers, groups, per_group * heads, LANES), BF16),
            pltpu.VMEM((groups, per_group, line * LANES), F32),
            [
                pltpu.VMEM((towers, line, own, width), BF16),
                pltpu.VMEM((towers, line, own, seconds), BF16),
                pltpu.VMEM((towers, line, own, seconds), BF16),
                pltpu.VMEM((towers, plane, line, own, width), BF16),
                pltpu.VMEM((towers, line, own, seconds), BF16),
                pltpu.VMEM((towers, line, own, seconds), BF16),
                pltpu.VMEM((towers, line, own, width), BF16),
                pltpu.VMEM((towers, line, own, width), BF16),
                DMA((5, line)),
                DMA((5, line)),
                DMA((plane,)),
                DMA((plane,)),
                pltpu.VMEM((towers, line, own, seconds), F32),
                pltpu.VMEM((towers, line, own, width), F32),
                pltpu.VMEM((pairs, 8), F32),
            ],
            pltpu.VMEM(w_one.shape, F32),
            pltpu.VMEM(w_two.shape, F32),
            pltpu.VMEM(w_three.shape, F32),
            DMA((3,)),
            pltpu.VMEM((towers, own, width), BF16),
            held(sizes[3]),
            held(sizes[4]),
            held(sizes[5]),
            pltpu.VMEM((line, plane // 2, 2, sizes[0], LANES), BF16),
            pltpu.VMEM((line, plane // 2, 2, sizes[1], LANES), BF16),
            held(sizes[2]),
            pltpu.VMEM((8, LANES), F32),
            pltpu.VMEM((3 * line, tokens, LANES), BF16),
            [pltpu.VMEM((line, plane // 2, size, LANES), BF16) for size in sizes[:2]],
            [pltpu.VMEM((plane // 2, size, LANES), BF16) for size in sizes[2:]],
            pltpu.VMEM((plane // 2, share, LANES), BF16),
            pltpu.VMEM((plane // 2 - 1, early, LANES), BF16),
            pltpu.VMEM((plane // 2 - 1, share - early, LANES), BF16),
            pltpu.VMEM((plane, 8, LANES), F32),
            DMA((towers, line)),
            DMA((towers, line)),
            DMA((6,)),
            DMA((6,)),
            DMA((2, plane // 2)),
            DMA((2, plane // 2)),
            DMA((plane,)),
            DMA((plane,)),
        ],
        compiler_params=params(60, collective_id=4, has_side_effects=True),
        name="towers",
    )(
        counts,
        embedded,
        w_in,
        norm_gain,
        weights,
        w_one,
        w_two,
        w_three,
        log_prior.reshape(-1, LANES),
        item_qid.reshape(1, pairs),
        got_lists,
        positive,
    )
    whole_at = line * (sizes[0] + sizes[1])
    whole_rows = sizes[2] + sizes[3]
    last_rows = sizes[4] + sizes[5]
    cuts = (
        ((0, sizes[0]), (line * sizes[0], sizes[1])),
        (whole_at, whole_rows),
        (whole_at + whole_rows, last_rows),
    )
    line_rows = sizes[0] + sizes[1] + whole_rows

    def tail(count, number):
        return lambda *given: pl.pallas_call(
            functools.partial(tail_kernel, plane, line, count, cuts),
            out_shape=[
                shape(embedding.shape, F32),
                shape((plane, line_rows + last_rows, LANES), BF16),
                shape((8, LANES), F32),
                shape((8, LANES), F32),
            ],
            in_specs=[SMEM] + [VMEM] * 4,
            out_specs=[VMEM] * 4,
            scratch_shapes=[
                pltpu.VMEM((requests, depth), F32),
                pltpu.VMEM((plane, count, depth), BF16),
                pltpu.VMEM((plane, count, depth), BF16),
                pltpu.VMEM((embedding.shape[0] // 2, 2 * depth), F32),
                pltpu.VMEM((line, line_rows, LANES), BF16),
                pltpu.VMEM((line, 8, LANES), F32),
                pltpu.VMEM((line, 8, LANES), F32),
                pltpu.VMEM((plane, 8, LANES), F32),
                DMA((plane,)),
                DMA((plane,)),
                DMA((3, line)),
                DMA((3, line)),
                DMA((line,)),
                DMA((line,)),
                DMA((line,)),
                DMA((line,)),
                DMA((plane,)),
                DMA((plane,)),
                DMA((plane // 2,)),
                DMA((plane // 2,)),
                DMA((plane // 2,)),
                DMA((plane // 2,)),
            ],
            compiler_params=params(36, collective_id=number, has_side_effects=True),
            name="tail",
        )(given[0][:, : -(-count // LANES)], *given[1:])

    medium = capacity * 5 // 8
    table_grad, dense_all, norm_sq, gain_all = lax.cond(
        most[1] > medium,
        tail(capacity, 8),
        tail(medium, 5),
        inverse.reshape(plane, per, LANES),
        got_lists,
        every.reshape(requests, depth),
        summed,
        gain_sum,
    )
    flat = lambda w: w.reshape(-1, w.shape[-1])
    turn = lambda w: flat(jnp.transpose(w, (0, 2, 1, 3)))
    given = [embedding, embedding_mom, embedding_avg]
    given += [turn(w) for w in (w_qkv, w_qkv_mom, w_qkv_avg)]
    rest = (w_out, w_out_mom, w_out_avg, w_in, w_in_mom, w_in_avg, w_three, w_three_mom, w_three_avg)
    rest += (w_one, w_one_mom, w_one_avg, w_two, w_two_mom, w_two_avg)
    given += [flat(w) for w in rest]
    given += [norm_gain, norm_gain_mom, norm_gain_avg]
    heights = (towers * 3 * width, LANES, depth, seconds, width, units)
    wides = (1, width // LANES, width // LANES, width // LANES, units // LANES, seconds // LANES)
    blocks = tuple((k + 1, size, height, wide) for k, (size, height, wide) in enumerate(zip(sizes, heights, wides)))
    *done, norm = pl.pallas_call(
        functools.partial(update_kernel, blocks),
        out_shape=[shape(w.shape, F32) for w in given] + [shape((1, 1), F32)],
        in_specs=[VMEM] * 4 + [HBM] * len(given),
        out_specs=[HBM] * len(given) + [SMEM],
        scratch_shapes=[pltpu.VMEM(w.shape, F32) for w in given] + [DMA((len(given),))] * 2,
        compiler_params=params(57),
        name="update",
    )(norm_sq, table_grad, dense_all, gain_all, *given)
    back = lambda k, w: [done[3 * k + j].reshape(w.shape) for j in range(3)]
    unturned = [
        jnp.transpose(w.reshape(towers, 3, width, LANES), (0, 2, 1, 3)) for w in done[3:6]
    ]
    new = done[:3] + back(3, w_in) + done[21:24] + unturned + back(2, w_out) + back(5, w_one) + back(6, w_two)
    return (loss.reshape(()), norm.reshape(()), *new, *back(4, w_three))


def solution(mesh):
    rows = P("dp", None)
    qkv = P(None, None, None, "mp")
    deep = P(None, "mp", None)
    wide = P(None, None, "mp")
    weights = (rows,) * 3 + (P(),) * 6 + (qkv,) * 3 + (deep,) * 3 + (wide,) * 3 + (deep,) * 3 + (P(),) * 3
    inputs = (P("dp", None, None, None), P("dp", None, None), P("dp", None), P(), P("dp"), P())
    return jax.shard_map(
        shards, mesh=mesh, in_specs=inputs + weights, out_specs=(P(), P()) + weights, check_vma=False
    )
```

```python
import functools
import math

import jax
import jax.numpy as jnp
from jax import lax
from jax.experimental import pallas as pl
from jax.experimental.pallas import tpu as pltpu
from jax.sharding import PartitionSpec as P

DH = 64
EPS = 1e-06
INV_TEMP = 20.0
CLIP_NORM = 0.1
ROW_RATE = 150000.0
GAIN_RATE = 8000.0
MATRIX_RATE = 600.0
MOMENTUM = 0.9
AVERAGE_DECAY = 0.6

MESH = pl.DeviceIdType.MESH
LANES = 128
F32 = jnp.float32
BF16 = jnp.bfloat16
I32 = jnp.int32
VMEM = pl.BlockSpec(memory_space=pltpu.VMEM)
HBM = pl.BlockSpec(memory_space=pltpu.HBM)
SMEM = pl.BlockSpec(memory_space=pltpu.SMEM)
DMA = pltpu.SemaphoreType.DMA


def nn(a, b):
    return lax.dot_general(a, b, (((1,), (0,)), ((), ())), preferred_element_type=F32)


def nt(a, b):
    return lax.dot_general(a, b, (((1,), (1,)), ((), ())), preferred_element_type=F32)


def tn(a, b):
    return lax.dot_general(a, b, (((0,), (0,)), ((), ())), preferred_element_type=F32)


def iota(shape, dim):
    return lax.broadcasted_iota(I32, shape, dim)


def split(value):
    high = value.astype(BF16)
    return high, (value - high.astype(F32)).astype(BF16)


def shape(dims, dtype):
    return jax.ShapeDtypeStruct(tuple(dims), dtype)


def params(limit, **more):
    return pltpu.CompilerParams(vmem_limit_bytes=limit << 20, **more)


def log2(value):
    return value.bit_length() - 1


def lists_of(owner, values, owners, capacity):
    chunks = owner.shape[0]
    width = owners * capacity
    his = width // LANES
    sub = iota((owners, LANES), 0)
    hot = [(owner[c : c + 1, :] == sub).astype(F32) for c in range(chunks)]
    hots = jnp.concatenate(hot, 0).astype(BF16)
    before = (iota((LANES, LANES), 0) < iota((LANES, LANES), 1)).astype(BF16)
    earlier = nn(hots, before)
    totals = nn(hots, jnp.ones((LANES, LANES), BF16))
    base = (sub * capacity).astype(F32)
    places = []
    for c in range(chunks):
        cut = slice(c * owners, (c + 1) * owners)
        here = jnp.sum(hot[c] * (earlier[cut] + base), 0, keepdims=True).astype(I32)
        places.append(jnp.where(owner[c : c + 1, :] < owners, here, width))
        base = base + totals[cut]
    parts = 2 * len(values)
    acc = jnp.zeros((his, parts * LANES), F32)
    for c in range(chunks):
        place = places[c]
        left = (lax.shift_right_logical(place, 7) == iota((his, LANES), 0)).astype(BF16)
        low = (place & 127) == iota((LANES, LANES), 0)
        cuts = []
        for value in values:
            value = value[c : c + 1, :]
            cuts += [lax.shift_right_logical(value, 6), value & 63]
        right = jnp.concatenate([jnp.where(low, cut.astype(F32), 0.0) for cut in cuts], 0)
        acc = acc + nt(left, right.astype(BF16))
    cuts = [acc[:, k * LANES : (k + 1) * LANES].astype(I32) for k in range(parts)]
    lists = [cuts[2 * k] * 64 + cuts[2 * k + 1] for k in range(len(values))]
    return places, lists, hot


class Slots:
    def __init__(self, owners, line, owner, row, count):
        towers, slots, batch = owner.shape
        own = batch // line
        side = lambda ref: jnp.concatenate([ref[t] for t in range(towers)], 1)
        counts = jnp.concatenate([count[t : t + 1, :] for t in range(towers)], 1)
        slot, lane = iota((slots, LANES), 0), iota((slots, LANES), 1)
        tower = lax.shift_right_logical(lane, log2(batch))
        self.row = side(row)
        self.owner = jnp.where(slot < counts, side(owner), owners)
        self.block = lax.shift_right_logical(lane & (batch - 1), log2(own))
        self.token = ((self.block * towers + tower) * own + (lane & (own - 1))) * slots + slot


def make_own_lists(slots, owners, capacity, small, height, own_lists, own_place, own_small):
    per = capacity // LANES
    owner = jnp.where(slots.block == lax.axis_index("mp"), slots.owner, owners)
    places, (rows,), _ = lists_of(owner, (slots.row,), owners, capacity)
    rows = jnp.minimum(jnp.maximum(rows, 0), height - 1)
    for d in range(owners):
        own_lists[d] = rows[d * per : (d + 1) * per, :]
    place = jnp.concatenate(places, 0)
    place = jnp.maximum(jnp.where(place < owners * capacity, place, 0), 0)
    own_place[...] = place
    rank = jnp.minimum(place & (capacity - 1), small - 1)
    own_small[...] = lax.shift_right_logical(place, log2(capacity)) * small + rank


def make_lists(slots, owners, capacity, batch, line, positive, lists, inverse):
    per = capacity // LANES
    _, (rows, tokens), hot = lists_of(slots.owner, (slots.row + 1, slots.token), owners, capacity)
    rows = rows - 1
    inverse[...] = tokens
    asked = hot[0]
    for more in hot[1:]:
        asked = asked + more
    own = batch // line
    near = lax.shift_right_logical(iota((LANES, LANES), 0) & (batch - 1), log2(own)) == iota((LANES, LANES), 1)
    asked = asked.astype(BF16)
    most = jnp.max(jnp.max(nn(asked, near.astype(BF16)), 0, keepdims=True), 1, keepdims=True)
    every = jnp.max(nn(asked, jnp.ones((LANES, LANES), BF16)), 0, keepdims=True)
    most = jnp.broadcast_to(most, (1, LANES))
    for d in range(owners):
        lists[d, 0:per, :] = rows[d * per : (d + 1) * per, :]
        lists[d, per : per + 1, 0:batch] = positive[...]
        lists[d, per + 1 : per + 2, :] = most.astype(I32)
        lists[d, per + 2 : per + 3, :] = every.astype(I32)


def announce(plane, line):
    me, part = lax.axis_index("dp"), lax.axis_index("mp")
    barrier = pltpu.get_barrier_semaphore()
    for k in range(1, plane):
        pl.semaphore_signal(barrier, inc=1, device_id=(lax.rem(me + k, plane), part), device_id_type=MESH)
    for k in range(1, line):
        pl.semaphore_signal(barrier, inc=1, device_id=(me, lax.rem(part + k, line)), device_id_type=MESH)
    return me, part


def await_others(plane, line):
    pl.semaphore_wait(pltpu.get_barrier_semaphore(), max(plane - 1, 0) + max(line - 1, 0))


def enter(plane, line):
    me, part = announce(plane, line)
    await_others(plane, line)
    return me, part


def partners(me, count):
    order = sorted(range(1, count), key=lambda k: (-bin(k >> 1).count("1"), k & 1, k))
    bits = [lax.rem(me // (1 << b), 2) for b in range(log2(count))]
    return [sum((1 << b) * (1 - bit if k >> b & 1 else bit) for b, bit in enumerate(bits)) for k in order]


def send(source, target, out_sem, in_sem, device):
    copy = pltpu.make_async_remote_copy(
        src_ref=source, dst_ref=target, send_sem=out_sem, recv_sem=in_sem, device_id=device, device_id_type=MESH
    )
    copy.start()
    return copy


def gather_rows(ids, table, target):
    def body(i, carry):
        at = ids(i)
        rows = [table[pl.ds(at(u), 1), :] for u in range(16)]
        target[pl.ds(pl.multiple_of(i * 16, 16), 16), :] = jnp.concatenate(rows, 0).astype(BF16)
        return carry

    lax.fori_loop(0, target.shape[0] // 16, body, 0, unroll=2)


def listed(ids, first):
    def at(i):
        block = first + lax.shift_right_logical(i, 3)
        start = (i & 7) * 16
        return lambda u: ids[block, start + u]

    return at


def placed(place, part, towers, own, slots):
    per = slots // 16

    def at(i):
        pair = lax.shift_right_logical(i, log2(per))
        tower = lax.shift_right_logical(pair, log2(own))
        lane = tower * (LANES // towers) + part * own + (pair & (own - 1))
        start = (i & (per - 1)) * 16
        return lambda u: place[start + u, lane]

    return at


def send_rows(plane, me, part, ids, table, sent, got, wide, out_sems, in_sems):
    capacity = sent.shape[1]
    copies = []
    for k, peer in enumerate(partners(me, plane)):
        gather_rows(listed(ids.at[peer], 0), table, sent.at[peer])
        copies.append(send(sent.at[peer], got.at[me], out_sems.at[k], in_sems.at[k], (peer, part)))
    gather_rows(listed(ids.at[me], 0), table, sent.at[me])
    wide[pl.ds(pl.multiple_of(me * capacity, capacity), capacity), :] = sent[me].astype(F32)
    return copies


def take_rows(plane, me, part, dims, copies, place, got, wide, out):
    capacity = got.shape[1]
    for copy, peer in zip(copies, partners(me, plane)):
        copy.wait_recv()
        wide[pl.ds(pl.multiple_of(peer * capacity, capacity), capacity), :] = got[peer].astype(F32)
    gather_rows(placed(place, part, *dims), wide, out)


def refetch_kernel(plane, dims, ids, place, table, out, sent, got, wide, out_sems, in_sems):
    me, part = enter(plane, 0)
    copies = send_rows(plane, me, part, ids, table, sent, got, wide, out_sems, in_sems)
    take_rows(plane, me, part, dims, copies, place, got, wide, out)
    for copy in copies:
        copy.wait_send()


def fetch_kernel(
    plane,
    line,
    dims,
    capacity,
    owner_in,
    row_in,
    count,
    positive,
    far_table,
    far_qkv,
    far_wout,
    out,
    got_own,
    got_lists,
    weights,
    inverse,
    own_place,
    own_lists,
    own_small,
    lists,
    table,
    w_qkv,
    w_out,
    place,
    ids,
    sent,
    got,
    wide,
    list_out,
    list_in,
    out_sems,
    in_sems,
    far_out,
    far_in,
    side_out,
    side_in,
    near_out,
    near_in,
    own_sems,
    load_sems,
):
    loads = [
        pltpu.make_async_copy(source, target, load_sems.at[j])
        for j, (source, target) in enumerate(((far_qkv, w_qkv), (far_wout, w_out), (far_table, table)))
    ]
    for copy in loads:
        copy.start()
    me, part = announce(plane, line)
    core = lax.rem(me, 2)
    half = lax.rem(me // 2, 2)
    sibling = me + 1 - 2 * core
    partner = me + 2 - 4 * half
    batch = positive.shape[1]
    slots = Slots(plane, line, owner_in, row_in, count)
    make_own_lists(slots, plane, capacity, sent.shape[1], table.shape[0], own_lists, own_place, own_small)
    places = pltpu.make_async_copy(own_small, place, own_sems.at[0])
    places.start()
    for copy in loads[:2]:
        copy.wait()
    rows = weights.shape[3] // 2
    for c in range(3):
        weights[part, :, c] = w_qkv[:, c].astype(BF16)
    for j in range(2):
        weights[part, :, 3, j * LANES : (j + 1) * LANES, :] = w_out[:, :, j * LANES : (j + 1) * LANES].astype(BF16)
    quarter = lambda m, h: weights.at[m, core, :, pl.ds(pl.multiple_of(h * rows, rows), rows), :]
    await_others(plane, line)
    far, asked, told = [], [], []
    for k in range(1, line):
        peer = lax.rem(part + k, line)
        far.append(send(quarter(part, half), quarter(part, half), far_out.at[k], far_in.at[k], (me, peer)))
    for k in range(1, plane):
        peer = lax.rem(me + k, plane)
        asked.append(send(own_lists.at[peer], got_own.at[me], list_out.at[0, k], list_in.at[0, k], (peer, part)))
    make_lists(slots, plane, capacity, batch, line, positive, lists, inverse)
    for k in range(1, plane):
        peer = lax.rem(me + k, plane)
        told.append(send(lists.at[peer], got_lists.at[me], list_out.at[1, k], list_in.at[1, k], (peer, part)))
    mine = [
        pltpu.make_async_copy(own_lists.at[me], got_own.at[me], own_sems.at[1]),
        pltpu.make_async_copy(lists.at[me], got_lists.at[me], own_sems.at[2]),
    ]
    for copy in mine:
        copy.start()
    for copy in asked:
        copy.wait()
    mine[0].wait()
    numbers = pltpu.make_async_copy(got_own.at[:, 0 : ids.shape[1]], ids, own_sems.at[3])
    numbers.start()
    for copy in (numbers, places, loads[2]):
        copy.wait()
    copies = send_rows(plane, me, part, ids, table, sent, got, wide, out_sems, in_sems)
    sides, near = [], []
    for k in range(1, line):
        peer = lax.rem(part - k + line, line)
        far[k - 1].wait_recv()
        at = quarter(peer, half)
        sides.append(send(at, at, side_out.at[k], side_in.at[k], (partner, part)))
        near.append(send(at, at, near_out.at[0, k], near_in.at[0, k], (sibling, part)))
    take_rows(plane, me, part, dims, copies, place, got, wide, out)
    for k in range(1, line):
        peer = lax.rem(part - k + line, line)
        sides[k - 1].wait_recv()
        at = quarter(peer, 1 - half)
        near.append(send(at, at, near_out.at[1, k], near_in.at[1, k], (sibling, part)))
    mine[1].wait()
    for copy in copies + far + sides:
        copy.wait_send()
    for copy in told + near:
        copy.wait()


def add_rows(ids, count, blocks, grads, total, fresh):
    height = total.shape[0]
    rows = []
    for block in blocks:
        for r in range(-(-count // LANES)):
            rows.append(ids[block, r : r + 1, 0 : min(LANES, count - r * LANES)])
    numbers = jnp.concatenate(rows, 1)
    values = jnp.concatenate([ref[...] for ref in grads], 0)
    turned = jnp.transpose(jnp.broadcast_to(numbers.astype(F32), (8, numbers.shape[1])), (1, 0))[:, 0:1]
    upper = turned >= height
    none = jnp.zeros_like(values)
    values = jnp.concatenate([jnp.where(upper, none, values), jnp.where(upper, values, none)], 1)
    low = jnp.where(numbers >= 0, numbers & (height - 1), -1)
    step = min(height, 1024)

    def body(i, carry):
        at = pl.multiple_of(i * step, step)
        hot = jnp.where(low - at == iota((step, low.shape[1]), 0), 1.0, 0.0).astype(BF16)
        part = nn(hot, values)
        at = pl.ds(at, step)
        total[at, :] = part if fresh else total[at, :] + part
        return carry

    lax.fori_loop(0, height // step, body, 0)


def tail_kernel(
    plane,
    line,
    capacity,
    cuts,
    tokens,
    ids,
    rows,
    summed,
    gain,
    table,
    dense_all,
    norm_sq,
    gain_all,
    wide,
    sent,
    back,
    total,
    got,
    gains,
    along,
    across,
    out_sems,
    in_sems,
    far_out,
    far_in,
    gain_out,
    gain_in,
    along_out,
    along_in,
    across_out,
    across_in,
    chip_out,
    chip_in,
    near_out,
    near_in,
):
    me, part = enter(plane, line)
    chips = plane // 2
    core = lax.rem(me, 2)
    chip = me // 2
    sibling = me + 1 - 2 * core
    far = []
    split_cuts, (whole_at, whole_rows), (last_at, last_rows) = cuts
    for k in range(1, line):
        peer = lax.rem(part + k, line)
        to = 0
        for j, (at, count) in enumerate(split_cuts):
            begin = pl.multiple_of(at + peer * count, 16)
            far.append(
                send(summed.at[pl.ds(begin, count)], got.at[part, to : to + count], far_out.at[j, k], far_in.at[j, k], (me, peer))
            )
            to += count
        target = got.at[part, to : to + whole_rows]
        source = summed.at[whole_at : whole_at + whole_rows]
        far.append(send(source, target, far_out.at[2, k], far_in.at[2, k], (me, peer)))
        far.append(send(gain, gains.at[part], gain_out.at[k], gain_in.at[k], (me, peer)))
    gains[part] = gain[...]
    split_rows = sum(count for _, count in split_cuts)
    done = split_rows + whole_rows
    dense_all[me, done:, :] = summed[last_at : last_at + last_rows, :]
    spread, near = [], []

    def gather_shares(stage, begin, end):
        block = dense_all.at[me, begin:end]
        for k in range(1, chips):
            to = 2 * lax.rem(chip + k, chips) + core
            spread.append(send(block, block, chip_out.at[stage, k], chip_in.at[stage, k], (to, part)))
        near.append(send(block, block, near_out.at[stage, 0], near_in.at[stage, 0], (sibling, part)))

    def pass_shares(stage, begin, end):
        for k in range(1, chips):
            peer = 2 * lax.rem(chip - k + chips, chips) + core
            spread[stage * (chips - 1) + k - 1].wait_recv()
            block = dense_all.at[peer, begin:end]
            near.append(send(block, block, near_out.at[stage, k], near_in.at[stage, k], (sibling, part)))

    gather_shares(0, done, done + last_rows)
    wide[...] = rows[...].astype(F32)
    copies = []
    others = partners(me, plane)
    for k, peer in enumerate(others):
        gather_rows(listed(tokens.at[peer], 0), wide, sent.at[peer])
        copies.append(send(sent.at[peer], back.at[me], out_sems.at[k], in_sems.at[k], (peer, part)))
    gather_rows(listed(tokens.at[me], 0), wide, sent.at[me])
    to = 0
    for at, count in split_cuts:
        got[part, to : to + count] = summed[pl.ds(pl.multiple_of(at + part * count, 16), count), :]
        to += count
    got[part, to : to + whole_rows] = summed[whole_at : whole_at + whole_rows, :]
    for copy in far:
        copy.wait()
    share = got[0].astype(F32)
    for m in range(1, line):
        share = share + got[m].astype(F32)
    dense_all[me, 0 : to + whole_rows, :] = share.astype(BF16)
    group = max(1, 1280 // capacity)
    order = [me] + others
    for first in range(0, plane, group):
        blocks = order[first : first + group]
        grads = [sent.at[blocks[0]] if first == 0 else back.at[blocks[0]]] + [back.at[block] for block in blocks[1:]]
        for k in range(max(first, 1), min(first + group, plane)):
            copies[k - 1].wait_recv()
        if first + group >= plane:
            gather_shares(1, 0, done)
            pass_shares(0, done, done + last_rows)
        add_rows(ids, capacity, blocks, grads, total, first == 0)
    square = jnp.zeros((8, LANES), F32)
    for begin, count, weight in ((0, to, 1.0), (to, whole_rows, 1.0 / line), (to + whole_rows, last_rows, 1.0)):
        block = dense_all[me, begin : begin + count, :].astype(F32)
        square = square + weight * jnp.sum((block * block).reshape(count // 8, 8, LANES), 0)
    height = total.shape[0]

    def settle(i, carry):
        at = pl.multiple_of(i * 32, 32)
        for half in range(2):
            block = total[pl.ds(at, 32), half * LANES : (half + 1) * LANES]
            table[pl.ds(at + half * height, 32), :] = block
            block = block * block
            for r in range(4):
                carry = carry + block[r * 8 : (r + 1) * 8, :]
        return carry

    table_sq = lax.fori_loop(0, height // 32, settle, jnp.zeros((8, LANES), F32))
    across[me] = square + table_sq * (1.0 / line)
    tiny = [
        send(across.at[me], across.at[me], across_out.at[k], across_in.at[k], (lax.rem(me + k, plane), part))
        for k in range(1, plane)
    ]
    for copy in tiny:
        copy.wait()
    sums = across[0]
    for d in range(1, plane):
        sums = sums + across[d]
    along[part] = sums
    peers = [lax.rem(part + k, line) for k in range(1, line)]
    tiny = [
        send(along.at[part], along.at[part], along_out.at[k], along_in.at[k], (me, peer)) for k, peer in enumerate(peers)
    ]
    pass_shares(1, 0, done)
    gain_sum = gains[0]
    for m in range(1, line):
        gain_sum = gain_sum + gains[m]
    gain_all[...] = gain_sum
    for copy in tiny:
        copy.wait()
    sums = along[0]
    for m in range(1, line):
        sums = sums + along[m]
    norm_sq[...] = jnp.broadcast_to(jnp.sum(sums + gain_sum * gain_sum), norm_sq.shape)
    for copy in copies + spread:
        copy.wait_send()
    for copy in near:
        copy.wait()


def chain(index, values):
    out = jnp.full(index.shape, values[0], values[0].dtype)
    for k in range(1, len(values)):
        out = jnp.where(index >= k, values[k], out)
    return out


def two_by_two(parts):
    blocks = [(c, m) for m in range(parts) for c in range(2)] + [(2, m) for m in range(parts)]
    return list(zip(blocks[::2], blocks[1::2]))


def forward_tower(tower, slots, cnt, x, w_in, gain, w_all, pooled, pm_out, normed_out, qkv, prob, a_out, pm_acc):
    pairs = pooled.shape[1]
    first = lax.axis_index("mp") * pairs
    parts = w_all.shape[0]
    per = LANES // slots
    groups = pairs // per
    heads = 2 * parts
    xs = x[tower]
    hidden = nn(xs, w_in[tower].astype(BF16))
    inverse = lax.rsqrt(jnp.mean(hidden * hidden, -1, keepdims=True) + EPS)
    normed = (hidden * inverse * gain[tower : tower + 1, :]).astype(BF16)
    normed_out[tower] = normed
    for (c, m), (d, n) in two_by_two(parts):
        both = jnp.concatenate([w_all[m, tower, c], w_all[n, tower, d]], 1)
        both = nn(normed, both).astype(BF16)
        qkv[tower, c * parts + m] = both[:, :LANES]
        qkv[tower, d * parts + n] = both[:, LANES:]
    lane = iota((LANES, LANES), 1)
    line = iota((LANES, LANES), 0)
    shift = slots.bit_length() - 1
    pair_r, pair_s = lax.shift_right_logical(lane, shift), lax.shift_right_logical(line, shift)
    same = pair_r == pair_s
    halves = [lane < DH, lane >= DH]
    own_head = iota((per * heads, LANES), 0) & (heads - 1)

    def group(g, carry):
        counts = [cnt[tower, first + g * per + k] for k in range(per)]
        live_r = same & ((lane & (slots - 1)) < chain(pair_r, counts))
        live_s = (line & (slots - 1)) < chain(pair_s, counts)
        rows = pl.ds(pl.multiple_of(g * LANES, LANES), LANES)
        sums = []
        for m in range(parts):
            query, key = qkv[tower, m, rows, :], qkv[tower, parts + m, rows, :]
            for half in range(2):
                scores = nt(jnp.where(halves[half], query, jnp.zeros_like(query)), key) * 0.125
                scores = jnp.where(live_r, scores, -1000000000.0)
                expo = jnp.exp(scores - jnp.max(scores, 1, keepdims=True))
                p = (expo * (1.0 / jnp.sum(expo, 1, keepdims=True))).astype(BF16)
                prob[tower, g, 2 * m + half] = p
                sums.append(jnp.sum(jnp.where(live_s, p.astype(F32), 0.0), 0, keepdims=True))
        sums = jnp.concatenate(sums, 0)
        pair_l = lax.shift_right_logical(iota((heads, LANES), 1), shift)
        stack = jnp.concatenate([jnp.where(pair_l == k, sums, 0.0) for k in range(per)], 0).astype(BF16)
        a_out[tower, g] = stack
        for m in range(parts):
            mix = nn(stack, qkv[tower, 2 * parts + m, rows, :])
            head = iota((per * heads, LANES), 1) // DH + 2 * m
            mix = jnp.where(own_head == head, mix, 0.0)
            pm_acc[g, :, m * LANES : (m + 1) * LANES] = jnp.concatenate(
                [jnp.sum(mix[k * heads : (k + 1) * heads], 0, keepdims=True) for k in range(per)], 0
            )
        return carry

    lax.fori_loop(0, groups, group, 0)
    pm = jnp.concatenate([pm_acc[g] for g in range(groups)], 0).astype(BF16)
    pm_out[tower] = pm
    every = [cnt[tower, first + k] for k in range(pairs)]
    tokens = iota((pairs, pairs * slots), 1)
    mine = lax.shift_right_logical(tokens, shift) == iota(tokens.shape, 0)
    live = mine & ((tokens & (slots - 1)) < chain(iota(tokens.shape, 0), every))
    high, low = split(nn(live.astype(BF16), xs))
    w = w_in[tower].astype(BF16)
    total = nn(high, w) + nn(low, w)
    sides = []
    for j in range(2):
        side = total[:, j * LANES : (j + 1) * LANES]
        for m in range(parts):
            side = side + nn(pm[:, m * LANES : (m + 1) * LANES], w_all[m, tower, 3, j * LANES : (j + 1) * LANES, :])
        sides.append(side)
    total = jnp.concatenate(sides, 1)
    count = chain(iota(total.shape, 0), every).astype(F32)
    pooled[tower] = (total / count).astype(BF16)


def put(target, size, first, value):
    done = 0
    while done < value.shape[0]:
        share, inside = divmod(first + done, size)
        count = min(size - inside, value.shape[0] - done)
        target[share // 2, share % 2, inside : inside + count, :] = value[done : done + count]
        done += count


def backward_tower(
    tower, slots, cnt, x, w_in, gain, w_all, normed_in, qkv, prob, a_in, pm_in, dpooled, demb, d_in, d_gain, d_qkv, d_out, dqkv
):
    pairs, width = dpooled.shape[1:]
    parts = w_all.shape[0]
    per = LANES // slots
    groups = pairs // per
    heads = 2 * parts
    shift = slots.bit_length() - 1
    tokens = pairs * slots
    first = lax.axis_index("mp") * pairs
    every = [cnt[tower, first + k] for k in range(pairs)]
    count = chain(iota((pairs, width), 0), every).astype(F32)
    dsum = dpooled[tower].astype(F32) / count
    branch = dsum.astype(BF16)
    dmix = []
    for m in range(parts):
        grad = tn(pm_in[tower, :, m * LANES : (m + 1) * LANES], branch).astype(BF16)
        for j in range(width // LANES):
            begin = (tower * (width // LANES) + j) * LANES
            put(d_out.at[m], d_out.shape[3], begin, grad[:, j * LANES : (j + 1) * LANES])
        mix = 0.0
        for j in range(2):
            cut = slice(j * LANES, (j + 1) * LANES)
            mix = mix + nt(branch[:, cut], w_all[m, tower, 3, cut, :])
        dmix.append(mix)
    lane = iota((LANES, LANES), 1)
    line = iota((LANES, LANES), 0)
    pair_s = lax.shift_right_logical(line, shift)
    halves = [lane < DH, lane >= DH]
    own_head = iota((per * heads, LANES), 0) & (heads - 1)
    own_pair = lax.shift_right_logical(iota((per * heads, LANES), 0), heads.bit_length() - 1)
    token_pair = lax.shift_right_logical(iota((per * heads, LANES), 1), shift)
    for g in range(groups):
        rows = slice(g * LANES, (g + 1) * LANES)
        live_s = (line & (slots - 1)) < chain(pair_s, every[g * per : (g + 1) * per])
        scale = jnp.where(live_s, 0.125, 0.0)
        dots = jnp.zeros((per * heads, LANES), F32)
        stacks = []
        for m in range(parts):
            cut = dmix[m][g * per : (g + 1) * per]
            spread = jnp.concatenate([jnp.broadcast_to(cut[k : k + 1], (heads, LANES)) for k in range(per)], 0)
            head = iota((per * heads, LANES), 1) // DH + 2 * m
            stack = jnp.where(own_head == head, spread, 0.0).astype(BF16)
            stacks.append(stack)
            dots = dots + nt(stack, qkv[tower, 2 * parts + m, rows, :])
        dots = jnp.where(own_pair == token_pair, dots, 0.0)
        pull = dots[0:heads]
        for k in range(1, per):
            pull = pull + dots[k * heads : (k + 1) * heads]
        for m in range(parts):
            query, key = qkv[tower, m, rows, :], qkv[tower, parts + m, rows, :]
            none = jnp.zeros_like(query)
            dq = jnp.zeros((LANES, LANES), F32)
            dk = jnp.zeros((LANES, LANES), F32)
            for half in range(2):
                h = 2 * m + half
                p = prob[tower, g, h].astype(F32)
                t = p * pull[h : h + 1, :]
                ds = ((t - p * jnp.sum(t, 1, keepdims=True)) * scale).astype(BF16)
                dq = dq + nn(ds, jnp.where(halves[half], key, none))
                dk = dk + tn(ds, jnp.where(halves[half], query, none))
            dqkv[m, rows, :] = dq.astype(BF16)
            dqkv[parts + m, rows, :] = dk.astype(BF16)
            dqkv[2 * parts + m, rows, :] = tn(a_in[tower, g], stacks[m]).astype(BF16)
    normed = normed_in[tower]
    dnormed = jnp.zeros((tokens, width), F32)
    for (c, m), (d, n) in two_by_two(parts):
        both = jnp.concatenate([dqkv[c * parts + m], dqkv[d * parts + n]], 1)
        dnormed = dnormed + nt(both, jnp.concatenate([w_all[m, tower, c], w_all[n, tower, d]], 1))
        both = tn(normed, both).astype(BF16)
        put(d_qkv.at[m], d_qkv.shape[3], (tower * 3 + c) * width, both[:, :LANES])
        put(d_qkv.at[n], d_qkv.shape[3], (tower * 3 + d) * width, both[:, LANES:])
    dnormed = dnormed.astype(BF16).astype(F32)
    xs = x[tower]
    w = w_in[tower].astype(BF16)
    hidden = nn(xs, w)
    inverse = lax.rsqrt(jnp.mean(hidden * hidden, -1, keepdims=True) + EPS)
    unit = hidden * inverse
    grad = jnp.sum(dnormed * unit, 0, keepdims=True)
    for j in range(width // LANES):
        r = tower * (width // LANES) + j
        d_gain[r : r + 1, :] = grad[:, j * LANES : (j + 1) * LANES]
    scaled = dnormed * gain[tower : tower + 1, :]
    dh = inverse * (scaled - unit * jnp.mean(scaled * unit, -1, keepdims=True))
    spread = jnp.broadcast_to(dsum[:, None, :], (pairs, slots, width))
    slot = iota((pairs, slots, width), 1)
    counts = chain(iota((pairs, slots, width), 0), every)
    spread = jnp.where(slot < counts, spread, 0.0).reshape(tokens, width)
    dhidden = (spread + dh).astype(BF16)
    grad = tn(xs, dhidden).astype(BF16)
    for j in range(width // LANES):
        begin = (tower * (width // LANES) + j) * xs.shape[1]
        put(d_in, d_in.shape[2], begin, grad[:, j * LANES : (j + 1) * LANES])
    demb[...] = nt(dhidden, w).astype(BF16)


def gelu_parts(v):
    c = 0.7978845608028654
    inner = jnp.tanh(c * (v + 0.044715 * (v * v * v)))
    value = 0.5 * v * (1.0 + inner)
    slope = 0.5 * (1.0 + inner) + 0.5 * v * (1.0 - inner * inner) * (c * (1.0 + 3.0 * 0.044715 * (v * v)))
    return value, slope


def upper_layers(
    me,
    part,
    plane,
    line,
    pooled,
    log_prior,
    item_qid,
    lists,
    positive,
    dpooled,
    d_one,
    d_two,
    d_three,
    loss,
    pooled_all,
    second_send,
    second_got,
    vec,
    dsec_send,
    dsec_all,
    dpool_send,
    dpool_got,
    out_sems,
    in_sems,
    vec_out,
    vec_in,
    w_one,
    w_two,
    w_three,
    loads,
    second_mine,
    dpool_mine,
    prior_col,
):
    towers, own, width = pooled.shape
    per = lists.shape[1] - 8
    rows = own * line
    pairs = rows * plane
    peers = [lax.rem(part + k, line) for k in range(1, line)]

    pooled_all[:, part] = pooled[...]
    first = [
        send(pooled_all.at[:, part], pooled_all.at[:, part], out_sems.at[0, k], in_sems.at[0, k], (me, peers[k]))
        for k in range(line - 1)
    ]
    for copy in loads:
        copy.wait()
    one = [w_one[t].astype(BF16) for t in range(towers)]
    two = [w_two[t].astype(BF16) for t in range(towers)]
    three = [w_three[t].astype(BF16) for t in range(towers)]
    qid = item_qid[...]
    hot = (lax.shift_right_logical(qid, 7) == iota((log_prior.shape[0], pairs), 0)).astype(BF16)
    high, rest = log_prior[...].astype(BF16), log_prior[...]
    rest = rest - high.astype(F32)
    middle, low = split(rest)
    table = tn(high, hot) + tn(middle, hot) + tn(low, hot)
    prior_row = jnp.sum(jnp.where((qid & 127) == iota((LANES, pairs), 0), table, 0.0), 0, keepdims=True)
    prior_col[...] = jnp.transpose(jnp.broadcast_to(prior_row, (8, pairs)), (1, 0))
    pos_row = jnp.concatenate([lists[d, per : per + 1, 0:rows] for d in range(plane)], 1)
    pos_own = chain(iota((own, pairs), 0), [positive[part * own + k] for k in range(own)])
    for copy in first:
        copy.wait()
    act_one, slope_one, pools = [], [], []
    for t in range(towers):
        pools.append(pooled_all[t].reshape(rows, width))
        value, slope = gelu_parts(nn(pools[t], one[t]))
        act_one.append(value.astype(BF16))
        slope_one.append(slope)
        partial = nn(act_one[t], two[t]).reshape(line, own, -1)
        second_mine[t] = partial
        second_send[t] = partial.astype(BF16)
    second = [
        send(
            second_send.at[:, peers[k]], second_got.at[:, part], out_sems.at[1, k], in_sems.at[1, k], (me, peers[k])
        )
        for k in range(line - 1)
    ]
    for copy in second:
        copy.wait()
    act_two, slope_two, third, length, vectors = [], [], [], [], []
    for t in range(towers):
        total = second_mine[t, part]
        for peer in peers:
            total = total + second_got[t, peer].astype(F32)
        value, slope = gelu_parts(total)
        act_two.append(value.astype(BF16))
        slope_two.append(slope)
        third.append(nn(act_two[t], three[t]))
        length.append(lax.rsqrt(jnp.sum(third[t] * third[t], -1, keepdims=True) + EPS))
        vectors.append((third[t] * length[t]).astype(BF16))
        vec[t, me, part] = vectors[t]
    along = [
        send(vec.at[:, me, part], vec.at[:, me, part], out_sems.at[2, k], in_sems.at[2, k], (me, peers[k]))
        for k in range(line - 1)
    ]
    for copy in along:
        copy.wait()
    chips = plane // 2
    core = lax.rem(me, 2)
    chip = me // 2
    sibling = me + 1 - 2 * core
    near = [send(vec.at[:, me], vec.at[:, me], vec_out.at[0], vec_in.at[0], (sibling, part))]
    across = []
    for k in range(1, chips):
        other = 2 * lax.rem(chip + k, chips) + core
        across.append(send(vec.at[:, me], vec.at[:, me], vec_out.at[k], vec_in.at[k], (other, part)))
    for k in range(1, chips):
        peer = 2 * lax.rem(chip - k + chips, chips) + core
        across[k - 1].wait_recv()
        sems = vec_out.at[chips + k], vec_in.at[chips + k]
        near.append(send(vec.at[:, peer], vec.at[:, peer], *sems, (sibling, part)))
    for copy in across:
        copy.wait_send()
    for copy in near:
        copy.wait()

    queries = vec[0].reshape(pairs, width)
    items = vec[1].reshape(pairs, width)
    logits = INV_TEMP * nt(items, queries) - prior_col[:, 0:1]
    peak = jnp.max(logits, 0, keepdims=True)
    log_total = peak + jnp.log(jnp.sum(jnp.exp(logits - peak), 0, keepdims=True))
    picked = jnp.where(iota((pairs, pairs), 0) == pos_row, logits, 0.0)
    gap = log_total - jnp.sum(picked, 0, keepdims=True)
    loss[0, 0] = jnp.sum(gap)
    ahead = me * rows + part * own
    mine = INV_TEMP * nt(vectors[0], items) - prior_row
    top = jnp.max(mine, 1, keepdims=True)
    expo = jnp.exp(mine - top)
    chance = expo / jnp.sum(expo, 1, keepdims=True)
    target = (iota(mine.shape, 1) == pos_own).astype(F32)
    dlog = ((chance - target) / pairs).astype(BF16)
    dvec = [(INV_TEMP * nn(dlog, items)).astype(BF16)]
    own_prior = prior_col[pl.ds(pl.multiple_of(ahead, own), own), 0:1]
    theirs = INV_TEMP * nt(vectors[1], queries) - own_prior
    target = (iota(theirs.shape, 0) + ahead == pos_row).astype(F32)
    dlog = ((jnp.exp(theirs - log_total) - target) / pairs).astype(BF16)
    dvec.append((INV_TEMP * nn(dlog, queries)).astype(BF16))

    dthirds = []
    for t in range(towers):
        dv = dvec[t].astype(F32)
        inner = jnp.sum(dv * third[t], -1, keepdims=True)
        dthird = (length[t] * dv - third[t] * (length[t] * length[t] * length[t] * inner)).astype(BF16)
        dact = nt(dthird, three[t]).astype(BF16).astype(F32)
        dsec_all[t, part] = (dact * slope_two[t]).astype(BF16)
        dthirds.append(dthird)
    spread = [
        send(dsec_all.at[:, part], dsec_all.at[:, part], out_sems.at[3, k], in_sems.at[3, k], (me, peers[k]))
        for k in range(line - 1)
    ]
    for t in range(towers):
        grad = tn(act_two[t], dthirds[t]).astype(BF16)
        for j in range(width // LANES):
            put(d_three, d_three.shape[2], (t * (width // LANES) + j) * grad.shape[0], grad[:, j * LANES : (j + 1) * LANES])
    for copy in spread:
        copy.wait()
    dfirsts = []
    for t in range(towers):
        dsecond = dsec_all[t].reshape(rows, -1)
        dact = nt(dsecond, two[t]).astype(BF16).astype(F32)
        dfirst = (dact * slope_one[t]).astype(BF16)
        partial = nt(dfirst, one[t]).reshape(line, own, width)
        dpool_mine[t] = partial
        dpool_send[t] = partial.astype(BF16)
        dfirsts.append(dfirst)
    back = [
        send(dpool_send.at[:, peers[k]], dpool_got.at[:, part], out_sems.at[4, k], in_sems.at[4, k], (me, peers[k]))
        for k in range(line - 1)
    ]
    for t in range(towers):
        dsecond = dsec_all[t].reshape(rows, -1)
        for grads, grad in ((d_two, tn(act_one[t], dsecond)), (d_one, tn(pools[t], dfirsts[t]))):
            grad = grad.astype(BF16)
            wide = grad.shape[1] // LANES
            for j in range(wide):
                begin = (t * wide + j) * grad.shape[0]
                put(grads, grads.shape[2], begin, grad[:, j * LANES : (j + 1) * LANES])
    for copy in back:
        copy.wait()
    for t in range(towers):
        total = dpool_mine[t, part]
        for peer in peers:
            total = total + dpool_got[t, peer].astype(F32)
        dpooled[t] = total.astype(BF16)


def towers_kernel(
    plane,
    line,
    slots,
    cnt,
    x,
    w_in,
    gain,
    w_all,
    far_one,
    far_two,
    far_three,
    log_prior,
    item_qid,
    lists,
    positive,
    out,
    summed,
    gain_sum,
    loss,
    pooled,
    pm,
    normed,
    qkv,
    prob,
    a_in,
    pm_acc,
    upper_scratch,
    w_one,
    w_two,
    w_three,
    load_sems,
    dpooled,
    d_three,
    d_one,
    d_two,
    d_qkv,
    d_out,
    d_in,
    d_gain,
    dqkv,
    near_split,
    near_whole,
    half,
    got,
    got_late,
    gains,
    far_out,
    far_in,
    near_out,
    near_in,
    sum_out,
    sum_in,
    gain_out,
    gain_in,
):
    loads = [
        pltpu.make_async_copy(source, target, load_sems.at[j])
        for j, (source, target) in enumerate(((far_one, w_one), (far_two, w_two), (far_three, w_three)))
    ]
    for copy in loads:
        copy.start()
    me, part = announce(plane, line)
    for t in range(x.shape[0]):
        forward_tower(t, slots, cnt, x, w_in, gain, w_all, pooled, pm, normed, qkv, prob, a_in, pm_acc)
    await_others(plane, line)
    upper_layers(
        me,
        part,
        plane,
        line,
        pooled,
        log_prior,
        item_qid,
        lists,
        positive,
        dpooled,
        d_one,
        d_two,
        d_three,
        loss,
        *upper_scratch[:-3],
        w_one,
        w_two,
        w_three,
        loads,
        *upper_scratch[-3:],
    )
    chips = plane // 2
    core = lax.rem(me, 2)
    chip = me // 2
    sibling = me + 1 - 2 * core
    towers, tokens = x.shape[:2]
    late, early = (d_in,), (d_three, d_one, d_two)
    nears = [send(grad.at[:, 1 - core], near_whole[1 + j], near_out.at[j], near_in.at[j], (sibling, part)) for j, grad in enumerate(early)]
    copies = []

    def tower(t):
        demb = out.at[part, t * tokens : (t + 1) * tokens]
        backward_tower(
            t, slots, cnt, x, w_in, gain, w_all, normed, qkv, prob, a_in, pm, dpooled, demb, d_in, d_gain, d_qkv, d_out, dqkv
        )
        for k in range(1, line):
            peer = lax.rem(part + k, line)
            copies.append(send(demb, demb, far_out.at[t, k], far_in.at[t, k], (me, peer)))

    def whole(c, at, grad, near):
        rows = grad.shape[2]
        half[c, at : at + rows, :] = (grad[c, core].astype(F32) + near[c].astype(F32)).astype(BF16)
        return at + rows

    def exchange(begin, end, target, sems):
        sums = []
        for k in range(1, chips):
            to = lax.rem(chip + k, chips)
            source = half.at[to, begin:end]
            sums.append(send(source, target.at[k - 1], sum_out.at[sems, k], sum_in.at[sems, k], (2 * to + core, part)))
        return sums

    def collect(begin, end, target, sums):
        for copy in sums:
            copy.wait()
        total = half[chip, begin:end, :].astype(F32)
        for k in range(chips - 1):
            total = total + target[k].astype(F32)
        summed[begin:end, :] = total.astype(BF16)

    first = line * (d_qkv.shape[3] + d_out.shape[3]) + d_in.shape[2]
    d_gain[...] = jnp.zeros_like(d_gain)
    tower(0)
    for copy in nears:
        copy.wait()
    for c in range(chips):
        at = first
        for j, grad in enumerate(early):
            at = whole(c, at, grad, near_whole[1 + j])
    last = at
    sums = exchange(first, last, got, 0)
    for t in range(1, towers):
        tower(t)
    nears = []
    for j, grad in enumerate((d_qkv, d_out)):
        nears.append(send(grad.at[:, :, 1 - core], near_split[j], near_out.at[3 + j], near_in.at[3 + j], (sibling, part)))
    nears.append(send(d_in.at[:, 1 - core], near_whole[0], near_out.at[5], near_in.at[5], (sibling, part)))
    for k in range(1, plane):
        peer = lax.rem(me + k, plane)
        copies.append(send(d_gain, gains.at[me], gain_out.at[k], gain_in.at[k], (peer, part)))
    gains[me] = d_gain[...]
    for copy in nears:
        copy.wait()
    for c in range(chips):
        at = 0
        for grad, near in zip((d_qkv, d_out), near_split):
            rows = grad.shape[3]
            for m in range(line):
                total = grad[m, c, core].astype(F32) + near[m, c].astype(F32)
                half[c, at : at + rows, :] = total.astype(BF16)
                at += rows
        whole(c, at, d_in, near_whole[0])
    late_sums = exchange(0, first, got_late, 1)
    collect(first, last, got, sums)
    collect(0, first, got_late, late_sums)
    for copy in copies:
        copy.wait()
    total = gains[0]
    for d in range(1, plane):
        total = total + gains[d]
    gain_sum[...] = total


def update(weight, grad, moment, average, factor, rate):
    clipped = grad * factor
    moment_new = MOMENTUM * moment + clipped
    weight_new = weight - rate * (clipped + MOMENTUM * moment_new)
    average_new = AVERAGE_DECAY * average + (1.0 - AVERAGE_DECAY) * weight_new
    return [weight_new, moment_new, average_new]


def update_kernel(blocks, norm_sq, table_grad, dense, gain, *refs):
    arrays = 3 * 8
    sources, targets, norm = refs[:arrays], refs[arrays : 2 * arrays], refs[2 * arrays]
    held, in_sems, out_sems = refs[2 * arrays + 1 : 3 * arrays + 1], refs[-2], refs[-1]
    loads = [pltpu.make_async_copy(sources[k], held[k], in_sems.at[k]) for k in range(arrays)]
    starts = {}
    for k, size, _, _ in blocks:
        starts[k] = sum(other[1] for other in blocks[: k - 1])
    order = sorted(blocks, key=lambda block: -block[1])
    for k in [0] + [block[0] for block in order] + [arrays // 3 - 1]:
        for copy in loads[3 * k : 3 * k + 3]:
            copy.start()
    root = jnp.sqrt(norm_sq[...])
    norm[0, 0] = jnp.max(root)
    factor = jnp.minimum(1.0, CLIP_NORM / root[0:1, :])
    stores = []

    def finish(k):
        for j in range(3 * k, 3 * k + 3):
            copy = pltpu.make_async_copy(held[j], targets[j], out_sems.at[j])
            copy.start()
            stores.append(copy)

    def apply(k, rows, lanes, grad, rate):
        cells = [ref.at[rows, lanes] for ref in held[3 * k : 3 * k + 3]]
        new = update(cells[0][...], grad, cells[1][...], cells[2][...], factor, rate)
        for cell, value in zip(cells, new):
            cell[...] = value

    def wait(k):
        for copy in loads[3 * k : 3 * k + 3]:
            copy.wait()

    def rows(i, carry):
        at = pl.ds(pl.multiple_of(i * 64, 64), 64)
        apply(0, at, slice(0, LANES), table_grad[at, :], ROW_RATE)
        return carry

    wait(0)
    lax.fori_loop(0, table_grad.shape[0] // 64, rows, 0, unroll=2)
    finish(0)
    for k, size, height, wide in order:
        wait(k)
        at = starts[k]
        total = dense.shape[0] * size
        step = math.gcd(size, 64)
        for first in range(0, total, min(size, height)):
            count = min(size, height)
            share, inside = first // size, first % size
            block, begin = first // height, first % height
            t, j = block // wide, block % wide
            top = t * height + begin

            def piece(i, carry):
                take = pl.ds(pl.multiple_of(at + inside + i * step, 16), step)
                rows = pl.ds(pl.multiple_of(top + i * step, 16), step)
                grad = dense[share, take, :].astype(F32)
                apply(k, rows, slice(j * LANES, (j + 1) * LANES), grad, MATRIX_RATE)
                return carry

            lax.fori_loop(0, count // step, piece, 0, unroll=2)
        finish(k)
    last = 7
    wait(last)
    for t in range(held[3 * last].shape[0]):
        for j in range(held[3 * last].shape[1] // LANES):
            r = t * (held[3 * last].shape[1] // LANES) + j
            apply(last, slice(t, t + 1), slice(j * LANES, (j + 1) * LANES), gain[r : r + 1, :], GAIN_RATE)
    finish(last)
    for copy in stores:
        copy.wait()


def shards(
    slot_owner,
    slot_row,
    slot_count,
    item_qid,
    positive,
    log_prior,
    embedding,
    embedding_mom,
    embedding_avg,
    w_in,
    w_in_mom,
    w_in_avg,
    norm_gain,
    norm_gain_mom,
    norm_gain_avg,
    w_qkv,
    w_qkv_mom,
    w_qkv_avg,
    w_out,
    w_out_mom,
    w_out_avg,
    w_one,
    w_one_mom,
    w_one_avg,
    w_two,
    w_two_mom,
    w_two_avg,
    w_three,
    w_three_mom,
    w_three_avg,
):
    plane = lax.axis_size("dp")
    line = lax.axis_size("mp")
    batch, towers, slots = slot_row.shape
    own = batch // line
    requests = batch * towers * slots
    own_requests = requests // line
    tokens = own * slots
    capacity = max(LANES, 2 * requests // plane)
    pairs = batch * plane
    part = lax.axis_index("mp")
    me = lax.axis_index("dp")
    width = w_in.shape[2]
    depth = w_in.shape[1]
    units = w_one.shape[2]
    seconds = w_two.shape[2]

    per = capacity // LANES
    small = capacity // 4
    dims = (towers, own, slots)

    def row_scratch(count):
        return [
            pltpu.VMEM((plane, count, depth), BF16),
            pltpu.VMEM((plane, count, depth), BF16),
            pltpu.VMEM((plane * count, depth), F32),
        ]

    turned = jnp.transpose(w_qkv, (0, 2, 1, 3))
    embedded, got_own, got_lists, weights, inverse, own_place = pl.pallas_call(
        functools.partial(fetch_kernel, plane, line, dims, capacity),
        out_shape=[
            shape((own_requests, depth), BF16),
            shape((plane, per, LANES), I32),
            shape((plane, per + 8, LANES), I32),
            shape((line, towers, 4, width, LANES), BF16),
            shape((plane * per, LANES), I32),
            shape((slots, LANES), I32),
        ],
        in_specs=[VMEM] * 4 + [HBM] * 3,
        out_specs=[VMEM] * 6,
        scratch_shapes=[
            pltpu.VMEM((plane, per, LANES), I32),
            pltpu.VMEM((slots, LANES), I32),
            pltpu.VMEM((plane, per + 8, LANES), I32),
            pltpu.VMEM(embedding.shape, F32),
            pltpu.VMEM(turned.shape, F32),
            pltpu.VMEM(w_out.shape, F32),
            pltpu.SMEM((slots, LANES), I32),
            pltpu.SMEM((plane, -(-small // LANES), LANES), I32),
            *row_scratch(small),
            DMA((2, plane)),
            DMA((2, plane)),
            DMA((plane,)),
            DMA((plane,)),
            DMA((line,)),
            DMA((line,)),
            DMA((line,)),
            DMA((line,)),
            DMA((2, line)),
            DMA((2, line)),
            DMA((4,)),
            DMA((3,)),
        ],
        compiler_params=params(60, collective_id=2, has_side_effects=True),
        name="fetch",
    )(
        jnp.transpose(slot_owner[..., 0], (1, 2, 0)),
        jnp.transpose(slot_row, (1, 2, 0)),
        jnp.transpose(slot_count),
        positive.reshape(1, batch),
        embedding,
        turned,
        w_out,
    )
    most = jnp.max(got_lists[:, per + 1 : per + 3, 0], 0)

    def refetch(ids, place, table, _):
        return pl.pallas_call(
            functools.partial(refetch_kernel, plane, dims),
            out_shape=shape((own_requests, depth), BF16),
            in_specs=[SMEM, SMEM, VMEM],
            out_specs=VMEM,
            scratch_shapes=[*row_scratch(capacity), DMA((plane,)), DMA((plane,))],
            compiler_params=params(16, collective_id=7, has_side_effects=True),
            name="refetch",
        )(ids, place, table)

    embedded = lax.cond(most[0] > small, refetch, lambda *given: given[3], got_own, own_place, embedding, embedded)
    embedded = embedded.reshape(towers, tokens, depth)

    counts = jnp.transpose(slot_count)
    heads = 2 * line
    groups = tokens // LANES
    per_group = LANES // slots
    totals = (towers * 3 * width, towers * width, towers * depth * width // LANES)
    totals += tuple(towers * size // LANES for size in (seconds * width, width * units, units * seconds))
    sizes = [total // plane for total in totals]
    held = lambda size: pltpu.VMEM((plane // 2, 2, size, LANES), BF16)
    share = line * (sizes[0] + sizes[1]) + sum(sizes[2:])
    early = sum(sizes[3:])
    every, summed, gain_sum, loss = pl.pallas_call(
        functools.partial(towers_kernel, plane, line, slots),
        out_shape=[
            shape((line, own_requests, depth), BF16),
            shape((share, LANES), BF16),
            shape((8, LANES), F32),
            shape((1, 1), F32),
        ],
        in_specs=[SMEM] + [VMEM] * 4 + [HBM] * 3 + [VMEM] * 3 + [SMEM],
        out_specs=[VMEM] * 3 + [SMEM],
        scratch_shapes=[
            pltpu.VMEM((towers, own, width), BF16),
            pltpu.VMEM((towers, own, line * LANES), BF16),
            pltpu.VMEM((towers, tokens, width), BF16),
            pltpu.VMEM((towers, 3 * line, tokens, LANES), BF16),
            pltpu.VMEM((towers, groups, heads, LANES, LANES), BF16),
            pltpu.VMEM((towers, groups, per_group * heads, LANES), BF16),
            pltpu.VMEM((groups, per_group, line * LANES), F32),
            [
                pltpu.VMEM((towers, line, own, width), BF16),
                pltpu.VMEM((towers, line, own, seconds), BF16),
                pltpu.VMEM((towers, line, own, seconds), BF16),
                pltpu.VMEM((towers, plane, line, own, width), BF16),
                pltpu.VMEM((towers, line, own, seconds), BF16),
                pltpu.VMEM((towers, line, own, seconds), BF16),
                pltpu.VMEM((towers, line, own, width), BF16),
                pltpu.VMEM((towers, line, own, width), BF16),
                DMA((5, line)),
                DMA((5, line)),
                DMA((plane,)),
                DMA((plane,)),
                pltpu.VMEM((towers, line, own, seconds), F32),
                pltpu.VMEM((towers, line, own, width), F32),
                pltpu.VMEM((pairs, 8), F32),
            ],
            pltpu.VMEM(w_one.shape, F32),
            pltpu.VMEM(w_two.shape, F32),
            pltpu.VMEM(w_three.shape, F32),
            DMA((3,)),
            pltpu.VMEM((towers, own, width), BF16),
            held(sizes[3]),
            held(sizes[4]),
            held(sizes[5]),
            pltpu.VMEM((line, plane // 2, 2, sizes[0], LANES), BF16),
            pltpu.VMEM((line, plane // 2, 2, sizes[1], LANES), BF16),
            held(sizes[2]),
            pltpu.VMEM((8, LANES), F32),
            pltpu.VMEM((3 * line, tokens, LANES), BF16),
            [pltpu.VMEM((line, plane // 2, size, LANES), BF16) for size in sizes[:2]],
            [pltpu.VMEM((plane // 2, size, LANES), BF16) for size in sizes[2:]],
            pltpu.VMEM((plane // 2, share, LANES), BF16),
            pltpu.VMEM((plane // 2 - 1, early, LANES), BF16),
            pltpu.VMEM((plane // 2 - 1, share - early, LANES), BF16),
            pltpu.VMEM((plane, 8, LANES), F32),
            DMA((towers, line)),
            DMA((towers, line)),
            DMA((6,)),
            DMA((6,)),
            DMA((2, plane // 2)),
            DMA((2, plane // 2)),
            DMA((plane,)),
            DMA((plane,)),
        ],
        compiler_params=params(60, collective_id=4, has_side_effects=True),
        name="towers",
    )(
        counts,
        embedded,
        w_in,
        norm_gain,
        weights,
        w_one,
        w_two,
        w_three,
        log_prior.reshape(-1, LANES),
        item_qid.reshape(1, pairs),
        got_lists,
        positive,
    )
    whole_at = line * (sizes[0] + sizes[1])
    whole_rows = sizes[2] + sizes[3]
    last_rows = sizes[4] + sizes[5]
    cuts = (
        ((0, sizes[0]), (line * sizes[0], sizes[1])),
        (whole_at, whole_rows),
        (whole_at + whole_rows, last_rows),
    )
    line_rows = sizes[0] + sizes[1] + whole_rows

    def tail(count, number):
        return lambda *given: pl.pallas_call(
            functools.partial(tail_kernel, plane, line, count, cuts),
            out_shape=[
                shape(embedding.shape, F32),
                shape((plane, line_rows + last_rows, LANES), BF16),
                shape((8, LANES), F32),
                shape((8, LANES), F32),
            ],
            in_specs=[SMEM] + [VMEM] * 4,
            out_specs=[VMEM] * 4,
            scratch_shapes=[
                pltpu.VMEM((requests, depth), F32),
                pltpu.VMEM((plane, count, depth), BF16),
                pltpu.VMEM((plane, count, depth), BF16),
                pltpu.VMEM((embedding.shape[0] // 2, 2 * depth), F32),
                pltpu.VMEM((line, line_rows, LANES), BF16),
                pltpu.VMEM((line, 8, LANES), F32),
                pltpu.VMEM((line, 8, LANES), F32),
                pltpu.VMEM((plane, 8, LANES), F32),
                DMA((plane,)),
                DMA((plane,)),
                DMA((3, line)),
                DMA((3, line)),
                DMA((line,)),
                DMA((line,)),
                DMA((line,)),
                DMA((line,)),
                DMA((plane,)),
                DMA((plane,)),
                DMA((2, plane // 2)),
                DMA((2, plane // 2)),
                DMA((2, plane // 2)),
                DMA((2, plane // 2)),
            ],
            compiler_params=params(36, collective_id=number, has_side_effects=True),
            name="tail",
        )(given[0][:, : -(-count // LANES)], *given[1:])

    medium = capacity * 5 // 8
    table_grad, dense_all, norm_sq, gain_all = lax.cond(
        most[1] > medium,
        tail(capacity, 8),
        tail(medium, 5),
        inverse.reshape(plane, per, LANES),
        got_lists,
        every.reshape(requests, depth),
        summed,
        gain_sum,
    )
    flat = lambda w: w.reshape(-1, w.shape[-1])
    turn = lambda w: flat(jnp.transpose(w, (0, 2, 1, 3)))
    given = [embedding, embedding_mom, embedding_avg]
    given += [turn(w) for w in (w_qkv, w_qkv_mom, w_qkv_avg)]
    rest = (w_out, w_out_mom, w_out_avg, w_in, w_in_mom, w_in_avg, w_three, w_three_mom, w_three_avg)
    rest += (w_one, w_one_mom, w_one_avg, w_two, w_two_mom, w_two_avg)
    given += [flat(w) for w in rest]
    given += [norm_gain, norm_gain_mom, norm_gain_avg]
    heights = (towers * 3 * width, LANES, depth, seconds, width, units)
    wides = (1, width // LANES, width // LANES, width // LANES, units // LANES, seconds // LANES)
    blocks = tuple((k + 1, size, height, wide) for k, (size, height, wide) in enumerate(zip(sizes, heights, wides)))
    *done, norm = pl.pallas_call(
        functools.partial(update_kernel, blocks),
        out_shape=[shape(w.shape, F32) for w in given] + [shape((1, 1), F32)],
        in_specs=[VMEM] * 4 + [HBM] * len(given),
        out_specs=[HBM] * len(given) + [SMEM],
        scratch_shapes=[pltpu.VMEM(w.shape, F32) for w in given] + [DMA((len(given),))] * 2,
        compiler_params=params(57),
        name="update",
    )(norm_sq, table_grad, dense_all, gain_all, *given)
    back = lambda k, w: [done[3 * k + j].reshape(w.shape) for j in range(3)]
    unturned = [
        jnp.transpose(w.reshape(towers, 3, width, LANES), (0, 2, 1, 3)) for w in done[3:6]
    ]
    new = done[:3] + back(3, w_in) + done[21:24] + unturned + back(2, w_out) + back(5, w_one) + back(6, w_two)
    return (loss.reshape(()), norm.reshape(()), *new, *back(4, w_three))


def solution(mesh):
    rows = P("dp", None)
    qkv = P(None, None, None, "mp")
    deep = P(None, "mp", None)
    wide = P(None, None, "mp")
    weights = (rows,) * 3 + (P(),) * 6 + (qkv,) * 3 + (deep,) * 3 + (wide,) * 3 + (deep,) * 3 + (P(),) * 3
    inputs = (P("dp", None, None, None), P("dp", None, None), P("dp", None), P(), P("dp"), P())
    return jax.shard_map(
        shards, mesh=mesh, in_specs=inputs + weights, out_specs=(P(), P()) + weights, check_vma=False
    )
```

```python
import functools
import math

import jax
import jax.numpy as jnp
from jax import lax
from jax.experimental import pallas as pl
from jax.experimental.pallas import tpu as pltpu
from jax.sharding import PartitionSpec as P

DH = 64
EPS = 1e-06
INV_TEMP = 20.0
CLIP_NORM = 0.1
ROW_RATE = 150000.0
GAIN_RATE = 8000.0
MATRIX_RATE = 600.0
MOMENTUM = 0.9
AVERAGE_DECAY = 0.6

MESH = pl.DeviceIdType.MESH
LANES = 128
F32 = jnp.float32
BF16 = jnp.bfloat16
I32 = jnp.int32
VMEM = pl.BlockSpec(memory_space=pltpu.VMEM)
HBM = pl.BlockSpec(memory_space=pltpu.HBM)
SMEM = pl.BlockSpec(memory_space=pltpu.SMEM)
DMA = pltpu.SemaphoreType.DMA


def nn(a, b):
    return lax.dot_general(a, b, (((1,), (0,)), ((), ())), preferred_element_type=F32)


def nt(a, b):
    return lax.dot_general(a, b, (((1,), (1,)), ((), ())), preferred_element_type=F32)


def tn(a, b):
    return lax.dot_general(a, b, (((0,), (0,)), ((), ())), preferred_element_type=F32)


def iota(shape, dim):
    return lax.broadcasted_iota(I32, shape, dim)


def split(value):
    high = value.astype(BF16)
    return high, (value - high.astype(F32)).astype(BF16)


def shape(dims, dtype):
    return jax.ShapeDtypeStruct(tuple(dims), dtype)


def params(limit, **more):
    return pltpu.CompilerParams(vmem_limit_bytes=limit << 20, **more)


def log2(value):
    return value.bit_length() - 1


def lists_of(owner, values, owners, capacity):
    chunks = owner.shape[0]
    width = owners * capacity
    his = width // LANES
    sub = iota((owners, LANES), 0)
    hot = [(owner[c : c + 1, :] == sub).astype(F32) for c in range(chunks)]
    hots = jnp.concatenate(hot, 0).astype(BF16)
    before = (iota((LANES, LANES), 0) < iota((LANES, LANES), 1)).astype(BF16)
    earlier = nn(hots, before)
    totals = nn(hots, jnp.ones((LANES, LANES), BF16))
    base = (sub * capacity).astype(F32)
    places = []
    for c in range(chunks):
        cut = slice(c * owners, (c + 1) * owners)
        here = jnp.sum(hot[c] * (earlier[cut] + base), 0, keepdims=True).astype(I32)
        places.append(jnp.where(owner[c : c + 1, :] < owners, here, width))
        base = base + totals[cut]
    parts = 2 * len(values)
    acc = jnp.zeros((his, parts * LANES), F32)
    for c in range(chunks):
        place = places[c]
        left = (lax.shift_right_logical(place, 7) == iota((his, LANES), 0)).astype(BF16)
        low = (place & 127) == iota((LANES, LANES), 0)
        cuts = []
        for value in values:
            value = value[c : c + 1, :]
            cuts += [lax.shift_right_logical(value, 6), value & 63]
        right = jnp.concatenate([jnp.where(low, cut.astype(F32), 0.0) for cut in cuts], 0)
        acc = acc + nt(left, right.astype(BF16))
    cuts = [acc[:, k * LANES : (k + 1) * LANES].astype(I32) for k in range(parts)]
    lists = [cuts[2 * k] * 64 + cuts[2 * k + 1] for k in range(len(values))]
    return places, lists, hot


class Slots:
    def __init__(self, owners, line, owner, row, count):
        towers, slots, batch = owner.shape
        own = batch // line
        side = lambda ref: jnp.concatenate([ref[t] for t in range(towers)], 1)
        counts = jnp.concatenate([count[t : t + 1, :] for t in range(towers)], 1)
        slot, lane = iota((slots, LANES), 0), iota((slots, LANES), 1)
        tower = lax.shift_right_logical(lane, log2(batch))
        self.row = side(row)
        self.owner = jnp.where(slot < counts, side(owner), owners)
        self.block = lax.shift_right_logical(lane & (batch - 1), log2(own))
        self.token = ((self.block * towers + tower) * own + (lane & (own - 1))) * slots + slot


def make_own_lists(slots, owners, capacity, small, height, own_lists, own_place, own_small):
    per = capacity // LANES
    owner = jnp.where(slots.block == lax.axis_index("mp"), slots.owner, owners)
    places, (rows,), _ = lists_of(owner, (slots.row,), owners, capacity)
    rows = jnp.minimum(jnp.maximum(rows, 0), height - 1)
    for d in range(owners):
        own_lists[d] = rows[d * per : (d + 1) * per, :]
    place = jnp.concatenate(places, 0)
    place = jnp.maximum(jnp.where(place < owners * capacity, place, 0), 0)
    own_place[...] = place
    rank = jnp.minimum(place & (capacity - 1), small - 1)
    own_small[...] = lax.shift_right_logical(place, log2(capacity)) * small + rank


def make_lists(slots, owners, capacity, batch, line, positive, lists, inverse):
    per = capacity // LANES
    _, (rows, tokens), hot = lists_of(slots.owner, (slots.row + 1, slots.token), owners, capacity)
    rows = rows - 1
    inverse[...] = tokens
    asked = hot[0]
    for more in hot[1:]:
        asked = asked + more
    own = batch // line
    near = lax.shift_right_logical(iota((LANES, LANES), 0) & (batch - 1), log2(own)) == iota((LANES, LANES), 1)
    asked = asked.astype(BF16)
    most = jnp.max(jnp.max(nn(asked, near.astype(BF16)), 0, keepdims=True), 1, keepdims=True)
    every = jnp.max(nn(asked, jnp.ones((LANES, LANES), BF16)), 0, keepdims=True)
    most = jnp.broadcast_to(most, (1, LANES))
    for d in range(owners):
        lists[d, 0:per, :] = rows[d * per : (d + 1) * per, :]
        lists[d, per : per + 1, 0:batch] = positive[...]
        lists[d, per + 1 : per + 2, :] = most.astype(I32)
        lists[d, per + 2 : per + 3, :] = every.astype(I32)


def announce(plane, line):
    me, part = lax.axis_index("dp"), lax.axis_index("mp")
    barrier = pltpu.get_barrier_semaphore()
    for k in range(1, plane):
        pl.semaphore_signal(barrier, inc=1, device_id=(lax.rem(me + k, plane), part), device_id_type=MESH)
    for k in range(1, line):
        pl.semaphore_signal(barrier, inc=1, device_id=(me, lax.rem(part + k, line)), device_id_type=MESH)
    return me, part


def await_others(plane, line):
    pl.semaphore_wait(pltpu.get_barrier_semaphore(), max(plane - 1, 0) + max(line - 1, 0))


def enter(plane, line):
    me, part = announce(plane, line)
    await_others(plane, line)
    return me, part


def partners(me, count):
    order = sorted(range(1, count), key=lambda k: (-bin(k >> 1).count("1"), k & 1, k))
    bits = [lax.rem(me // (1 << b), 2) for b in range(log2(count))]
    return [sum((1 << b) * (1 - bit if k >> b & 1 else bit) for b, bit in enumerate(bits)) for k in order]


def send(source, target, out_sem, in_sem, device):
    copy = pltpu.make_async_remote_copy(
        src_ref=source, dst_ref=target, send_sem=out_sem, recv_sem=in_sem, device_id=device, device_id_type=MESH
    )
    copy.start()
    return copy


def gather_rows(ids, table, target):
    def body(i, carry):
        at = ids(i)
        rows = [table[pl.ds(at(u), 1), :] for u in range(16)]
        target[pl.ds(pl.multiple_of(i * 16, 16), 16), :] = jnp.concatenate(rows, 0).astype(BF16)
        return carry

    lax.fori_loop(0, target.shape[0] // 16, body, 0, unroll=2)


def listed(ids, first):
    def at(i):
        block = first + lax.shift_right_logical(i, 3)
        start = (i & 7) * 16
        return lambda u: ids[block, start + u]

    return at


def placed(place, part, towers, own, slots):
    per = slots // 16

    def at(i):
        pair = lax.shift_right_logical(i, log2(per))
        tower = lax.shift_right_logical(pair, log2(own))
        lane = tower * (LANES // towers) + part * own + (pair & (own - 1))
        start = (i & (per - 1)) * 16
        return lambda u: place[start + u, lane]

    return at


def send_rows(plane, me, part, ids, table, sent, got, wide, out_sems, in_sems):
    capacity = sent.shape[1]
    copies = []
    for k, peer in enumerate(partners(me, plane)):
        gather_rows(listed(ids.at[peer], 0), table, sent.at[peer])
        copies.append(send(sent.at[peer], got.at[me], out_sems.at[k], in_sems.at[k], (peer, part)))
    gather_rows(listed(ids.at[me], 0), table, sent.at[me])
    wide[pl.ds(pl.multiple_of(me * capacity, capacity), capacity), :] = sent[me].astype(F32)
    return copies


def take_rows(plane, me, part, dims, copies, place, got, wide, out):
    capacity = got.shape[1]
    for copy, peer in zip(copies, partners(me, plane)):
        copy.wait_recv()
        wide[pl.ds(pl.multiple_of(peer * capacity, capacity), capacity), :] = got[peer].astype(F32)
    gather_rows(placed(place, part, *dims), wide, out)


def refetch_kernel(plane, dims, ids, place, table, out, sent, got, wide, out_sems, in_sems):
    me, part = enter(plane, 0)
    copies = send_rows(plane, me, part, ids, table, sent, got, wide, out_sems, in_sems)
    take_rows(plane, me, part, dims, copies, place, got, wide, out)
    for copy in copies:
        copy.wait_send()


def fetch_kernel(
    plane,
    line,
    dims,
    capacity,
    owner_in,
    row_in,
    count,
    positive,
    far_table,
    far_qkv,
    far_wout,
    out,
    got_own,
    got_lists,
    weights,
    inverse,
    own_place,
    own_lists,
    own_small,
    lists,
    table,
    w_qkv,
    w_out,
    place,
    ids,
    sent,
    got,
    wide,
    list_out,
    list_in,
    out_sems,
    in_sems,
    far_out,
    far_in,
    side_out,
    side_in,
    near_out,
    near_in,
    own_sems,
    load_sems,
):
    loads = [
        pltpu.make_async_copy(source, target, load_sems.at[j])
        for j, (source, target) in enumerate(((far_qkv, w_qkv), (far_wout, w_out), (far_table, table)))
    ]
    for copy in loads:
        copy.start()
    me, part = announce(plane, line)
    core = lax.rem(me, 2)
    half = lax.rem(me // 2, 2)
    sibling = me + 1 - 2 * core
    partner = me + 2 - 4 * half
    batch = positive.shape[1]
    slots = Slots(plane, line, owner_in, row_in, count)
    make_own_lists(slots, plane, capacity, sent.shape[1], table.shape[0], own_lists, own_place, own_small)
    places = pltpu.make_async_copy(own_small, place, own_sems.at[0])
    places.start()
    for copy in loads[:2]:
        copy.wait()
    rows = weights.shape[3] // 2
    for c in range(3):
        weights[part, :, c] = w_qkv[:, c].astype(BF16)
    for j in range(2):
        weights[part, :, 3, j * LANES : (j + 1) * LANES, :] = w_out[:, :, j * LANES : (j + 1) * LANES].astype(BF16)
    quarter = lambda m, h: weights.at[m, core, :, pl.ds(pl.multiple_of(h * rows, rows), rows), :]
    await_others(plane, line)
    far, asked, told = [], [], []
    for k in range(1, line):
        peer = lax.rem(part + k, line)
        far.append(send(quarter(part, half), quarter(part, half), far_out.at[k], far_in.at[k], (me, peer)))
    for k in range(1, plane):
        peer = lax.rem(me + k, plane)
        asked.append(send(own_lists.at[peer], got_own.at[me], list_out.at[0, k], list_in.at[0, k], (peer, part)))
    make_lists(slots, plane, capacity, batch, line, positive, lists, inverse)
    for k in range(1, plane):
        peer = lax.rem(me + k, plane)
        told.append(send(lists.at[peer], got_lists.at[me], list_out.at[1, k], list_in.at[1, k], (peer, part)))
    mine = [
        pltpu.make_async_copy(own_lists.at[me], got_own.at[me], own_sems.at[1]),
        pltpu.make_async_copy(lists.at[me], got_lists.at[me], own_sems.at[2]),
    ]
    for copy in mine:
        copy.start()
    for copy in asked:
        copy.wait()
    mine[0].wait()
    numbers = pltpu.make_async_copy(got_own.at[:, 0 : ids.shape[1]], ids, own_sems.at[3])
    numbers.start()
    for copy in (numbers, places, loads[2]):
        copy.wait()
    copies = send_rows(plane, me, part, ids, table, sent, got, wide, out_sems, in_sems)
    sides, near = [], []
    for k in range(1, line):
        peer = lax.rem(part - k + line, line)
        far[k - 1].wait_recv()
        at = quarter(peer, half)
        sides.append(send(at, at, side_out.at[k], side_in.at[k], (partner, part)))
        near.append(send(at, at, near_out.at[0, k], near_in.at[0, k], (sibling, part)))
    take_rows(plane, me, part, dims, copies, place, got, wide, out)
    for k in range(1, line):
        peer = lax.rem(part - k + line, line)
        sides[k - 1].wait_recv()
        at = quarter(peer, 1 - half)
        near.append(send(at, at, near_out.at[1, k], near_in.at[1, k], (sibling, part)))
    mine[1].wait()
    for copy in copies + far + sides:
        copy.wait_send()
    for copy in told + near:
        copy.wait()


def add_rows(ids, count, blocks, grads, total, fresh):
    height = total.shape[0]
    rows = []
    for block in blocks:
        for r in range(-(-count // LANES)):
            rows.append(ids[block, r : r + 1, 0 : min(LANES, count - r * LANES)])
    numbers = jnp.concatenate(rows, 1)
    values = jnp.concatenate([ref[...] for ref in grads], 0)
    turned = jnp.transpose(jnp.broadcast_to(numbers.astype(F32), (8, numbers.shape[1])), (1, 0))[:, 0:1]
    upper = turned >= height
    none = jnp.zeros_like(values)
    values = jnp.concatenate([jnp.where(upper, none, values), jnp.where(upper, values, none)], 1)
    low = jnp.where(numbers >= 0, numbers & (height - 1), -1)
    step = min(height, 1024)

    def body(i, carry):
        at = pl.multiple_of(i * step, step)
        hot = jnp.where(low - at == iota((step, low.shape[1]), 0), 1.0, 0.0).astype(BF16)
        part = nn(hot, values)
        at = pl.ds(at, step)
        total[at, :] = part if fresh else total[at, :] + part
        return carry

    lax.fori_loop(0, height // step, body, 0)


def tail_kernel(
    plane,
    line,
    capacity,
    cuts,
    tokens,
    ids,
    rows,
    summed,
    gain,
    table,
    dense_all,
    norm_sq,
    gain_all,
    wide,
    sent,
    back,
    total,
    got,
    gains,
    along,
    across,
    out_sems,
    in_sems,
    far_out,
    far_in,
    gain_out,
    gain_in,
    along_out,
    along_in,
    across_out,
    across_in,
    chip_out,
    chip_in,
    near_out,
    near_in,
):
    me, part = enter(plane, line)
    chips = plane // 2
    core = lax.rem(me, 2)
    chip = me // 2
    sibling = me + 1 - 2 * core
    far = []
    split_cuts, (whole_at, whole_rows), (last_at, last_rows) = cuts
    for k in range(1, line):
        peer = lax.rem(part + k, line)
        to = 0
        for j, (at, count) in enumerate(split_cuts):
            begin = pl.multiple_of(at + peer * count, 16)
            far.append(
                send(summed.at[pl.ds(begin, count)], got.at[part, to : to + count], far_out.at[j, k], far_in.at[j, k], (me, peer))
            )
            to += count
        target = got.at[part, to : to + whole_rows]
        source = summed.at[whole_at : whole_at + whole_rows]
        far.append(send(source, target, far_out.at[2, k], far_in.at[2, k], (me, peer)))
        far.append(send(gain, gains.at[part], gain_out.at[k], gain_in.at[k], (me, peer)))
    gains[part] = gain[...]
    split_rows = sum(count for _, count in split_cuts)
    done = split_rows + whole_rows
    dense_all[me, done:, :] = summed[last_at : last_at + last_rows, :]
    spread, near = [], []

    def gather_shares(stage, begin, end):
        block = dense_all.at[me, begin:end]
        for k in range(1, chips):
            to = 2 * lax.rem(chip + k, chips) + core
            spread.append(send(block, block, chip_out.at[stage, k], chip_in.at[stage, k], (to, part)))
        near.append(send(block, block, near_out.at[stage, 0], near_in.at[stage, 0], (sibling, part)))

    def pass_shares(stage, begin, end):
        for k in range(1, chips):
            peer = 2 * lax.rem(chip - k + chips, chips) + core
            spread[stage * (chips - 1) + k - 1].wait_recv()
            block = dense_all.at[peer, begin:end]
            near.append(send(block, block, near_out.at[stage, k], near_in.at[stage, k], (sibling, part)))

    gather_shares(0, done, done + last_rows)
    wide[...] = rows[...].astype(F32)
    copies = []
    others = partners(me, plane)
    for k, peer in enumerate(others):
        gather_rows(listed(tokens.at[peer], 0), wide, sent.at[peer])
        copies.append(send(sent.at[peer], back.at[me], out_sems.at[k], in_sems.at[k], (peer, part)))
    gather_rows(listed(tokens.at[me], 0), wide, sent.at[me])
    to = 0
    for at, count in split_cuts:
        got[part, to : to + count] = summed[pl.ds(pl.multiple_of(at + part * count, 16), count), :]
        to += count
    got[part, to : to + whole_rows] = summed[whole_at : whole_at + whole_rows, :]
    for copy in far:
        copy.wait()
    share = got[0].astype(F32)
    for m in range(1, line):
        share = share + got[m].astype(F32)
    dense_all[me, 0 : to + whole_rows, :] = share.astype(BF16)
    group = max(1, 1280 // capacity)
    order = [me] + others
    for first in range(0, plane, group):
        blocks = order[first : first + group]
        grads = [sent.at[blocks[0]] if first == 0 else back.at[blocks[0]]] + [back.at[block] for block in blocks[1:]]
        for k in range(max(first, 1), min(first + group, plane)):
            copies[k - 1].wait_recv()
        if first == 0:
            gather_shares(1, 0, done)
            pass_shares(0, done, done + last_rows)
        add_rows(ids, capacity, blocks, grads, total, first == 0)
    square = jnp.zeros((8, LANES), F32)
    for begin, count, weight in ((0, to, 1.0), (to, whole_rows, 1.0 / line), (to + whole_rows, last_rows, 1.0)):
        block = dense_all[me, begin : begin + count, :].astype(F32)
        square = square + weight * jnp.sum((block * block).reshape(count // 8, 8, LANES), 0)
    height = total.shape[0]

    def settle(i, carry):
        at = pl.multiple_of(i * 32, 32)
        for half in range(2):
            block = total[pl.ds(at, 32), half * LANES : (half + 1) * LANES]
            table[pl.ds(at + half * height, 32), :] = block
            block = block * block
            for r in range(4):
                carry = carry + block[r * 8 : (r + 1) * 8, :]
        return carry

    table_sq = lax.fori_loop(0, height // 32, settle, jnp.zeros((8, LANES), F32))
    across[me] = square + table_sq * (1.0 / line)
    tiny = [
        send(across.at[me], across.at[me], across_out.at[k], across_in.at[k], (lax.rem(me + k, plane), part))
        for k in range(1, plane)
    ]
    for copy in tiny:
        copy.wait()
    sums = across[0]
    for d in range(1, plane):
        sums = sums + across[d]
    along[part] = sums
    peers = [lax.rem(part + k, line) for k in range(1, line)]
    tiny = [
        send(along.at[part], along.at[part], along_out.at[k], along_in.at[k], (me, peer)) for k, peer in enumerate(peers)
    ]
    pass_shares(1, 0, done)
    gain_sum = gains[0]
    for m in range(1, line):
        gain_sum = gain_sum + gains[m]
    gain_all[...] = gain_sum
    for copy in tiny:
        copy.wait()
    sums = along[0]
    for m in range(1, line):
        sums = sums + along[m]
    norm_sq[...] = jnp.broadcast_to(jnp.sum(sums + gain_sum * gain_sum), norm_sq.shape)
    for copy in copies + spread:
        copy.wait_send()
    for copy in near:
        copy.wait()


def chain(index, values):
    out = jnp.full(index.shape, values[0], values[0].dtype)
    for k in range(1, len(values)):
        out = jnp.where(index >= k, values[k], out)
    return out


def two_by_two(parts):
    blocks = [(c, m) for m in range(parts) for c in range(2)] + [(2, m) for m in range(parts)]
    return list(zip(blocks[::2], blocks[1::2]))


def forward_tower(tower, slots, cnt, x, w_in, gain, w_all, pooled, pm_out, normed_out, qkv, prob, a_out, pm_acc):
    pairs = pooled.shape[1]
    first = lax.axis_index("mp") * pairs
    parts = w_all.shape[0]
    per = LANES // slots
    groups = pairs // per
    heads = 2 * parts
    xs = x[tower]
    hidden = nn(xs, w_in[tower].astype(BF16))
    inverse = lax.rsqrt(jnp.mean(hidden * hidden, -1, keepdims=True) + EPS)
    normed = (hidden * inverse * gain[tower : tower + 1, :]).astype(BF16)
    normed_out[tower] = normed
    for (c, m), (d, n) in two_by_two(parts):
        both = jnp.concatenate([w_all[m, tower, c], w_all[n, tower, d]], 1)
        both = nn(normed, both).astype(BF16)
        qkv[tower, c * parts + m] = both[:, :LANES]
        qkv[tower, d * parts + n] = both[:, LANES:]
    lane = iota((LANES, LANES), 1)
    line = iota((LANES, LANES), 0)
    shift = slots.bit_length() - 1
    pair_r, pair_s = lax.shift_right_logical(lane, shift), lax.shift_right_logical(line, shift)
    same = pair_r == pair_s
    halves = [lane < DH, lane >= DH]
    own_head = iota((per * heads, LANES), 0) & (heads - 1)

    def group(g, carry):
        counts = [cnt[tower, first + g * per + k] for k in range(per)]
        live_r = same & ((lane & (slots - 1)) < chain(pair_r, counts))
        live_s = (line & (slots - 1)) < chain(pair_s, counts)
        rows = pl.ds(pl.multiple_of(g * LANES, LANES), LANES)
        sums = []
        for m in range(parts):
            query, key = qkv[tower, m, rows, :], qkv[tower, parts + m, rows, :]
            none = jnp.zeros_like(key)
            both = nt(query, jnp.concatenate([jnp.where(side, key, none) for side in halves], 0)) * 0.125
            for half in range(2):
                scores = both[:, half * LANES : (half + 1) * LANES]
                scores = jnp.where(live_r, scores, -1000000000.0)
                expo = jnp.exp(scores - jnp.max(scores, 1, keepdims=True))
                p = (expo * (1.0 / jnp.sum(expo, 1, keepdims=True))).astype(BF16)
                prob[tower, g, 2 * m + half] = p
                sums.append(jnp.sum(jnp.where(live_s, p.astype(F32), 0.0), 0, keepdims=True))
        sums = jnp.concatenate(sums, 0)
        pair_l = lax.shift_right_logical(iota((heads, LANES), 1), shift)
        stack = jnp.concatenate([jnp.where(pair_l == k, sums, 0.0) for k in range(per)], 0).astype(BF16)
        a_out[tower, g] = stack
        for m in range(parts):
            mix = nn(stack, qkv[tower, 2 * parts + m, rows, :])
            head = iota((per * heads, LANES), 1) // DH + 2 * m
            mix = jnp.where(own_head == head, mix, 0.0)
            pm_acc[g, :, m * LANES : (m + 1) * LANES] = jnp.concatenate(
                [jnp.sum(mix[k * heads : (k + 1) * heads], 0, keepdims=True) for k in range(per)], 0
            )
        return carry

    lax.fori_loop(0, groups, group, 0)
    pm = jnp.concatenate([pm_acc[g] for g in range(groups)], 0).astype(BF16)
    pm_out[tower] = pm
    every = [cnt[tower, first + k] for k in range(pairs)]
    tokens = iota((pairs, pairs * slots), 1)
    mine = lax.shift_right_logical(tokens, shift) == iota(tokens.shape, 0)
    live = mine & ((tokens & (slots - 1)) < chain(iota(tokens.shape, 0), every))
    high, low = split(nn(live.astype(BF16), xs))
    w = w_in[tower].astype(BF16)
    total = nn(high, w) + nn(low, w)
    sides = []
    for j in range(2):
        side = total[:, j * LANES : (j + 1) * LANES]
        for m in range(parts):
            side = side + nn(pm[:, m * LANES : (m + 1) * LANES], w_all[m, tower, 3, j * LANES : (j + 1) * LANES, :])
        sides.append(side)
    total = jnp.concatenate(sides, 1)
    count = chain(iota(total.shape, 0), every).astype(F32)
    pooled[tower] = (total / count).astype(BF16)


def put(target, size, first, value):
    done = 0
    while done < value.shape[0]:
        share, inside = divmod(first + done, size)
        count = min(size - inside, value.shape[0] - done)
        target[share // 2, share % 2, inside : inside + count, :] = value[done : done + count]
        done += count


def backward_tower(
    tower, slots, cnt, x, w_in, gain, w_all, normed_in, qkv, prob, a_in, pm_in, dpooled, demb, d_in, d_gain, d_qkv, d_out, dqkv
):
    pairs, width = dpooled.shape[1:]
    parts = w_all.shape[0]
    per = LANES // slots
    groups = pairs // per
    heads = 2 * parts
    shift = slots.bit_length() - 1
    tokens = pairs * slots
    first = lax.axis_index("mp") * pairs
    every = [cnt[tower, first + k] for k in range(pairs)]
    count = chain(iota((pairs, width), 0), every).astype(F32)
    dsum = dpooled[tower].astype(F32) / count
    branch = dsum.astype(BF16)
    dmix = []
    for m in range(parts):
        grad = tn(pm_in[tower, :, m * LANES : (m + 1) * LANES], branch).astype(BF16)
        for j in range(width // LANES):
            begin = (tower * (width // LANES) + j) * LANES
            put(d_out.at[m], d_out.shape[3], begin, grad[:, j * LANES : (j + 1) * LANES])
        mix = 0.0
        for j in range(2):
            cut = slice(j * LANES, (j + 1) * LANES)
            mix = mix + nt(branch[:, cut], w_all[m, tower, 3, cut, :])
        dmix.append(mix)
    lane = iota((LANES, LANES), 1)
    line = iota((LANES, LANES), 0)
    pair_s = lax.shift_right_logical(line, shift)
    halves = [lane < DH, lane >= DH]
    own_head = iota((per * heads, LANES), 0) & (heads - 1)
    own_pair = lax.shift_right_logical(iota((per * heads, LANES), 0), heads.bit_length() - 1)
    token_pair = lax.shift_right_logical(iota((per * heads, LANES), 1), shift)
    for g in range(groups):
        rows = slice(g * LANES, (g + 1) * LANES)
        live_s = (line & (slots - 1)) < chain(pair_s, every[g * per : (g + 1) * per])
        scale = jnp.where(live_s, 0.125, 0.0)
        dots = jnp.zeros((per * heads, LANES), F32)
        stacks = []
        for m in range(parts):
            cut = dmix[m][g * per : (g + 1) * per]
            spread = jnp.concatenate([jnp.broadcast_to(cut[k : k + 1], (heads, LANES)) for k in range(per)], 0)
            head = iota((per * heads, LANES), 1) // DH + 2 * m
            stack = jnp.where(own_head == head, spread, 0.0).astype(BF16)
            stacks.append(stack)
            dots = dots + nt(stack, qkv[tower, 2 * parts + m, rows, :])
        dots = jnp.where(own_pair == token_pair, dots, 0.0)
        pull = dots[0:heads]
        for k in range(1, per):
            pull = pull + dots[k * heads : (k + 1) * heads]
        for m in range(parts):
            query, key = qkv[tower, m, rows, :], qkv[tower, parts + m, rows, :]
            none = jnp.zeros_like(query)
            pulls = []
            for half in range(2):
                h = 2 * m + half
                p = prob[tower, g, h].astype(F32)
                t = p * pull[h : h + 1, :]
                pulls.append(((t - p * jnp.sum(t, 1, keepdims=True)) * scale).astype(BF16))
            keys = jnp.concatenate([jnp.where(side, key, none) for side in halves], 0)
            queries = jnp.concatenate([jnp.where(side, query, none) for side in halves], 0)
            dq = nn(jnp.concatenate(pulls, 1), keys)
            dk = tn(jnp.concatenate(pulls, 0), queries)
            dqkv[m, rows, :] = dq.astype(BF16)
            dqkv[parts + m, rows, :] = dk.astype(BF16)
            dqkv[2 * parts + m, rows, :] = tn(a_in[tower, g], stacks[m]).astype(BF16)
    normed = normed_in[tower]
    dnormed = jnp.zeros((tokens, width), F32)
    for (c, m), (d, n) in two_by_two(parts):
        both = jnp.concatenate([dqkv[c * parts + m], dqkv[d * parts + n]], 1)
        dnormed = dnormed + nt(both, jnp.concatenate([w_all[m, tower, c], w_all[n, tower, d]], 1))
        both = tn(normed, both).astype(BF16)
        put(d_qkv.at[m], d_qkv.shape[3], (tower * 3 + c) * width, both[:, :LANES])
        put(d_qkv.at[n], d_qkv.shape[3], (tower * 3 + d) * width, both[:, LANES:])
    dnormed = dnormed.astype(BF16).astype(F32)
    xs = x[tower]
    w = w_in[tower].astype(BF16)
    hidden = nn(xs, w)
    inverse = lax.rsqrt(jnp.mean(hidden * hidden, -1, keepdims=True) + EPS)
    unit = hidden * inverse
    grad = jnp.sum(dnormed * unit, 0, keepdims=True)
    for j in range(width // LANES):
        r = tower * (width // LANES) + j
        d_gain[r : r + 1, :] = grad[:, j * LANES : (j + 1) * LANES]
    scaled = dnormed * gain[tower : tower + 1, :]
    dh = inverse * (scaled - unit * jnp.mean(scaled * unit, -1, keepdims=True))
    spread = jnp.broadcast_to(dsum[:, None, :], (pairs, slots, width))
    slot = iota((pairs, slots, width), 1)
    counts = chain(iota((pairs, slots, width), 0), every)
    spread = jnp.where(slot < counts, spread, 0.0).reshape(tokens, width)
    dhidden = (spread + dh).astype(BF16)
    grad = tn(xs, dhidden).astype(BF16)
    for j in range(width // LANES):
        begin = (tower * (width // LANES) + j) * xs.shape[1]
        put(d_in, d_in.shape[2], begin, grad[:, j * LANES : (j + 1) * LANES])
    demb[...] = nt(dhidden, w).astype(BF16)


def gelu_parts(v):
    c = 0.7978845608028654
    inner = jnp.tanh(c * (v + 0.044715 * (v * v * v)))
    value = 0.5 * v * (1.0 + inner)
    slope = 0.5 * (1.0 + inner) + 0.5 * v * (1.0 - inner * inner) * (c * (1.0 + 3.0 * 0.044715 * (v * v)))
    return value, slope


def upper_layers(
    me,
    part,
    plane,
    line,
    pooled,
    log_prior,
    item_qid,
    lists,
    positive,
    dpooled,
    d_one,
    d_two,
    d_three,
    loss,
    pooled_all,
    second_send,
    second_got,
    vec,
    dsec_send,
    dsec_all,
    dpool_send,
    dpool_got,
    out_sems,
    in_sems,
    vec_out,
    vec_in,
    w_one,
    w_two,
    w_three,
    loads,
    second_mine,
    dpool_mine,
    prior_col,
):
    towers, own, width = pooled.shape
    per = lists.shape[1] - 8
    rows = own * line
    pairs = rows * plane
    peers = [lax.rem(part + k, line) for k in range(1, line)]

    pooled_all[:, part] = pooled[...]
    first = [
        send(pooled_all.at[:, part], pooled_all.at[:, part], out_sems.at[0, k], in_sems.at[0, k], (me, peers[k]))
        for k in range(line - 1)
    ]
    for copy in loads:
        copy.wait()
    one = [w_one[t].astype(BF16) for t in range(towers)]
    two = [w_two[t].astype(BF16) for t in range(towers)]
    three = [w_three[t].astype(BF16) for t in range(towers)]
    qid = item_qid[...]
    hot = (lax.shift_right_logical(qid, 7) == iota((log_prior.shape[0], pairs), 0)).astype(BF16)
    high, rest = log_prior[...].astype(BF16), log_prior[...]
    rest = rest - high.astype(F32)
    middle, low = split(rest)
    table = tn(high, hot) + tn(middle, hot) + tn(low, hot)
    prior_row = jnp.sum(jnp.where((qid & 127) == iota((LANES, pairs), 0), table, 0.0), 0, keepdims=True)
    prior_col[...] = jnp.transpose(jnp.broadcast_to(prior_row, (8, pairs)), (1, 0))
    pos_row = jnp.concatenate([lists[d, per : per + 1, 0:rows] for d in range(plane)], 1)
    pos_own = chain(iota((own, pairs), 0), [positive[part * own + k] for k in range(own)])
    for copy in first:
        copy.wait()
    act_one, slope_one, pools = [], [], []
    for t in range(towers):
        pools.append(pooled_all[t].reshape(rows, width))
        value, slope = gelu_parts(nn(pools[t], one[t]))
        act_one.append(value.astype(BF16))
        slope_one.append(slope)
        partial = nn(act_one[t], two[t]).reshape(line, own, -1)
        second_mine[t] = partial
        second_send[t] = partial.astype(BF16)
    second = [
        send(
            second_send.at[:, peers[k]], second_got.at[:, part], out_sems.at[1, k], in_sems.at[1, k], (me, peers[k])
        )
        for k in range(line - 1)
    ]
    for copy in second:
        copy.wait()
    act_two, slope_two, third, length, vectors = [], [], [], [], []
    for t in range(towers):
        total = second_mine[t, part]
        for peer in peers:
            total = total + second_got[t, peer].astype(F32)
        value, slope = gelu_parts(total)
        act_two.append(value.astype(BF16))
        slope_two.append(slope)
        third.append(nn(act_two[t], three[t]))
        length.append(lax.rsqrt(jnp.sum(third[t] * third[t], -1, keepdims=True) + EPS))
        vectors.append((third[t] * length[t]).astype(BF16))
        vec[t, me, part] = vectors[t]
    along = [
        send(vec.at[:, me, part], vec.at[:, me, part], out_sems.at[2, k], in_sems.at[2, k], (me, peers[k]))
        for k in range(line - 1)
    ]
    for copy in along:
        copy.wait()
    chips = plane // 2
    core = lax.rem(me, 2)
    chip = me // 2
    sibling = me + 1 - 2 * core
    near = [send(vec.at[:, me], vec.at[:, me], vec_out.at[0], vec_in.at[0], (sibling, part))]
    across = []
    for k in range(1, chips):
        other = 2 * lax.rem(chip + k, chips) + core
        across.append(send(vec.at[:, me], vec.at[:, me], vec_out.at[k], vec_in.at[k], (other, part)))
    for k in range(1, chips):
        peer = 2 * lax.rem(chip - k + chips, chips) + core
        across[k - 1].wait_recv()
        sems = vec_out.at[chips + k], vec_in.at[chips + k]
        near.append(send(vec.at[:, peer], vec.at[:, peer], *sems, (sibling, part)))
    for copy in across:
        copy.wait_send()
    for copy in near:
        copy.wait()

    queries = vec[0].reshape(pairs, width)
    items = vec[1].reshape(pairs, width)
    logits = INV_TEMP * nt(items, queries) - prior_col[:, 0:1]
    peak = jnp.max(logits, 0, keepdims=True)
    log_total = peak + jnp.log(jnp.sum(jnp.exp(logits - peak), 0, keepdims=True))
    picked = jnp.where(iota((pairs, pairs), 0) == pos_row, logits, 0.0)
    gap = log_total - jnp.sum(picked, 0, keepdims=True)
    loss[0, 0] = jnp.sum(gap)
    ahead = me * rows + part * own
    mine = INV_TEMP * nt(vectors[0], items) - prior_row
    top = jnp.max(mine, 1, keepdims=True)
    expo = jnp.exp(mine - top)
    chance = expo / jnp.sum(expo, 1, keepdims=True)
    target = (iota(mine.shape, 1) == pos_own).astype(F32)
    dlog = ((chance - target) / pairs).astype(BF16)
    dvec = [(INV_TEMP * nn(dlog, items)).astype(BF16)]
    own_prior = prior_col[pl.ds(pl.multiple_of(ahead, own), own), 0:1]
    theirs = INV_TEMP * nt(vectors[1], queries) - own_prior
    target = (iota(theirs.shape, 0) + ahead == pos_row).astype(F32)
    dlog = ((jnp.exp(theirs - log_total) - target) / pairs).astype(BF16)
    dvec.append((INV_TEMP * nn(dlog, queries)).astype(BF16))

    dthirds = []
    for t in range(towers):
        dv = dvec[t].astype(F32)
        inner = jnp.sum(dv * third[t], -1, keepdims=True)
        dthird = (length[t] * dv - third[t] * (length[t] * length[t] * length[t] * inner)).astype(BF16)
        dact = nt(dthird, three[t]).astype(BF16).astype(F32)
        dsec_all[t, part] = (dact * slope_two[t]).astype(BF16)
        dthirds.append(dthird)
    spread = [
        send(dsec_all.at[:, part], dsec_all.at[:, part], out_sems.at[3, k], in_sems.at[3, k], (me, peers[k]))
        for k in range(line - 1)
    ]
    for t in range(towers):
        grad = tn(act_two[t], dthirds[t]).astype(BF16)
        for j in range(width // LANES):
            put(d_three, d_three.shape[2], (t * (width // LANES) + j) * grad.shape[0], grad[:, j * LANES : (j + 1) * LANES])
    for copy in spread:
        copy.wait()
    dfirsts = []
    for t in range(towers):
        dsecond = dsec_all[t].reshape(rows, -1)
        dact = nt(dsecond, two[t]).astype(BF16).astype(F32)
        dfirst = (dact * slope_one[t]).astype(BF16)
        partial = nt(dfirst, one[t]).reshape(line, own, width)
        dpool_mine[t] = partial
        dpool_send[t] = partial.astype(BF16)
        dfirsts.append(dfirst)
    back = [
        send(dpool_send.at[:, peers[k]], dpool_got.at[:, part], out_sems.at[4, k], in_sems.at[4, k], (me, peers[k]))
        for k in range(line - 1)
    ]
    for t in range(towers):
        dsecond = dsec_all[t].reshape(rows, -1)
        for grads, grad in ((d_two, tn(act_one[t], dsecond)), (d_one, tn(pools[t], dfirsts[t]))):
            grad = grad.astype(BF16)
            wide = grad.shape[1] // LANES
            for j in range(wide):
                begin = (t * wide + j) * grad.shape[0]
                put(grads, grads.shape[2], begin, grad[:, j * LANES : (j + 1) * LANES])
    for copy in back:
        copy.wait()
    for t in range(towers):
        total = dpool_mine[t, part]
        for peer in peers:
            total = total + dpool_got[t, peer].astype(F32)
        dpooled[t] = total.astype(BF16)


def towers_kernel(
    plane,
    line,
    slots,
    cnt,
    x,
    w_in,
    gain,
    w_all,
    far_one,
    far_two,
    far_three,
    log_prior,
    item_qid,
    lists,
    positive,
    out,
    summed,
    gain_sum,
    loss,
    pooled,
    pm,
    normed,
    qkv,
    prob,
    a_in,
    pm_acc,
    upper_scratch,
    w_one,
    w_two,
    w_three,
    load_sems,
    dpooled,
    d_three,
    d_one,
    d_two,
    d_qkv,
    d_out,
    d_in,
    d_gain,
    dqkv,
    near_split,
    near_whole,
    half,
    got,
    got_late,
    gains,
    far_out,
    far_in,
    near_out,
    near_in,
    sum_out,
    sum_in,
    gain_out,
    gain_in,
):
    loads = [
        pltpu.make_async_copy(source, target, load_sems.at[j])
        for j, (source, target) in enumerate(((far_one, w_one), (far_two, w_two), (far_three, w_three)))
    ]
    for copy in loads:
        copy.start()
    me, part = announce(plane, line)
    for t in range(x.shape[0]):
        forward_tower(t, slots, cnt, x, w_in, gain, w_all, pooled, pm, normed, qkv, prob, a_in, pm_acc)
    await_others(plane, line)
    upper_layers(
        me,
        part,
        plane,
        line,
        pooled,
        log_prior,
        item_qid,
        lists,
        positive,
        dpooled,
        d_one,
        d_two,
        d_three,
        loss,
        *upper_scratch[:-3],
        w_one,
        w_two,
        w_three,
        loads,
        *upper_scratch[-3:],
    )
    chips = plane // 2
    core = lax.rem(me, 2)
    chip = me // 2
    sibling = me + 1 - 2 * core
    towers, tokens = x.shape[:2]
    late, early = (d_in,), (d_three, d_one, d_two)
    nears = [send(grad.at[:, 1 - core], near_whole[1 + j], near_out.at[j], near_in.at[j], (sibling, part)) for j, grad in enumerate(early)]
    copies = []

    def tower(t):
        demb = out.at[part, t * tokens : (t + 1) * tokens]
        backward_tower(
            t, slots, cnt, x, w_in, gain, w_all, normed, qkv, prob, a_in, pm, dpooled, demb, d_in, d_gain, d_qkv, d_out, dqkv
        )
        for k in range(1, line):
            peer = lax.rem(part + k, line)
            copies.append(send(demb, demb, far_out.at[t, k], far_in.at[t, k], (me, peer)))

    def whole(c, at, grad, near):
        rows = grad.shape[2]
        half[c, at : at + rows, :] = (grad[c, core].astype(F32) + near[c].astype(F32)).astype(BF16)
        return at + rows

    def exchange(begin, end, target, sems):
        sums = []
        for k in range(1, chips):
            to = lax.rem(chip + k, chips)
            source = half.at[to, begin:end]
            sums.append(send(source, target.at[k - 1], sum_out.at[sems, k], sum_in.at[sems, k], (2 * to + core, part)))
        return sums

    def collect(begin, end, target, sums):
        for copy in sums:
            copy.wait()
        total = half[chip, begin:end, :].astype(F32)
        for k in range(chips - 1):
            total = total + target[k].astype(F32)
        summed[begin:end, :] = total.astype(BF16)

    first = line * (d_qkv.shape[3] + d_out.shape[3]) + d_in.shape[2]
    d_gain[...] = jnp.zeros_like(d_gain)
    tower(0)
    for copy in nears:
        copy.wait()
    for c in range(chips):
        at = first
        for j, grad in enumerate(early):
            at = whole(c, at, grad, near_whole[1 + j])
    last = at
    sums = exchange(first, last, got, 0)
    for t in range(1, towers):
        tower(t)
    nears = []
    for j, grad in enumerate((d_qkv, d_out)):
        nears.append(send(grad.at[:, :, 1 - core], near_split[j], near_out.at[3 + j], near_in.at[3 + j], (sibling, part)))
    nears.append(send(d_in.at[:, 1 - core], near_whole[0], near_out.at[5], near_in.at[5], (sibling, part)))
    for k in range(1, plane):
        peer = lax.rem(me + k, plane)
        copies.append(send(d_gain, gains.at[me], gain_out.at[k], gain_in.at[k], (peer, part)))
    gains[me] = d_gain[...]
    for copy in nears:
        copy.wait()
    for c in range(chips):
        at = 0
        for grad, near in zip((d_qkv, d_out), near_split):
            rows = grad.shape[3]
            for m in range(line):
                total = grad[m, c, core].astype(F32) + near[m, c].astype(F32)
                half[c, at : at + rows, :] = total.astype(BF16)
                at += rows
        whole(c, at, d_in, near_whole[0])
    late_sums = exchange(0, first, got_late, 1)
    collect(first, last, got, sums)
    collect(0, first, got_late, late_sums)
    for copy in copies:
        copy.wait()
    total = gains[0]
    for d in range(1, plane):
        total = total + gains[d]
    gain_sum[...] = total


def update(weight, grad, moment, average, factor, rate):
    clipped = grad * factor
    moment_new = MOMENTUM * moment + clipped
    weight_new = weight - rate * (clipped + MOMENTUM * moment_new)
    average_new = AVERAGE_DECAY * average + (1.0 - AVERAGE_DECAY) * weight_new
    return [weight_new, moment_new, average_new]


def update_kernel(blocks, norm_sq, table_grad, dense, gain, *refs):
    arrays = 3 * 8
    sources, targets, norm = refs[:arrays], refs[arrays : 2 * arrays], refs[2 * arrays]
    held, in_sems, out_sems = refs[2 * arrays + 1 : 3 * arrays + 1], refs[-2], refs[-1]
    loads = [pltpu.make_async_copy(sources[k], held[k], in_sems.at[k]) for k in range(arrays)]
    starts = {}
    for k, size, _, _ in blocks:
        starts[k] = sum(other[1] for other in blocks[: k - 1])
    order = sorted(blocks, key=lambda block: -block[1])
    for k in [0] + [block[0] for block in order] + [arrays // 3 - 1]:
        for copy in loads[3 * k : 3 * k + 3]:
            copy.start()
    root = jnp.sqrt(norm_sq[...])
    norm[0, 0] = jnp.max(root)
    factor = jnp.minimum(1.0, CLIP_NORM / root[0:1, :])
    stores = []

    def finish(k):
        for j in range(3 * k, 3 * k + 3):
            copy = pltpu.make_async_copy(held[j], targets[j], out_sems.at[j])
            copy.start()
            stores.append(copy)

    def apply(k, rows, lanes, grad, rate):
        cells = [ref.at[rows, lanes] for ref in held[3 * k : 3 * k + 3]]
        new = update(cells[0][...], grad, cells[1][...], cells[2][...], factor, rate)
        for cell, value in zip(cells, new):
            cell[...] = value

    def wait(k):
        for copy in loads[3 * k : 3 * k + 3]:
            copy.wait()

    def rows(i, carry):
        at = pl.ds(pl.multiple_of(i * 64, 64), 64)
        apply(0, at, slice(0, LANES), table_grad[at, :], ROW_RATE)
        return carry

    wait(0)
    lax.fori_loop(0, table_grad.shape[0] // 64, rows, 0, unroll=2)
    finish(0)
    for k, size, height, wide in order:
        wait(k)
        at = starts[k]
        total = dense.shape[0] * size
        step = math.gcd(size, 64)
        for first in range(0, total, min(size, height)):
            count = min(size, height)
            share, inside = first // size, first % size
            block, begin = first // height, first % height
            t, j = block // wide, block % wide
            top = t * height + begin

            def piece(i, carry):
                take = pl.ds(pl.multiple_of(at + inside + i * step, 16), step)
                rows = pl.ds(pl.multiple_of(top + i * step, 16), step)
                grad = dense[share, take, :].astype(F32)
                apply(k, rows, slice(j * LANES, (j + 1) * LANES), grad, MATRIX_RATE)
                return carry

            lax.fori_loop(0, count // step, piece, 0, unroll=2)
        finish(k)
    last = 7
    wait(last)
    for t in range(held[3 * last].shape[0]):
        for j in range(held[3 * last].shape[1] // LANES):
            r = t * (held[3 * last].shape[1] // LANES) + j
            apply(last, slice(t, t + 1), slice(j * LANES, (j + 1) * LANES), gain[r : r + 1, :], GAIN_RATE)
    finish(last)
    for copy in stores:
        copy.wait()


def shards(
    slot_owner,
    slot_row,
    slot_count,
    item_qid,
    positive,
    log_prior,
    embedding,
    embedding_mom,
    embedding_avg,
    w_in,
    w_in_mom,
    w_in_avg,
    norm_gain,
    norm_gain_mom,
    norm_gain_avg,
    w_qkv,
    w_qkv_mom,
    w_qkv_avg,
    w_out,
    w_out_mom,
    w_out_avg,
    w_one,
    w_one_mom,
    w_one_avg,
    w_two,
    w_two_mom,
    w_two_avg,
    w_three,
    w_three_mom,
    w_three_avg,
):
    plane = lax.axis_size("dp")
    line = lax.axis_size("mp")
    batch, towers, slots = slot_row.shape
    own = batch // line
    requests = batch * towers * slots
    own_requests = requests // line
    tokens = own * slots
    capacity = max(LANES, 2 * requests // plane)
    pairs = batch * plane
    part = lax.axis_index("mp")
    me = lax.axis_index("dp")
    width = w_in.shape[2]
    depth = w_in.shape[1]
    units = w_one.shape[2]
    seconds = w_two.shape[2]

    per = capacity // LANES
    small = capacity // 4
    dims = (towers, own, slots)

    def row_scratch(count):
        return [
            pltpu.VMEM((plane, count, depth), BF16),
            pltpu.VMEM((plane, count, depth), BF16),
            pltpu.VMEM((plane * count, depth), F32),
        ]

    turned = jnp.transpose(w_qkv, (0, 2, 1, 3))
    embedded, got_own, got_lists, weights, inverse, own_place = pl.pallas_call(
        functools.partial(fetch_kernel, plane, line, dims, capacity),
        out_shape=[
            shape((own_requests, depth), BF16),
            shape((plane, per, LANES), I32),
            shape((plane, per + 8, LANES), I32),
            shape((line, towers, 4, width, LANES), BF16),
            shape((plane * per, LANES), I32),
            shape((slots, LANES), I32),
        ],
        in_specs=[VMEM] * 4 + [HBM] * 3,
        out_specs=[VMEM] * 6,
        scratch_shapes=[
            pltpu.VMEM((plane, per, LANES), I32),
            pltpu.VMEM((slots, LANES), I32),
            pltpu.VMEM((plane, per + 8, LANES), I32),
            pltpu.VMEM(embedding.shape, F32),
            pltpu.VMEM(turned.shape, F32),
            pltpu.VMEM(w_out.shape, F32),
            pltpu.SMEM((slots, LANES), I32),
            pltpu.SMEM((plane, -(-small // LANES), LANES), I32),
            *row_scratch(small),
            DMA((2, plane)),
            DMA((2, plane)),
            DMA((plane,)),
            DMA((plane,)),
            DMA((line,)),
            DMA((line,)),
            DMA((line,)),
            DMA((line,)),
            DMA((2, line)),
            DMA((2, line)),
            DMA((4,)),
            DMA((3,)),
        ],
        compiler_params=params(60, collective_id=2, has_side_effects=True),
        name="fetch",
    )(
        jnp.transpose(slot_owner[..., 0], (1, 2, 0)),
        jnp.transpose(slot_row, (1, 2, 0)),
        jnp.transpose(slot_count),
        positive.reshape(1, batch),
        embedding,
        turned,
        w_out,
    )
    most = jnp.max(got_lists[:, per + 1 : per + 3, 0], 0)

    def refetch(ids, place, table, _):
        return pl.pallas_call(
            functools.partial(refetch_kernel, plane, dims),
            out_shape=shape((own_requests, depth), BF16),
            in_specs=[SMEM, SMEM, VMEM],
            out_specs=VMEM,
            scratch_shapes=[*row_scratch(capacity), DMA((plane,)), DMA((plane,))],
            compiler_params=params(16, collective_id=7, has_side_effects=True),
            name="refetch",
        )(ids, place, table)

    embedded = lax.cond(most[0] > small, refetch, lambda *given: given[3], got_own, own_place, embedding, embedded)
    embedded = embedded.reshape(towers, tokens, depth)

    counts = jnp.transpose(slot_count)
    heads = 2 * line
    groups = tokens // LANES
    per_group = LANES // slots
    totals = (towers * 3 * width, towers * width, towers * depth * width // LANES)
    totals += tuple(towers * size // LANES for size in (seconds * width, width * units, units * seconds))
    sizes = [total // plane for total in totals]
    held = lambda size: pltpu.VMEM((plane // 2, 2, size, LANES), BF16)
    share = line * (sizes[0] + sizes[1]) + sum(sizes[2:])
    early = sum(sizes[3:])
    every, summed, gain_sum, loss = pl.pallas_call(
        functools.partial(towers_kernel, plane, line, slots),
        out_shape=[
            shape((line, own_requests, depth), BF16),
            shape((share, LANES), BF16),
            shape((8, LANES), F32),
            shape((1, 1), F32),
        ],
        in_specs=[SMEM] + [VMEM] * 4 + [HBM] * 3 + [VMEM] * 3 + [SMEM],
        out_specs=[VMEM] * 3 + [SMEM],
        scratch_shapes=[
            pltpu.VMEM((towers, own, width), BF16),
            pltpu.VMEM((towers, own, line * LANES), BF16),
            pltpu.VMEM((towers, tokens, width), BF16),
            pltpu.VMEM((towers, 3 * line, tokens, LANES), BF16),
            pltpu.VMEM((towers, groups, heads, LANES, LANES), BF16),
            pltpu.VMEM((towers, groups, per_group * heads, LANES), BF16),
            pltpu.VMEM((groups, per_group, line * LANES), F32),
            [
                pltpu.VMEM((towers, line, own, width), BF16),
                pltpu.VMEM((towers, line, own, seconds), BF16),
                pltpu.VMEM((towers, line, own, seconds), BF16),
                pltpu.VMEM((towers, plane, line, own, width), BF16),
                pltpu.VMEM((towers, line, own, seconds), BF16),
                pltpu.VMEM((towers, line, own, seconds), BF16),
                pltpu.VMEM((towers, line, own, width), BF16),
                pltpu.VMEM((towers, line, own, width), BF16),
                DMA((5, line)),
                DMA((5, line)),
                DMA((plane,)),
                DMA((plane,)),
                pltpu.VMEM((towers, line, own, seconds), F32),
                pltpu.VMEM((towers, line, own, width), F32),
                pltpu.VMEM((pairs, 8), F32),
            ],
            pltpu.VMEM(w_one.shape, F32),
            pltpu.VMEM(w_two.shape, F32),
            pltpu.VMEM(w_three.shape, F32),
            DMA((3,)),
            pltpu.VMEM((towers, own, width), BF16),
            held(sizes[3]),
            held(sizes[4]),
            held(sizes[5]),
            pltpu.VMEM((line, plane // 2, 2, sizes[0], LANES), BF16),
            pltpu.VMEM((line, plane // 2, 2, sizes[1], LANES), BF16),
            held(sizes[2]),
            pltpu.VMEM((8, LANES), F32),
            pltpu.VMEM((3 * line, tokens, LANES), BF16),
            [pltpu.VMEM((line, plane // 2, size, LANES), BF16) for size in sizes[:2]],
            [pltpu.VMEM((plane // 2, size, LANES), BF16) for size in sizes[2:]],
            pltpu.VMEM((plane // 2, share, LANES), BF16),
            pltpu.VMEM((plane // 2 - 1, early, LANES), BF16),
            pltpu.VMEM((plane // 2 - 1, share - early, LANES), BF16),
            pltpu.VMEM((plane, 8, LANES), F32),
            DMA((towers, line)),
            DMA((towers, line)),
            DMA((6,)),
            DMA((6,)),
            DMA((2, plane // 2)),
            DMA((2, plane // 2)),
            DMA((plane,)),
            DMA((plane,)),
        ],
        compiler_params=params(60, collective_id=4, has_side_effects=True),
        name="towers",
    )(
        counts,
        embedded,
        w_in,
        norm_gain,
        weights,
        w_one,
        w_two,
        w_three,
        log_prior.reshape(-1, LANES),
        item_qid.reshape(1, pairs),
        got_lists,
        positive,
    )
    whole_at = line * (sizes[0] + sizes[1])
    whole_rows = sizes[2] + sizes[3]
    last_rows = sizes[4] + sizes[5]
    cuts = (
        ((0, sizes[0]), (line * sizes[0], sizes[1])),
        (whole_at, whole_rows),
        (whole_at + whole_rows, last_rows),
    )
    line_rows = sizes[0] + sizes[1] + whole_rows

    def tail(count, number):
        return lambda *given: pl.pallas_call(
            functools.partial(tail_kernel, plane, line, count, cuts),
            out_shape=[
                shape(embedding.shape, F32),
                shape((plane, line_rows + last_rows, LANES), BF16),
                shape((8, LANES), F32),
                shape((8, LANES), F32),
            ],
            in_specs=[SMEM] + [VMEM] * 4,
            out_specs=[VMEM] * 4,
            scratch_shapes=[
                pltpu.VMEM((requests, depth), F32),
                pltpu.VMEM((plane, count, depth), BF16),
                pltpu.VMEM((plane, count, depth), BF16),
                pltpu.VMEM((embedding.shape[0] // 2, 2 * depth), F32),
                pltpu.VMEM((line, line_rows, LANES), BF16),
                pltpu.VMEM((line, 8, LANES), F32),
                pltpu.VMEM((line, 8, LANES), F32),
                pltpu.VMEM((plane, 8, LANES), F32),
                DMA((plane,)),
                DMA((plane,)),
                DMA((3, line)),
                DMA((3, line)),
                DMA((line,)),
                DMA((line,)),
                DMA((line,)),
                DMA((line,)),
                DMA((plane,)),
                DMA((plane,)),
                DMA((2, plane // 2)),
                DMA((2, plane // 2)),
                DMA((2, plane // 2)),
                DMA((2, plane // 2)),
            ],
            compiler_params=params(36, collective_id=number, has_side_effects=True),
            name="tail",
        )(given[0][:, : -(-count // LANES)], *given[1:])

    medium = capacity * 5 // 8
    table_grad, dense_all, norm_sq, gain_all = lax.cond(
        most[1] > medium,
        tail(capacity, 8),
        tail(medium, 5),
        inverse.reshape(plane, per, LANES),
        got_lists,
        every.reshape(requests, depth),
        summed,
        gain_sum,
    )
    flat = lambda w: w.reshape(-1, w.shape[-1])
    turn = lambda w: flat(jnp.transpose(w, (0, 2, 1, 3)))
    given = [embedding, embedding_mom, embedding_avg]
    given += [turn(w) for w in (w_qkv, w_qkv_mom, w_qkv_avg)]
    rest = (w_out, w_out_mom, w_out_avg, w_in, w_in_mom, w_in_avg, w_three, w_three_mom, w_three_avg)
    rest += (w_one, w_one_mom, w_one_avg, w_two, w_two_mom, w_two_avg)
    given += [flat(w) for w in rest]
    given += [norm_gain, norm_gain_mom, norm_gain_avg]
    heights = (towers * 3 * width, LANES, depth, seconds, width, units)
    wides = (1, width // LANES, width // LANES, width // LANES, units // LANES, seconds // LANES)
    blocks = tuple((k + 1, size, height, wide) for k, (size, height, wide) in enumerate(zip(sizes, heights, wides)))
    *done, norm = pl.pallas_call(
        functools.partial(update_kernel, blocks),
        out_shape=[shape(w.shape, F32) for w in given] + [shape((1, 1), F32)],
        in_specs=[VMEM] * 4 + [HBM] * len(given),
        out_specs=[HBM] * len(given) + [SMEM],
        scratch_shapes=[pltpu.VMEM(w.shape, F32) for w in given] + [DMA((len(given),))] * 2,
        compiler_params=params(57),
        name="update",
    )(norm_sq, table_grad, dense_all, gain_all, *given)
    back = lambda k, w: [done[3 * k + j].reshape(w.shape) for j in range(3)]
    unturned = [
        jnp.transpose(w.reshape(towers, 3, width, LANES), (0, 2, 1, 3)) for w in done[3:6]
    ]
    new = done[:3] + back(3, w_in) + done[21:24] + unturned + back(2, w_out) + back(5, w_one) + back(6, w_two)
    return (loss.reshape(()), norm.reshape(()), *new, *back(4, w_three))


def solution(mesh):
    rows = P("dp", None)
    qkv = P(None, None, None, "mp")
    deep = P(None, "mp", None)
    wide = P(None, None, "mp")
    weights = (rows,) * 3 + (P(),) * 6 + (qkv,) * 3 + (deep,) * 3 + (wide,) * 3 + (deep,) * 3 + (P(),) * 3
    inputs = (P("dp", None, None, None), P("dp", None, None), P("dp", None), P(), P("dp"), P())
    return jax.shard_map(
        shards, mesh=mesh, in_specs=inputs + weights, out_specs=(P(), P()) + weights, check_vma=False
    )
```
